32 devices in a mesh: dp: 8 (over y, x, core), mp: 4 (over z).
Axes of the slice: x: 2, y: 2, z: 4, core: 2. Of those that a mesh axis runs over, the one named last changes fastest.
Arguments:
- inputs: bfloat16 [16384, 1024], P(('dp', 'mp')), may hold values from -6 to 6
- documents: int32 [16, 1024], P('dp'), may hold values from 0 to 3, never falling along the last dimension, each value on 1 to 512 neighbouring positions
- cotangent: bfloat16 [16384, 1024], P(('dp', 'mp')), may hold values from -7.5 to 7.5
- qkv_weight: float32 [2, 1024, 3, 1024], P(None, 'dp', None, 'mp'), may hold values from -0.1875 to 0.1875
- qkv_moment: float32 [2, 1024, 3, 1024], P(None, 'dp', None, 'mp'), may hold values from -5.6969053e-05 to 5.6969053e-05
- qkv_square: float32 [2, 1024, 3, 1024], P(None, 'dp', None, 'mp'), may hold values from 3.7252904e-10 to 1.4901161e-09
- proj_weight: float32 [2, 1024, 1024], P(None, 'mp', 'dp'), may hold values from -0.75 to 0.75
- proj_moment: float32 [2, 1024, 1024], P(None, 'mp', 'dp'), may hold values from -5.6969053e-05 to 5.6969053e-05
- proj_square: float32 [2, 1024, 1024], P(None, 'mp', 'dp'), may hold values from 3.7252904e-10 to 1.4901161e-09
- upper_weight: float32 [2, 1024, 4096], P(None, 'dp', 'mp'), may hold values from -0.1875 to 0.1875
- upper_moment: float32 [2, 1024, 4096], P(None, 'dp', 'mp'), may hold values from -9.840109e-05 to 9.840109e-05
- upper_square: float32 [2, 1024, 4096], P(None, 'dp', 'mp'), may hold values from 1.1175871e-09 to 4.4703485e-09
- lower_weight: float32 [2, 4096, 1024], P(None, 'mp', 'dp'), may hold values from -0.09375 to 0.09375
- lower_moment: float32 [2, 4096, 1024], P(None, 'mp', 'dp'), may hold values from -0.00020198118 to 0.00020198118
- lower_square: float32 [2, 4096, 1024], P(None, 'mp', 'dp'), may hold values from 4.4703485e-09 to 1.7881394e-08
- hidden_bias: float32 [2, 4096], P(None, ('mp', 'dp')), may hold values from -3 to 3
- bias_moment: float32 [2, 4096], P(None, ('mp', 'dp')), may hold values from -9.840109e-05 to 9.840109e-05
- bias_square: float32 [2, 4096], P(None, ('mp', 'dp')), may hold values from 1.1175871e-09 to 4.4703485e-09
- norm_gains: float32 [2, 2, 1024], P(None, None, 'dp'), may hold values from 0.2 to 2.2
- gains_moment: float32 [2, 2, 1024], P(None, None, 'dp'), may hold values from -0.00028484527 to 0.00028484527
- gains_square: float32 [2, 2, 1024], P(None, None, 'dp'), may hold values from 9.313226e-09 to 3.7252903e-08
- shift_params: float32 [2, 3, 1024], P(None, None, 'dp'), may hold values from -1.2 to 1.2
- shifts_moment: float32 [2, 3, 1024], P(None, None, 'dp'), may hold values from -0.00028484527 to 0.00028484527
- shifts_square: float32 [2, 3, 1024], P(None, None, 'dp'), may hold values from 9.313226e-09 to 3.7252903e-08
Outputs:
- output_stream: float32 [16384, 1024], P(('dp', 'mp'))
- input_grad: float32 [16384, 1024], P(('dp', 'mp'))
- qkv_weight_new: float32 [2, 1024, 3, 1024], P(None, 'dp', None, 'mp')
- qkv_moment_new: float32 [2, 1024, 3, 1024], P(None, 'dp', None, 'mp')
- qkv_square_new: float32 [2, 1024, 3, 1024], P(None, 'dp', None, 'mp')
- proj_weight_new: float32 [2, 1024, 1024], P(None, 'mp', 'dp')
- proj_moment_new: float32 [2, 1024, 1024], P(None, 'mp', 'dp')
- proj_square_new: float32 [2, 1024, 1024], P(None, 'mp', 'dp')
- upper_weight_new: float32 [2, 1024, 4096], P(None, 'dp', 'mp')
- upper_moment_new: float32 [2, 1024, 4096], P(None, 'dp', 'mp')
- upper_square_new: float32 [2, 1024, 4096], P(None, 'dp', 'mp')
- lower_weight_new: float32 [2, 4096, 1024], P(None, 'mp', 'dp')
- lower_moment_new: float32 [2, 4096, 1024], P(None, 'mp', 'dp')
- lower_square_new: float32 [2, 4096, 1024], P(None, 'mp', 'dp')
- hidden_bias_new: float32 [2, 4096], P(None, ('mp', 'dp'))
- bias_moment_new: float32 [2, 4096], P(None, ('mp', 'dp'))
- bias_square_new: float32 [2, 4096], P(None, ('mp', 'dp'))
- norm_gains_new: float32 [2, 2, 1024], P(None, None, 'dp')
- gains_moment_new: float32 [2, 2, 1024], P(None, None, 'dp')
- gains_square_new: float32 [2, 2, 1024], P(None, None, 'dp')
- shift_params_new: float32 [2, 3, 1024], P(None, None, 'dp')
- shifts_moment_new: float32 [2, 3, 1024], P(None, None, 'dp')
- shifts_square_new: float32 [2, 3, 1024], P(None, None, 'dp')
- grad_norm: float32 [], replicated
The draws below stay inside these ranges and needn't reach their ends.
Inputs may be any that keep to these rules, and one draw needn't show every extreme that they name: `documents`: ids never fall along a sequence; a document has at most 512 tokens, and the longest has exactly that many.
All inputs are finite; a program needn't handle non-finite values.
Results may differ from the reference program's by a relative error of at most 0.035.
Values may be sent and summed in bfloat16 or wider, within the bound.
A program may use at most 256 MiB of HBM per device.

```python
import math
import jax
import jax.numpy as jnp
import numpy as np
from jax import lax

D = 1024
H = 8
HD = 128
FF = 4096
LAYERS = 2
LEN = 1024
STEP = 5
NSEQ = 16
TOKENS = 16384


def feature_ramp(low_end):
    steps = jnp.arange(D, dtype=jnp.float32) / (D - 1)
    return low_end + steps


def draw_norm_gains(key, part):
    noise_key = jax.random.fold_in(key, 11)
    ramp = feature_ramp(0.5)
    spread = jax.random.uniform(noise_key, (LAYERS, 2, D), jnp.float32, 0.8, 1.2)
    return (ramp[None, None, :] * spread).astype(jnp.float32)


def draw_cotangent(key, part):
    noise_key = jax.random.fold_in(key, 23)
    ramp = feature_ramp(0.5)
    values = jnp.clip(jax.random.normal(noise_key, (TOKENS, D), jnp.float32), -4.5, 4.5)
    return (values * ramp[None, :]).astype(jnp.bfloat16)


def shard_levels(own_key, dims, cuts, low, high):
    level = 1.0
    for axis_at, parts in cuts:
        heights = jax.random.uniform(jax.random.fold_in(jax.random.fold_in(own_key, 6), axis_at), (parts,), jnp.float32, low / len(cuts), high / len(cuts))
        level = level * jnp.repeat(jnp.exp(heights), dims[axis_at] // parts).reshape((-1,) + (1,) * (len(dims) - 1 - axis_at))
    return level


def length_profile(amount, total, limit, lean):
    portions = [(1 << 20) // math.isqrt(rank ** lean) + 1 for rank in range(2, amount + 1)]
    rest, counts = total - limit - (amount - 1), [1] * (amount - 1)
    while rest > 0:
        free = [i for i in range(amount - 1) if counts[i] < limit]
        whole, left = sum([portions[i] for i in free]), rest
        for i in free:
            more = min(limit - counts[i], max(1, left * portions[i] // whole), rest)
            counts[i] = counts[i] + more
            rest = rest - more
    return np.array([limit] + counts)


def uneven_parts(key, count, total, bound, slope):
    if count == 2:
        one = jax.random.randint(key, (), max(1, total - bound), min(bound, total - 1) + 1)
        return jnp.stack([one, total - one])
    sizes = jnp.asarray(length_profile(count, total, bound, slope), jnp.int32)
    twos = (count - 1) // 2
    donor, receiver = sizes[1:1 + 2 * twos:2], sizes[2:2 + 2 * twos:2]
    margin = jnp.minimum(donor - 1, bound - receiver)
    shifted = jax.random.randint(jax.random.fold_in(key, 1), (twos,), 0, 1 << 20) % (margin + 1)
    sizes = sizes.at[1:1 + 2 * twos:2].set(donor - shifted).at[2:2 + 2 * twos:2].set(receiver + shifted)
    return sizes[jax.random.permutation(jax.random.fold_in(key, 2), count)]


def centred(key, dims, deviation, most, cuts=(), held_as=jnp.bfloat16):
    entries = jax.random.normal(key, dims, jnp.float32) * deviation
    if len(cuts) > 0:
        entries = shard_levels(key, dims, cuts, -0.22, 0.18) * entries
    return jnp.clip(entries, min=-most, max=most).astype(held_as)


def setup_inputs(seed: int = 0) -> dict:
    streams_of = jax.random.split(jax.random.key(seed), 25)
    return {
        "inputs": centred(streams_of[0], (TOKENS, D), 1.0, 6.0, ((0, 32),)),
        "documents": jax.vmap(lambda own: jnp.searchsorted(jnp.cumsum(uneven_parts(own, 4, LEN, LEN // 2, 0)), jnp.arange(LEN), side="right"))(jax.random.split(streams_of[1], NSEQ)).reshape((NSEQ, LEN)).astype(jnp.int32),
        "cotangent": draw_cotangent(jax.random.fold_in(streams_of[24], 71), 0),
        "qkv_weight": centred(streams_of[3], (LAYERS, D, 3, D), D ** -0.5, 0.1875, ((1, 8), (3, 4)), jnp.float32),
        "qkv_moment": centred(streams_of[4], (LAYERS, D, 3, D), (0.11 * (LAYERS * (4 * D * D + 15 * D * FF)) ** -0.5), 5.696905282093212e-05, ((1, 8), (3, 4)), jnp.float32),
        "qkv_square": jnp.clip(jnp.exp(math.log(1.4901161415892261e-09) - 1.3862944 * jax.random.uniform(streams_of[5], (LAYERS, D, 3, D), jnp.float32) ** shard_levels(streams_of[5], (LAYERS, D, 3, D), ((1, 8), (3, 4)), -0.2, 0.2)), 3.7252903539730653e-10, 1.4901161415892261e-09),
        "proj_weight": centred(streams_of[6], (LAYERS, D, D), (D // 16) ** -0.5, 0.75, ((1, 4), (2, 8)), jnp.float32),
        "proj_moment": centred(streams_of[7], (LAYERS, D, D), (0.11 * (LAYERS * (4 * D * D + 15 * D * FF)) ** -0.5), 5.696905282093212e-05, ((1, 4), (2, 8)), jnp.float32),
        "proj_square": jnp.clip(jnp.exp(math.log(1.4901161415892261e-09) - 1.3862944 * jax.random.uniform(streams_of[8], (LAYERS, D, D), jnp.float32) ** shard_levels(streams_of[8], (LAYERS, D, D), ((1, 4), (2, 8)), -0.2, 0.2)), 3.7252903539730653e-10, 1.4901161415892261e-09),
        "upper_weight": centred(streams_of[9], (LAYERS, D, FF), D ** -0.5, 0.1875, ((1, 8), (2, 4)), jnp.float32),
        "upper_moment": centred(streams_of[10], (LAYERS, D, FF), (0.19 * (LAYERS * (4 * D * D + 15 * D * FF)) ** -0.5), 9.840109123615548e-05, ((1, 8), (2, 4)), jnp.float32),
        "upper_square": jnp.clip(jnp.exp(math.log(4.470348535789981e-09) - 1.3862944 * jax.random.uniform(streams_of[11], (LAYERS, D, FF), jnp.float32) ** shard_levels(streams_of[11], (LAYERS, D, FF), ((1, 8), (2, 4)), -0.2, 0.2)), 1.1175871339474952e-09, 4.470348535789981e-09),
        "lower_weight": centred(streams_of[12], (LAYERS, FF, D), FF ** -0.5, 0.09375, ((1, 4), (2, 8)), jnp.float32),
        "lower_moment": centred(streams_of[13], (LAYERS, FF, D), (0.39 * (LAYERS * (4 * D * D + 15 * D * FF)) ** -0.5), 0.00020198118, ((1, 4), (2, 8)), jnp.float32),
        "lower_square": jnp.clip(jnp.exp(math.log(1.7881394143159923e-08) - 1.3862944 * jax.random.uniform(streams_of[14], (LAYERS, FF, D), jnp.float32) ** shard_levels(streams_of[14], (LAYERS, FF, D), ((1, 4), (2, 8)), -0.2, 0.2)), 4.470348535789981e-09, 1.7881394143159923e-08),
        "hidden_bias": centred(streams_of[15], (LAYERS, FF), 0.5, 3.0, ((1, 32),), jnp.float32),
        "bias_moment": centred(streams_of[16], (LAYERS, FF), (0.19 * (LAYERS * (4 * D * D + 15 * D * FF)) ** -0.5), 9.840109123615548e-05, ((1, 32),), jnp.float32),
        "bias_square": jnp.clip(jnp.exp(math.log(4.470348535789981e-09) - 1.3862944 * jax.random.uniform(streams_of[17], (LAYERS, FF), jnp.float32) ** shard_levels(streams_of[17], (LAYERS, FF), ((1, 32),), -0.2, 0.2)), 1.1175871339474952e-09, 4.470348535789981e-09),
        "norm_gains": draw_norm_gains(jax.random.fold_in(streams_of[24], 71), 0),
        "gains_moment": centred(streams_of[19], (LAYERS, 2, D), (0.55 * (LAYERS * (4 * D * D + 15 * D * FF)) ** -0.5), 0.00028484527, ((2, 8),), jnp.float32),
        "gains_square": jnp.clip(jnp.exp(math.log(3.725290298461914e-08) - 1.3862944 * jax.random.uniform(streams_of[20], (LAYERS, 2, D), jnp.float32) ** shard_levels(streams_of[20], (LAYERS, 2, D), ((2, 8),), -0.2, 0.2)), 9.313225746154785e-09, 3.725290298461914e-08),
        "shift_params": centred(streams_of[21], (LAYERS, 3, D), 0.2, 1.2, ((2, 8),), jnp.float32),
        "shifts_moment": centred(streams_of[22], (LAYERS, 3, D), (0.55 * (LAYERS * (4 * D * D + 15 * D * FF)) ** -0.5), 0.00028484527, ((2, 8),), jnp.float32),
        "shifts_square": jnp.clip(jnp.exp(math.log(3.725290298461914e-08) - 1.3862944 * jax.random.uniform(streams_of[23], (LAYERS, 3, D), jnp.float32) ** shard_levels(streams_of[23], (LAYERS, 3, D), ((2, 8),), -0.2, 0.2)), 9.313225746154785e-09, 3.725290298461914e-08),
    }


norm_eps = 1e-05
clip_bound = 1.0
beta_first = 0.9
beta_second = 0.95
adam_eps = 1e-08
masked_score = -1e+30
group_rates = (0.03, 0.12, 0.03, 0.015, 0.3, 0.7, 0.3)
group_decays = (0.1, 0.1, 0.1, 0.1, 0.0, 0.0, 0.0)

@jax.custom_vjp
def low(v):
    return lax.optimization_barrier(v.astype(jnp.bfloat16)).astype(jnp.float32)

@jax.custom_vjp
def low_back(v):
    return v

def low_keep(v):
    return (low(v), None)

def low_pass(kept, grad):
    return (grad,)

def back_keep(v):
    return (v, None)

def back_low(kept, grad):
    return (low(grad),)
low.defvjp(low_keep, low_pass)
low_back.defvjp(back_keep, back_low)

def matmul_high(left, right):
    return jnp.dot(left, right, precision=lax.Precision.HIGHEST, preferred_element_type=jnp.float32)

def gelu_tanh(values):
    return jax.nn.gelu(values, approximate=True)

def layer_norm(values, scale_vec, shift_vec):
    center = values - lax.optimization_barrier(jnp.mean(values, axis=-1, keepdims=True))
    spread = lax.optimization_barrier(jnp.mean(center * center, axis=-1, keepdims=True))
    return center * lax.rsqrt(spread + norm_eps) * scale_vec + shift_vec

def attend_sequence(packed, slopes):
    queries, key_rows, value_rows, doc_rows = packed
    query_heads = jnp.transpose(queries.reshape(LEN, H, HD), (1, 0, 2))
    key_heads = jnp.transpose(key_rows.reshape(LEN, H, HD), (1, 0, 2))
    value_heads = jnp.transpose(value_rows.reshape(LEN, H, HD), (1, 0, 2))
    block_rows = min(512, LEN)
    scale_factor = 1.0 / math.sqrt(HD)
    col_ids = jnp.arange(LEN, dtype=jnp.int32)
    pieces = []
    for first_row in range(0, LEN, block_rows):
        row_ids = first_row + jnp.arange(block_rows, dtype=jnp.int32)
        scores = jnp.einsum('hqd,hkd->hqk', query_heads[:, first_row:first_row + block_rows], key_heads, precision=lax.Precision.HIGHEST) * scale_factor
        distance = (row_ids[:, None] - col_ids[None, :]).astype(jnp.float32)
        scores = scores - slopes[:, None, None] * distance[None]
        allowed = (row_ids[:, None] >= col_ids[None, :]) & (doc_rows[first_row:first_row + block_rows][:, None] == doc_rows[None, :])
        scores = low_back(jnp.where(allowed[None], scores, masked_score))
        probs = low(jax.nn.softmax(scores, axis=-1))
        pieces.append(jnp.einsum('hqk,hkd->hqd', probs, value_heads, precision=lax.Precision.HIGHEST))
    merged = jnp.concatenate(pieces, axis=1)
    return jnp.transpose(merged, (1, 0, 2)).reshape(LEN, H * HD)

def forward(stream, documents, qkv_all, proj_all, upper_all, lower_all, bias_all, gains_all, shifts_all):
    slopes = jnp.asarray(0.5 ** (np.arange(H) + 1.0), dtype=jnp.float32)
    attend_one = jax.checkpoint(lambda packed: attend_sequence(packed, slopes))
    for layer_index in range(LAYERS):
        qkv_low = low(qkv_all[layer_index])
        proj_low = low(proj_all[layer_index])
        upper_low = low(upper_all[layer_index])
        lower_low = low(lower_all[layer_index])
        bias_low = low(bias_all[layer_index])
        gain_rows = low(gains_all[layer_index])
        shift_rows = low(shifts_all[layer_index])
        normed = low(layer_norm(stream, gain_rows[0], shift_rows[0]))
        queries = low_back(low(matmul_high(normed, qkv_low[:, 0, :])))
        key_rows = low_back(low(matmul_high(normed, qkv_low[:, 1, :])))
        value_rows = low_back(low(matmul_high(normed, qkv_low[:, 2, :])))
        attended = lax.map(attend_one, (queries.reshape(-1, LEN, D), key_rows.reshape(-1, LEN, D), value_rows.reshape(-1, LEN, D), documents))
        attended = low_back(low(attended.reshape(-1, D)))
        middle = stream + low_back(matmul_high(attended, proj_low))
        normed_two = low(layer_norm(middle, gain_rows[1], shift_rows[1]))
        hidden = low_back(matmul_high(normed_two, upper_low) + bias_low)
        active = low(gelu_tanh(hidden))
        stream = middle + low_back(matmul_high(active, lower_low)) + shift_rows[2]
    return stream

def adam_update(master, moment, square, gradient, factor, step_rate, decay_rate):
    clipped = gradient * factor
    moment_new = beta_first * moment + (1.0 - beta_first) * clipped
    square_new = beta_second * square + (1.0 - beta_second) * clipped * clipped
    first_hat = moment_new / (1.0 - beta_first ** STEP)
    second_hat = square_new / (1.0 - beta_second ** STEP)
    master_new = master - step_rate * (first_hat / (jnp.sqrt(second_hat) + adam_eps) + decay_rate * master)
    return (master_new, moment_new, square_new)

def reference(inputs, documents, cotangent, qkv_weight, qkv_moment, qkv_square, proj_weight, proj_moment, proj_square, upper_weight, upper_moment, upper_square, lower_weight, lower_moment, lower_square, hidden_bias, bias_moment, bias_square, norm_gains, gains_moment, gains_square, shift_params, shifts_moment, shifts_square):
    masters = (qkv_weight, proj_weight, upper_weight, lower_weight, hidden_bias, norm_gains, shift_params)
    moments = (qkv_moment, proj_moment, upper_moment, lower_moment, bias_moment, gains_moment, shifts_moment)
    squares = (qkv_square, proj_square, upper_square, lower_square, bias_square, gains_square, shifts_square)

    def apply_layers(stream, *params):
        return forward(stream, documents, *params)
    output_stream, pullback = jax.vjp(apply_layers, inputs.astype(jnp.float32), *masters)
    gradients = pullback(cotangent.astype(jnp.float32))
    input_grad = gradients[0]
    weight_grads = gradients[1:]
    sum_squares = jnp.float32(0.0)
    for gradient in weight_grads:
        sum_squares = sum_squares + jnp.sum(gradient * gradient)
    grad_norm = jnp.sqrt(sum_squares)
    factor = jnp.minimum(1.0, clip_bound / grad_norm)
    results = [output_stream, input_grad]
    for group_at in range(7):
        results.extend(adam_update(masters[group_at], moments[group_at], squares[group_at], weight_grads[group_at], factor, group_rates[group_at], group_decays[group_at]))
    results.append(grad_norm)
    return tuple(results)
```

```python
import functools
import math

import jax
import jax.numpy as jnp
import numpy as np
from jax import lax
from jax.experimental import pallas as pl
from jax.experimental.pallas import tpu as pltpu
from jax.sharding import PartitionSpec as P

H = 8
HD = 128
STEP = 5
MAX_DOC = 512

norm_eps = 1e-05
clip_bound = 1.0
beta_first = 0.9
beta_second = 0.95
adam_eps = 1e-08
masked_score = -1e30
group_rates = (0.03, 0.12, 0.03, 0.015, 0.3, 0.7, 0.3)
group_decays = (0.1, 0.1, 0.1, 0.1, 0.0, 0.0, 0.0)
contract_rows = (((0,), (0,)), ((), ()))
contract_cols = (((1,), (1,)), ((), ()))
f32 = jnp.float32
bf16 = jnp.bfloat16
score_scale = 1.0 / math.sqrt(HD)


def adam_update(master, moment, square, gradient, factor, step_rate, decay_rate):
    clipped = gradient * factor
    moment_new = beta_first * moment + (1.0 - beta_first) * clipped
    square_new = beta_second * square + (1.0 - beta_second) * clipped * clipped
    first_hat = moment_new / (1.0 - beta_first**STEP)
    second_hat = square_new / (1.0 - beta_second**STEP)
    master_new = master - step_rate * (
        first_hat / (jnp.sqrt(second_hat) + adam_eps) + decay_rate * master
    )
    return (master_new, moment_new, square_new)


def gelu_tanh(values):
    return jax.nn.gelu(values, approximate=True)


def layer_norm(values, scale_vec, shift_vec):
    center = values - jnp.mean(values, axis=-1, keepdims=True)
    spread = jnp.mean(center * center, axis=-1, keepdims=True)
    return center * lax.rsqrt(spread + norm_eps) * scale_vec + shift_vec


def dot(left, right):
    return jnp.dot(left, right, preferred_element_type=f32)


def dot_rows(left, right):
    return lax.dot_general(left, right, contract_rows, preferred_element_type=f32)


def dot_cols(left, right):
    return lax.dot_general(left, right, contract_cols, preferred_element_type=f32)


def masked_scores(slope, doc_col, doc_row, query, key, first_row, first_col):
    scores = dot_cols(query, key) * score_scale
    rows = first_row + lax.broadcasted_iota(jnp.int32, scores.shape, 0)
    cols = first_col + lax.broadcasted_iota(jnp.int32, scores.shape, 1)
    distance = rows - cols
    allowed = (distance >= 0) & (doc_col == doc_row)
    return jnp.where(allowed, scores - slope * distance.astype(f32), masked_score)


def key_range(first_row, block):
    low = max(0, first_row - (MAX_DOC - 1)) // block * block
    return low, first_row + block


def attend_kernel(heads, block, slope_ref, dcol_ref, drow_ref, qk_ref, v_ref, o_ref):
    length = v_ref.shape[0]
    for head in range(heads):
        slope = slope_ref[pl.program_id(0) * heads + head]
        at = head * HD
        kat = (heads + head) * HD
        for first_row in range(0, length, block):
            low, high = key_range(first_row, block)
            scores = masked_scores(
                slope,
                dcol_ref[first_row : first_row + block, :],
                drow_ref[:, low:high],
                qk_ref[first_row : first_row + block, at : at + HD],
                qk_ref[low:high, kat : kat + HD],
                first_row,
                low,
            )
            shifted = jnp.exp(scores - jnp.max(scores, axis=-1, keepdims=True))
            total = jnp.sum(shifted, axis=-1, keepdims=True)
            prob_low = (shifted * (1.0 / total)).astype(bf16)
            o_ref[first_row : first_row + block, at : at + HD] = dot(
                prob_low, v_ref[low:high, at : at + HD]
            ).astype(bf16)


def attend_back_kernel(
    heads, block, slope_ref, dcol_ref, drow_ref, qk_ref, v_ref, o_ref, do_ref,
    dqk_ref, dv_ref, key_acc, value_acc,
):
    length = v_ref.shape[0]
    for head in range(heads):
        slope = slope_ref[pl.program_id(0) * heads + head]
        at = head * HD
        kat = (heads + head) * HD
        key_acc[...] = jnp.zeros_like(key_acc)
        value_acc[...] = jnp.zeros_like(value_acc)
        for first_row in range(0, length, block):
            low, high = key_range(first_row, block)
            rows = slice(first_row, first_row + block)
            query = qk_ref[rows, at : at + HD]
            key = qk_ref[low:high, kat : kat + HD]
            scores = masked_scores(
                slope, dcol_ref[rows, :], drow_ref[:, low:high], query, key, first_row, low
            )
            shifted = jnp.exp(scores - jnp.max(scores, axis=-1, keepdims=True))
            total = jnp.sum(shifted, axis=-1, keepdims=True)
            probs = shifted * (1.0 / total)
            out_grad = do_ref[rows, at : at + HD]
            value_acc[low:high, :] += dot_rows(probs.astype(bf16), out_grad)
            prob_grad = dot_cols(out_grad, v_ref[low:high, at : at + HD])
            inner = jnp.sum(
                out_grad.astype(f32) * o_ref[rows, at : at + HD].astype(f32),
                axis=-1,
                keepdims=True,
            )
            score_grad = (probs * (prob_grad - inner)).astype(bf16)
            dqk_ref[rows, at : at + HD] = (dot(score_grad, key) * score_scale).astype(bf16)
            key_acc[low:high, :] += dot_rows(score_grad, query)
        dqk_ref[:, kat : kat + HD] = (key_acc[...] * score_scale).astype(bf16)
        dv_ref[:, at : at + HD] = value_acc[...].astype(bf16)


def attend_specs(length, width, slots):
    def columns(each):
        return pl.BlockSpec((length, each), lambda s: (0, s))

    fixed = [
        pl.BlockSpec(memory_space=pltpu.SMEM),
        pl.BlockSpec((length, 1), lambda s: (0, 0)),
        pl.BlockSpec((1, length), lambda s: (0, 0)),
    ]
    return fixed, columns(2 * width), columns(width)


def attend(slopes, docs, qk, v, slots):
    length = v.shape[0]
    width = v.shape[1] // slots
    fixed, wide, narrow = attend_specs(length, width, slots)
    pairs = slots * width // HD * length * length
    return pl.pallas_call(
        functools.partial(attend_kernel, width // HD, min(256, length)),
        grid=(slots,),
        in_specs=fixed + [wide, narrow],
        out_specs=narrow,
        out_shape=jax.ShapeDtypeStruct(v.shape, bf16),
        compiler_params=pltpu.CompilerParams(vmem_limit_bytes=32 * 2**20),
        cost_estimate=pl.CostEstimate(
            flops=4 * pairs * HD, bytes_accessed=8 * v.size, transcendentals=pairs
        ),
    )(slopes, docs.reshape(-1, 1), docs.reshape(1, -1), qk, v)


def attend_back(slopes, docs, qk, v, o, do, slots):
    length = v.shape[0]
    width = v.shape[1] // slots
    fixed, wide, narrow = attend_specs(length, width, slots)
    pairs = slots * width // HD * length * length
    return pl.pallas_call(
        functools.partial(attend_back_kernel, width // HD, min(256, length)),
        grid=(slots,),
        in_specs=fixed + [wide, narrow, narrow, narrow],
        out_specs=[wide, narrow],
        out_shape=[jax.ShapeDtypeStruct(qk.shape, bf16), jax.ShapeDtypeStruct(v.shape, bf16)],
        scratch_shapes=[pltpu.VMEM((length, HD), f32), pltpu.VMEM((length, HD), f32)],
        compiler_params=pltpu.CompilerParams(vmem_limit_bytes=32 * 2**20),
        cost_estimate=pl.CostEstimate(
            flops=10 * pairs * HD, bytes_accessed=20 * v.size, transcendentals=pairs
        ),
    )(slopes, docs.reshape(-1, 1), docs.reshape(1, -1), qk, v, o, do)


def bits_of(size):
    return [1 << at for at in range(size.bit_length() - 1)]


def program(dp_size, mp_size, args):
    (
        inputs, documents, cotangent,
        qkv_weight, qkv_moment, qkv_square,
        proj_weight, proj_moment, proj_square,
        upper_weight, upper_moment, upper_square,
        lower_weight, lower_moment, lower_square,
        hidden_bias, bias_moment, bias_square,
        norm_gains, gains_moment, gains_square,
        shift_params, shifts_moment, shifts_square,
    ) = args
    layers = qkv_weight.shape[0]
    tokens, features = inputs.shape
    length = documents.shape[1]
    pieces = length // tokens
    slots = mp_size // pieces
    wide = features // dp_size
    z_cols = qkv_weight.shape[3]
    heads_slot = z_cols // HD
    me_dp = lax.axis_index("dp")
    me_mp = lax.axis_index("mp")
    core = me_dp & 1
    dp_bits = bits_of(dp_size)
    mp_bits = bits_of(mp_size)
    upper_bits = dp_bits[1:]

    def swap(values, axis, bit):
        size = dp_size if axis == "dp" else mp_size
        return lax.ppermute(values, axis, [(at, at ^ bit) for at in range(size)])

    order = [2 * k + c for c in (0, 1) for k in range(dp_size // 2)]

    def to_relative(values):
        parts = [lax.dynamic_slice_in_dim(values, (me_dp ^ r) * wide, wide, 1) for r in order]
        return jnp.concatenate(parts, axis=1)

    place_of = np.zeros((dp_size,), np.int32)
    for place, r in enumerate(order):
        place_of[r] = place
    place_table = jnp.asarray(place_of)

    def to_absolute(values):
        parts = [
            lax.dynamic_slice_in_dim(values, place_table[me_dp ^ b] * wide, wide, 1)
            for b in range(dp_size)
        ]
        return jnp.concatenate(parts, axis=1)

    def gather(shard, bits):
        for bit in mp_bits:
            shard = jnp.concatenate([shard, swap(shard, "mp", bit)], axis=1)
        parts = {0: shard}
        for bit in list(bits) + [1]:
            for r in sorted(parts):
                parts[r | bit] = swap(parts[r], "dp", bit)
        return [parts[r] for r in order]

    def scatter(kept, sent, bits):
        values = (kept.astype(f32) + swap(sent, "dp", 1).astype(f32)).astype(bf16)
        cols = values.shape[1] // mp_size
        values = values.reshape((2,) * len(upper_bits) + (wide, mp_size * cols))
        left = list(upper_bits)
        for bit in bits:
            axis = len(left) - 1 - left.index(bit)
            left.remove(bit)
            sent = swap(lax.index_in_dim(values, 1, axis, False), "dp", bit)
            kept = lax.index_in_dim(values, 0, axis, False)
            values = (kept.astype(f32) + sent.astype(f32)).astype(bf16)
        for bit in reversed(mp_bits):
            half = values.shape[1] // 2
            sent = swap(values[:, half:], "mp", bit)
            values = values[:, :half].astype(f32) + sent.astype(f32)
            if bit != 1:
                values = values.astype(bf16)
        return values

    def by_core(own, other, axis):
        first = jnp.where(core == 0, own, other)
        second = jnp.where(core == 0, other, own)
        return jnp.concatenate([first, second], axis=axis)

    paired = pieces == 2 and dp_size % 2 == 0 and mp_size % 2 == 0
    if paired:
        moved = core != (me_mp & 1)
        pairs = []
        for d in range(dp_size):
            for m in range(mp_size):
                if (d & 1) != (m & 1):
                    pairs.append((d * mp_size + m, (d ^ 1) * mp_size + (m ^ 1)))

        def trade(values):
            other = lax.ppermute(values, ("dp", "mp"), pairs)
            return jnp.where(moved, other, values)

        doc_rows = jnp.where(moved, swap(documents, "dp", 1), documents)
        docs = lax.dynamic_index_in_dim(doc_rows, me_mp // 2, 0, False)
        first_slot = core * slots

        def share_heads(values):
            half = values.shape[1] // 2
            own = lax.dynamic_slice_in_dim(values, core * half, half, 1)
            sent = lax.dynamic_slice_in_dim(values, (1 - core) * half, half, 1)
            return by_core(own, swap(sent, "dp", 1), 0)

        def return_heads(values):
            own = lax.dynamic_slice_in_dim(values, core * tokens, tokens, 0)
            sent = lax.dynamic_slice_in_dim(values, (1 - core) * tokens, tokens, 0)
            return by_core(own, swap(sent, "dp", 1), 1)

        slot_ids = me_mp ^ (first_slot + jnp.arange(slots))
    else:
        groups = [list(range(g * pieces, (g + 1) * pieces)) for g in range(mp_size // pieces)]

        def trade(values):
            return values

        docs = lax.dynamic_index_in_dim(documents, me_mp // pieces, 0, False)
        flipped = jnp.arange(mp_size) ^ me_mp

        def flip(values):
            parts = values.reshape(values.shape[0], mp_size, -1)
            return jnp.take(parts, flipped, axis=1).reshape(values.shape)

        def share_heads(values):
            return lax.all_to_all(
                flip(values), "mp", 1, 0, axis_index_groups=groups, tiled=True
            )

        def return_heads(values):
            return flip(
                lax.all_to_all(values, "mp", 0, 1, axis_index_groups=groups, tiled=True)
            )

        slot_ids = (me_mp % pieces) * slots + jnp.arange(slots)

    head_ids = (slot_ids[:, None] * heads_slot + jnp.arange(heads_slot)[None, :]).reshape(-1)
    slope_table = jnp.asarray(0.5 ** (np.arange(H) + 1.0), dtype=f32)
    slopes = jnp.take(slope_table, head_ids)

    small = jnp.concatenate(
        [
            norm_gains.reshape(-1, wide),
            shift_params.reshape(-1, wide),
            hidden_bias.reshape(-1, wide),
        ],
        axis=0,
    ).astype(bf16)
    small_all = lax.all_gather(small, ("mp", "dp"), axis=0).astype(f32)
    small_all = small_all.reshape(mp_size, dp_size, small.shape[0], wide)
    rel = jnp.asarray(order, dtype=jnp.int32) ^ me_dp
    gain_rows = norm_gains.shape[1]
    shift_count = shift_params.shape[1]
    vectors = jnp.take(small_all[0], rel, axis=0).transpose(1, 0, 2).reshape(-1, features)
    gains = vectors[: layers * gain_rows].reshape(layers, gain_rows, features)
    shifts = vectors[layers * gain_rows : layers * (gain_rows + shift_count)].reshape(
        layers, shift_count, features
    )
    bias_parts = small_all[:, :, layers * (gain_rows + shift_count) :]
    bias_parts = jnp.take(bias_parts, jnp.arange(mp_size) ^ me_mp, axis=0)
    biases = bias_parts.transpose(2, 0, 1, 3).reshape(layers, -1)

    first_order = upper_bits
    second_order = upper_bits[::-1]
    gathered = []
    for layer in range(layers):
        qk_shard = qkv_weight[layer, :, :2].astype(bf16).reshape(wide, 2 * z_cols)
        vo_shard = jnp.concatenate(
            [qkv_weight[layer, :, 2].astype(bf16), proj_weight[layer].astype(bf16).T], axis=1
        )
        up_shard = upper_weight[layer].astype(bf16)
        down_shard = lower_weight[layer].astype(bf16).T
        qk = jnp.concatenate(gather(qk_shard, first_order), axis=0)
        vo = [
            part.reshape(wide, mp_size, 2, z_cols) for part in gather(vo_shard, second_order)
        ]
        value = jnp.concatenate([part[:, :, 0] for part in vo], axis=0).reshape(features, -1)
        proj = jnp.concatenate([part[:, :, 1] for part in vo], axis=0).reshape(features, -1)
        upper = jnp.concatenate(gather(up_shard, first_order), axis=0)
        lower = jnp.concatenate(gather(down_shard, second_order), axis=0)
        gathered.append((qk, value, proj, upper, lower))

    stream = to_relative(trade(inputs)).astype(f32)
    grad_stream = to_relative(trade(cotangent)).astype(f32)
    stored = []
    for layer in range(layers):
        qk_w, value_w, proj_w, upper_w, lower_w = gathered[layer]
        normed = layer_norm(stream, gains[layer, 0], shifts[layer, 0]).astype(bf16)
        qk = share_heads(dot(normed, qk_w).astype(bf16))
        value = share_heads(dot(normed, value_w).astype(bf16))
        mixed = attend(slopes, docs, qk, value, slots)
        attended = return_heads(mixed)
        middle = stream + dot_cols(attended, proj_w)
        normed_two = layer_norm(middle, gains[layer, 1], shifts[layer, 1]).astype(bf16)
        hidden = dot(normed_two, upper_w) + biases[layer]
        active = gelu_tanh(hidden).astype(bf16)
        stored.append(
            (stream, middle, normed, qk, value, mixed, attended, normed_two, hidden, active)
        )
        stream = middle + dot_cols(active, lower_w) + shifts[layer, 2]
    output_stream = to_absolute(stream)
    if paired:
        other = lax.ppermute(output_stream.astype(bf16), ("dp", "mp"), pairs)
        output_stream = jnp.where(moved, other.astype(f32), output_stream)

    half = features // 2

    def weight_gradient(left, right, bits):
        sent = dot_rows(left[:, half:], right).astype(bf16)
        kept = dot_rows(left[:, :half], right).astype(bf16)
        return scatter(kept, sent, bits)

    weight_grads = [None] * layers
    small_grads = [None] * layers
    for layer in reversed(range(layers)):
        qk_w, value_w, proj_w, upper_w, lower_w = gathered[layer]
        (
            stream_in, middle, normed, qk, value, mixed, attended, normed_two, hidden, active
        ) = stored[layer]
        no_shift = jnp.zeros((features,), f32)
        out_shift_grad = jnp.sum(grad_stream, axis=0)
        grad_low = grad_stream.astype(bf16)
        active_grad = dot(grad_low, lower_w)
        _, pull_gelu = jax.vjp(gelu_tanh, hidden)
        hidden_grad = pull_gelu(active_grad)[0].astype(bf16)
        lower_grad = weight_gradient(grad_low, active, second_order)
        upper_grad = weight_gradient(normed_two, hidden_grad, first_order)
        bias_grad = jnp.sum(hidden_grad, axis=0, dtype=f32)
        normed_two_grad = dot_cols(hidden_grad, upper_w)
        _, pull_two = jax.vjp(layer_norm, middle, gains[layer, 1], no_shift)
        middle_part, gain_two, shift_two = pull_two(normed_two_grad)
        middle_grad = grad_stream + middle_part
        middle_low = middle_grad.astype(bf16)
        attended_grad = dot(middle_low, proj_w).astype(bf16)
        proj_grad = weight_gradient(middle_low, attended, second_order)
        mixed_grad = share_heads(attended_grad)
        qk_grad, value_grad = attend_back(slopes, docs, qk, value, mixed, mixed_grad, slots)
        qk_grad = return_heads(qk_grad)
        value_grad = return_heads(value_grad)
        normed_grad = dot_cols(qk_grad, qk_w) + dot_cols(value_grad, value_w)
        qk_weight_grad = weight_gradient(normed, qk_grad, first_order)
        value_weight_grad = weight_gradient(normed, value_grad, second_order)
        _, pull_one = jax.vjp(layer_norm, stream_in, gains[layer, 0], no_shift)
        stream_part, gain_one, shift_one = pull_one(normed_grad)
        grad_stream = middle_grad + stream_part
        weight_grads[layer] = (
            jnp.concatenate([qk_weight_grad, value_weight_grad], axis=1).reshape(
                wide, 3, z_cols
            ),
            proj_grad.T,
            upper_grad,
            lower_grad.T,
        )
        vectors = to_absolute(
            jnp.stack([gain_one, gain_two, shift_one, shift_two, out_shift_grad])
        )
        bias_grad = jnp.take(
            bias_grad.reshape(mp_size, -1), jnp.arange(mp_size) ^ me_mp, axis=0
        ).reshape(-1, features)
        small_grads[layer] = lax.psum(
            jnp.concatenate([vectors, bias_grad], axis=0), ("dp", "mp")
        )
    input_grad = to_absolute(grad_stream)
    if paired:
        other = lax.ppermute(input_grad.astype(bf16), ("dp", "mp"), pairs)
        input_grad = jnp.where(moved, other.astype(f32), input_grad)

    owned = jnp.float32(0.0)
    for member in range(4):
        for layer in range(layers):
            gradient = weight_grads[layer][member]
            owned = owned + jnp.sum(gradient * gradient)
    stacked = [jnp.stack([weight_grads[at][member] for at in range(layers)]) for member in range(4)]
    small_grad = jnp.stack(small_grads)
    sum_squares = lax.psum(owned, ("dp", "mp")) + jnp.sum(small_grad * small_grad)
    grad_norm = jnp.sqrt(sum_squares)
    factor = jnp.minimum(1.0, clip_bound / grad_norm)
    vector_grads = lax.dynamic_slice_in_dim(small_grad[:, :5], me_dp * wide, wide, 2)
    bias_wide = hidden_bias.shape[1]
    bias_grads = lax.dynamic_slice_in_dim(
        small_grad[:, 5:].reshape(layers, -1),
        (me_mp * dp_size + me_dp) * bias_wide,
        bias_wide,
        1,
    )
    masters = (
        qkv_weight, proj_weight, upper_weight, lower_weight, hidden_bias, norm_gains, shift_params
    )
    moments = (
        qkv_moment, proj_moment, upper_moment, lower_moment, bias_moment, gains_moment,
        shifts_moment,
    )
    squares = (
        qkv_square, proj_square, upper_square, lower_square, bias_square, gains_square,
        shifts_square,
    )
    gradients = (*stacked, bias_grads, vector_grads[:, :2], vector_grads[:, 2:])
    results = [output_stream, input_grad]
    for at in range(7):
        results.extend(
            adam_update(
                masters[at], moments[at], squares[at], gradients[at], factor,
                group_rates[at], group_decays[at],
            )
        )
    results.append(grad_norm)
    return tuple(results)


def solution(mesh):
    dp_size = mesh.shape["dp"]
    mp_size = mesh.shape["mp"]
    rows = P(("dp", "mp"), None)
    split_rows = P(None, "dp", None, "mp")
    split_upper = P(None, "dp", "mp")
    split_lower = P(None, "mp", "dp")
    split_bias = P(None, ("mp", "dp"))
    split_vector = P(None, None, "dp")
    groups = (
        split_rows, split_lower, split_upper, split_lower, split_bias, split_vector, split_vector
    )
    placed = tuple(spec for spec in groups for _ in range(3))

    def shards(*args):
        return program(dp_size, mp_size, args)

    return jax.shard_map(
        shards,
        mesh=mesh,
        in_specs=(rows, P("dp", None), rows) + placed,
        out_specs=(rows, rows) + placed + (P(),),
        check_vma=False,
    )
```

```python
import functools
import math

import jax
import jax.numpy as jnp
import numpy as np
from jax import lax
from jax.experimental import pallas as pl
from jax.experimental.pallas import tpu as pltpu
from jax.sharding import PartitionSpec as P

H = 8
HD = 128
STEP = 5
MAX_DOC = 512

norm_eps = 1e-05
clip_bound = 1.0
beta_first = 0.9
beta_second = 0.95
adam_eps = 1e-08
masked_score = -1e30
group_rates = (0.03, 0.12, 0.03, 0.015, 0.3, 0.7, 0.3)
group_decays = (0.1, 0.1, 0.1, 0.1, 0.0, 0.0, 0.0)
contract_rows = (((0,), (0,)), ((), ()))
contract_cols = (((1,), (1,)), ((), ()))
f32 = jnp.float32
bf16 = jnp.bfloat16
score_scale = 1.0 / math.sqrt(HD)
MESH = pl.DeviceIdType.MESH


def adam_update(master, moment, square, gradient, factor, step_rate, decay_rate):
    clipped = gradient * factor
    moment_new = beta_first * moment + (1.0 - beta_first) * clipped
    square_new = beta_second * square + (1.0 - beta_second) * clipped * clipped
    first_hat = moment_new / (1.0 - beta_first**STEP)
    second_hat = square_new / (1.0 - beta_second**STEP)
    master_new = master - step_rate * (
        first_hat / (jnp.sqrt(second_hat) + adam_eps) + decay_rate * master
    )
    return (master_new, moment_new, square_new)


def gelu_tanh(values):
    return jax.nn.gelu(values, approximate=True)


def layer_norm(values, scale_vec, shift_vec):
    center = values - jnp.mean(values, axis=-1, keepdims=True)
    spread = jnp.mean(center * center, axis=-1, keepdims=True)
    return center * lax.rsqrt(spread + norm_eps) * scale_vec + shift_vec


def dot(left, right):
    return jnp.dot(left, right, preferred_element_type=f32)


def dot_rows(left, right):
    return lax.dot_general(left, right, contract_rows, preferred_element_type=f32)


def dot_cols(left, right):
    return lax.dot_general(left, right, contract_cols, preferred_element_type=f32)


def masked_scores(slope, doc_col, doc_row, query, key, first_row, first_col):
    scores = dot_cols(query, key) * score_scale
    rows = first_row + lax.broadcasted_iota(jnp.int32, scores.shape, 0)
    cols = first_col + lax.broadcasted_iota(jnp.int32, scores.shape, 1)
    distance = rows - cols
    allowed = (distance >= 0) & (doc_col == doc_row)
    return jnp.where(allowed, scores - slope * distance.astype(f32), masked_score)


def key_range(first_row, block):
    low = max(0, first_row - (MAX_DOC - 1)) // block * block
    return low, first_row + block


def attend_kernel(heads, block, slope_ref, dcol_ref, drow_ref, qkv_ref, o_ref):
    length = o_ref.shape[0]
    for head in range(heads):
        slope = slope_ref[pl.program_id(0) * heads + head]
        at = head * HD
        kat = (heads + head) * HD
        vat = (2 * heads + head) * HD
        for first_row in range(0, length, block):
            low, high = key_range(first_row, block)
            scores = masked_scores(
                slope,
                dcol_ref[first_row : first_row + block, :],
                drow_ref[:, low:high],
                qkv_ref[first_row : first_row + block, at : at + HD],
                qkv_ref[low:high, kat : kat + HD],
                first_row,
                low,
            )
            shifted = jnp.exp(scores - jnp.max(scores, axis=-1, keepdims=True))
            total = jnp.sum(shifted, axis=-1, keepdims=True)
            prob_low = (shifted * (1.0 / total)).astype(bf16)
            o_ref[first_row : first_row + block, at : at + HD] = dot(
                prob_low, qkv_ref[low:high, vat : vat + HD]
            ).astype(bf16)


def attend_back_kernel(
    heads, block, slope_ref, dcol_ref, drow_ref, qkv_ref, o_ref, do_ref,
    grad_ref, key_acc, value_acc,
):
    length = o_ref.shape[0]
    for head in range(heads):
        slope = slope_ref[pl.program_id(0) * heads + head]
        at = head * HD
        kat = (heads + head) * HD
        vat = (2 * heads + head) * HD
        key_acc[...] = jnp.zeros_like(key_acc)
        value_acc[...] = jnp.zeros_like(value_acc)
        for first_row in range(0, length, block):
            low, high = key_range(first_row, block)
            rows = slice(first_row, first_row + block)
            query = qkv_ref[rows, at : at + HD]
            key = qkv_ref[low:high, kat : kat + HD]
            scores = masked_scores(
                slope, dcol_ref[rows, :], drow_ref[:, low:high], query, key, first_row, low
            )
            shifted = jnp.exp(scores - jnp.max(scores, axis=-1, keepdims=True))
            total = jnp.sum(shifted, axis=-1, keepdims=True)
            probs = shifted * (1.0 / total)
            out_grad = do_ref[rows, at : at + HD]
            value_acc[low:high, :] += dot_rows(probs.astype(bf16), out_grad)
            prob_grad = dot_cols(out_grad, qkv_ref[low:high, vat : vat + HD])
            inner = jnp.sum(
                out_grad.astype(f32) * o_ref[rows, at : at + HD].astype(f32),
                axis=-1,
                keepdims=True,
            )
            score_grad = (probs * (prob_grad - inner)).astype(bf16)
            grad_ref[rows, at : at + HD] = (dot(score_grad, key) * score_scale).astype(bf16)
            key_acc[low:high, :] += dot_rows(score_grad, query)
        grad_ref[:, kat : kat + HD] = (key_acc[...] * score_scale).astype(bf16)
        grad_ref[:, vat : vat + HD] = value_acc[...].astype(bf16)


def attend_specs(length, width):
    def columns(each):
        return pl.BlockSpec((length, each), lambda s: (0, s))

    fixed = [
        pl.BlockSpec(memory_space=pltpu.SMEM),
        pl.BlockSpec((length, 1), lambda s: (0, 0)),
        pl.BlockSpec((1, length), lambda s: (0, 0)),
    ]
    return fixed, columns(3 * width), columns(width)


def attend(slopes, docs, qkv, slots):
    length = qkv.shape[0]
    width = qkv.shape[1] // (3 * slots)
    fixed, wide, narrow = attend_specs(length, width)
    pairs = slots * width // HD * length * length
    return pl.pallas_call(
        functools.partial(attend_kernel, width // HD, min(256, length)),
        grid=(slots,),
        in_specs=fixed + [wide],
        out_specs=narrow,
        out_shape=jax.ShapeDtypeStruct((length, slots * width), bf16),
        compiler_params=pltpu.CompilerParams(vmem_limit_bytes=32 * 2**20),
        cost_estimate=pl.CostEstimate(
            flops=4 * pairs * HD, bytes_accessed=3 * qkv.size, transcendentals=pairs
        ),
    )(slopes, docs.reshape(-1, 1), docs.reshape(1, -1), qkv)


def attend_back(slopes, docs, qkv, o, do, slots):
    length = qkv.shape[0]
    width = qkv.shape[1] // (3 * slots)
    fixed, wide, narrow = attend_specs(length, width)
    pairs = slots * width // HD * length * length
    return pl.pallas_call(
        functools.partial(attend_back_kernel, width // HD, min(256, length)),
        grid=(slots,),
        in_specs=fixed + [wide, narrow, narrow],
        out_specs=wide,
        out_shape=jax.ShapeDtypeStruct(qkv.shape, bf16),
        scratch_shapes=[pltpu.VMEM((length, HD), f32), pltpu.VMEM((length, HD), f32)],
        compiler_params=pltpu.CompilerParams(vmem_limit_bytes=32 * 2**20),
        cost_estimate=pl.CostEstimate(
            flops=10 * pairs * HD, bytes_accessed=6 * qkv.size, transcendentals=pairs
        ),
    )(slopes, docs.reshape(-1, 1), docs.reshape(1, -1), qkv, o, do)


def flip(value, mask):
    bit = 1
    while bit <= mask:
        if mask & bit:
            value = value + bit * (1 - 2 * ((value // bit) % 2))
        bit *= 2
    return value


def place(at, size):
    return pl.multiple_of(at * size, size)


class Spread:
    def __init__(self, dims, mp_size):
        self.dims = tuple(dims)
        self.events = []
        masks, spread = [0], False
        for stage, dim in enumerate(self.dims):
            for mask in masks:
                if dim == "mp":
                    for hops in range(1, mp_size):
                        self.events += [(stage, mask, way, hops) for way in (1, -1)]
                else:
                    places = range(mp_size) if spread else (0,)
                    self.events += [(stage, mask | dim, 0, at) for at in places]
            if dim == "mp":
                spread = True
            else:
                masks = masks + [mask | dim for mask in masks]
        self.events += [(len(self.dims), mask | 1, 0, 0) for mask in masks]

    def full(self, stage):
        return "mp" in self.dims[:stage]


class Fold:
    def __init__(self, dims, mp_size):
        self.dims = tuple(dims)
        masks = [0]
        for dim in self.dims:
            if dim != "mp":
                masks = masks + [mask | dim for mask in masks]
        self.masks = masks
        self.kept = {}
        self.events = [(0, mask, 0, 0) for mask in sorted(masks, key=self.leaves)]
        rows = list(masks)
        for stage, dim in enumerate(self.dims, 1):
            if dim != "mp":
                rows = [mask for mask in rows if not mask & dim]
            self.kept[stage] = list(rows)
            if dim == "mp":
                for hops in reversed(range(mp_size - 1)):
                    for mask in rows:
                        self.events += [(stage, mask, way, hops) for way in (1, -1)]
            else:
                places = reversed(range(mp_size)) if self.full(stage) else (0,)
                places = list(places)
                for mask in rows:
                    self.events += [(stage, mask, 0, at) for at in places]

    def leaves(self, mask):
        for at, dim in enumerate(self.dims):
            if dim != "mp" and mask & dim:
                return at
        return len(self.dims)

    def full(self, stage):
        return "mp" not in self.dims[: stage - 1]


def number(plans, mp_size, single):
    index, total = {}, 0
    for t, plan in enumerate(plans):
        for event in plan.events:
            stage, mask, way, at = event
            if way or single(plan, stage):
                index[(t,) + event] = total
                total += 1
            elif (t, stage, mask) not in index:
                index[t, stage, mask] = total
                total += mp_size
    return index, total


def spread_single(plan, stage):
    return stage == len(plan.dims)


def fold_single(plan, stage):
    return stage == 0


def merge_small(order, plans):
    t = len(plans) - 1
    small = [(t, event) for event in plans[t].events]
    out, used = [], 0
    for at, step in enumerate(order):
        out.append(step)
        while used < len(small) and (used + 1) * len(order) <= (at + 1) * (len(small) + 1):
            out.append(small[used])
            used += 1
    return out + small[used:]


def step_order(plans, table, by_stage):
    steps = [(t, event) for t, plan in enumerate(plans[:-1]) for event in plan.events]
    if len(table) == len(steps):
        return merge_small([steps[at] for at in table], plans)
    ranked = sorted(range(len(steps)), key=lambda at: (by_stage(steps[at][0], steps[at][1][0]), at))
    return merge_small([steps[at] for at in ranked], plans)


def greet(z, d, upper, mp_size):
    barrier = pltpu.get_barrier_semaphore()
    for bit in [1] + upper:
        pl.semaphore_signal(
            barrier, inc=1, device_id={"dp": flip(d, bit)}, device_id_type=MESH
        )
    for way in (1, -1):

        @pl.when((z + way >= 0) & (z + way < mp_size))
        def _(way=way):
            pl.semaphore_signal(
                barrier, inc=1, device_id={"mp": z + way}, device_id_type=MESH
            )

    around = jnp.where(z > 0, 1, 0) + jnp.where(z < mp_size - 1, 1, 0)
    pl.semaphore_wait(barrier, 1 + len(upper) + around)


def spread_kernel(plans, order, mp_size, *refs):
    n = len(plans)
    shards, outs = refs[:n], refs[n : 2 * n]
    send_sems, recv_sems, own_sems = refs[2 * n :]
    z = lax.axis_index("mp")
    d = lax.axis_index("dp")
    upper = [dim for dim in plans[0].dims if dim != "mp"]
    index, _ = number(plans, mp_size, spread_single)

    def inside(at):
        return (at >= 0) & (at < mp_size)

    def region(t, mask, block):
        wide, cols = shards[t].shape
        rows = pl.ds(place(flip(d, mask), wide), wide)
        if block is None:
            return outs[t].at[rows, :]
        return outs[t].at[rows, pl.ds(place(block, cols), cols)]

    def remote(t, event, block, src, dst, to):
        stage, mask, way, at = event
        if way or stage == len(plans[t].dims):
            sem = index[(t,) + event]
        else:
            sem = index[t, stage, mask] + block
        return pltpu.make_async_remote_copy(
            src_ref=src,
            dst_ref=dst,
            send_sem=send_sems.at[sem],
            recv_sem=recv_sems.at[sem],
            device_id=to,
            device_id_type=MESH,
        )

    def sending(t, event, block, to, own=False):
        stage, mask, way, at = event
        dims = plans[t].dims
        bit = 0 if way else 1 if stage == len(dims) else dims[stage]
        dst = region(t, mask ^ bit, block)
        return remote(t, event, block, shards[t] if own else dst, dst, to)

    def arrival(t, event, block):
        dst = region(t, event[1], block)
        return remote(t, event, block, dst, dst, {"dp": d, "mp": z})

    def on_line(t, stage, mask, block, way, hops, own):
        @pl.when(inside(z + way))
        def _():
            sending(t, (stage, mask, way, hops), block, {"mp": z + way}, own).start()

    def onward(t, stage, mask, block, own=False):
        dims = plans[t].dims
        for later in range(stage, len(dims)):
            if dims[later] == "mp":
                for way in (1, -1):
                    on_line(t, later, mask, block, way, 1, own)
            else:
                to = {"dp": flip(d, dims[later])}
                sending(t, (later, mask | dims[later], 0, None), block, to, own).start()

    greet(z, d, upper, mp_size)
    owns = []
    for t in range(n):
        onward(t, 0, 0, z, True)
        owns.append(pltpu.make_async_copy(shards[t], region(t, 0, z), own_sems.at[t]))
        owns[t].start()

    left = {}
    for t, event in order:
        if event[0] < len(plans[t].dims):
            left[t, event[1]] = left.get((t, event[1]), 0) + 1

    def place_of(t, event):
        stage, mask, way, at = event
        return flip(z, at) if plans[t].full(stage) else z

    for t, event in order:
        stage, mask, way, at = event
        last = len(plans[t].dims)
        if stage == last:
            arrival(t, event, None).wait_recv()
            continue
        if way:
            block = z - way * at

            @pl.when(inside(block))
            def _():
                arrival(t, event, block).wait_recv()
                if at + 1 < mp_size:
                    on_line(t, stage, mask, block, way, at + 1, False)
                onward(t, stage + 1, mask, block)

        else:
            block = place_of(t, event)
            arrival(t, event, block).wait_recv()
            onward(t, stage + 1, mask, block)
        left[t, mask] -= 1
        if left[t, mask] == 0:
            if mask == 0:
                owns[t].wait()
            sending(t, (last, mask | 1, 0, 0), None, {"dp": flip(d, 1)}).start()

    for t, event in order:
        stage, mask, way, at = event
        if stage == len(plans[t].dims):
            sending(t, event, None, {"dp": flip(d, 1)}).wait_send()
        elif way:

            @pl.when(inside(z - way * (at - 1)) & inside(z + way))
            def _():
                sending(t, event, z - way * (at - 1), {"mp": z + way}).wait_send()

        else:
            to = {"dp": flip(d, plans[t].dims[stage])}
            sending(t, event, place_of(t, event), to).wait_send()


def spread_all(shards, plans, order, dp_size, mp_size):
    _, total = number(plans, mp_size, spread_single)
    return pl.pallas_call(
        functools.partial(spread_kernel, plans, order, mp_size),
        out_shape=[
            jax.ShapeDtypeStruct((s.shape[0] * dp_size, s.shape[1] * mp_size), s.dtype)
            for s in shards
        ],
        in_specs=[pl.BlockSpec(memory_space=pl.ANY)] * len(shards),
        out_specs=[pl.BlockSpec(memory_space=pl.ANY)] * len(shards),
        scratch_shapes=[
            pltpu.SemaphoreType.DMA((total,)),
            pltpu.SemaphoreType.DMA((total,)),
            pltpu.SemaphoreType.DMA((len(shards),)),
        ],
        compiler_params=pltpu.CompilerParams(collective_id=0, has_side_effects=True),
    )(*shards)


def fold_kernel(plans, order, mp_size, *refs):
    n = len(plans)
    grads, outs, landed, sums = (refs[at * n : (at + 1) * n] for at in range(4))
    at = 4 * n
    recv = {}
    for t, plan in enumerate(plans):
        for stage in range(1, len(plan.dims) + 1):
            recv[t, stage] = refs[at]
            at += 1
    staging, load_sems, own_sems, send_sems, recv_sems = refs[at:]
    z = lax.axis_index("mp")
    d = lax.axis_index("dp")
    upper = [dim for dim in plans[0].dims if dim != "mp"]
    index, _ = number(plans, mp_size, fold_single)
    wides = [out.shape[0] for out in outs]
    cols = [out.shape[1] for out in outs]

    def inside(at):
        return (at >= 0) & (at < mp_size)

    def rows_of(t, mask):
        return pl.ds(plans[t].masks.index(mask) * wides[t], wides[t])

    def sum_at(t, mask, block):
        return sums[t].at[rows_of(t, mask), pl.ds(place(block, cols[t]), cols[t])]

    def landing(t, event, block):
        stage, mask, way, at = event
        kept = plans[t].kept[stage].index(mask)
        if way:
            return recv[t, stage].at[kept, (0 if way == 1 else mp_size - 1) + at]
        return recv[t, stage].at[kept, block if plans[t].full(stage) else 0]

    def remote(t, event, block, src, dst, to):
        stage, mask, way, at = event
        if way or stage == 0:
            sem = index[(t,) + event]
        else:
            sem = index[t, stage, mask] + block
        return pltpu.make_async_remote_copy(
            src_ref=src,
            dst_ref=dst,
            send_sem=send_sems.at[sem],
            recv_sem=recv_sems.at[sem],
            device_id=to,
            device_id_type=MESH,
        )

    def core_copy(t, mask):
        rows = pl.ds(place(flip(d, mask | 1), wides[t]), wides[t])
        dst = landed[t].at[rows_of(t, mask), :]
        return remote(t, (0, mask, 0, 0), 0, grads[t].at[rows, :], dst, {"dp": flip(d, 1)})

    def own_copy(t, mask):
        rows = pl.ds(place(flip(d, mask), wides[t]), wides[t])
        return pltpu.make_async_copy(
            grads[t].at[rows, :],
            sums[t].at[rows_of(t, mask), :],
            own_sems.at[t, plans[t].masks.index(mask)],
        )

    def bit_copy(t, stage, mask, block):
        dim = plans[t].dims[stage - 1]
        event = (stage, mask & ~dim, 0, None)
        dst = landing(t, event, block)
        return remote(t, event, block, sum_at(t, mask, block), dst, {"dp": flip(d, dim)})

    def line_copy(t, stage, mask, way, hops):
        event = (stage, mask, way, hops - 1)
        src = sum_at(t, mask, z + way * hops)
        return remote(t, event, None, src, landing(t, event, None), {"mp": z + way})

    def arrival(t, event, block):
        dst = landing(t, event, block)
        return remote(t, event, block, dst, dst, {"dp": d, "mp": z})

    def add(dst, src, wide):
        step = 16

        def some_rows(at, carry):
            rows = pl.ds(pl.multiple_of(at * step, step), step)
            total = dst[rows, :].astype(f32) + src[rows, :].astype(f32)
            dst[rows, :] = total.astype(bf16)
            return carry

        lax.fori_loop(0, wide // step, some_rows, 0)

    def advance(t, stage, mask, block, other):
        if stage > len(plans[t].dims):
            return
        dim = plans[t].dims[stage - 1]
        if dim == "mp":
            if other:
                for way, end in ((1, 0), (-1, mp_size - 1)):

                    @pl.when(z == end)
                    def _(way=way):
                        line_copy(t, stage, mask, way, other).start()

        elif mask & dim:
            bit_copy(t, stage, mask, block).start()

    greet(z, d, upper, mp_size)
    cores = [(t, event[1]) for t, event in order if event[0] == 0]
    for t, mask in cores:
        core_copy(t, mask).start()
        own_copy(t, mask).start()

    def load(at):
        t, mask = cores[at]
        return pltpu.make_async_copy(
            landed[t].at[rows_of(t, mask), :],
            staging.at[at % 2, pl.ds(0, wides[t]), pl.ds(0, cols[t] * mp_size)],
            load_sems.at[at % 2],
        )

    seen = 0
    brought = {}
    for t, event in order:
        stage, mask, way, at = event
        plan = plans[t]
        if stage == 0:
            for ahead in (0, 1) if seen == 0 else (seen + 1,):
                if ahead < len(cores):
                    core_copy(*cores[ahead]).wait_recv()
                    load(ahead).start()
            load(seen).wait()
            own_copy(t, mask).wait()
            part = staging.at[seen % 2, pl.ds(0, wides[t]), pl.ds(0, cols[t] * mp_size)]
            add(sums[t].at[rows_of(t, mask), :], part, wides[t])
            seen += 1
            for other in reversed(range(mp_size)):
                advance(t, 1, mask, flip(z, other), other)
        elif way:
            block = z + way * at

            @pl.when(inside(block) & inside(z - way))
            def _():
                arrival(t, event, None).wait_recv()
                add(sum_at(t, mask, block), landing(t, event, None), wides[t])
                if at > 0:
                    line_copy(t, stage, mask, way, at).start()

            if at == 0:
                brought[t, mask] = brought.get((t, mask), 0) + 1
                if brought[t, mask] == 2:
                    advance(t, stage + 1, mask, z, 0)
        else:
            block = flip(z, at) if plan.full(stage) else z
            arrival(t, event, block).wait_recv()
            add(sum_at(t, mask, block), landing(t, event, block), wides[t])
            advance(t, stage + 1, mask, block, at)

    for t in range(n):
        outs[t][...] = sum_at(t, 0, z)[...].astype(f32)

    for t, event in order:
        stage, mask, way, at = event
        if stage == 0:
            core_copy(t, mask).wait_send()
        elif way:

            @pl.when(inside(z + way) & inside(z + way * (at + 1)))
            def _():
                line_copy(t, stage, mask, way, at + 1).wait_send()

        else:
            block = flip(z, at) if plans[t].full(stage) else z
            bit_copy(t, stage, mask | plans[t].dims[stage - 1], block).wait_send()


def fold_all(grads, plans, order, dp_size, mp_size):
    n = len(grads)
    _, total = number(plans, mp_size, fold_single)
    wides = [g.shape[0] // dp_size for g in grads]
    cols = [g.shape[1] // mp_size for g in grads]
    halves = [(dp_size // 2 * wide, mp_size * each) for wide, each in zip(wides, cols)]
    scratch = [pltpu.VMEM(half, bf16) for half in halves]
    for plan, wide, each in zip(plans, wides, cols):
        for stage, dim in enumerate(plan.dims, 1):
            blocks = 2 * (mp_size - 1) if dim == "mp" else mp_size if plan.full(stage) else 1
            scratch.append(pltpu.VMEM((len(plan.kept[stage]), blocks, wide, each), bf16))
    scratch += [
        pltpu.VMEM((2, max(wides), mp_size * max(cols)), bf16),
        pltpu.SemaphoreType.DMA((2,)),
        pltpu.SemaphoreType.DMA((n, dp_size // 2)),
        pltpu.SemaphoreType.DMA((total,)),
        pltpu.SemaphoreType.DMA((total,)),
    ]
    out = pl.pallas_call(
        functools.partial(fold_kernel, plans, order, mp_size),
        out_shape=[jax.ShapeDtypeStruct((wide, each), f32) for wide, each in zip(wides, cols)]
        + [jax.ShapeDtypeStruct(half, bf16) for half in halves],
        in_specs=[pl.BlockSpec(memory_space=pl.ANY)] * n,
        out_specs=[pl.BlockSpec(memory_space=pltpu.VMEM)] * n
        + [pl.BlockSpec(memory_space=pl.ANY)] * n,
        scratch_shapes=scratch,
        compiler_params=pltpu.CompilerParams(
            collective_id=1, has_side_effects=True, vmem_limit_bytes=63 * 2**20
        ),
    )(*grads)
    return list(out[:n])


spread_table = (
    45, 0, 46, 22, 23, 94, 116, 1, 95, 117, 2, 3, 25, 119, 118, 24, 97, 120, 26, 4, 96, 47, 71, 5,
    27, 69, 140, 165, 28, 7, 44, 6, 121, 99, 98, 125, 48, 30, 51, 8, 70, 122, 76, 72, 53, 128, 77,
    33, 34, 78, 50, 9, 112, 35, 129, 15, 123, 107, 29, 104, 73, 124, 79, 103, 101, 102, 52, 31,
    54, 80, 127, 49, 81, 139, 56, 19, 75, 106, 57, 74, 164, 60, 126, 141, 142, 40, 55, 100, 88,
    87, 105, 166, 167, 138, 12, 144, 136, 83, 111, 38, 113, 168, 82, 134, 13, 59, 169, 66, 184,
    64, 143, 163, 86, 32, 146, 16, 159, 18, 89, 176, 85, 41, 110, 58, 10, 151, 42, 145, 84, 61,
    148, 93, 11, 63, 39, 37, 131, 65, 130, 36, 17, 170, 154, 114, 147, 171, 62, 132, 152, 108,
    109, 20, 177, 91, 150, 172, 153, 135, 149, 14, 179, 68, 178, 90, 173, 175, 174, 180, 161, 43,
    160, 182, 156, 181, 133, 92, 155, 67, 157, 158, 115, 21, 186, 185, 137, 183, 162, 187,
)
fold_table = (
    50, 25, 1, 28, 29, 122, 169, 2, 8, 30, 9, 0, 145, 119, 31, 95, 53, 51, 55, 3, 74, 11, 10, 26,
    15, 4, 6, 96, 146, 75, 123, 32, 72, 97, 19, 147, 7, 27, 102, 124, 14, 38, 125, 73, 5, 52, 94,
    126, 37, 12, 103, 131, 54, 132, 136, 104, 105, 76, 109, 42, 18, 33, 57, 36, 168, 135, 166,
    113, 34, 35, 108, 144, 39, 98, 16, 40, 46, 120, 80, 112, 58, 81, 13, 170, 140, 99, 20, 101,
    172, 79, 56, 78, 83, 41, 60, 77, 148, 100, 82, 167, 44, 106, 107, 17, 121, 150, 43, 59, 110,
    127, 111, 84, 173, 129, 128, 47, 153, 61, 130, 85, 87, 174, 133, 62, 134, 114, 149, 86, 171,
    45, 89, 175, 88, 65, 178, 137, 138, 63, 152, 151, 177, 154, 156, 48, 176, 179, 21, 64, 91,
    157, 67, 90, 115, 116, 22, 181, 66, 155, 180, 117, 142, 182, 159, 183, 69, 158, 161, 141, 93,
    23, 160, 68, 92, 185, 184, 162, 71, 70, 163, 139, 24, 49, 118, 187, 143, 186, 164, 165,
)


def bits_of(size):
    return [1 << at for at in range(size.bit_length() - 1)]


def program(dp_size, mp_size, args):
    (
        inputs, documents, cotangent,
        qkv_weight, qkv_moment, qkv_square,
        proj_weight, proj_moment, proj_square,
        upper_weight, upper_moment, upper_square,
        lower_weight, lower_moment, lower_square,
        hidden_bias, bias_moment, bias_square,
        norm_gains, gains_moment, gains_square,
        shift_params, shifts_moment, shifts_square,
    ) = args
    layers = qkv_weight.shape[0]
    tokens, features = inputs.shape
    length = documents.shape[1]
    pieces = length // tokens
    slots = mp_size // pieces
    wide = features // dp_size
    z_cols = qkv_weight.shape[3]
    heads_slot = z_cols // HD
    me_dp = lax.axis_index("dp")
    me_mp = lax.axis_index("mp")
    core = me_dp % 2

    def swap(values):
        return lax.ppermute(values, "dp", [(at, at ^ 1) for at in range(dp_size)])

    def by_core(own, other, axis):
        first = jnp.where(core == 0, own, other)
        second = jnp.where(core == 0, other, own)
        return jnp.concatenate([first, second], axis=axis)

    paired = pieces == 2 and dp_size % 2 == 0 and mp_size % 2 == 0
    if paired:
        moved = core != me_mp % 2
        pairs = []
        for d in range(dp_size):
            for m in range(mp_size):
                if d % 2 != m % 2:
                    pairs.append((d * mp_size + m, (d ^ 1) * mp_size + (m ^ 1)))

        def trade(values):
            other = lax.ppermute(values, ("dp", "mp"), pairs)
            return jnp.where(moved, other, values)

        doc_rows = jnp.where(moved, swap(documents), documents)
        docs = lax.dynamic_index_in_dim(doc_rows, me_mp // 2, 0, False)

        def share_heads(values):
            half = values.shape[1] // 2
            own = lax.dynamic_slice_in_dim(values, core * half, half, 1)
            sent = lax.dynamic_slice_in_dim(values, (1 - core) * half, half, 1)
            return by_core(own, swap(sent), 0)

        def return_heads(values):
            own = lax.dynamic_slice_in_dim(values, core * tokens, tokens, 0)
            sent = lax.dynamic_slice_in_dim(values, (1 - core) * tokens, tokens, 0)
            return by_core(own, swap(sent), 1)

        first_slot = core * slots
    else:
        groups = [list(range(g * pieces, (g + 1) * pieces)) for g in range(mp_size // pieces)]

        def trade(values):
            return values

        docs = lax.dynamic_index_in_dim(documents, me_mp // pieces, 0, False)

        def share_heads(values):
            return lax.all_to_all(values, "mp", 1, 0, axis_index_groups=groups, tiled=True)

        def return_heads(values):
            return lax.all_to_all(values, "mp", 0, 1, axis_index_groups=groups, tiled=True)

        first_slot = (me_mp % pieces) * slots
    slope_table = jnp.asarray(0.5 ** (np.arange(H) + 1.0), dtype=f32)
    slopes = lax.dynamic_slice_in_dim(
        slope_table, first_slot * heads_slot, slots * heads_slot
    )

    bits = bits_of(dp_size)[1:]
    line_first = [("mp", *bits), ("mp", *bits[::-1])]
    line_second = [(bits[0], "mp", *bits[1:]), (bits[-1], "mp", *bits[:-1][::-1])]

    gain_rows = norm_gains.shape[1]
    shift_rows = shift_params.shape[1]
    vector_count = layers * (gain_rows + shift_rows)
    bias_wide = hidden_bias.shape[1]
    lanes = max(wide, HD)
    small_rows = -(-(vector_count + layers) // 16) * 16

    def padded(values):
        return jnp.pad(values, [(0, 0)] * (values.ndim - 1) + [(0, lanes - values.shape[-1])])

    small = jnp.concatenate(
        [
            padded(norm_gains.reshape(-1, wide)),
            padded(shift_params.reshape(-1, wide)),
            padded(hidden_bias),
            jnp.zeros((small_rows - vector_count - layers, lanes), f32),
        ],
        axis=0,
    ).astype(bf16)

    shards = []
    spreads = []
    for layer in range(layers):
        shards += [
            qkv_weight[layer].astype(bf16).reshape(wide, 3 * z_cols),
            proj_weight[layer].astype(bf16).T,
            upper_weight[layer].astype(bf16),
            lower_weight[layer].astype(bf16).T,
        ]
        spreads += line_first[:: 1 if layer % 2 == 0 else -1] + line_second
    shards.append(small)
    spreads.append(line_first[0])
    spreads = [Spread(dims, mp_size) for dims in spreads]
    tabled = dp_size == 8 and mp_size == 4 and layers == 2
    spread_order = step_order(
        spreads, spread_table if tabled else (), lambda t, stage: t // 2 + stage
    )
    full = spread_all(shards, spreads, spread_order, dp_size, mp_size)
    small_all = full[-1].reshape(dp_size, small_rows, mp_size, lanes).astype(f32)
    vectors = small_all[:, :vector_count, 0, :wide].transpose(1, 0, 2)
    vectors = vectors.reshape(vector_count, features)
    gains = vectors[: layers * gain_rows].reshape(layers, gain_rows, features)
    shifts = vectors[layers * gain_rows :].reshape(layers, shift_rows, features)
    biases = small_all[:, vector_count : vector_count + layers, :, :bias_wide]
    biases = biases.transpose(1, 2, 0, 3).reshape(layers, -1)

    stream = trade(inputs).astype(f32)
    grad_stream = trade(cotangent).astype(f32)
    stored = []
    for layer in range(layers):
        qkv_w, proj_w, upper_w, lower_w = full[4 * layer : 4 * layer + 4]
        normed = layer_norm(stream, gains[layer, 0], shifts[layer, 0]).astype(bf16)
        qkv = share_heads(dot(normed, qkv_w).astype(bf16))
        mixed = attend(slopes, docs, qkv, slots)
        attended = return_heads(mixed)
        middle = stream + dot_cols(attended, proj_w)
        normed_two = layer_norm(middle, gains[layer, 1], shifts[layer, 1]).astype(bf16)
        hidden = dot(normed_two, upper_w) + biases[layer]
        active = gelu_tanh(hidden).astype(bf16)
        stored.append((stream, middle, normed, qkv, mixed, attended, normed_two, hidden, active))
        stream = middle + dot_cols(active, lower_w) + shifts[layer, 2]
    output_stream = stream
    if paired:
        other = lax.ppermute(output_stream.astype(bf16), ("dp", "mp"), pairs)
        output_stream = jnp.where(moved, other.astype(f32), output_stream)

    weight_grads = [None] * layers
    vector_grads = [None] * layers
    bias_grads = [None] * layers
    no_shift = jnp.zeros((features,), f32)
    for layer in reversed(range(layers)):
        qkv_w, proj_w, upper_w, lower_w = full[4 * layer : 4 * layer + 4]
        stream_in, middle, normed, qkv, mixed, attended, normed_two, hidden, active = stored[layer]
        out_shift_grad = jnp.sum(grad_stream, axis=0)
        grad_low = grad_stream.astype(bf16)
        active_grad = dot(grad_low, lower_w)
        _, pull_gelu = jax.vjp(gelu_tanh, hidden)
        hidden_grad = pull_gelu(active_grad)[0].astype(bf16)
        lower_grad = dot_rows(grad_low, active).astype(bf16)
        upper_grad = dot_rows(normed_two, hidden_grad).astype(bf16)
        bias_grads[layer] = jnp.sum(hidden_grad, axis=0, dtype=f32)
        normed_two_grad = dot_cols(hidden_grad, upper_w)
        _, pull_two = jax.vjp(layer_norm, middle, gains[layer, 1], no_shift)
        middle_part, gain_two, shift_two = pull_two(normed_two_grad)
        middle_grad = grad_stream + middle_part
        middle_low = middle_grad.astype(bf16)
        mixed_grad = share_heads(dot(middle_low, proj_w).astype(bf16))
        proj_grad = dot_rows(middle_low, attended).astype(bf16)
        qkv_grad = return_heads(attend_back(slopes, docs, qkv, mixed, mixed_grad, slots))
        normed_grad = dot_cols(qkv_grad, qkv_w)
        qkv_weight_grad = dot_rows(normed, qkv_grad).astype(bf16)
        _, pull_one = jax.vjp(layer_norm, stream_in, gains[layer, 0], no_shift)
        stream_part, gain_one, shift_one = pull_one(normed_grad)
        grad_stream = middle_grad + stream_part
        weight_grads[layer] = (lower_grad, upper_grad, proj_grad, qkv_weight_grad)
        vector_grads[layer] = (
            jnp.stack([gain_one, gain_two]),
            jnp.stack([shift_one, shift_two, out_shift_grad]),
        )
    input_grad = grad_stream
    if paired:
        other = lax.ppermute(input_grad.astype(bf16), ("dp", "mp"), pairs)
        input_grad = jnp.where(moved, other.astype(f32), input_grad)

    vector_sums = jnp.concatenate(
        [jnp.concatenate([vector_grads[at][kind] for at in range(layers)]) for kind in (0, 1)]
    )
    vector_sums = padded(vector_sums.reshape(vector_count, dp_size, wide)).transpose(1, 0, 2)
    vector_sums = jnp.broadcast_to(
        vector_sums[:, :, None], (dp_size, vector_count, mp_size, lanes)
    )
    bias_sums = padded(jnp.stack(bias_grads).reshape(layers, mp_size, dp_size, bias_wide))
    bias_sums = bias_sums.transpose(2, 0, 1, 3)
    rest = jnp.zeros((dp_size, small_rows - vector_count - layers, mp_size, lanes), f32)
    small_grad = jnp.concatenate([vector_sums, bias_sums, rest], axis=1)
    small_grad = small_grad.reshape(dp_size * small_rows, mp_size * lanes).astype(bf16)

    folds = []
    local = []
    for layer in reversed(range(layers)):
        local += weight_grads[layer]
        folds += fold_dims(line_first, line_second, layer)
    local.append(small_grad)
    folds.append(line_first[0][::-1])
    folds = [Fold(dims, mp_size) for dims in folds]
    fold_order = step_order(
        folds, fold_table if tabled else (), lambda t, stage: t // 2 + stage
    )
    owned = fold_all(local, folds, fold_order, dp_size, mp_size)
    small_owned = owned.pop()

    squares_sum = jnp.float32(0.0)
    for gradient in owned:
        squares_sum = squares_sum + jnp.sum(gradient * gradient)
    vector_owned = small_owned[:vector_count, :wide]
    bias_owned = small_owned[vector_count : vector_count + layers, :bias_wide]
    squares_sum = squares_sum + jnp.sum(vector_owned * vector_owned) / mp_size
    squares_sum = squares_sum + jnp.sum(bias_owned * bias_owned)
    grad_norm = jnp.sqrt(lax.psum(squares_sum, ("dp", "mp")))
    factor = jnp.minimum(1.0, clip_bound / grad_norm)

    by_layer = [owned[4 * at : 4 * at + 4] for at in reversed(range(layers))]
    gradients = (
        jnp.stack([each[3].reshape(wide, 3, z_cols) for each in by_layer]),
        jnp.stack([each[2].T for each in by_layer]),
        jnp.stack([each[1] for each in by_layer]),
        jnp.stack([each[0].T for each in by_layer]),
        bias_owned,
        vector_owned[: layers * gain_rows].reshape(layers, gain_rows, wide),
        vector_owned[layers * gain_rows :].reshape(layers, shift_rows, wide),
    )
    masters = (
        qkv_weight, proj_weight, upper_weight, lower_weight, hidden_bias, norm_gains, shift_params
    )
    moments = (
        qkv_moment, proj_moment, upper_moment, lower_moment, bias_moment, gains_moment,
        shifts_moment,
    )
    squares = (
        qkv_square, proj_square, upper_square, lower_square, bias_square, gains_square,
        shifts_square,
    )
    results = [output_stream, input_grad]
    for at in range(7):
        results.extend(
            adam_update(
                masters[at], moments[at], squares[at], gradients[at], factor,
                group_rates[at], group_decays[at],
            )
        )
    results.append(grad_norm)
    return tuple(results)


def fold_dims(line_first, line_second, layer):
    first = [dims[::-1] for dims in line_first]
    second = [dims[::-1] for dims in line_second]
    return second + (first if layer % 2 else first[::-1])


def solution(mesh):
    dp_size = mesh.shape["dp"]
    mp_size = mesh.shape["mp"]
    rows = P(("dp", "mp"), None)
    split_rows = P(None, "dp", None, "mp")
    split_upper = P(None, "dp", "mp")
    split_lower = P(None, "mp", "dp")
    split_bias = P(None, ("mp", "dp"))
    split_vector = P(None, None, "dp")
    groups = (
        split_rows, split_lower, split_upper, split_lower, split_bias, split_vector, split_vector
    )
    placed = tuple(spec for spec in groups for _ in range(3))

    def shards(*args):
        return program(dp_size, mp_size, args)

    return jax.shard_map(
        shards,
        mesh=mesh,
        in_specs=(rows, P("dp", None), rows) + placed,
        out_specs=(rows, rows) + placed + (P(),),
        check_vma=False,
    )
```

```python
import functools
import math

import jax
import jax.numpy as jnp
import numpy as np
from jax import lax
from jax.experimental import pallas as pl
from jax.experimental.pallas import tpu as pltpu
from jax.sharding import PartitionSpec as P

H = 8
HD = 128
STEP = 5
MAX_DOC = 512

norm_eps = 1e-05
clip_bound = 1.0
beta_first = 0.9
beta_second = 0.95
adam_eps = 1e-08
masked_score = -1e30
group_rates = (0.03, 0.12, 0.03, 0.015, 0.3, 0.7, 0.3)
group_decays = (0.1, 0.1, 0.1, 0.1, 0.0, 0.0, 0.0)
contract_rows = (((0,), (0,)), ((), ()))
contract_cols = (((1,), (1,)), ((), ()))
f32 = jnp.float32
bf16 = jnp.bfloat16
score_scale = 1.0 / math.sqrt(HD)
MESH = pl.DeviceIdType.MESH


def adam_update(master, moment, square, gradient, factor, step_rate, decay_rate):
    clipped = gradient * factor
    moment_new = beta_first * moment + (1.0 - beta_first) * clipped
    square_new = beta_second * square + (1.0 - beta_second) * clipped * clipped
    first_hat = moment_new / (1.0 - beta_first**STEP)
    second_hat = square_new / (1.0 - beta_second**STEP)
    master_new = master - step_rate * (
        first_hat / (jnp.sqrt(second_hat) + adam_eps) + decay_rate * master
    )
    return (master_new, moment_new, square_new)


def gelu_tanh(values):
    return jax.nn.gelu(values, approximate=True)


def layer_norm(values, scale_vec, shift_vec):
    center = values - jnp.mean(values, axis=-1, keepdims=True)
    spread = jnp.mean(center * center, axis=-1, keepdims=True)
    return center * lax.rsqrt(spread + norm_eps) * scale_vec + shift_vec


def dot(left, right):
    return jnp.dot(left, right, preferred_element_type=f32)


def dot_rows(left, right):
    return lax.dot_general(left, right, contract_rows, preferred_element_type=f32)


def dot_cols(left, right):
    return lax.dot_general(left, right, contract_cols, preferred_element_type=f32)


def masked_scores(slope, doc_col, doc_row, query, key, first_row, first_col):
    scores = dot_cols(query, key) * score_scale
    rows = first_row + lax.broadcasted_iota(jnp.int32, scores.shape, 0)
    cols = first_col + lax.broadcasted_iota(jnp.int32, scores.shape, 1)
    distance = rows - cols
    allowed = (distance >= 0) & (doc_col == doc_row)
    return jnp.where(allowed, scores - slope * distance.astype(f32), masked_score)


def key_range(first_row, block):
    low = max(0, first_row - (MAX_DOC - 1)) // block * block
    return low, first_row + block


def attend_kernel(heads, block, slope_ref, dcol_ref, drow_ref, qkv_ref, o_ref):
    length = o_ref.shape[0]
    for head in range(heads):
        slope = slope_ref[pl.program_id(0) * heads + head]
        at = head * HD
        kat = (heads + head) * HD
        vat = (2 * heads + head) * HD
        for first_row in range(0, length, block):
            low, high = key_range(first_row, block)
            scores = masked_scores(
                slope,
                dcol_ref[first_row : first_row + block, :],
                drow_ref[:, low:high],
                qkv_ref[first_row : first_row + block, at : at + HD],
                qkv_ref[low:high, kat : kat + HD],
                first_row,
                low,
            )
            shifted = jnp.exp(scores - jnp.max(scores, axis=-1, keepdims=True))
            total = jnp.sum(shifted, axis=-1, keepdims=True)
            prob_low = (shifted * (1.0 / total)).astype(bf16)
            o_ref[first_row : first_row + block, at : at + HD] = dot(
                prob_low, qkv_ref[low:high, vat : vat + HD]
            ).astype(bf16)


def attend_back_kernel(
    heads, block, slope_ref, dcol_ref, drow_ref, qkv_ref, o_ref, do_ref,
    grad_ref, key_acc, value_acc,
):
    length = o_ref.shape[0]
    for head in range(heads):
        slope = slope_ref[pl.program_id(0) * heads + head]
        at = head * HD
        kat = (heads + head) * HD
        vat = (2 * heads + head) * HD
        key_acc[...] = jnp.zeros_like(key_acc)
        value_acc[...] = jnp.zeros_like(value_acc)
        for first_row in range(0, length, block):
            low, high = key_range(first_row, block)
            rows = slice(first_row, first_row + block)
            query = qkv_ref[rows, at : at + HD]
            key = qkv_ref[low:high, kat : kat + HD]
            scores = masked_scores(
                slope, dcol_ref[rows, :], drow_ref[:, low:high], query, key, first_row, low
            )
            shifted = jnp.exp(scores - jnp.max(scores, axis=-1, keepdims=True))
            total = jnp.sum(shifted, axis=-1, keepdims=True)
            probs = shifted * (1.0 / total)
            out_grad = do_ref[rows, at : at + HD]
            value_acc[low:high, :] += dot_rows(probs.astype(bf16), out_grad)
            prob_grad = dot_cols(out_grad, qkv_ref[low:high, vat : vat + HD])
            inner = jnp.sum(
                out_grad.astype(f32) * o_ref[rows, at : at + HD].astype(f32),
                axis=-1,
                keepdims=True,
            )
            score_grad = (probs * (prob_grad - inner)).astype(bf16)
            grad_ref[rows, at : at + HD] = (dot(score_grad, key) * score_scale).astype(bf16)
            key_acc[low:high, :] += dot_rows(score_grad, query)
        grad_ref[:, kat : kat + HD] = (key_acc[...] * score_scale).astype(bf16)
        grad_ref[:, vat : vat + HD] = value_acc[...].astype(bf16)


def attend_specs(length, width):
    def columns(each):
        return pl.BlockSpec((length, each), lambda s: (0, s))

    fixed = [
        pl.BlockSpec(memory_space=pltpu.SMEM),
        pl.BlockSpec((length, 1), lambda s: (0, 0)),
        pl.BlockSpec((1, length), lambda s: (0, 0)),
    ]
    return fixed, columns(3 * width), columns(width)


def attend(slopes, docs, qkv, slots):
    length = qkv.shape[0]
    width = qkv.shape[1] // (3 * slots)
    fixed, wide, narrow = attend_specs(length, width)
    pairs = slots * width // HD * length * length
    return pl.pallas_call(
        functools.partial(attend_kernel, width // HD, min(256, length)),
        grid=(slots,),
        in_specs=fixed + [wide],
        out_specs=narrow,
        out_shape=jax.ShapeDtypeStruct((length, slots * width), bf16),
        compiler_params=pltpu.CompilerParams(vmem_limit_bytes=32 * 2**20),
        cost_estimate=pl.CostEstimate(
            flops=4 * pairs * HD, bytes_accessed=3 * qkv.size, transcendentals=pairs
        ),
    )(slopes, docs.reshape(-1, 1), docs.reshape(1, -1), qkv)


def attend_back(slopes, docs, qkv, o, do, slots):
    length = qkv.shape[0]
    width = qkv.shape[1] // (3 * slots)
    fixed, wide, narrow = attend_specs(length, width)
    pairs = slots * width // HD * length * length
    return pl.pallas_call(
        functools.partial(attend_back_kernel, width // HD, min(256, length)),
        grid=(slots,),
        in_specs=fixed + [wide, narrow, narrow],
        out_specs=wide,
        out_shape=jax.ShapeDtypeStruct(qkv.shape, bf16),
        scratch_shapes=[pltpu.VMEM((length, HD), f32), pltpu.VMEM((length, HD), f32)],
        compiler_params=pltpu.CompilerParams(vmem_limit_bytes=32 * 2**20),
        cost_estimate=pl.CostEstimate(
            flops=10 * pairs * HD, bytes_accessed=6 * qkv.size, transcendentals=pairs
        ),
    )(slopes, docs.reshape(-1, 1), docs.reshape(1, -1), qkv, o, do)


def bits_of(size):
    return [1 << at for at in range(size.bit_length() - 1)]


def flip(value, mask):
    bit = 1
    while bit <= mask:
        if mask & bit:
            value = value + bit * (1 - 2 * ((value // bit) % 2))
        bit *= 2
    return value


def place(at, size):
    return pl.multiple_of(at * size, size)


class Spread:
    def __init__(self, dims, mp_size):
        self.dims = tuple(dims)
        self.events = []
        masks, spread = [0], False
        for stage, dim in enumerate(self.dims):
            for mask in masks:
                if dim == "mp":
                    for hops in range(1, mp_size):
                        self.events += [(stage, mask, way, hops) for way in (1, -1)]
                else:
                    places = range(mp_size) if spread else (0,)
                    self.events += [(stage, mask | dim, 0, at) for at in places]
            if dim == "mp":
                spread = True
            else:
                masks = masks + [mask | dim for mask in masks]
        self.events += [(len(self.dims), mask | 1, 0, 0) for mask in masks]

    def full(self, stage):
        return "mp" in self.dims[:stage]


class Fold:
    def __init__(self, dims, mp_size):
        self.dims = tuple(dims)
        masks = [0]
        for dim in self.dims:
            if dim != "mp":
                masks = masks + [mask | dim for mask in masks]
        self.masks = masks
        self.kept = {}
        self.events = [(0, mask, 0, 0) for mask in sorted(masks, key=self.leaves)]
        rows = list(masks)
        for stage, dim in enumerate(self.dims, 1):
            if dim != "mp":
                rows = [mask for mask in rows if not mask & dim]
            self.kept[stage] = list(rows)
            if dim == "mp":
                for hops in reversed(range(mp_size - 1)):
                    for mask in rows:
                        self.events += [(stage, mask, way, hops) for way in (1, -1)]
            else:
                places = reversed(range(mp_size)) if self.full(stage) else (0,)
                places = list(places)
                for mask in rows:
                    self.events += [(stage, mask, 0, at) for at in places]

    def leaves(self, mask):
        for at, dim in enumerate(self.dims):
            if dim != "mp" and mask & dim:
                return at
        return len(self.dims)

    def full(self, stage):
        return "mp" not in self.dims[: stage - 1]


def number(plans, mp_size, single):
    index, total = {}, 0
    for t, plan in enumerate(plans):
        for event in plan.events:
            stage, mask, way, at = event
            if way or single(plan, stage):
                index[(t,) + event] = total
                total += 1
            elif (t, stage, mask) not in index:
                index[t, stage, mask] = total
                total += mp_size
    return index, total


def spread_single(plan, stage):
    return stage == len(plan.dims)


def fold_single(plan, stage):
    return stage == 0


def merge_small(order, plans):
    t = len(plans) - 1
    small = [(t, event) for event in plans[t].events]
    out, used = [], 0
    for at, step in enumerate(order):
        out.append(step)
        while used < len(small) and (used + 1) * len(order) <= (at + 1) * (len(small) + 1):
            out.append(small[used])
            used += 1
    return out + small[used:]


def step_order(plans, table, by_stage):
    steps = [(t, event) for t, plan in enumerate(plans[:-1]) for event in plan.events]
    if len(table) == len(steps):
        return merge_small([steps[at] for at in table], plans)
    ranked = sorted(range(len(steps)), key=lambda at: (by_stage(steps[at][0], steps[at][1][0]), at))
    return merge_small([steps[at] for at in ranked], plans)


def forward_order(plans, layers, table):
    steps = [(t, event) for t, plan in enumerate(plans) for event in plan.events]
    compute = [(layer, name) for layer in range(layers) for name in FORWARD_STEPS]
    if len(table) == len(steps) + len(compute):
        steps += compute
        return [steps[at] for at in table]
    return steps + compute


def greet(z, d, upper, mp_size, mp_bits=(), across=None, moved=None):
    barrier = pltpu.get_barrier_semaphore()
    for bit in mp_bits:
        pl.semaphore_signal(
            barrier, inc=1, device_id={"mp": flip(z, bit)}, device_id_type=MESH
        )
    for bit in [1] + upper:
        pl.semaphore_signal(
            barrier, inc=1, device_id={"dp": flip(d, bit)}, device_id_type=MESH
        )
    also = 0
    if across is not None:

        @pl.when(moved)
        def _():
            pl.semaphore_signal(barrier, inc=1, device_id=across, device_id_type=MESH)

        also = jnp.where(moved, 1, 0)
    for way in (1, -1):

        @pl.when((z + way >= 0) & (z + way < mp_size))
        def _(way=way):
            pl.semaphore_signal(
                barrier, inc=1, device_id={"mp": z + way}, device_id_type=MESH
            )

    around = jnp.where(z > 0, 1, 0) + jnp.where(z < mp_size - 1, 1, 0)
    pl.semaphore_wait(barrier, 1 + len(upper) + len(mp_bits) + around + also)


class SpreadWork:
    def __init__(self, plans, order, mp_size, shards, outs, send_sems, recv_sems, own_sems):
        self.plans, self.mp_size = plans, mp_size
        self.order = [step for step in order if not isinstance(step[1], str)]
        self.shards, self.outs = shards, outs
        self.sems = send_sems, recv_sems
        self.own_sems = own_sems
        self.z = lax.axis_index("mp")
        self.d = lax.axis_index("dp")
        self.upper = [dim for dim in plans[0].dims if dim != "mp"]
        self.index, _ = number(plans, mp_size, spread_single)
        self.owns = []
        self.left = {}
        for t, event in self.order:
            if event[0] < len(plans[t].dims):
                self.left[t, event[1]] = self.left.get((t, event[1]), 0) + 1

    def inside(self, at):
        return (at >= 0) & (at < self.mp_size)

    def region(self, t, mask, block):
        wide, cols = self.shards[t].shape
        rows = pl.ds(place(flip(self.d, mask), wide), wide)
        if block is None:
            return self.outs[t].at[rows, :]
        return self.outs[t].at[rows, pl.ds(place(block, cols), cols)]

    def remote(self, t, event, block, src, dst, to):
        stage, mask, way, at = event
        if way or stage == len(self.plans[t].dims):
            sem = self.index[(t,) + event]
        else:
            sem = self.index[t, stage, mask] + block
        return pltpu.make_async_remote_copy(
            src_ref=src,
            dst_ref=dst,
            send_sem=self.sems[0].at[sem],
            recv_sem=self.sems[1].at[sem],
            device_id=to,
            device_id_type=MESH,
        )

    def sending(self, t, event, block, to, own=False):
        stage, mask, way, at = event
        dims = self.plans[t].dims
        bit = 0 if way else 1 if stage == len(dims) else dims[stage]
        dst = self.region(t, mask ^ bit, block)
        return self.remote(t, event, block, self.shards[t] if own else dst, dst, to)

    def arrival(self, t, event, block):
        dst = self.region(t, event[1], block)
        return self.remote(t, event, block, dst, dst, {"dp": self.d, "mp": self.z})

    def on_line(self, t, stage, mask, block, way, hops, own):
        @pl.when(self.inside(self.z + way))
        def _():
            to = {"mp": self.z + way}
            self.sending(t, (stage, mask, way, hops), block, to, own).start()

    def onward(self, t, stage, mask, block, own=False):
        dims = self.plans[t].dims
        for later in range(stage, len(dims)):
            if dims[later] == "mp":
                for way in (1, -1):
                    self.on_line(t, later, mask, block, way, 1, own)
            else:
                to = {"dp": flip(self.d, dims[later])}
                self.sending(t, (later, mask | dims[later], 0, None), block, to, own).start()

    def place_of(self, t, event):
        return flip(self.z, event[3]) if self.plans[t].full(event[0]) else self.z

    def begin(self):
        for t in range(len(self.plans)):
            self.onward(t, 0, 0, self.z, True)
            own = pltpu.make_async_copy(
                self.shards[t], self.region(t, 0, self.z), self.own_sems.at[t]
            )
            own.start()
            self.owns.append(own)

    def step(self, t, event):
        stage, mask, way, at = event
        last = len(self.plans[t].dims)
        if stage == last:
            self.arrival(t, event, None).wait_recv()
            return
        if way:
            block = self.z - way * at

            @pl.when(self.inside(block))
            def _():
                self.arrival(t, event, block).wait_recv()
                if at + 1 < self.mp_size:
                    self.on_line(t, stage, mask, block, way, at + 1, False)
                self.onward(t, stage + 1, mask, block)

        else:
            block = self.place_of(t, event)
            self.arrival(t, event, block).wait_recv()
            self.onward(t, stage + 1, mask, block)
        self.left[t, mask] -= 1
        if self.left[t, mask] == 0:
            if mask == 0:
                self.owns[t].wait()
            to = {"dp": flip(self.d, 1)}
            self.sending(t, (last, mask | 1, 0, 0), None, to).start()

    def finish(self):
        for t, event in self.order:
            stage, mask, way, at = event
            if stage == len(self.plans[t].dims):
                self.sending(t, event, None, {"dp": flip(self.d, 1)}).wait_send()
            elif way:

                @pl.when(self.inside(self.z - way * (at - 1)) & self.inside(self.z + way))
                def _():
                    to = {"mp": self.z + way}
                    self.sending(t, event, self.z - way * (at - 1), to).wait_send()

            else:
                to = {"dp": flip(self.d, self.plans[t].dims[stage])}
                self.sending(t, event, self.place_of(t, event), to).wait_send()


def spread_kernel(plans, order, mp_size, *refs):
    n = len(plans)
    work = SpreadWork(plans, order, mp_size, refs[:n], refs[n : 2 * n], *refs[2 * n :])
    greet(work.z, work.d, work.upper, mp_size)
    work.begin()
    for t, event in order:
        work.step(t, event)
    work.finish()


def spread_all(shards, plans, order, dp_size, mp_size):
    _, total = number(plans, mp_size, spread_single)
    return pl.pallas_call(
        functools.partial(spread_kernel, plans, order, mp_size),
        out_shape=[
            jax.ShapeDtypeStruct((s.shape[0] * dp_size, s.shape[1] * mp_size), s.dtype)
            for s in shards
        ],
        in_specs=[pl.BlockSpec(memory_space=pl.ANY)] * len(shards),
        out_specs=[pl.BlockSpec(memory_space=pl.ANY)] * len(shards),
        scratch_shapes=[
            pltpu.SemaphoreType.DMA((total,)),
            pltpu.SemaphoreType.DMA((total,)),
            pltpu.SemaphoreType.DMA((len(shards),)),
        ],
        compiler_params=pltpu.CompilerParams(collective_id=0, has_side_effects=True),
    )(*shards)


def fold_kernel(plans, order, mp_size, vector_count, *refs):
    n = len(plans)
    grads, outs = refs[:n], refs[n : 2 * n]
    norm_ref = refs[2 * n]
    landed, sums = refs[2 * n + 1 : 3 * n + 1], refs[3 * n + 1 : 4 * n + 1]
    at = 4 * n + 1
    recv = {}
    for t, plan in enumerate(plans):
        for stage in range(1, len(plan.dims) + 1):
            recv[t, stage] = refs[at]
            at += 1
    staging, tiles, load_sems, own_sems, tile_sems, send_sems, recv_sems = refs[at:]
    z = lax.axis_index("mp")
    d = lax.axis_index("dp")
    upper = [dim for dim in plans[0].dims if dim != "mp"]
    index, _ = number(plans, mp_size, fold_single)
    wides = [out.shape[0] for out in outs]
    cols = [out.shape[1] for out in outs]

    def inside(at):
        return (at >= 0) & (at < mp_size)

    def rows_of(t, mask):
        return pl.ds(plans[t].masks.index(mask) * wides[t], wides[t])

    def sum_at(t, mask, block):
        return sums[t].at[rows_of(t, mask), pl.ds(place(block, cols[t]), cols[t])]

    def landing(t, event, block):
        stage, mask, way, at = event
        kept = plans[t].kept[stage].index(mask)
        if way:
            return recv[t, stage].at[kept, (0 if way == 1 else mp_size - 1) + at]
        return recv[t, stage].at[kept, block if plans[t].full(stage) else 0]

    def remote(t, event, block, src, dst, to):
        stage, mask, way, at = event
        if way or stage == 0:
            sem = index[(t,) + event]
        else:
            sem = index[t, stage, mask] + block
        return pltpu.make_async_remote_copy(
            src_ref=src,
            dst_ref=dst,
            send_sem=send_sems.at[sem],
            recv_sem=recv_sems.at[sem],
            device_id=to,
            device_id_type=MESH,
        )

    def core_copy(t, mask):
        rows = pl.ds(place(flip(d, mask | 1), wides[t]), wides[t])
        dst = landed[t].at[rows_of(t, mask), :]
        return remote(t, (0, mask, 0, 0), 0, grads[t].at[rows, :], dst, {"dp": flip(d, 1)})

    def own_copy(t, mask):
        rows = pl.ds(place(flip(d, mask), wides[t]), wides[t])
        return pltpu.make_async_copy(
            grads[t].at[rows, :],
            sums[t].at[rows_of(t, mask), :],
            own_sems.at[t, plans[t].masks.index(mask)],
        )

    def bit_copy(t, stage, mask, block):
        dim = plans[t].dims[stage - 1]
        event = (stage, mask & ~dim, 0, None)
        dst = landing(t, event, block)
        return remote(t, event, block, sum_at(t, mask, block), dst, {"dp": flip(d, dim)})

    def line_copy(t, stage, mask, way, hops):
        event = (stage, mask, way, hops - 1)
        src = sum_at(t, mask, z + way * hops)
        return remote(t, event, None, src, landing(t, event, None), {"mp": z + way})

    def arrival(t, event, block):
        dst = landing(t, event, block)
        return remote(t, event, block, dst, dst, {"dp": d, "mp": z})

    def add(dst, src, wide):
        step = 16

        def some_rows(at, carry):
            rows = pl.ds(pl.multiple_of(at * step, step), step)
            total = dst[rows, :].astype(f32) + src[rows, :].astype(f32)
            dst[rows, :] = total.astype(bf16)
            return carry

        lax.fori_loop(0, wide // step, some_rows, 0)

    def advance(t, stage, mask, block, other):
        if stage > len(plans[t].dims):
            return
        dim = plans[t].dims[stage - 1]
        if dim == "mp":
            if other:
                for way, end in ((1, 0), (-1, mp_size - 1)):

                    @pl.when(z == end)
                    def _(way=way):
                        line_copy(t, stage, mask, way, other).start()

        elif mask & dim:
            bit_copy(t, stage, mask, block).start()

    mp_bits = bits_of(mp_size)
    greet(z, d, upper, mp_size, mp_bits)
    cores = [(t, event[1]) for t, event in order if event[0] == 0]
    for t, mask in cores:
        core_copy(t, mask).start()
        own_copy(t, mask).start()

    def load(at):
        t, mask = cores[at]
        return pltpu.make_async_copy(
            landed[t].at[rows_of(t, mask), :],
            staging.at[at % 2, pl.ds(0, wides[t]), pl.ds(0, cols[t] * mp_size)],
            load_sems.at[at % 2],
        )

    seen = 0
    brought = {}
    for t, event in order:
        stage, mask, way, at = event
        plan = plans[t]
        if stage == 0:
            for ahead in (0, 1) if seen == 0 else (seen + 1,):
                if ahead < len(cores):
                    core_copy(*cores[ahead]).wait_recv()
                    load(ahead).start()
            load(seen).wait()
            own_copy(t, mask).wait()
            part = staging.at[seen % 2, pl.ds(0, wides[t]), pl.ds(0, cols[t] * mp_size)]
            add(sums[t].at[rows_of(t, mask), :], part, wides[t])
            seen += 1
            for other in reversed(range(mp_size)):
                advance(t, 1, mask, flip(z, other), other)
        elif way:
            block = z + way * at

            @pl.when(inside(block) & inside(z - way))
            def _():
                arrival(t, event, None).wait_recv()
                add(sum_at(t, mask, block), landing(t, event, None), wides[t])
                if at > 0:
                    line_copy(t, stage, mask, way, at).start()

            if at == 0:
                brought[t, mask] = brought.get((t, mask), 0) + 1
                if brought[t, mask] == 2:
                    advance(t, stage + 1, mask, z, 0)
        else:
            block = flip(z, at) if plan.full(stage) else z
            arrival(t, event, block).wait_recv()
            add(sum_at(t, mask, block), landing(t, event, block), wides[t])
            advance(t, stage + 1, mask, block, at)

    tiles[0] = jnp.zeros(tiles.shape[1:], f32)
    for t in range(n):
        step = 16

        def some_rows(at, carry, t=t):
            rows = pl.ds(pl.multiple_of(at * step, step), step)
            part = sums[t][rows, pl.ds(place(z, cols[t]), cols[t])].astype(f32)
            outs[t][rows, :] = part
            part = part * part
            total = carry
            for low in range(0, step, 8):
                for left in range(0, cols[t], HD):
                    total = total + part[low : low + 8, left : left + HD]
            return total

        if t == n - 1:
            whole = sums[t][pl.ds(0, wides[t]), pl.ds(place(z, cols[t]), cols[t])].astype(f32)
            outs[t][...] = whole
            row = lax.broadcasted_iota(jnp.int32, whole.shape, 0)
            whole = whole * whole
            whole = jnp.where(row < vector_count, whole * (1.0 / mp_size), whole)
            for low in range(0, wides[t], 8):
                tiles[0] += whole[low : low + 8, :HD]
        else:
            zero = jnp.zeros((8, HD), f32)
            tiles[0] += lax.fori_loop(0, wides[t] // step, some_rows, zero)
    pairs = [{"dp": flip(d, bit)} for bit in [1] + upper]
    pairs += [{"mp": flip(z, bit)} for bit in mp_bits]
    for at, to in enumerate(pairs):
        exchange = pltpu.make_async_remote_copy(
            src_ref=tiles.at[2 * at],
            dst_ref=tiles.at[2 * at + 1],
            send_sem=tile_sems.at[2 * at],
            recv_sem=tile_sems.at[2 * at + 1],
            device_id=to,
            device_id_type=MESH,
        )
        exchange.start()
        exchange.wait()
        tiles[2 * at + 2] = tiles[2 * at] + tiles[2 * at + 1]
    norm_ref[...] = tiles[2 * len(pairs)]

    for t, event in order:
        stage, mask, way, at = event
        if stage == 0:
            core_copy(t, mask).wait_send()
        elif way:

            @pl.when(inside(z + way) & inside(z + way * (at + 1)))
            def _():
                line_copy(t, stage, mask, way, at + 1).wait_send()

        else:
            block = flip(z, at) if plans[t].full(stage) else z
            bit_copy(t, stage, mask | plans[t].dims[stage - 1], block).wait_send()


def fold_all(grads, plans, order, dp_size, mp_size, vector_count):
    n = len(grads)
    _, total = number(plans, mp_size, fold_single)
    wides = [g.shape[0] // dp_size for g in grads]
    cols = [g.shape[1] // mp_size for g in grads]
    rounds = len(bits_of(dp_size)) + len(bits_of(mp_size))
    halves = [(dp_size // 2 * wide, mp_size * each) for wide, each in zip(wides, cols)]
    scratch = [pltpu.VMEM(half, bf16) for half in halves]
    for plan, wide, each in zip(plans, wides, cols):
        for stage, dim in enumerate(plan.dims, 1):
            blocks = 2 * (mp_size - 1) if dim == "mp" else mp_size if plan.full(stage) else 1
            scratch.append(pltpu.VMEM((len(plan.kept[stage]), blocks, wide, each), bf16))
    scratch += [
        pltpu.VMEM((2, max(wides), mp_size * max(cols)), bf16),
        pltpu.VMEM((2 * rounds + 1, 8, HD), f32),
        pltpu.SemaphoreType.DMA((2,)),
        pltpu.SemaphoreType.DMA((n, dp_size // 2)),
        pltpu.SemaphoreType.DMA((2 * rounds,)),
        pltpu.SemaphoreType.DMA((total,)),
        pltpu.SemaphoreType.DMA((total,)),
    ]
    out = pl.pallas_call(
        functools.partial(fold_kernel, plans, order, mp_size, vector_count),
        out_shape=[jax.ShapeDtypeStruct((wide, each), f32) for wide, each in zip(wides, cols)]
        + [jax.ShapeDtypeStruct((8, HD), f32)]
        + [jax.ShapeDtypeStruct(half, bf16) for half in halves],
        in_specs=[pl.BlockSpec(memory_space=pl.ANY)] * n,
        out_specs=[pl.BlockSpec(memory_space=pltpu.VMEM)] * (n + 1)
        + [pl.BlockSpec(memory_space=pl.ANY)] * n,
        scratch_shapes=scratch,
        compiler_params=pltpu.CompilerParams(
            collective_id=1, has_side_effects=True, vmem_limit_bytes=63 * 2**20
        ),
    )(*grads)
    return list(out[:n]), out[n]


def adam_kernel(
    factor_ref, qkv_1, qkv_0, proj_1, proj_0, upper_1, upper_0, lower_1, lower_0, *refs
):
    factor = factor_ref[0, 0]
    ins, outs = refs[:12], refs[12:]

    def update(group, at, gradient):
        found = [ins[3 * group + which][at] for which in range(3)]
        new = adam_update(
            *found, gradient, factor, group_rates[group], group_decays[group]
        )
        for which in range(3):
            outs[3 * group + which][at] = new[which]

    for layer, gradient in enumerate((qkv_0, qkv_1)):
        wide, cols = gradient.shape[0], gradient.shape[1] // 3
        for part in range(3):
            for low in range(0, wide, 64):
                update(
                    0,
                    (layer, part, slice(low, low + 64)),
                    gradient[low : low + 64, part * cols : (part + 1) * cols],
                )
    for layer, gradient in enumerate((proj_0, proj_1)):
        for low in range(0, gradient.shape[1], HD):
            update(1, (layer, slice(low, low + HD)), gradient[:, low : low + HD].T)
    for layer, gradient in enumerate((upper_0, upper_1)):
        for low in range(0, gradient.shape[0], 16):
            update(2, (layer, slice(low, low + 16)), gradient[low : low + 16, :])
    for layer, gradient in enumerate((lower_0, lower_1)):
        for low in range(0, gradient.shape[1], HD):
            update(3, (layer, slice(low, low + HD)), gradient[:, low : low + HD].T)


def adam_all(factor, gradients, states):
    vmem = pl.BlockSpec(memory_space=pltpu.VMEM)
    return pl.pallas_call(
        adam_kernel,
        out_shape=[jax.ShapeDtypeStruct(state.shape, f32) for state in states],
        in_specs=[pl.BlockSpec(memory_space=pltpu.SMEM)] + [vmem] * (8 + len(states)),
        out_specs=[vmem] * len(states),
        compiler_params=pltpu.CompilerParams(vmem_limit_bytes=60 * 2**20),
    )(factor.reshape(1, 1), *gradients, *states)


ROWS = 64
TILE = 256


def norm_rows(src, dst, gain, shift):
    def some_rows(at, carry):
        rows = pl.ds(pl.multiple_of(at * ROWS, ROWS), ROWS)
        dst[rows, :] = layer_norm(src[rows, :], gain, shift).astype(bf16)
        return carry

    lax.fori_loop(0, src.shape[0] // ROWS, some_rows, 0)


def tiles_of(width, body):
    def one(at, carry):
        body(pl.multiple_of(at * TILE, TILE))
        return carry

    lax.fori_loop(0, width // TILE, one, 0)


def attend_head(qkv, out, at, width, out_at, slope, doc_cols, doc_rows):
    length = qkv.shape[0]
    block = min(256, length)
    for first_row in range(0, length, block):
        low, high = key_range(first_row, block)
        scores = masked_scores(
            slope,
            doc_cols[first_row : first_row + block, :],
            doc_rows[:, low:high],
            qkv[first_row : first_row + block, at : at + HD],
            qkv[low:high, at + width : at + width + HD],
            first_row,
            low,
        )
        shifted = jnp.exp(scores - jnp.max(scores, axis=-1, keepdims=True))
        total = jnp.sum(shifted, axis=-1, keepdims=True)
        prob_low = (shifted * (1.0 / total)).astype(bf16)
        value = qkv[low:high, at + 2 * width : at + 2 * width + HD]
        out[first_row : first_row + block, out_at : out_at + HD] = dot(prob_low, value).astype(bf16)


FORWARD_STEPS = (
    ("norm_one", "other_0", "other_1", "own_0", "own_1", "share")
    + tuple(f"head_{at}" for at in range(4))
    + ("back", "proj", "norm_two")
    + tuple(f"up_{at}" for at in range(8))
    + tuple(f"down_{at}" for at in range(4))
)


def forward_kernel(plans, order, mp_size, layers, vector_count, gain_rows, shift_rows, *refs):
    n = len(plans)
    shards = refs[:n]
    inputs, doc_cols, doc_rows = refs[n : n + 3]
    outs = refs[n + 3 : 2 * n + 3]
    at = 2 * n + 3
    saved = [refs[at + 9 * layer : at + 9 * layer + 9] for layer in range(layers)]
    at += 9 * layers
    last_stream = refs[at]
    (
        streams, middles, normed_one, normed_two, send_buf, qkv_full, mixed, attended,
        hidden, active, w_qkv, w_proj, w_up, w_down, small_buf, vectors, biases, traded,
        load_sems, save_sems, trade_sems, head_sems, send_sems, recv_sems, own_sems,
    ) = refs[at + 1 :]
    work = SpreadWork(plans, order, mp_size, shards, outs, send_sems, recv_sems, own_sems)
    z, d = work.z, work.d
    core = d % 2
    moved = core != z % 2
    partner = {"dp": flip(d, 1)}
    across = {"dp": flip(d, 1), "mp": flip(z, 1)}
    tokens = inputs.shape[0]
    features = inputs.shape[1]
    half = attended.shape[2] // 2
    wide_small = shards[-1].shape[0]
    lanes = shards[-1].shape[1]
    third = w_qkv.shape[2] // 3
    slots = qkv_full.shape[2] // w_qkv.shape[2]
    heads_slot = third // HD

    greet(z, d, work.upper, mp_size, (), across, moved)
    trade = pltpu.make_async_remote_copy(
        src_ref=inputs, dst_ref=traded, send_sem=trade_sems.at[0], recv_sem=trade_sems.at[1],
        device_id=across, device_id_type=MESH,
    )
    keep = pltpu.make_async_copy(inputs, traded, trade_sems.at[2])

    @pl.when(moved)
    def _():
        trade.start()

    @pl.when(jnp.logical_not(moved))
    def _():
        keep.start()

    work.begin()

    saves = []

    def save(src, dst):
        copy = pltpu.make_async_copy(src, dst, save_sems.at[len(saves)])
        copy.start()
        saves.append(copy)
        return copy

    loads = {}

    def load(key, src, dst, slot):
        copy = pltpu.make_async_copy(src, dst, load_sems.at[slot])
        copy.start()
        loads[key] = copy

    def load_tile(layer, kind, at):
        full = outs[4 * layer : 4 * layer + 4]
        if kind == "qkv":
            cols = w_qkv.shape[2]
            first = (1 - core) * slots if at < slots else core * slots
            where = pl.ds(place(first + at % slots, cols), cols)
            load((layer, kind, at), full[0].at[:, where], w_qkv.at[at % 2], at % 2)
        elif kind == "proj":
            load((layer, kind, at), full[1], w_proj, 2)
        elif kind == "up":
            cols = w_up.shape[2]
            where = pl.ds(at * cols, cols)
            load((layer, kind, at), full[2].at[:, where], w_up.at[at % 2], 3 + at % 2)
        else:
            rows = w_down.shape[1]
            where = pl.ds(at * rows, rows)
            load((layer, kind, at), full[3].at[where, :], w_down.at[at % 2], 5 + at % 2)

    def tile(layer, kind, at, count):
        if (layer, kind, at) not in loads:
            load_tile(layer, kind, at)
        loads[layer, kind, at].wait()
        if at + 1 < count:
            load_tile(layer, kind, at + 1)

    def share_copy(layer):
        rows = pl.ds(place(core, tokens), tokens)
        return pltpu.make_async_remote_copy(
            src_ref=send_buf.at[layer], dst_ref=qkv_full.at[layer, rows, :],
            send_sem=head_sems.at[4 * layer], recv_sem=head_sems.at[4 * layer + 1],
            device_id=partner, device_id_type=MESH,
        )

    def back_copy(layer):
        rows = pl.ds(place(1 - core, tokens), tokens)
        return pltpu.make_async_remote_copy(
            src_ref=mixed.at[layer, rows, :],
            dst_ref=attended.at[layer, :, pl.ds(place(core, half), half)],
            send_sem=head_sems.at[4 * layer + 2], recv_sem=head_sems.at[4 * layer + 3],
            device_id=partner, device_id_type=MESH,
        )

    def vector(at):
        return vectors[at : at + 1, :]

    ahead = {
        "norm_one": ("qkv", 0), "head_0": ("proj", 1), "proj": ("up", 2), "up_6": ("down", 3)
    }

    def compute(layer, name):
        kind, _, at = name.partition("_")
        if name in ahead and 4 * layer + ahead[name][1] not in missing:
            load_tile(layer, ahead[name][0], 0)
        gain = layer * gain_rows
        shift = layers * gain_rows + layer * shift_rows
        keeps = saved[layer]
        if name == "norm_one":
            if layer == 0:
                small = pltpu.make_async_copy(outs[-1], small_buf, load_sems.at[7])
                small.start()

                @pl.when(moved)
                def _():
                    trade.wait_recv()

                @pl.when(jnp.logical_not(moved))
                def _():
                    keep.wait()

                streams[0] = traded[...].astype(f32)
                small.wait()
                for b in range(outs[-1].shape[0] // wide_small):
                    rows = small_buf[b * wide_small : (b + 1) * wide_small, :].astype(f32)
                    vectors[:, b * lanes : (b + 1) * lanes] = rows[:, :lanes]
                    for m in range(mp_size):
                        first = m * (biases.shape[1] // mp_size) + b * lanes
                        biases[:, first : first + lanes] = rows[:, m * lanes : (m + 1) * lanes]
            norm_rows(streams.at[layer], normed_one.at[layer], vector(gain), vector(shift))
            save(streams.at[layer], keeps[0])
            save(normed_one.at[layer], keeps[2])
        elif kind in ("other", "own"):
            at = int(at)
            tile(layer, "qkv", at + (slots if kind == "own" else 0), 2 * slots)
            weight = w_qkv.at[at % 2]
            cols = w_qkv.shape[2]

            def piece(first):
                values = dot(normed_one[layer], weight[:, pl.ds(first, TILE)]).astype(bf16)
                to = pl.ds(pl.multiple_of(at * cols + first, TILE), TILE)
                if kind == "own":
                    qkv_full[layer, pl.ds(place(core, tokens), tokens), to] = values
                else:
                    send_buf[layer, :, to] = values

            tiles_of(cols, piece)
            if kind == "other" and at == slots - 1:
                share_copy(layer).start()
        elif kind == "share":
            arrived = pltpu.make_async_remote_copy(
                src_ref=send_buf.at[layer],
                dst_ref=qkv_full.at[layer, pl.ds(place(1 - core, tokens), tokens), :],
                send_sem=head_sems.at[4 * layer], recv_sem=head_sems.at[4 * layer + 1],
                device_id=partner, device_id_type=MESH,
            )
            arrived.wait_recv()
            save(qkv_full.at[layer], keeps[3])
        elif kind == "head":
            head = int(at)
            slot, place_in = head // heads_slot, head % heads_slot
            slope = 0.5 ** (head + 1.0) * jnp.where(core == 0, 1.0, 0.5 ** (slots * heads_slot))
            attend_head(
                qkv_full.at[layer], mixed.at[layer], slot * 3 * third + place_in * HD, third,
                head * HD, slope, doc_cols, doc_rows,
            )
            if head == slots * heads_slot - 1:
                back_copy(layer).start()
                rows = pl.ds(place(core, tokens), tokens)
                attended[layer, :, pl.ds(place(core, half), half)] = mixed[layer, rows, :]
                save(mixed.at[layer], keeps[4])
        elif kind == "back":
            arrived = pltpu.make_async_remote_copy(
                src_ref=mixed.at[layer, pl.ds(0, tokens), :],
                dst_ref=attended.at[layer, :, pl.ds(place(1 - core, half), half)],
                send_sem=head_sems.at[4 * layer + 2], recv_sem=head_sems.at[4 * layer + 3],
                device_id=partner, device_id_type=MESH,
            )
            arrived.wait_recv()
            save(attended.at[layer], keeps[5])
        elif kind == "proj":
            tile(layer, "proj", 0, 1)

            def piece(first):
                cols = pl.ds(first, TILE)
                values = dot_cols(attended[layer], w_proj[cols, :])
                middles[layer, :, cols] = streams[layer, :, cols] + values

            tiles_of(features, piece)
        elif name == "norm_two":
            norm_rows(
                middles.at[layer], normed_two.at[layer], vector(gain + 1), vector(shift + 1)
            )
            save(middles.at[layer], keeps[1])
            save(normed_two.at[layer], keeps[6])
        elif kind == "up":
            at = int(at)
            if at == 0 and layer > 0:
                for copy in big_saves[layer - 1]:
                    copy.wait()
            cols = w_up.shape[2]
            tile(layer, "up", at, hidden.shape[1] // cols)
            weight = w_up.at[at % 2]

            def piece(first):
                to = pl.ds(pl.multiple_of(at * cols + first, TILE), TILE)
                bias = biases[vector_count + layer : vector_count + layer + 1, to]
                values = dot(normed_two[layer], weight[:, pl.ds(first, TILE)]) + bias
                hidden[:, to] = values.astype(bf16)
                active[:, to] = gelu_tanh(values).astype(bf16)

            tiles_of(cols, piece)
            if (at + 1) * cols == hidden.shape[1]:
                big_saves[layer] = [save(hidden, keeps[7]), save(active, keeps[8])]
        elif kind == "down":
            at = int(at)
            rows = w_down.shape[1]
            tile(layer, "down", at, features // rows)
            weight = w_down.at[at % 2]
            out = streams.at[layer + 1]
            cols = pl.ds(at * rows, rows)
            out[:, cols] = middles[layer, :, cols] + vector(shift + 2)[:, at * rows : (at + 1) * rows]

            def piece(step, carry):
                inner = pl.ds(pl.multiple_of(step * 1024, 1024), 1024)
                out[:, cols] += dot_cols(active[:, inner], weight[:, inner])
                return carry

            lax.fori_loop(0, hidden.shape[1] // 1024, piece, 0)

    big_saves = {}
    missing = {}
    for t, _ in work.order:
        missing[t] = missing.get(t, 0) + 1
    for step in order:
        if isinstance(step[1], str):
            compute(*step)
        else:
            work.step(*step)
            missing[step[0]] -= 1
            if missing[step[0]] == 0:
                del missing[step[0]]
    save(streams.at[layers], last_stream)
    done_already = [id(copy) for layer in range(layers - 1) for copy in big_saves[layer]]
    for copy in saves:
        if id(copy) not in done_already:
            copy.wait()
    for layer in range(layers):
        share_copy(layer).wait_send()
        back_copy(layer).wait_send()

    @pl.when(moved)
    def _():
        trade.wait_send()

    work.finish()


def forward_all(
    shards, inputs, docs, plans, order, dp_size, mp_size, layers, vector_count, gain_rows, shift_rows
):
    _, total = number(plans, mp_size, spread_single)
    tokens, features = inputs.shape
    length = docs.shape[0]
    half = features // 2
    units = shards[2].shape[1] * mp_size
    cols = shards[0].shape[1]
    slots = mp_size // 2
    any_place = pl.BlockSpec(memory_space=pl.ANY)
    vmem = pl.BlockSpec(memory_space=pltpu.VMEM)
    saved = [
        jax.ShapeDtypeStruct((tokens, features), f32),
        jax.ShapeDtypeStruct((tokens, features), f32),
        jax.ShapeDtypeStruct((tokens, features), bf16),
        jax.ShapeDtypeStruct((length, slots * cols), bf16),
        jax.ShapeDtypeStruct((length, half), bf16),
        jax.ShapeDtypeStruct((tokens, features), bf16),
        jax.ShapeDtypeStruct((tokens, features), bf16),
        jax.ShapeDtypeStruct((tokens, units), bf16),
        jax.ShapeDtypeStruct((tokens, units), bf16),
    ]
    small_shape = (shards[-1].shape[0] * dp_size, shards[-1].shape[1] * mp_size)
    out_shape = [
        jax.ShapeDtypeStruct((s.shape[0] * dp_size, s.shape[1] * mp_size), s.dtype)
        for s in shards
    ]
    out_shape += saved * layers + [jax.ShapeDtypeStruct((tokens, features), f32)]
    out = pl.pallas_call(
        functools.partial(
            forward_kernel, plans, order, mp_size, layers, vector_count, gain_rows, shift_rows
        ),
        out_shape=out_shape,
        in_specs=[any_place] * (len(shards) + 1) + [vmem] * 2,
        out_specs=[any_place] * len(out_shape),
        scratch_shapes=[
            pltpu.VMEM((layers + 1, tokens, features), f32),
            pltpu.VMEM((layers, tokens, features), f32),
            pltpu.VMEM((layers, tokens, features), bf16),
            pltpu.VMEM((layers, tokens, features), bf16),
            pltpu.VMEM((layers, tokens, slots * cols), bf16),
            pltpu.VMEM((layers, length, slots * cols), bf16),
            pltpu.VMEM((layers, length, half), bf16),
            pltpu.VMEM((layers, tokens, features), bf16),
            pltpu.VMEM((tokens, units), bf16),
            pltpu.VMEM((tokens, units), bf16),
            pltpu.VMEM((2, features, cols), bf16),
            pltpu.VMEM((features, features), bf16),
            pltpu.VMEM((2, features, units // 8), bf16),
            pltpu.VMEM((2, features // 4, units), bf16),
            pltpu.VMEM(small_shape, bf16),
            pltpu.VMEM((shards[-1].shape[0], features), f32),
            pltpu.VMEM((shards[-1].shape[0], units), f32),
            pltpu.VMEM((tokens, features), bf16),
            pltpu.SemaphoreType.DMA((8,)),
            pltpu.SemaphoreType.DMA((9 * layers + 1,)),
            pltpu.SemaphoreType.DMA((3,)),
            pltpu.SemaphoreType.DMA((4 * layers,)),
            pltpu.SemaphoreType.DMA((total,)),
            pltpu.SemaphoreType.DMA((total,)),
            pltpu.SemaphoreType.DMA((len(shards),)),
        ],
        compiler_params=pltpu.CompilerParams(
            collective_id=2, has_side_effects=True, vmem_limit_bytes=62 * 2**20
        ),
    )(*shards, inputs, docs.reshape(-1, 1), docs.reshape(1, -1))
    n = len(shards)
    return out[:n], [out[n + 9 * at : n + 9 * at + 9] for at in range(layers)], out[-1]


forward_table = (
    23, 22, 117, 25, 95, 0, 189, 27, 94, 119, 1, 116, 188, 2, 191, 96, 190, 3, 24, 4, 45, 121,
    118, 26, 97, 46, 98, 193, 70, 192, 47, 69, 5, 71, 194, 48, 197, 13, 196, 195, 28, 120, 49, 18,
    200, 99, 30, 124, 34, 31, 29, 76, 10, 9, 123, 50, 72, 12, 198, 199, 129, 126, 41, 207, 11, 58,
    8, 6, 32, 73, 77, 7, 201, 101, 112, 78, 33, 125, 122, 105, 44, 208, 205, 203, 127, 74, 75,
    134, 128, 59, 107, 36, 35, 103, 106, 60, 204, 104, 39, 83, 135, 37, 40, 79, 17, 102, 202, 57,
    65, 80, 131, 52, 42, 90, 82, 38, 209, 114, 206, 136, 81, 86, 100, 67, 51, 16, 165, 210, 20,
    84, 132, 164, 14, 43, 91, 19, 54, 113, 15, 53, 140, 163, 87, 133, 130, 21, 211, 212, 167, 137,
    213, 109, 85, 214, 55, 56, 138, 215, 216, 88, 142, 217, 218, 219, 166, 171, 62, 111, 139, 145,
    89, 61, 170, 63, 66, 110, 92, 220, 169, 64, 221, 222, 68, 108, 223, 224, 225, 226, 227, 93,
    228, 141, 229, 230, 147, 146, 231, 115, 232, 233, 234, 148, 144, 143, 153, 168, 172, 235, 236,
    237, 150, 184, 238, 173, 239, 149, 177, 176, 157, 240, 241, 178, 174, 175, 242, 179, 154, 180,
    243, 244, 156, 151, 152, 159, 160, 181, 158, 155, 182, 183, 186, 245, 246, 161, 247, 162, 248,
    249, 250, 251, 185, 187, 252, 253, 254, 255, 256, 257, 258, 259,
)
fold_table = (
    50, 25, 1, 28, 29, 122, 169, 2, 8, 30, 9, 0, 145, 119, 31, 95, 53, 51, 55, 3, 74, 11, 10, 26,
    15, 4, 6, 96, 146, 75, 123, 32, 72, 97, 19, 147, 7, 27, 102, 124, 14, 38, 125, 73, 5, 52, 94,
    126, 37, 12, 103, 131, 54, 132, 136, 104, 105, 76, 109, 42, 18, 33, 57, 36, 168, 135, 166,
    113, 34, 35, 108, 144, 39, 98, 16, 40, 46, 120, 80, 112, 58, 81, 13, 170, 140, 99, 20, 101,
    172, 79, 56, 78, 83, 41, 60, 77, 148, 100, 82, 167, 44, 106, 107, 17, 121, 150, 43, 59, 110,
    127, 111, 84, 173, 129, 128, 47, 153, 61, 130, 85, 87, 174, 133, 62, 134, 114, 149, 86, 171,
    45, 89, 175, 88, 65, 178, 137, 138, 63, 152, 151, 177, 154, 156, 48, 176, 179, 21, 64, 91,
    157, 67, 90, 115, 116, 22, 181, 66, 155, 180, 117, 142, 182, 159, 183, 69, 158, 161, 141, 93,
    23, 160, 68, 92, 185, 184, 162, 71, 70, 163, 139, 24, 49, 118, 187, 143, 186, 164, 165,
)


def program(dp_size, mp_size, args):
    (
        inputs, documents, cotangent,
        qkv_weight, qkv_moment, qkv_square,
        proj_weight, proj_moment, proj_square,
        upper_weight, upper_moment, upper_square,
        lower_weight, lower_moment, lower_square,
        hidden_bias, bias_moment, bias_square,
        norm_gains, gains_moment, gains_square,
        shift_params, shifts_moment, shifts_square,
    ) = args
    layers = qkv_weight.shape[0]
    tokens, features = inputs.shape
    length = documents.shape[1]
    pieces = length // tokens
    slots = mp_size // pieces
    wide = features // dp_size
    z_cols = qkv_weight.shape[3]
    heads_slot = z_cols // HD
    me_dp = lax.axis_index("dp")
    me_mp = lax.axis_index("mp")
    core = me_dp % 2

    def swap(values):
        return lax.ppermute(values, "dp", [(at, at ^ 1) for at in range(dp_size)])

    def by_core(own, other, axis):
        first = jnp.where(core == 0, own, other)
        second = jnp.where(core == 0, other, own)
        return jnp.concatenate([first, second], axis=axis)

    paired = pieces == 2 and dp_size % 2 == 0 and mp_size % 2 == 0
    if paired:
        moved = core != me_mp % 2
        pairs = []
        for d in range(dp_size):
            for m in range(mp_size):
                if d % 2 != m % 2:
                    pairs.append((d * mp_size + m, (d ^ 1) * mp_size + (m ^ 1)))

        def trade(values):
            other = lax.ppermute(values, ("dp", "mp"), pairs)
            return jnp.where(moved, other, values)

        doc_rows = jnp.where(moved, swap(documents), documents)
        docs = lax.dynamic_index_in_dim(doc_rows, me_mp // 2, 0, False)

        def share_heads(values):
            half = values.shape[1] // 2
            own = lax.dynamic_slice_in_dim(values, core * half, half, 1)
            sent = lax.dynamic_slice_in_dim(values, (1 - core) * half, half, 1)
            return by_core(own, swap(sent), 0)

        def return_heads(values):
            own = lax.dynamic_slice_in_dim(values, core * tokens, tokens, 0)
            sent = lax.dynamic_slice_in_dim(values, (1 - core) * tokens, tokens, 0)
            return by_core(own, swap(sent), 1)

        first_slot = core * slots
    else:
        groups = [list(range(g * pieces, (g + 1) * pieces)) for g in range(mp_size // pieces)]

        def trade(values):
            return values

        docs = lax.dynamic_index_in_dim(documents, me_mp // pieces, 0, False)

        def share_heads(values):
            return lax.all_to_all(values, "mp", 1, 0, axis_index_groups=groups, tiled=True)

        def return_heads(values):
            return lax.all_to_all(values, "mp", 0, 1, axis_index_groups=groups, tiled=True)

        first_slot = (me_mp % pieces) * slots
    slope_table = jnp.asarray(0.5 ** (np.arange(H) + 1.0), dtype=f32)
    slopes = lax.dynamic_slice_in_dim(
        slope_table, first_slot * heads_slot, slots * heads_slot
    )

    bits = bits_of(dp_size)[1:]
    line_first = [("mp", *bits), ("mp", *bits[::-1])]
    line_second = [(bits[0], "mp", *bits[1:]), (bits[-1], "mp", *bits[:-1][::-1])]

    gain_rows = norm_gains.shape[1]
    shift_rows = shift_params.shape[1]
    vector_count = layers * (gain_rows + shift_rows)
    bias_wide = hidden_bias.shape[1]
    lanes = max(wide, HD)
    small_rows = -(-(vector_count + layers) // 16) * 16

    def padded(values):
        return jnp.pad(values, [(0, 0)] * (values.ndim - 1) + [(0, lanes - values.shape[-1])])

    small = jnp.concatenate(
        [
            padded(norm_gains.reshape(-1, wide)),
            padded(shift_params.reshape(-1, wide)),
            padded(hidden_bias),
            jnp.zeros((small_rows - vector_count - layers, lanes), f32),
        ],
        axis=0,
    ).astype(bf16)

    shards = []
    spreads = []
    for layer in range(layers):
        shards += [
            qkv_weight[layer].astype(bf16).reshape(wide, 3 * z_cols),
            proj_weight[layer].astype(bf16).T,
            upper_weight[layer].astype(bf16),
            lower_weight[layer].astype(bf16).T,
        ]
        spreads += line_first[:: 1 if layer % 2 == 0 else -1] + line_second
    shards.append(small)
    spreads.append(line_first[0])
    spreads = [Spread(dims, mp_size) for dims in spreads]
    tabled = dp_size == 8 and mp_size == 4 and layers == 2
    if paired:
        spread_order = forward_order(spreads, layers, forward_table if tabled else ())
        full, stored, stream = forward_all(
            shards, inputs, docs, spreads, spread_order, dp_size, mp_size, layers,
            vector_count, gain_rows, shift_rows,
        )
    else:
        spread_order = step_order(spreads, (), lambda t, stage: t // 2 + stage)
        full = spread_all(shards, spreads, spread_order, dp_size, mp_size)
    small_all = full[-1].reshape(dp_size, small_rows, mp_size, lanes).astype(f32)
    vectors = small_all[:, :vector_count, 0, :wide].transpose(1, 0, 2)
    vectors = vectors.reshape(vector_count, features)
    gains = vectors[: layers * gain_rows].reshape(layers, gain_rows, features)
    shifts = vectors[layers * gain_rows :].reshape(layers, shift_rows, features)
    biases = small_all[:, vector_count : vector_count + layers, :, :bias_wide]
    biases = biases.transpose(1, 2, 0, 3).reshape(layers, -1)

    grad_stream = trade(cotangent).astype(f32)
    if not paired:
        stream = inputs.astype(f32)
        stored = []
        for layer in range(layers):
            qkv_w, proj_w, upper_w, lower_w = full[4 * layer : 4 * layer + 4]
            normed = layer_norm(stream, gains[layer, 0], shifts[layer, 0]).astype(bf16)
            qkv = share_heads(dot(normed, qkv_w).astype(bf16))
            mixed = attend(slopes, docs, qkv, slots)
            attended = return_heads(mixed)
            middle = stream + dot_cols(attended, proj_w)
            normed_two = layer_norm(middle, gains[layer, 1], shifts[layer, 1]).astype(bf16)
            hidden = dot(normed_two, upper_w) + biases[layer]
            active = gelu_tanh(hidden).astype(bf16)
            stored.append(
                (stream, middle, normed, qkv, mixed, attended, normed_two, hidden, active)
            )
            stream = middle + dot_cols(active, lower_w) + shifts[layer, 2]
    output_stream = stream
    if paired:
        other = lax.ppermute(output_stream.astype(bf16), ("dp", "mp"), pairs)
        output_stream = jnp.where(moved, other.astype(f32), output_stream)

    weight_grads = [None] * layers
    vector_grads = [None] * layers
    bias_grads = [None] * layers
    no_shift = jnp.zeros((features,), f32)
    for layer in reversed(range(layers)):
        qkv_w, proj_w, upper_w, lower_w = full[4 * layer : 4 * layer + 4]
        stream_in, middle, normed, qkv, mixed, attended, normed_two, hidden, active = stored[layer]
        out_shift_grad = jnp.sum(grad_stream, axis=0)
        grad_low = grad_stream.astype(bf16)
        active_grad = dot(grad_low, lower_w)
        _, pull_gelu = jax.vjp(gelu_tanh, hidden.astype(f32))
        hidden_grad = pull_gelu(active_grad)[0].astype(bf16)
        lower_grad = dot_rows(grad_low, active).astype(bf16)
        upper_grad = dot_rows(normed_two, hidden_grad).astype(bf16)
        bias_grads[layer] = jnp.sum(hidden_grad, axis=0, dtype=f32)
        normed_two_grad = dot_cols(hidden_grad, upper_w)
        _, pull_two = jax.vjp(layer_norm, middle, gains[layer, 1], no_shift)
        middle_part, gain_two, shift_two = pull_two(normed_two_grad)
        middle_grad = grad_stream + middle_part
        middle_low = middle_grad.astype(bf16)
        mixed_grad = share_heads(dot(middle_low, proj_w).astype(bf16))
        proj_grad = dot_rows(middle_low, attended).astype(bf16)
        qkv_grad = return_heads(attend_back(slopes, docs, qkv, mixed, mixed_grad, slots))
        normed_grad = dot_cols(qkv_grad, qkv_w)
        qkv_weight_grad = dot_rows(normed, qkv_grad).astype(bf16)
        _, pull_one = jax.vjp(layer_norm, stream_in, gains[layer, 0], no_shift)
        stream_part, gain_one, shift_one = pull_one(normed_grad)
        grad_stream = middle_grad + stream_part
        weight_grads[layer] = (lower_grad, upper_grad, proj_grad, qkv_weight_grad)
        vector_grads[layer] = (
            jnp.stack([gain_one, gain_two]),
            jnp.stack([shift_one, shift_two, out_shift_grad]),
        )
    input_grad = grad_stream
    if paired:
        other = lax.ppermute(input_grad.astype(bf16), ("dp", "mp"), pairs)
        input_grad = jnp.where(moved, other.astype(f32), input_grad)

    vector_sums = jnp.concatenate(
        [jnp.concatenate([vector_grads[at][kind] for at in range(layers)]) for kind in (0, 1)]
    )
    vector_sums = padded(vector_sums.reshape(vector_count, dp_size, wide)).transpose(1, 0, 2)
    vector_sums = jnp.broadcast_to(
        vector_sums[:, :, None], (dp_size, vector_count, mp_size, lanes)
    )
    bias_sums = padded(jnp.stack(bias_grads).reshape(layers, mp_size, dp_size, bias_wide))
    bias_sums = bias_sums.transpose(2, 0, 1, 3)
    rest = jnp.zeros((dp_size, small_rows - vector_count - layers, mp_size, lanes), f32)
    small_grad = jnp.concatenate([vector_sums, bias_sums, rest], axis=1)
    small_grad = small_grad.reshape(dp_size * small_rows, mp_size * lanes).astype(bf16)

    folds = []
    local = []
    for layer in reversed(range(layers)):
        local += weight_grads[layer]
        folds += fold_dims(line_first, line_second, layer)
    local.append(small_grad)
    folds.append(line_first[0][::-1])
    folds = [Fold(dims, mp_size) for dims in folds]
    fold_order = step_order(
        folds, fold_table if tabled else (), lambda t, stage: t // 2 + stage
    )
    owned, norm_tile = fold_all(local, folds, fold_order, dp_size, mp_size, vector_count)
    small_owned = owned.pop()
    vector_owned = small_owned[:vector_count, :wide]
    bias_owned = small_owned[vector_count : vector_count + layers, :bias_wide]
    grad_norm = jnp.sqrt(jnp.sum(norm_tile))
    factor = jnp.minimum(1.0, clip_bound / grad_norm)

    states = []
    for each in (qkv_weight, qkv_moment, qkv_square):
        states.append(each.transpose(0, 2, 1, 3))
    states += [
        proj_weight, proj_moment, proj_square, upper_weight, upper_moment, upper_square,
        lower_weight, lower_moment, lower_square,
    ]
    ordered = [owned[4 * layer + kind] for kind in (3, 2, 1, 0) for layer in range(layers)]
    matrices = list(adam_all(factor, ordered, states))
    matrices[:3] = [each.transpose(0, 2, 1, 3) for each in matrices[:3]]
    results = [output_stream, input_grad] + matrices
    rest = (
        (hidden_bias, bias_moment, bias_square, bias_owned),
        (
            norm_gains, gains_moment, gains_square,
            vector_owned[: layers * gain_rows].reshape(layers, gain_rows, wide),
        ),
        (
            shift_params, shifts_moment, shifts_square,
            vector_owned[layers * gain_rows :].reshape(layers, shift_rows, wide),
        ),
    )
    for at, group in enumerate(rest, 4):
        results.extend(adam_update(*group, factor, group_rates[at], group_decays[at]))
    results.append(grad_norm)
    return tuple(results)


def fold_dims(line_first, line_second, layer):
    first = [dims[::-1] for dims in line_first]
    second = [dims[::-1] for dims in line_second]
    return second + (first if layer % 2 else first[::-1])


def solution(mesh):
    dp_size = mesh.shape["dp"]
    mp_size = mesh.shape["mp"]
    rows = P(("dp", "mp"), None)
    split_rows = P(None, "dp", None, "mp")
    split_upper = P(None, "dp", "mp")
    split_lower = P(None, "mp", "dp")
    split_bias = P(None, ("mp", "dp"))
    split_vector = P(None, None, "dp")
    groups = (
        split_rows, split_lower, split_upper, split_lower, split_bias, split_vector, split_vector
    )
    placed = tuple(spec for spec in groups for _ in range(3))

    def shards(*args):
        return program(dp_size, mp_size, args)

    return jax.shard_map(
        shards,
        mesh=mesh,
        in_specs=(rows, P("dp", None), rows) + placed,
        out_specs=(rows, rows) + placed + (P(),),
        check_vma=False,
    )
```

```python
import functools
import math

import jax
import jax.numpy as jnp
import numpy as np
from jax import lax
from jax.experimental import pallas as pl
from jax.experimental.pallas import tpu as pltpu
from jax.sharding import PartitionSpec as P

DP = "dp"
MP = "mp"
H = 8
HD = 128
STEP = 5
MAX_DOC = 512

norm_eps = 1e-05
clip_bound = 1.0
beta_first = 0.9
beta_second = 0.95
adam_eps = 1e-08
masked_score = -1e30
group_rates = (0.03, 0.12, 0.03, 0.015, 0.3, 0.7, 0.3)
group_decays = (0.1, 0.1, 0.1, 0.1, 0.0, 0.0, 0.0)
contract_rows = (((0,), (0,)), ((), ()))
contract_cols = (((1,), (1,)), ((), ()))
f32 = jnp.float32
bf16 = jnp.bfloat16
score_scale = 1.0 / math.sqrt(HD)
MESH = pl.DeviceIdType.MESH


def adam_update(master, moment, square, gradient, factor, step_rate, decay_rate):
    clipped = gradient * factor
    moment_new = beta_first * moment + (1.0 - beta_first) * clipped
    square_new = beta_second * square + (1.0 - beta_second) * clipped * clipped
    first_hat = moment_new / (1.0 - beta_first**STEP)
    second_hat = square_new / (1.0 - beta_second**STEP)
    master_new = master - step_rate * (
        first_hat / (jnp.sqrt(second_hat) + adam_eps) + decay_rate * master
    )
    return (master_new, moment_new, square_new)


def gelu_tanh(values):
    return jax.nn.gelu(values, approximate=True)


def layer_norm(values, scale_vec, shift_vec):
    center = values - jnp.mean(values, axis=-1, keepdims=True)
    spread = jnp.mean(center * center, axis=-1, keepdims=True)
    return center * lax.rsqrt(spread + norm_eps) * scale_vec + shift_vec


def dot(left, right):
    return jnp.dot(left, right, preferred_element_type=f32)


def dot_rows(left, right):
    return lax.dot_general(left, right, contract_rows, preferred_element_type=f32)


def dot_cols(left, right):
    return lax.dot_general(left, right, contract_cols, preferred_element_type=f32)


def masked_scores(slope, doc_col, doc_row, query, key, first_row, first_col):
    scores = dot_cols(query, key) * score_scale
    rows = first_row + lax.broadcasted_iota(jnp.int32, scores.shape, 0)
    cols = first_col + lax.broadcasted_iota(jnp.int32, scores.shape, 1)
    distance = rows - cols
    allowed = (distance >= 0) & (doc_col == doc_row)
    return jnp.where(allowed, scores - slope * distance.astype(f32), masked_score)


def key_range(first_row, block):
    low = max(0, first_row - (MAX_DOC - 1)) // block * block
    return low, first_row + block


def attend_kernel(heads, block, slope_ref, dcol_ref, drow_ref, qkv_ref, o_ref):
    length = o_ref.shape[0]
    for head in range(heads):
        slope = slope_ref[pl.program_id(0) * heads + head]
        at = head * HD
        kat = (heads + head) * HD
        vat = (2 * heads + head) * HD
        for first_row in range(0, length, block):
            low, high = key_range(first_row, block)
            scores = masked_scores(
                slope,
                dcol_ref[first_row : first_row + block, :],
                drow_ref[:, low:high],
                qkv_ref[first_row : first_row + block, at : at + HD],
                qkv_ref[low:high, kat : kat + HD],
                first_row,
                low,
            )
            shifted = jnp.exp(scores - jnp.max(scores, axis=-1, keepdims=True))
            total = jnp.sum(shifted, axis=-1, keepdims=True)
            prob_low = (shifted * (1.0 / total)).astype(bf16)
            o_ref[first_row : first_row + block, at : at + HD] = dot(
                prob_low, qkv_ref[low:high, vat : vat + HD]
            ).astype(bf16)


def attend_back_kernel(
    heads, block, slope_ref, dcol_ref, drow_ref, qkv_ref, o_ref, do_ref,
    grad_ref, key_acc, value_acc,
):
    length = o_ref.shape[0]
    for head in range(heads):
        slope = slope_ref[pl.program_id(0) * heads + head]
        at = head * HD
        kat = (heads + head) * HD
        vat = (2 * heads + head) * HD
        key_acc[...] = jnp.zeros_like(key_acc)
        value_acc[...] = jnp.zeros_like(value_acc)
        for first_row in range(0, length, block):
            low, high = key_range(first_row, block)
            rows = slice(first_row, first_row + block)
            query = qkv_ref[rows, at : at + HD]
            key = qkv_ref[low:high, kat : kat + HD]
            scores = masked_scores(
                slope, dcol_ref[rows, :], drow_ref[:, low:high], query, key, first_row, low
            )
            shifted = jnp.exp(scores - jnp.max(scores, axis=-1, keepdims=True))
            total = jnp.sum(shifted, axis=-1, keepdims=True)
            probs = shifted * (1.0 / total)
            out_grad = do_ref[rows, at : at + HD]
            value_acc[low:high, :] += dot_rows(probs.astype(bf16), out_grad)
            prob_grad = dot_cols(out_grad, qkv_ref[low:high, vat : vat + HD])
            inner = jnp.sum(
                out_grad.astype(f32) * o_ref[rows, at : at + HD].astype(f32),
                axis=-1,
                keepdims=True,
            )
            score_grad = (probs * (prob_grad - inner)).astype(bf16)
            grad_ref[rows, at : at + HD] = (dot(score_grad, key) * score_scale).astype(bf16)
            key_acc[low:high, :] += dot_rows(score_grad, query)
        grad_ref[:, kat : kat + HD] = (key_acc[...] * score_scale).astype(bf16)
        grad_ref[:, vat : vat + HD] = value_acc[...].astype(bf16)


def attend_specs(length, width):
    def columns(each):
        return pl.BlockSpec((length, each), lambda s: (0, s))

    fixed = [
        pl.BlockSpec(memory_space=pltpu.SMEM),
        pl.BlockSpec((length, 1), lambda s: (0, 0)),
        pl.BlockSpec((1, length), lambda s: (0, 0)),
    ]
    return fixed, columns(3 * width), columns(width)


def attend(slopes, docs, qkv, slots):
    length = qkv.shape[0]
    width = qkv.shape[1] // (3 * slots)
    fixed, wide, narrow = attend_specs(length, width)
    pairs = slots * width // HD * length * length
    return pl.pallas_call(
        functools.partial(attend_kernel, width // HD, min(256, length)),
        grid=(slots,),
        in_specs=fixed + [wide],
        out_specs=narrow,
        out_shape=jax.ShapeDtypeStruct((length, slots * width), bf16),
        compiler_params=pltpu.CompilerParams(vmem_limit_bytes=32 * 2**20),
        cost_estimate=pl.CostEstimate(
            flops=4 * pairs * HD, bytes_accessed=3 * qkv.size, transcendentals=pairs
        ),
    )(slopes, docs.reshape(-1, 1), docs.reshape(1, -1), qkv)


def attend_back(slopes, docs, qkv, o, do, slots):
    length = qkv.shape[0]
    width = qkv.shape[1] // (3 * slots)
    fixed, wide, narrow = attend_specs(length, width)
    pairs = slots * width // HD * length * length
    return pl.pallas_call(
        functools.partial(attend_back_kernel, width // HD, min(256, length)),
        grid=(slots,),
        in_specs=fixed + [wide, narrow, narrow],
        out_specs=wide,
        out_shape=jax.ShapeDtypeStruct(qkv.shape, bf16),
        scratch_shapes=[pltpu.VMEM((length, HD), f32), pltpu.VMEM((length, HD), f32)],
        compiler_params=pltpu.CompilerParams(vmem_limit_bytes=32 * 2**20),
        cost_estimate=pl.CostEstimate(
            flops=10 * pairs * HD, bytes_accessed=6 * qkv.size, transcendentals=pairs
        ),
    )(slopes, docs.reshape(-1, 1), docs.reshape(1, -1), qkv, o, do)


def bits_of(size):
    return [1 << at for at in range(size.bit_length() - 1)]


def flip(value, mask):
    bit = 1
    while bit <= mask:
        if mask & bit:
            value = value + bit * (1 - 2 * ((value // bit) % 2))
        bit *= 2
    return value


def place(at, size):
    if isinstance(at, int):
        return at * size
    return pl.multiple_of(at * size, size)


class Spread:
    def __init__(self, dims, mp_size):
        self.dims = tuple(dims)
        self.events = []
        masks, spread = [0], False
        for stage, dim in enumerate(self.dims):
            for mask in masks:
                if dim == MP:
                    for hops in range(1, mp_size):
                        self.events += [(stage, mask, way, hops) for way in (1, -1)]
                else:
                    places = range(mp_size) if spread else (0,)
                    self.events += [(stage, mask | dim, 0, at) for at in places]
            if dim == MP:
                spread = True
            else:
                masks = masks + [mask | dim for mask in masks]
        self.events += [(len(self.dims), mask | 1, 0, 0) for mask in masks]

    def full(self, stage):
        return MP in self.dims[:stage]


class Fold:
    def __init__(self, dims, mp_size, halves=1):
        self.dims = tuple(dims)
        masks = [0]
        for dim in self.dims:
            if dim != MP:
                masks = masks + [mask | dim for mask in masks]
        self.masks = masks
        self.kept = {}
        sent_first = sorted(masks, key=self.leaves)
        self.events = [(0, mask, 0, half) for mask in sent_first for half in range(halves)]
        rows = list(masks)
        for stage, dim in enumerate(self.dims, 1):
            if dim != MP:
                rows = [mask for mask in rows if not mask & dim]
            self.kept[stage] = list(rows)
            if dim == MP:
                for hops in reversed(range(mp_size - 1)):
                    for mask in rows:
                        self.events += [(stage, mask, way, hops) for way in (1, -1)]
            else:
                places = reversed(range(mp_size)) if self.full(stage) else (0,)
                places = list(places)
                for mask in rows:
                    self.events += [(stage, mask, 0, at) for at in places]

    def leaves(self, mask):
        for at, dim in enumerate(self.dims):
            if dim != MP and mask & dim:
                return at
        return len(self.dims)

    def full(self, stage):
        return MP not in self.dims[: stage - 1]


def number(plans, mp_size, single):
    index, total = {}, 0
    for t, plan in enumerate(plans):
        for event in plan.events:
            stage, mask, way, at = event
            if way or single(plan, stage):
                index[(t,) + event] = total
                total += 1
            elif (t, stage, mask) not in index:
                index[t, stage, mask] = total
                total += mp_size
    return index, total


def spread_single(plan, stage):
    return stage == len(plan.dims)


def fold_single(plan, stage):
    return stage == 0


def merge_small(order, plans):
    t = len(plans) - 1
    small = [(t, event) for event in plans[t].events]
    out, used = [], 0
    for at, step in enumerate(order):
        out.append(step)
        while used < len(small) and (used + 1) * len(order) <= (at + 1) * (len(small) + 1):
            out.append(small[used])
            used += 1
    return out + small[used:]


def step_order(plans, table, by_stage):
    steps = [(t, event) for t, plan in enumerate(plans[:-1]) for event in plan.events]
    if len(table) == len(steps):
        return merge_small([steps[at] for at in table], plans)
    ranked = sorted(range(len(steps)), key=lambda at: (by_stage(steps[at][0], steps[at][1][0]), at))
    return merge_small([steps[at] for at in ranked], plans)


def forward_order(plans, layers, table):
    steps = [(t, event) for t, plan in enumerate(plans) for event in plan.events]
    compute = [(layer, name) for layer in range(layers) for name in FORWARD_STEPS]
    if len(table) == len(steps) + len(compute):
        steps += compute
        return [steps[at] for at in table]
    return steps + compute


def greet(z, d, upper, mp_size, mp_bits=(), across=None, moved=None):
    barrier = pltpu.get_barrier_semaphore()
    for bit in mp_bits:
        pl.semaphore_signal(
            barrier, inc=1, device_id={MP: flip(z, bit)}, device_id_type=MESH
        )
    for bit in [1] + upper:
        pl.semaphore_signal(
            barrier, inc=1, device_id={DP: flip(d, bit)}, device_id_type=MESH
        )
    also = 0
    if across is not None:

        @pl.when(moved)
        def _():
            pl.semaphore_signal(barrier, inc=1, device_id=across, device_id_type=MESH)

        also = jnp.where(moved, 1, 0)
    for way in (1, -1):

        @pl.when((z + way >= 0) & (z + way < mp_size))
        def _(way=way):
            pl.semaphore_signal(
                barrier, inc=1, device_id={MP: z + way}, device_id_type=MESH
            )

    around = jnp.where(z > 0, 1, 0) + jnp.where(z < mp_size - 1, 1, 0)
    pl.semaphore_wait(barrier, 1 + len(upper) + len(mp_bits) + around + also)


class SpreadWork:
    def __init__(self, plans, order, mp_size, shards, outs, send_sems, recv_sems, own_sems):
        self.plans, self.mp_size = plans, mp_size
        self.order = [step for step in order if not isinstance(step[1], str)]
        self.shards, self.outs = shards, outs
        self.sems = send_sems, recv_sems
        self.own_sems = own_sems
        self.z = lax.axis_index(MP)
        self.d = lax.axis_index(DP)
        self.upper = [dim for dim in plans[0].dims if dim != MP]
        self.index, _ = number(plans, mp_size, spread_single)
        self.owns = []
        self.left = {}
        for t, event in self.order:
            if event[0] < len(plans[t].dims):
                self.left[t, event[1]] = self.left.get((t, event[1]), 0) + 1

    def inside(self, at):
        return (at >= 0) & (at < self.mp_size)

    def region(self, t, mask, block):
        wide, cols = self.shards[t].shape
        rows = pl.ds(place(flip(self.d, mask), wide), wide)
        if block is None:
            return self.outs[t].at[rows, :]
        return self.outs[t].at[rows, pl.ds(place(block, cols), cols)]

    def remote(self, t, event, block, src, dst, to):
        stage, mask, way, at = event
        if way or stage == len(self.plans[t].dims):
            sem = self.index[(t,) + event]
        else:
            sem = self.index[t, stage, mask] + block
        return pltpu.make_async_remote_copy(
            src_ref=src,
            dst_ref=dst,
            send_sem=self.sems[0].at[sem],
            recv_sem=self.sems[1].at[sem],
            device_id=to,
            device_id_type=MESH,
        )

    def sending(self, t, event, block, to, own=False):
        stage, mask, way, at = event
        dims = self.plans[t].dims
        bit = 0 if way else 1 if stage == len(dims) else dims[stage]
        dst = self.region(t, mask ^ bit, block)
        return self.remote(t, event, block, self.shards[t] if own else dst, dst, to)

    def arrival(self, t, event, block):
        dst = self.region(t, event[1], block)
        return self.remote(t, event, block, dst, dst, {DP: self.d, MP: self.z})

    def on_line(self, t, stage, mask, block, way, hops, own):
        @pl.when(self.inside(self.z + way))
        def _():
            to = {MP: self.z + way}
            self.sending(t, (stage, mask, way, hops), block, to, own).start()

    def onward(self, t, stage, mask, block, own=False):
        dims = self.plans[t].dims
        for later in range(stage, len(dims)):
            if dims[later] == MP:
                for way in (1, -1):
                    self.on_line(t, later, mask, block, way, 1, own)
            else:
                to = {DP: flip(self.d, dims[later])}
                self.sending(t, (later, mask | dims[later], 0, None), block, to, own).start()

    def place_of(self, t, event):
        return flip(self.z, event[3]) if self.plans[t].full(event[0]) else self.z

    def begin(self):
        for t in range(len(self.plans)):
            self.onward(t, 0, 0, self.z, True)
            own = pltpu.make_async_copy(
                self.shards[t], self.region(t, 0, self.z), self.own_sems.at[t]
            )
            own.start()
            self.owns.append(own)

    def step(self, t, event):
        stage, mask, way, at = event
        last = len(self.plans[t].dims)
        if stage == last:
            self.arrival(t, event, None).wait_recv()
            return
        if way:
            block = self.z - way * at

            @pl.when(self.inside(block))
            def _():
                self.arrival(t, event, block).wait_recv()
                if at + 1 < self.mp_size:
                    self.on_line(t, stage, mask, block, way, at + 1, False)
                self.onward(t, stage + 1, mask, block)

        else:
            block = self.place_of(t, event)
            self.arrival(t, event, block).wait_recv()
            self.onward(t, stage + 1, mask, block)
        self.left[t, mask] -= 1
        if self.left[t, mask] == 0:
            if mask == 0:
                self.owns[t].wait()
            to = {DP: flip(self.d, 1)}
            self.sending(t, (last, mask | 1, 0, 0), None, to).start()

    def finish(self):
        for t, event in self.order:
            stage, mask, way, at = event
            if stage == len(self.plans[t].dims):
                self.sending(t, event, None, {DP: flip(self.d, 1)}).wait_send()
            elif way:

                @pl.when(self.inside(self.z - way * (at - 1)) & self.inside(self.z + way))
                def _():
                    to = {MP: self.z + way}
                    self.sending(t, event, self.z - way * (at - 1), to).wait_send()

            else:
                to = {DP: flip(self.d, self.plans[t].dims[stage])}
                self.sending(t, event, self.place_of(t, event), to).wait_send()


def spread_kernel(plans, order, mp_size, *refs):
    n = len(plans)
    work = SpreadWork(plans, order, mp_size, refs[:n], refs[n : 2 * n], *refs[2 * n :])
    greet(work.z, work.d, work.upper, mp_size)
    work.begin()
    for t, event in order:
        work.step(t, event)
    work.finish()


def spread_all(shards, plans, order, dp_size, mp_size):
    _, total = number(plans, mp_size, spread_single)
    return pl.pallas_call(
        functools.partial(spread_kernel, plans, order, mp_size),
        out_shape=[
            jax.ShapeDtypeStruct((s.shape[0] * dp_size, s.shape[1] * mp_size), s.dtype)
            for s in shards
        ],
        in_specs=[pl.BlockSpec(memory_space=pl.ANY)] * len(shards),
        out_specs=[pl.BlockSpec(memory_space=pl.ANY)] * len(shards),
        scratch_shapes=[
            pltpu.SemaphoreType.DMA((total,)),
            pltpu.SemaphoreType.DMA((total,)),
            pltpu.SemaphoreType.DMA((len(shards),)),
        ],
        compiler_params=pltpu.CompilerParams(collective_id=0, has_side_effects=True),
    )(*shards)


def fold_kernel(plans, order, mp_size, vector_count, *refs):
    n = len(plans)
    grads, outs = refs[:n], refs[n : 2 * n]
    norm_ref = refs[2 * n]
    landed, sums = refs[2 * n + 1 : 3 * n + 1], refs[3 * n + 1 : 4 * n + 1]
    at = 4 * n + 1
    recv = {}
    for t, plan in enumerate(plans):
        for stage in range(1, len(plan.dims) + 1):
            recv[t, stage] = refs[at]
            at += 1
    staging, tiles, load_sems, own_sems, tile_sems, send_sems, recv_sems = refs[at:]
    z = lax.axis_index(MP)
    d = lax.axis_index(DP)
    upper = [dim for dim in plans[0].dims if dim != MP]
    index, _ = number(plans, mp_size, fold_single)
    wides = [out.shape[0] for out in outs]
    cols = [out.shape[1] for out in outs]

    def inside(at):
        return (at >= 0) & (at < mp_size)

    def rows_of(t, mask):
        return pl.ds(plans[t].masks.index(mask) * wides[t], wides[t])

    def sum_at(t, mask, block):
        return sums[t].at[rows_of(t, mask), pl.ds(place(block, cols[t]), cols[t])]

    def landing(t, event, block):
        stage, mask, way, at = event
        kept = plans[t].kept[stage].index(mask)
        if way:
            return recv[t, stage].at[kept, (0 if way == 1 else mp_size - 1) + at]
        return recv[t, stage].at[kept, block if plans[t].full(stage) else 0]

    def remote(t, event, block, src, dst, to):
        stage, mask, way, at = event
        if way or stage == 0:
            sem = index[(t,) + event]
        else:
            sem = index[t, stage, mask] + block
        return pltpu.make_async_remote_copy(
            src_ref=src,
            dst_ref=dst,
            send_sem=send_sems.at[sem],
            recv_sem=recv_sems.at[sem],
            device_id=to,
            device_id_type=MESH,
        )

    def core_copy(t, mask):
        rows = pl.ds(place(flip(d, mask | 1), wides[t]), wides[t])
        dst = landed[t].at[rows_of(t, mask), :]
        return remote(t, (0, mask, 0, 0), 0, grads[t].at[rows, :], dst, {DP: flip(d, 1)})

    def own_copy(t, mask):
        rows = pl.ds(place(flip(d, mask), wides[t]), wides[t])
        return pltpu.make_async_copy(
            grads[t].at[rows, :],
            sums[t].at[rows_of(t, mask), :],
            own_sems.at[t, plans[t].masks.index(mask)],
        )

    def bit_copy(t, stage, mask, block):
        dim = plans[t].dims[stage - 1]
        event = (stage, mask & ~dim, 0, None)
        dst = landing(t, event, block)
        return remote(t, event, block, sum_at(t, mask, block), dst, {DP: flip(d, dim)})

    def line_copy(t, stage, mask, way, hops):
        event = (stage, mask, way, hops - 1)
        src = sum_at(t, mask, z + way * hops)
        return remote(t, event, None, src, landing(t, event, None), {MP: z + way})

    def arrival(t, event, block):
        dst = landing(t, event, block)
        return remote(t, event, block, dst, dst, {DP: d, MP: z})

    def add(dst, src, wide):
        step = 16

        def some_rows(at, carry):
            rows = pl.ds(pl.multiple_of(at * step, step), step)
            total = dst[rows, :].astype(f32) + src[rows, :].astype(f32)
            dst[rows, :] = total.astype(bf16)
            return carry

        lax.fori_loop(0, wide // step, some_rows, 0)

    def advance(t, stage, mask, block, other):
        if stage > len(plans[t].dims):
            return
        dim = plans[t].dims[stage - 1]
        if dim == MP:
            if other:
                for way, end in ((1, 0), (-1, mp_size - 1)):

                    @pl.when(z == end)
                    def _(way=way):
                        line_copy(t, stage, mask, way, other).start()

        elif mask & dim:
            bit_copy(t, stage, mask, block).start()

    mp_bits = bits_of(mp_size)
    greet(z, d, upper, mp_size, mp_bits)
    cores = [(t, event[1]) for t, event in order if event[0] == 0]
    for t, mask in cores:
        core_copy(t, mask).start()
        own_copy(t, mask).start()

    def load(at):
        t, mask = cores[at]
        return pltpu.make_async_copy(
            landed[t].at[rows_of(t, mask), :],
            staging.at[at % 2, pl.ds(0, wides[t]), pl.ds(0, cols[t] * mp_size)],
            load_sems.at[at % 2],
        )

    seen = 0
    brought = {}
    for t, event in order:
        stage, mask, way, at = event
        plan = plans[t]
        if stage == 0:
            for ahead in (0, 1) if seen == 0 else (seen + 1,):
                if ahead < len(cores):
                    core_copy(*cores[ahead]).wait_recv()
                    load(ahead).start()
            load(seen).wait()
            own_copy(t, mask).wait()
            part = staging.at[seen % 2, pl.ds(0, wides[t]), pl.ds(0, cols[t] * mp_size)]
            add(sums[t].at[rows_of(t, mask), :], part, wides[t])
            seen += 1
            for other in reversed(range(mp_size)):
                advance(t, 1, mask, flip(z, other), other)
        elif way:
            block = z + way * at

            @pl.when(inside(block) & inside(z - way))
            def _():
                arrival(t, event, None).wait_recv()
                add(sum_at(t, mask, block), landing(t, event, None), wides[t])
                if at > 0:
                    line_copy(t, stage, mask, way, at).start()

            if at == 0:
                brought[t, mask] = brought.get((t, mask), 0) + 1
                if brought[t, mask] == 2:
                    advance(t, stage + 1, mask, z, 0)
        else:
            block = flip(z, at) if plan.full(stage) else z
            arrival(t, event, block).wait_recv()
            add(sum_at(t, mask, block), landing(t, event, block), wides[t])
            advance(t, stage + 1, mask, block, at)

    tiles[0] = jnp.zeros(tiles.shape[1:], f32)
    for t in range(n):
        step = 16

        def some_rows(at, carry, t=t):
            rows = pl.ds(pl.multiple_of(at * step, step), step)
            part = sums[t][rows, pl.ds(place(z, cols[t]), cols[t])].astype(f32)
            outs[t][rows, :] = part
            part = part * part
            total = carry
            for low in range(0, step, 8):
                for left in range(0, cols[t], HD):
                    total = total + part[low : low + 8, left : left + HD]
            return total

        if t == n - 1:
            whole = sums[t][pl.ds(0, wides[t]), pl.ds(place(z, cols[t]), cols[t])].astype(f32)
            outs[t][...] = whole
            row = lax.broadcasted_iota(jnp.int32, whole.shape, 0)
            whole = whole * whole
            whole = jnp.where(row < vector_count, whole * (1.0 / mp_size), whole)
            for low in range(0, wides[t], 8):
                tiles[0] += whole[low : low + 8, :HD]
        else:
            zero = jnp.zeros((8, HD), f32)
            tiles[0] += lax.fori_loop(0, wides[t] // step, some_rows, zero)
    pairs = [{DP: flip(d, bit)} for bit in [1] + upper]
    pairs += [{MP: flip(z, bit)} for bit in mp_bits]
    for at, to in enumerate(pairs):
        exchange = pltpu.make_async_remote_copy(
            src_ref=tiles.at[2 * at],
            dst_ref=tiles.at[2 * at + 1],
            send_sem=tile_sems.at[2 * at],
            recv_sem=tile_sems.at[2 * at + 1],
            device_id=to,
            device_id_type=MESH,
        )
        exchange.start()
        exchange.wait()
        tiles[2 * at + 2] = tiles[2 * at] + tiles[2 * at + 1]
    norm_ref[...] = tiles[2 * len(pairs)]

    for t, event in order:
        stage, mask, way, at = event
        if stage == 0:
            core_copy(t, mask).wait_send()
        elif way:

            @pl.when(inside(z + way) & inside(z + way * (at + 1)))
            def _():
                line_copy(t, stage, mask, way, at + 1).wait_send()

        else:
            block = flip(z, at) if plans[t].full(stage) else z
            bit_copy(t, stage, mask | plans[t].dims[stage - 1], block).wait_send()


def fold_all(grads, plans, order, dp_size, mp_size, vector_count):
    n = len(grads)
    _, total = number(plans, mp_size, fold_single)
    wides = [g.shape[0] // dp_size for g in grads]
    cols = [g.shape[1] // mp_size for g in grads]
    rounds = len(bits_of(dp_size)) + len(bits_of(mp_size))
    halves = [(dp_size // 2 * wide, mp_size * each) for wide, each in zip(wides, cols)]
    scratch = [pltpu.VMEM(half, bf16) for half in halves]
    for plan, wide, each in zip(plans, wides, cols):
        for stage, dim in enumerate(plan.dims, 1):
            blocks = 2 * (mp_size - 1) if dim == MP else mp_size if plan.full(stage) else 1
            scratch.append(pltpu.VMEM((len(plan.kept[stage]), blocks, wide, each), bf16))
    scratch += [
        pltpu.VMEM((2, max(wides), mp_size * max(cols)), bf16),
        pltpu.VMEM((2 * rounds + 1, 8, HD), f32),
        pltpu.SemaphoreType.DMA((2,)),
        pltpu.SemaphoreType.DMA((n, dp_size // 2)),
        pltpu.SemaphoreType.DMA((2 * rounds,)),
        pltpu.SemaphoreType.DMA((total,)),
        pltpu.SemaphoreType.DMA((total,)),
    ]
    out = pl.pallas_call(
        functools.partial(fold_kernel, plans, order, mp_size, vector_count),
        out_shape=[jax.ShapeDtypeStruct((wide, each), f32) for wide, each in zip(wides, cols)]
        + [jax.ShapeDtypeStruct((8, HD), f32)]
        + [jax.ShapeDtypeStruct(half, bf16) for half in halves],
        in_specs=[pl.BlockSpec(memory_space=pl.ANY)] * n,
        out_specs=[pl.BlockSpec(memory_space=pltpu.VMEM)] * (n + 1)
        + [pl.BlockSpec(memory_space=pl.ANY)] * n,
        scratch_shapes=scratch,
        compiler_params=pltpu.CompilerParams(
            collective_id=1, has_side_effects=True, vmem_limit_bytes=63 * 2**20
        ),
    )(*grads)
    return list(out[:n]), out[n]


def prepare_kernel(layers, *refs):
    count = 4 * layers + 1
    states, outs = refs[:7], refs[7 : 7 + count]
    held, made = refs[7 + count : 14 + count], refs[14 + count : 14 + 2 * count]
    in_sems, out_sems = refs[14 + 2 * count :]
    loads = [pltpu.make_async_copy(a, b, in_sems.at[at]) for at, (a, b) in enumerate(zip(states, held))]
    for copy in loads:
        copy.start()
    qkv, proj, upper, lower, gains, shifts, bias = held
    stores = [pltpu.make_async_copy(a, b, out_sems.at[at]) for at, (a, b) in enumerate(zip(made, outs))]
    for kind in range(4):
        loads[kind].wait()
        for layer in range(layers):
            out = made[4 * layer + kind]
            if kind == 0:
                cols = qkv.shape[3]
                for part in range(3):
                    out[:, part * cols : (part + 1) * cols] = qkv[layer, part].astype(bf16)
            elif kind == 2:
                for low in range(0, upper.shape[2], 256):
                    out[:, low : low + 256] = upper[layer, :, low : low + 256].astype(bf16)
            else:
                from_ref = proj if kind == 1 else lower
                for low in range(0, from_ref.shape[1], HD):
                    out[:, low : low + HD] = from_ref[layer, low : low + HD, :].T.astype(bf16)
            stores[4 * layer + kind].start()
    for copy in loads[4:]:
        copy.wait()
    small = made[-1]
    rows = [each[layer] for each in (gains, shifts) for layer in range(layers)] + [bias[...]]
    used = sum(each.shape[0] for each in rows)
    rows.append(jnp.zeros((small.shape[0] - used, small.shape[1]), f32))
    small[...] = jnp.concatenate(rows, axis=0).astype(bf16)
    stores[-1].start()
    for copy in stores:
        copy.wait()


def prepare_all(states, small_rows):
    qkv, proj, upper, lower = states[:4]
    layers = qkv.shape[0]
    wide = upper.shape[1]
    each = [3 * qkv.shape[3], proj.shape[1], upper.shape[2], lower.shape[1]] * layers
    shapes = [(wide, cols) for cols in each] + [(small_rows, wide)]
    any_place = pl.BlockSpec(memory_space=pl.ANY)
    return pl.pallas_call(
        functools.partial(prepare_kernel, layers),
        out_shape=[jax.ShapeDtypeStruct(shape, bf16) for shape in shapes],
        in_specs=[any_place] * 7,
        out_specs=[any_place] * len(shapes),
        scratch_shapes=[pltpu.VMEM(state.shape, f32) for state in states]
        + [pltpu.VMEM(shape, bf16) for shape in shapes]
        + [pltpu.SemaphoreType.DMA((7,)), pltpu.SemaphoreType.DMA((len(shapes),))],
        compiler_params=pltpu.CompilerParams(vmem_limit_bytes=56 * 2**20),
    )(*states)


def adam_kernel(streams, scalars, *refs):
    ins = 20 + 2 * streams
    news = 12 + streams
    sources, outs = refs[:ins], refs[ins : ins + news]
    held, made = refs[ins + news : 2 * ins + news], refs[2 * ins + news : 2 * (ins + news)]
    in_sems, out_sems = refs[2 * (ins + news) :]
    loads = [
        pltpu.make_async_copy(a, b, in_sems.at[at]) for at, (a, b) in enumerate(zip(sources, held))
    ]
    stores = [pltpu.make_async_copy(a, b, out_sems.at[at]) for at, (a, b) in enumerate(zip(made, outs))]
    order = []
    for group in range(4):
        order += [2 * group, 2 * group + 1] + [8 + 3 * group + which for which in range(3)]
    for at in order + list(range(20, ins)):
        loads[at].start()
    factor = scalars[0, 0]

    def update(group, at, gradient):
        found = [held[8 + 3 * group + which][at] for which in range(3)]
        new = adam_update(
            *found, gradient.astype(f32), factor, group_rates[group], group_decays[group]
        )
        for which in range(3):
            made[3 * group + which][at] = new[which]

    for group in range(4):
        for at in order[5 * group : 5 * group + 5]:
            loads[at].wait()
        for layer, gradient in enumerate((held[2 * group + 1], held[2 * group])):
            if group == 0:
                wide, cols = gradient.shape[0], gradient.shape[1] // 3
                for part in range(3):
                    for low in range(0, wide, 64):
                        update(
                            0,
                            (layer, part, slice(low, low + 64)),
                            gradient[low : low + 64, part * cols : (part + 1) * cols],
                        )
            elif group == 2:
                for low in range(0, gradient.shape[0], 16):
                    update(2, (layer, slice(low, low + 16)), gradient[low : low + 16, :])
            else:
                for low in range(0, gradient.shape[1], HD):
                    part = gradient[:, low : low + HD].astype(f32).T
                    update(group, (layer, slice(low, low + HD)), part)
        for which in range(3):
            stores[3 * group + which].start()
    for at in range(streams):
        for which in range(2):
            loads[20 + 2 * at + which].wait()
        ours, others = held[20 + 2 * at : 22 + 2 * at]
        for low in range(0, ours.shape[0], 64):
            rows = slice(low, low + 64)
            values = jnp.where(scalars[0, 1] > 0.5, others[rows, :].astype(f32), ours[rows, :])
            made[12 + at][rows, :] = values
        stores[12 + at].start()
    for copy in stores:
        copy.wait()


def adam_all(factor, moved, gradients, states, streams):
    scalars = jnp.stack([factor, jnp.where(moved, 1.0, 0.0).astype(f32)]).reshape(1, 2)
    any_place = pl.BlockSpec(memory_space=pl.ANY)
    operands = list(gradients) + list(states) + list(streams)
    news = [jax.ShapeDtypeStruct(each.shape, f32) for each in list(states) + list(streams[::2])]
    return pl.pallas_call(
        functools.partial(adam_kernel, len(streams) // 2),
        out_shape=news,
        in_specs=[pl.BlockSpec(memory_space=pltpu.SMEM)] + [any_place] * len(operands),
        out_specs=[any_place] * len(news),
        scratch_shapes=[pltpu.VMEM(each.shape, each.dtype) for each in operands + news]
        + [
            pltpu.SemaphoreType.DMA((len(operands),)),
            pltpu.SemaphoreType.DMA((len(news),)),
        ],
        compiler_params=pltpu.CompilerParams(vmem_limit_bytes=60 * 2**20),
    )(scalars, *operands)


ROWS = 64
SAVED = 9
TILE = 256


def norm_rows(src, dst, low, gain, shift):
    def some_rows(at, carry):
        rows = pl.ds(pl.multiple_of(at * ROWS, ROWS), ROWS)
        values = src[rows, :]
        low[rows, :] = values.astype(bf16)
        dst[rows, :] = layer_norm(values, gain, shift).astype(bf16)
        return carry

    lax.fori_loop(0, src.shape[0] // ROWS, some_rows, 0)


def tiles_of(width, body):
    def one(at, carry):
        body(pl.multiple_of(at * TILE, TILE))
        return carry

    lax.fori_loop(0, width // TILE, one, 0)


def block_scores(query, key, slope, doc_col, doc_row, first_col, diagonal):
    cols = first_col + lax.broadcasted_iota(jnp.int32, (1, key.shape[0]), 1)
    scores = dot_cols(query, key) * score_scale + slope * cols.astype(f32)
    allowed = doc_col == doc_row
    if diagonal:
        row = lax.broadcasted_iota(jnp.int32, scores.shape, 0)
        col = lax.broadcasted_iota(jnp.int32, scores.shape, 1)
        allowed = allowed & (row >= col)
    return jnp.where(allowed, scores, masked_score)


def lane_of(values, lane):
    return lax.broadcasted_iota(jnp.int32, values.shape, 1) == lane


def head_slope(slot, inner, slots, heads_slot, core):
    slope = 0.5 ** (slot * heads_slot + 1.0)
    for later in range(1, heads_slot):
        slope = jnp.where(inner == later, 0.5 ** (slot * heads_slot + later + 1.0), slope)
    return slope * jnp.where(core == 0, 1.0, 0.5 ** (slots * heads_slot))


def attend_head(qkv, out, logs, head, at, width, slope, doc_cols, doc_rows):
    query_cols, key_cols, value_cols = (
        pl.ds(pl.multiple_of(at + part * width, HD), HD) for part in range(3)
    )
    length = qkv.shape[0]
    block = min(256, length)
    for first_row in range(0, length, block):
        rows = slice(first_row, first_row + block)
        low, high = key_range(first_row, block)
        blocks = [slice(first, first + block) for first in range(low, high, block)]
        query = qkv[rows, query_cols]
        scores = [
            block_scores(
                query, qkv[cols, key_cols], slope, doc_cols[rows, :],
                doc_rows[:, cols], cols.start, cols == rows,
            )
            for cols in blocks
        ]
        top = scores[0]
        for each in scores[1:]:
            top = jnp.maximum(top, each)
        top = jnp.max(top, axis=-1, keepdims=True)
        total, mixed = 0.0, 0.0
        for cols, each in zip(blocks, scores):
            shifted = jnp.exp(each - top)
            total = total + jnp.sum(shifted, axis=-1, keepdims=True)
            mixed = mixed + dot(shifted.astype(bf16), qkv[cols, value_cols])
        to = pl.ds(pl.multiple_of(head * HD, HD), HD)
        out[rows, to] = (mixed * (1.0 / total)).astype(bf16)
        logs[rows, :] = jnp.where(lane_of(logs[rows, :], head), top + jnp.log(total), logs[rows, :])


FORWARD_STEPS = (
    ("norm_one", "other_0", "other_1", "own_0", "own_1", "share")
    + ("head_0", "head_1")
    + ("back", "proj", "norm_two")
    + tuple(f"up_{at}" for at in range(8))
    + tuple(f"down_{at}" for at in range(4))
)


def forward_kernel(plans, order, mp_size, layers, vector_count, gain_rows, shift_rows, *refs):
    n = len(plans)
    shards = refs[:n]
    inputs, doc_cols, doc_rows = refs[n : n + 3]
    outs = refs[n + 3 : 2 * n + 3]
    at = 2 * n + 3
    saved = [refs[at + SAVED * layer : at + SAVED * (layer + 1)] for layer in range(layers)]
    at += SAVED * layers
    last_stream, last_low, vectors = refs[at : at + 3]
    (
        streams, middles, lows, normed_one, normed_two, send_buf, qkv_full, mixed, logs, attended,
        hidden, active, w_qkv, w_proj, w_up, w_down, small_buf, biases, traded,
        load_sems, save_sems, trade_sems, head_sems, send_sems, recv_sems, own_sems,
    ) = refs[at + 3 :]
    work = SpreadWork(plans, order, mp_size, shards, outs, send_sems, recv_sems, own_sems)
    z, d = work.z, work.d
    core = d % 2
    moved = core != z % 2
    partner = {DP: flip(d, 1)}
    across = {DP: flip(d, 1), MP: flip(z, 1)}
    tokens = inputs.shape[0]
    features = inputs.shape[1]
    half = attended.shape[2] // 2
    wide_small = shards[-1].shape[0]
    lanes = shards[-1].shape[1]
    third = w_qkv.shape[2] // 3
    slots = qkv_full.shape[2] // w_qkv.shape[2]
    heads_slot = third // HD

    greet(z, d, work.upper, mp_size, (), across, moved)
    trade = pltpu.make_async_remote_copy(
        src_ref=inputs, dst_ref=traded, send_sem=trade_sems.at[0], recv_sem=trade_sems.at[1],
        device_id=across, device_id_type=MESH,
    )
    keep = pltpu.make_async_copy(inputs, traded, trade_sems.at[2])

    @pl.when(moved)
    def _():
        trade.start()

    @pl.when(jnp.logical_not(moved))
    def _():
        keep.start()

    work.begin()

    saves = []

    def save(src, dst):
        copy = pltpu.make_async_copy(src, dst, save_sems.at[len(saves)])
        copy.start()
        saves.append(copy)
        return copy

    loads = {}

    def load(key, src, dst, slot):
        copy = pltpu.make_async_copy(src, dst, load_sems.at[slot])
        copy.start()
        loads[key] = copy

    def load_tile(layer, kind, at):
        full = outs[4 * layer : 4 * layer + 4]
        if kind == "qkv":
            cols = w_qkv.shape[2]
            first = (1 - core) * slots if at < slots else core * slots
            where = pl.ds(place(first + at % slots, cols), cols)
            load((layer, kind, at), full[0].at[:, where], w_qkv.at[at % 2], at % 2)
        elif kind == "proj":
            load((layer, kind, at), full[1], w_proj, 2)
        elif kind == "up":
            cols = w_up.shape[2]
            where = pl.ds(at * cols, cols)
            load((layer, kind, at), full[2].at[:, where], w_up.at[at % 2], 3 + at % 2)
        else:
            rows = w_down.shape[1]
            where = pl.ds(at * rows, rows)
            load((layer, kind, at), full[3].at[where, :], w_down.at[at % 2], 5 + at % 2)

    def tile(layer, kind, at, count):
        if (layer, kind, at) not in loads:
            load_tile(layer, kind, at)
        loads[layer, kind, at].wait()
        if at + 1 < count:
            load_tile(layer, kind, at + 1)

    def share_copy(layer):
        rows = pl.ds(place(core, tokens), tokens)
        return pltpu.make_async_remote_copy(
            src_ref=send_buf.at[layer], dst_ref=qkv_full.at[layer, rows, :],
            send_sem=head_sems.at[4 * layer], recv_sem=head_sems.at[4 * layer + 1],
            device_id=partner, device_id_type=MESH,
        )

    def back_copy(layer):
        rows = pl.ds(place(1 - core, tokens), tokens)
        return pltpu.make_async_remote_copy(
            src_ref=mixed.at[layer, rows, :],
            dst_ref=attended.at[layer, :, pl.ds(place(core, half), half)],
            send_sem=head_sems.at[4 * layer + 2], recv_sem=head_sems.at[4 * layer + 3],
            device_id=partner, device_id_type=MESH,
        )

    def active_copy(layer):
        rows = pl.ds(place(core, tokens), tokens)
        return pltpu.make_async_remote_copy(
            src_ref=active, dst_ref=saved[layer][7].at[rows, :],
            send_sem=head_sems.at[4 * layers + 2 * layer],
            recv_sem=head_sems.at[4 * layers + 2 * layer + 1],
            device_id=partner, device_id_type=MESH,
        )

    def vector(at):
        return vectors[at : at + 1, :]

    ahead = {
        "norm_one": ("qkv", 0), "head_0": ("proj", 1), "proj": ("up", 2), "up_6": ("down", 3)
    }

    def compute(layer, name):
        kind, _, at = name.partition("_")
        if name in ahead and 4 * layer + ahead[name][1] not in missing:
            load_tile(layer, ahead[name][0], 0)
        gain = layer * gain_rows
        shift = layers * gain_rows + layer * shift_rows
        keeps = saved[layer]
        if name == "norm_one":
            if layer == 0:
                small = pltpu.make_async_copy(outs[-1], small_buf, load_sems.at[7])
                small.start()

                @pl.when(moved)
                def _():
                    trade.wait_recv()

                @pl.when(jnp.logical_not(moved))
                def _():
                    keep.wait()

                streams[0] = traded[...].astype(f32)
                small.wait()
                for b in range(outs[-1].shape[0] // wide_small):
                    rows = small_buf[b * wide_small : (b + 1) * wide_small, :].astype(f32)
                    vectors[:, b * lanes : (b + 1) * lanes] = rows[:, :lanes]
                    for m in range(mp_size):
                        first = m * (biases.shape[1] // mp_size) + b * lanes
                        biases[:, first : first + lanes] = rows[:, m * lanes : (m + 1) * lanes]
            norm_rows(
                streams.at[layer], normed_one.at[layer], lows.at[2 * layer],
                vector(gain), vector(shift),
            )
            save(lows.at[2 * layer], keeps[0])
            save(normed_one.at[layer], keeps[2])
        elif kind in ("other", "own"):
            at = int(at)
            tile(layer, "qkv", at + (slots if kind == "own" else 0), 2 * slots)
            weight = w_qkv.at[at % 2]
            cols = w_qkv.shape[2]

            def piece(first):
                values = dot(normed_one[layer], weight[:, pl.ds(first, TILE)]).astype(bf16)
                to = pl.ds(pl.multiple_of(at * cols + first, TILE), TILE)
                if kind == "own":
                    qkv_full[layer, pl.ds(place(core, tokens), tokens), to] = values
                else:
                    send_buf[layer, :, to] = values

            tiles_of(cols, piece)
            if kind == "other" and at == slots - 1:
                share_copy(layer).start()
        elif kind == "share":
            arrived = pltpu.make_async_remote_copy(
                src_ref=send_buf.at[layer],
                dst_ref=qkv_full.at[layer, pl.ds(place(1 - core, tokens), tokens), :],
                send_sem=head_sems.at[4 * layer], recv_sem=head_sems.at[4 * layer + 1],
                device_id=partner, device_id_type=MESH,
            )
            arrived.wait_recv()
            save(qkv_full.at[layer], keeps[3])
        elif kind == "head":
            slot = int(at)
            if slot == 0:
                logs[layer] = jnp.zeros(logs.shape[1:], f32)

            def one_head(inner, carry):
                attend_head(
                    qkv_full.at[layer], mixed.at[layer], logs.at[layer], slot * heads_slot + inner,
                    slot * 3 * third + inner * HD, third,
                    head_slope(slot, inner, slots, heads_slot, core), doc_cols, doc_rows,
                )
                return carry

            lax.fori_loop(0, heads_slot, one_head, 0)
            if slot == slots - 1:
                back_copy(layer).start()
                rows = pl.ds(place(core, tokens), tokens)
                attended[layer, :, pl.ds(place(core, half), half)] = mixed[layer, rows, :]
                save(mixed.at[layer], keeps[4])
                save(logs.at[layer], keeps[8])
        elif kind == "back":
            arrived = pltpu.make_async_remote_copy(
                src_ref=mixed.at[layer, pl.ds(0, tokens), :],
                dst_ref=attended.at[layer, :, pl.ds(place(1 - core, half), half)],
                send_sem=head_sems.at[4 * layer + 2], recv_sem=head_sems.at[4 * layer + 3],
                device_id=partner, device_id_type=MESH,
            )
            arrived.wait_recv()
        elif kind == "proj":
            tile(layer, "proj", 0, 1)

            def piece(first):
                cols = pl.ds(first, TILE)
                values = dot_cols(attended[layer], w_proj[cols, :])
                middles[layer, :, cols] = streams[layer, :, cols] + values

            tiles_of(features, piece)
        elif name == "norm_two":
            norm_rows(
                middles.at[layer], normed_two.at[layer], lows.at[2 * layer + 1],
                vector(gain + 1), vector(shift + 1),
            )
            save(lows.at[2 * layer + 1], keeps[1])
            save(normed_two.at[layer], keeps[5])
        elif kind == "up":
            at = int(at)
            if at == 0 and layer > 0:
                for copy in big_saves[layer - 1]:
                    copy.wait()
                active_copy(layer - 1).wait_send()
            cols = w_up.shape[2]
            tile(layer, "up", at, hidden.shape[1] // cols)
            weight = w_up.at[at % 2]

            def piece(first):
                to = pl.ds(pl.multiple_of(at * cols + first, TILE), TILE)
                bias = biases[vector_count + layer : vector_count + layer + 1, to]
                values = dot(normed_two[layer], weight[:, pl.ds(first, TILE)]) + bias
                hidden[:, to] = values.astype(bf16)
                active[:, to] = gelu_tanh(values).astype(bf16)

            tiles_of(cols, piece)
            if (at + 1) * cols == hidden.shape[1]:
                rows = pl.ds(place(core, tokens), tokens)
                big_saves[layer] = [save(hidden, keeps[6]), save(active, keeps[7].at[rows, :])]
                active_copy(layer).start()
        elif kind == "down":
            at = int(at)
            rows = w_down.shape[1]
            tile(layer, "down", at, features // rows)
            weight = w_down.at[at % 2]
            out = streams.at[layer + 1]
            cols = pl.ds(at * rows, rows)
            out[:, cols] = middles[layer, :, cols] + vector(shift + 2)[:, at * rows : (at + 1) * rows]

            def piece(step, carry):
                inner = pl.ds(pl.multiple_of(step * 1024, 1024), 1024)
                out[:, cols] += dot_cols(active[:, inner], weight[:, inner])
                return carry

            lax.fori_loop(0, hidden.shape[1] // 1024, piece, 0)

    big_saves = {}
    missing = {}
    for t, _ in work.order:
        missing[t] = missing.get(t, 0) + 1
    for step in order:
        if isinstance(step[1], str):
            compute(*step)
        else:
            work.step(*step)
            missing[step[0]] -= 1
            if missing[step[0]] == 0:
                del missing[step[0]]
    save(streams.at[layers], last_stream)
    traded[...] = streams[layers].astype(bf16)
    save(traded, last_low)
    done_already = [id(copy) for layer in range(layers - 1) for copy in big_saves[layer]]
    for copy in saves:
        if id(copy) not in done_already:
            copy.wait()
    for layer in range(layers):
        share_copy(layer).wait_send()
        back_copy(layer).wait_send()
        rows = pl.ds(place(1 - core, tokens), tokens)
        pltpu.make_async_remote_copy(
            src_ref=active, dst_ref=saved[layer][7].at[rows, :],
            send_sem=head_sems.at[4 * layers + 2 * layer],
            recv_sem=head_sems.at[4 * layers + 2 * layer + 1],
            device_id=partner, device_id_type=MESH,
        ).wait_recv()
    active_copy(layers - 1).wait_send()

    @pl.when(moved)
    def _():
        trade.wait_send()

    work.finish()


def forward_all(
    shards, inputs, docs, plans, order, dp_size, mp_size, layers, vector_count, gain_rows, shift_rows
):
    _, total = number(plans, mp_size, spread_single)
    tokens, features = inputs.shape
    length = docs.shape[0]
    half = features // 2
    units = shards[2].shape[1] * mp_size
    cols = shards[0].shape[1]
    slots = mp_size // 2
    any_place = pl.BlockSpec(memory_space=pl.ANY)
    vmem = pl.BlockSpec(memory_space=pltpu.VMEM)
    saved = [
        jax.ShapeDtypeStruct((tokens, features), bf16),
        jax.ShapeDtypeStruct((tokens, features), bf16),
        jax.ShapeDtypeStruct((tokens, features), bf16),
        jax.ShapeDtypeStruct((length, slots * cols), bf16),
        jax.ShapeDtypeStruct((length, half), bf16),
        jax.ShapeDtypeStruct((tokens, features), bf16),
        jax.ShapeDtypeStruct((tokens, units), bf16),
        jax.ShapeDtypeStruct((length, units), bf16),
        jax.ShapeDtypeStruct((length, HD), f32),
    ]
    small_shape = (shards[-1].shape[0] * dp_size, shards[-1].shape[1] * mp_size)
    out_shape = [
        jax.ShapeDtypeStruct((s.shape[0] * dp_size, s.shape[1] * mp_size), s.dtype)
        for s in shards
    ]
    out_shape += saved * layers + [
        jax.ShapeDtypeStruct((tokens, features), f32),
        jax.ShapeDtypeStruct((tokens, features), bf16),
    ]
    out_shape.append(jax.ShapeDtypeStruct((shards[-1].shape[0], features), f32))
    out = pl.pallas_call(
        functools.partial(
            forward_kernel, plans, order, mp_size, layers, vector_count, gain_rows, shift_rows
        ),
        out_shape=out_shape,
        in_specs=[any_place] * (len(shards) + 1) + [vmem] * 2,
        out_specs=[any_place] * (len(out_shape) - 1) + [vmem],
        scratch_shapes=[
            pltpu.VMEM((layers + 1, tokens, features), f32),
            pltpu.VMEM((layers, tokens, features), f32),
            pltpu.VMEM((2 * layers, tokens, features), bf16),
            pltpu.VMEM((layers, tokens, features), bf16),
            pltpu.VMEM((layers, tokens, features), bf16),
            pltpu.VMEM((layers, tokens, slots * cols), bf16),
            pltpu.VMEM((layers, length, slots * cols), bf16),
            pltpu.VMEM((layers, length, half), bf16),
            pltpu.VMEM((layers, length, HD), f32),
            pltpu.VMEM((layers, tokens, features), bf16),
            pltpu.VMEM((tokens, units), bf16),
            pltpu.VMEM((tokens, units), bf16),
            pltpu.VMEM((2, features, cols), bf16),
            pltpu.VMEM((features, features), bf16),
            pltpu.VMEM((2, features, units // 8), bf16),
            pltpu.VMEM((2, features // 4, units), bf16),
            pltpu.VMEM(small_shape, bf16),
            pltpu.VMEM((shards[-1].shape[0], units), f32),
            pltpu.VMEM((tokens, features), bf16),
            pltpu.SemaphoreType.DMA((8,)),
            pltpu.SemaphoreType.DMA((SAVED * layers + 2,)),
            pltpu.SemaphoreType.DMA((3,)),
            pltpu.SemaphoreType.DMA((6 * layers,)),
            pltpu.SemaphoreType.DMA((total,)),
            pltpu.SemaphoreType.DMA((total,)),
            pltpu.SemaphoreType.DMA((len(shards),)),
        ],
        compiler_params=pltpu.CompilerParams(
            collective_id=2, has_side_effects=True, vmem_limit_bytes=62 * 2**20
        ),
    )(*shards, inputs, docs.reshape(-1, 1), docs.reshape(1, -1))
    n = len(shards)
    stored = [out[n + SAVED * at : n + SAVED * (at + 1)] for at in range(layers)]
    return out[:n], stored, out[-3], out[-2], out[-1]


KINDS = ("down", "up", "proj", "qkv")
BACKWARD_STEPS = (
    "turn_down", "W0", "W1", "W2", "W3",
    "turn_up", "hidden_0", "hidden_1", "hidden_2", "hidden_3", "W0",
    "hidden_4", "hidden_5", "W1", "hidden_6", "hidden_7", "norm_two", "mixed_0", "mixed_1",
    "W2", "W3", "turn_proj", "W0", "W1", "W2", "W3", "turn_qkv",
    "share", "head_0", "head_1", "rows_0", "rows_1", "rows_2",
    "back", "W0", "W1", "W2", "W3", "rows_3", "rows_4", "rows_5", "norm_one",
)


def gelu_slope(v):
    root = math.sqrt(2.0 / math.pi)
    t = jnp.tanh(root * (v + 0.044715 * v * v * v))
    return 0.5 * (1.0 + t) + 0.5 * v * (1.0 - t * t) * root * (1.0 + 3 * 0.044715 * v * v)


def norm_back(src, upstream, total, low, gain):
    features = src.shape[1]

    def some_rows(at, carry):
        rows = pl.ds(pl.multiple_of(at * ROWS, ROWS), ROWS)
        value = src[rows, :].astype(f32)
        center = value - jnp.mean(value, axis=-1, keepdims=True)
        scale = lax.rsqrt(jnp.mean(center * center, axis=-1, keepdims=True) + norm_eps)
        normal = center * scale
        grad = upstream[rows, :]
        inner = grad * gain
        mean_inner = jnp.mean(inner, axis=-1, keepdims=True)
        mean_both = jnp.mean(inner * normal, axis=-1, keepdims=True)
        new = total[rows, :] + scale * (inner - mean_inner - normal * mean_both)
        total[rows, :] = new
        low[rows, :] = new.astype(bf16)
        return (
            carry[0] + jnp.sum(grad * normal, axis=0, keepdims=True),
            carry[1] + jnp.sum(grad, axis=0, keepdims=True),
            carry[2] + jnp.sum(new, axis=0, keepdims=True),
        )

    zero = jnp.zeros((1, features), f32)
    return lax.fori_loop(0, src.shape[0] // ROWS, some_rows, (zero, zero, zero))


def attend_back_head(
    qkv, mixed, mixed_grad, logs, key_acc, value_acc, head, at, width, slope, doc_cols, doc_rows
):
    length = qkv.shape[0]
    block = min(256, length)
    key_acc[...] = jnp.zeros_like(key_acc)
    value_acc[...] = jnp.zeros_like(value_acc)
    query_cols, key_cols, value_cols = (
        pl.ds(pl.multiple_of(at + part * width, HD), HD) for part in range(3)
    )
    mine = pl.ds(pl.multiple_of(head * HD, HD), HD)
    for first_row in range(0, length, block):
        rows = slice(first_row, first_row + block)
        low, high = key_range(first_row, block)
        query = qkv[rows, query_cols]
        out_grad = mixed_grad[rows, mine]
        values = mixed[rows, mine]
        inner = jnp.sum(out_grad.astype(f32) * values.astype(f32), axis=-1, keepdims=True)
        log = logs[rows, :]
        log = jnp.sum(jnp.where(lane_of(log, head), log, 0.0), axis=-1, keepdims=True)
        query_grad = 0.0
        for first in range(low, high, block):
            cols = slice(first, first + block)
            key = qkv[cols, key_cols]
            scores = block_scores(
                query, key, slope, doc_cols[rows, :], doc_rows[:, cols], first, first == first_row
            )
            probs = jnp.exp(scores - log)
            value_acc[cols, :] += dot_rows(probs.astype(bf16), out_grad)
            prob_grad = dot_cols(out_grad, qkv[cols, value_cols])
            score_grad = (probs * (prob_grad - inner)).astype(bf16)
            query_grad = query_grad + dot(score_grad, key)
            key_acc[cols, :] += dot_rows(score_grad, query)
        qkv[rows, query_cols] = (query_grad * score_scale).astype(bf16)
    qkv[:, key_cols] = (key_acc[...] * score_scale).astype(bf16)
    qkv[:, value_cols] = value_acc[...].astype(bf16)


class Rows:
    def __init__(self, dims, mp_size, merged=False):
        self.dims = tuple(dims)
        self.merged = merged
        self.masks = [0]
        for dim in reversed([dim for dim in self.dims if dim != MP]):
            self.masks = self.masks + [mask | dim for mask in self.masks]
        self.kept = {0: len(self.masks)}
        self.events = []
        for stage, dim in enumerate(self.dims, 1):
            self.kept[stage] = self.kept[stage - 1] // (1 if dim == MP else 2)
            if dim == MP:
                for hops in reversed(range(mp_size - 1)):
                    self.events += [(stage, way, hops) for way in (1, -1)]
            else:
                count = mp_size if self.full(stage) and not merged else 1
                self.events += [(stage, 0, at) for at in range(count)]

    def full(self, stage):
        return MP not in self.dims[: stage - 1]


def number_rows(plans, mp_size):
    index, total = {}, 0
    for t, plan in enumerate(plans):
        for stage, way, at in plan.events:
            if way:
                index[t, stage, way, at] = total
                total += 1
            elif (t, stage) not in index:
                index[t, stage] = total
                total += mp_size
    return index, total


class RowsWork:
    def __init__(self, plans, mp_size, wides, cols, sums, recv, sems):
        self.plans, self.mp_size = plans, mp_size
        self.wides, self.cols = wides, cols
        self.sums, self.recv = sums, recv
        self.send_sems, self.recv_sems, self.credit_sems = sems
        self.z = lax.axis_index(MP)
        self.d = lax.axis_index(DP)
        self.index, _ = number_rows(plans, mp_size)
        self.brought = {}
        self.credited = set()
        self.outgoing = {}
        self.left, self.left_stage = {}, {}
        for t, plan in enumerate(plans):
            self.left[t] = len(plan.events)
            for event in plan.events:
                key = t, event[0]
                self.left_stage[key] = self.left_stage.get(key, 0) + 1

    def inside(self, at):
        return (at >= 0) & (at < self.mp_size)

    def slab(self, t):
        return t % 4 if t < 8 else 4

    def part(self, t, low, high, block):
        wide, cols = self.wides[t], self.cols[t]
        where = pl.ds(0, cols * self.mp_size) if block is None else pl.ds(place(block, cols), cols)
        return self.sums[self.slab(t)].at[pl.ds(low * wide, (high - low) * wide), where]

    def landing(self, t, event, block):
        stage, way, at = event
        ref = self.recv[self.slab(t), stage]
        if way:
            return ref.at[block if way == 1 or at > 0 else self.mp_size]
        if block is None:
            return ref.at[0]
        return ref.at[block if self.plans[t].full(stage) else 0]

    def remote(self, t, event, block, src, dst, to):
        stage, way, at = event
        if way:
            sem = self.index[(t,) + event]
        else:
            sem = self.index[t, stage] + (0 if block is None else block)
        return pltpu.make_async_remote_copy(
            src_ref=src,
            dst_ref=dst,
            send_sem=self.send_sems.at[sem],
            recv_sem=self.recv_sems.at[sem],
            device_id=to,
            device_id_type=MESH,
        )

    def launch(self, t, copy, when=None):
        if when is None:
            copy.start()
        else:
            pl.when(when)(copy.start)
        self.outgoing.setdefault(t, []).append((copy, when))

    def settle(self, t):
        for copy, when in self.outgoing.pop(t, []):
            if when is None:
                copy.wait_send()
            else:
                pl.when(when)(copy.wait_send)

    def take_credit(self, t, stage, way=0):
        if not 4 <= t < 8 or (t, stage, way) in self.credited:
            return
        self.credited.add((t, stage, way))
        sem = self.credit_sems.at[t - 4, stage, 1 if way == -1 else 0]
        if way:
            pl.when(self.inside(self.z + way))(lambda: pl.semaphore_wait(sem, 1))
        else:
            pl.semaphore_wait(sem, 1)

    def give_credit(self, t, stage):
        dim = self.plans[t + 4].dims[stage - 1]
        if dim != MP:
            pl.semaphore_signal(
                self.credit_sems.at[t, stage, 0], inc=1,
                device_id={DP: flip(self.d, dim)}, device_id_type=MESH,
            )
            return
        for way in (1, -1):

            @pl.when(self.inside(self.z - way))
            def _(way=way):
                pl.semaphore_signal(
                    self.credit_sems.at[t, stage, 1 if way == -1 else 0], inc=1,
                    device_id={MP: self.z - way}, device_id_type=MESH,
                )

    def line_copy(self, t, stage, way, hops):
        event = (stage, way, hops - 1)
        block = self.z + way * hops
        dst = self.landing(t, event, block)
        src = self.part(t, 0, self.plans[t].kept[stage], block)
        return self.remote(t, event, block, src, dst, {MP: self.z + way})

    def arrival(self, t, event, block):
        dst = self.landing(t, event, block)
        return self.remote(t, event, block, dst, dst, {DP: self.d, MP: self.z})

    def add(self, dst, src, rows_count):
        step = 16

        def some_rows(at, carry):
            rows = pl.ds(pl.multiple_of(at * step, step), step)
            dst[rows, :] += src[rows, :]
            return carry

        lax.fori_loop(0, rows_count // step, some_rows, 0)

    def advance(self, t, stage, block, other):
        plan = self.plans[t]
        if stage > len(plan.dims):
            return
        dim = plan.dims[stage - 1]
        if dim == MP:
            for way, end in ((1, 0), (-1, self.mp_size - 1)):
                self.take_credit(t, stage, way)
                for hops in range(1, self.mp_size) if block is None else (other,) * (other > 0):
                    copy = self.line_copy(t, stage, way, hops)
                    self.launch(t, copy, self.z == end)
            return
        self.take_credit(t, stage)
        event = (stage, 0, None)
        src = self.part(t, plan.kept[stage], plan.kept[stage - 1], block)
        dst = self.landing(t, event, block)
        self.launch(t, self.remote(t, event, block, src, dst, {DP: flip(self.d, dim)}))

    def step(self, t, event, finish):
        stage, way, at = event
        plan = self.plans[t]
        kept = plan.kept[stage]
        if way:
            block = self.z + way * at
            here = self.inside(block) & self.inside(self.z - way)
            if at > 0:
                self.take_credit(t, stage, way)

            @pl.when(here)
            def _():
                self.arrival(t, event, block).wait_recv()
                self.add(
                    self.part(t, 0, kept, block), self.landing(t, event, block),
                    kept * self.wides[t],
                )

            if at > 0:
                self.launch(t, self.line_copy(t, stage, way, at), here)
            else:
                self.brought[t] = self.brought.get(t, 0) + 1
                if self.brought[t] == 2:
                    self.advance(t, stage + 1, self.z, 0)
        else:
            if plan.full(stage):
                block = None if plan.merged else flip(self.z, at)
            else:
                block = self.z
            self.arrival(t, event, block).wait_recv()
            self.add(
                self.part(t, 0, kept, block), self.landing(t, event, block), kept * self.wides[t]
            )
            self.advance(t, stage + 1, block, at)
        self.left[t] -= 1
        self.left_stage[t, stage] -= 1
        if t < 4 and self.left_stage[t, stage] == 0:
            self.give_credit(t, stage)
        if self.left[t] == 0:
            finish(t)


def backward_kernel(
    plans, order, mp_size, layers, vector_count, gain_rows, shift_rows, *refs
):
    n = len(plans)
    full = [refs[4 * layer : 4 * layer + 4] for layer in range(layers)]
    at = 4 * layers
    cotangent, vectors, doc_cols, doc_rows = refs[at : at + 4]
    at += 4
    saved = [refs[at + SAVED * layer : at + SAVED * (layer + 1)] for layer in range(layers)]
    at += SAVED * layers
    outs, (norm_ref, input_grad, input_low) = refs[at : at + n], refs[at + n : at + n + 3]
    at += n + 3
    sums = refs[at : at + 5]
    at += 5
    recv = {}
    for slab, plan in zip((0, 1, 2, 3, 4), plans[:4] + plans[8:]):
        for stage in range(1, len(plan.dims) + 1):
            recv[slab, stage] = refs[at]
            at += 1
    (
        blocks, left_t, turn_send, grad, acc, low, hidden_buf, w_a, w_b, normed,
        source, qkv, mixed, mixed_other, logs, mixed_grad, mixed_send, row_other, key_acc,
        value_acc, vector_sums, bias_sums, tiles,
        load_sems, core_sems, out_sems, tile_sems, send_sems, recv_sems, credit_sems,
        block_credit, left_credit,
    ) = refs[at:]
    cols = [out.shape[1] for out in outs]
    wides = [out.shape[0] for out in outs]
    work = RowsWork(plans, mp_size, wides, cols, sums, recv, (send_sems, recv_sems, credit_sems))
    z, d = work.z, work.d
    core = d % 2
    partner = {DP: flip(d, 1)}
    upper = [dim for dim in plans[0].dims if dim != MP]
    mp_bits = bits_of(mp_size)
    tokens, features = low.shape
    half = features // 2
    own_rows = pl.ds(place(core, tokens), tokens)
    other_rows = pl.ds(place(1 - core, tokens), tokens)
    half_qkv = qkv.shape[1]
    slots = mp_size // 2
    third = half_qkv // slots // 3
    heads_slot = third // HD
    wide = w_a.shape[2]
    per_block = cols[0] // wide

    greet(z, d, upper, mp_size, mp_bits)

    loads = {}

    def fetch(key, src, dst):
        copy = pltpu.make_async_copy(src, dst, load_sems.at[len(loads)])
        copy.start()
        loads[key] = copy

    pushes = {}

    def push(key, src, dst):
        at = 2 * len(pushes)
        copy = pltpu.make_async_remote_copy(
            src_ref=src, dst_ref=dst, send_sem=core_sems.at[at], recv_sem=core_sems.at[at + 1],
            device_id=partner, device_id_type=MESH,
        )
        copy.start()
        pushes[key] = at, copy

    def pushed(key):
        pushes[key][1].wait_send()

    def arrived(key, dst):
        at = pushes[key][0]
        pltpu.make_async_remote_copy(
            src_ref=dst, dst_ref=dst, send_sem=core_sems.at[at], recv_sem=core_sems.at[at + 1],
            device_id=partner, device_id_type=MESH,
        ).wait_recv()

    def give(sem):
        pl.semaphore_signal(sem, inc=1, device_id=partner, device_id_type=MESH)

    fetch("cotangent", cotangent, low)
    vector_sums[...] = jnp.zeros_like(vector_sums)
    bias_sums[...] = jnp.zeros_like(bias_sums)

    def block_cols(at):
        block = flip(z, at // per_block)
        return pl.ds(pl.multiple_of(block * cols[0] + (at % per_block) * wide, wide), wide)

    def row_cols(at):
        count = half_qkv // wide
        part = core if at < count else 1 - core
        return pl.ds(pl.multiple_of(part * half_qkv + (at % count) * wide, wide), wide)

    def fetch_tile(layer, name, at):
        qkv_w, proj, up, down = full[layer]
        slot = at % 2
        if name == "hidden":
            where = block_cols(at)
            fetch((layer, "w_a", name, at), down.at[:, where], w_a.at[slot])
            fetch((layer, "w_b", name, at), up.at[:, where], w_b.at[slot])
            fetch((layer, "z", name, at), saved[layer][6].at[:, where], hidden_buf.at[slot])
        elif name == "mixed":
            first = place(1 - core if at == 0 else core, half)
            fetch((layer, "w_a", name, at), proj.at[:, pl.ds(first, half)], w_a.at[slot])
        else:
            fetch((layer, "w_b", name, at), qkv_w.at[:, row_cols(at)], w_b.at[slot])

    counts = {"hidden": mp_size * per_block, "mixed": 2, "rows": 2 * half_qkv // wide}

    def use_tile(layer, name, at):
        for which in ("w_a", "w_b", "z"):
            if (layer, which, name, at) in loads:
                loads[layer, which, name, at].wait()
        if at + 1 < counts[name]:
            fetch_tile(layer, name, at + 1)

    def fetch_block(layer, s):
        where = pl.ds(place(flip(z, s), cols[0]), cols[0])
        fetch((layer, "block", s), saved[layer][7].at[:, where], blocks.at[s % 2])

    def accumulate(left, weight, first):
        def piece(at, carry):
            rows = pl.ds(pl.multiple_of(at * TILE, TILE), TILE)
            values = dot_cols(left[...], weight[rows, :])
            if first:
                acc[:, rows] = values
            else:
                acc[:, rows] += values
            return carry

        lax.fori_loop(0, features // TILE, piece, 0)

    def put_vector(row, values):
        vector_sums[row : row + 1, :] = values

    def turn(use, src):
        slot = use % 2
        masks = plans[use].masks
        if use >= 2:
            pushed(("left", use - 2))
            pl.semaphore_wait(left_credit.at[slot], 1)
        for row, mask in enumerate(masks):
            there = pl.ds(row * wides[use], wides[use])
            theirs = pl.ds(place(flip(d, mask | 1), wides[use]), wides[use])
            mine = pl.ds(place(flip(d, mask), wides[use]), wides[use])
            turn_send[slot, there, :] = src[:, theirs].astype(f32).T.astype(bf16)
            left_t[slot, there, own_rows] = src[:, mine].astype(f32).T.astype(bf16)
        push(("left", use), turn_send.at[slot], left_t.at[slot, :, own_rows])

    def compute(layer, name):
        kind, _, at = name.partition("_")
        keeps = saved[layer]
        gain = layer * gain_rows
        shift = layers * gain_rows + layer * shift_rows
        last = layer == layers - 1
        use = 4 * (layers - 1 - layer)
        if name == "turn_down":
            if last:
                fetch_block(layer, 0)
                fetch_block(layer, 1)
                loads["cotangent"].wait()

                def some_rows(at, carry):
                    rows = pl.ds(pl.multiple_of(at * ROWS, ROWS), ROWS)
                    values = low[rows, :].astype(f32)
                    grad[rows, :] = values
                    return carry + jnp.sum(values, axis=0, keepdims=True)

                total = lax.fori_loop(
                    0, tokens // ROWS, some_rows, jnp.zeros((1, features), f32)
                )
                put_vector(shift + 2, total)
            else:
                pushed((layer + 1, "back"))
                pushed((layer + 1, "mixed"))
            fetch_tile(layer, "hidden", 0)
            fetch((layer, "normed_two"), keeps[5], normed)
            fetch((layer, "middle"), keeps[1], source)
            fetch((layer, "qkv"), keeps[3], qkv)
            fetch((layer, "mixed"), keeps[4], mixed)
            fetch((layer, "logs"), keeps[8], logs)
            push((layer, "mixed"), keeps[4], mixed_other)
            turn(use, low)
        elif name == "turn_up":
            loads[layer, "normed_two"].wait()
            turn(use + 1, normed)
            fetch((layer, "normed_one"), keeps[2], normed)
        elif name == "turn_proj":
            turn(use + 2, low)
        elif name == "turn_qkv":
            loads[layer, "normed_one"].wait()
            turn(use + 3, normed)
        elif kind == "hidden":
            at = int(at)
            use_tile(layer, "hidden", at)
            slot = at % 2
            s, inner = at // per_block, at % per_block
            to_block = s % 2
            if inner == 0 and s >= 2:
                pushed((layer, "grads", s - 2))

            def piece(first):
                here = pl.ds(first, TILE)
                values = dot(low[...], w_a[slot, :, here])
                values = values * gelu_slope(hidden_buf[slot, :, here].astype(f32))
                to = pl.multiple_of(flip(z, s) * cols[0] + inner * wide + first, TILE)
                bias_sums[vector_count + layer : vector_count + layer + 1, pl.ds(to, TILE)] = (
                    jnp.sum(values, axis=0, keepdims=True)
                )
                to = pl.ds(pl.multiple_of(inner * wide + first, TILE), TILE)
                blocks[to_block, own_rows, to] = values.astype(bf16)

            tiles_of(wide, piece)
            left = blocks.at[to_block, own_rows, pl.ds(inner * wide, wide)]
            accumulate(left, w_b.at[slot], at == 0)
            if inner == per_block - 1:
                pl.semaphore_wait(block_credit.at[s], 1)
                part = blocks.at[to_block, own_rows, :]
                push((layer, "grads", s), part, part)
        elif name == "norm_two":
            loads[layer, "middle"].wait()
            sums_of = norm_back(source, acc, grad, low, vectors[gain + 1 : gain + 2, :])
            put_vector(gain + 1, sums_of[0])
            put_vector(shift + 1, sums_of[1])
            fetch((layer, "stream"), keeps[0], source)
            fetch_tile(layer, "mixed", 0)
        elif kind == "mixed":
            at = int(at)
            use_tile(layer, "mixed", at)
            if at == 0 and not last:
                pushed((layer + 1, "share"))

            def piece(first):
                here = pl.ds(first, TILE)
                values = dot(low[...], w_a[at % 2, :, here]).astype(bf16)
                if at == 0:
                    mixed_send[:, here] = values
                else:
                    mixed_grad[own_rows, here] = values

            tiles_of(half, piece)
            if at == 0:
                push((layer, "share"), mixed_send, mixed_grad.at[own_rows, :])
        elif name == "share":
            arrived((layer, "share"), mixed_grad.at[other_rows, :])
            loads[layer, "qkv"].wait()
            loads[layer, "logs"].wait()
            fetch_tile(layer, "rows", 0)
        elif kind == "head":
            slot = int(at)
            if slot == 0 and layer > 0:
                pushed((layer, "grads", 2))
                pushed((layer, "grads", 3))
                fetch_block(layer - 1, 0)
                fetch_block(layer - 1, 1)

            def one_head(inner, carry):
                attend_back_head(
                    qkv, mixed, mixed_grad, logs, key_acc, value_acc, slot * heads_slot + inner,
                    slot * 3 * third + inner * HD, third,
                    head_slope(slot, inner, slots, heads_slot, core), doc_cols, doc_rows,
                )
                return carry

            lax.fori_loop(0, heads_slot, one_head, 0)
            if slot == slots - 1:
                push((layer, "back"), qkv, row_other)
        elif name == "back":
            arrived((layer, "back"), row_other)
        elif kind == "rows":
            at = int(at)
            use_tile(layer, "rows", at)
            count = half_qkv // wide
            here = pl.ds(at % count * wide, wide)
            left = (qkv if at < count else row_other).at[own_rows, here]
            accumulate(left, w_b.at[at % 2], at == 0)
        elif name == "norm_one":
            loads[layer, "stream"].wait()
            sums_of = norm_back(source, acc, grad, low, vectors[gain : gain + 1, :])
            put_vector(gain, sums_of[0])
            put_vector(shift, sums_of[1])
            if layer > 0:
                put_vector(shift - shift_rows + 2, sums_of[2])
            else:
                copy = pltpu.make_async_copy(grad, input_grad, out_sems.at[n])
                copy.start()
                loads["input_grad"] = copy
                copy = pltpu.make_async_copy(low, input_low, out_sems.at[n + 1])
                copy.start()
                loads["input_low"] = copy

    def weight(t, s):
        slab = work.slab(t)
        out = sums[slab]
        if t == 8:
            for row, mask in enumerate(plans[t].masks):
                block = flip(d, mask)
                part = vector_sums[:, pl.ds(place(block, cols[t]), cols[t])]
                for m in range(mp_size):
                    first = pl.multiple_of(m * (bias_sums.shape[1] // mp_size) + block * cols[t], cols[t])
                    values = part + bias_sums[:, pl.ds(first, cols[t])]
                    rows = slice(row * wides[t], (row + 1) * wides[t])
                    out[rows, m * cols[t] : (m + 1) * cols[t]] = values.astype(bf16)
            work.advance(t, 1, None, 0)
            return
        layer = layers - 1 - t // 4
        if s == 0:
            if t >= 4:
                work.settle(t - 4)
                loads["out", t - 4].wait()
            arrived(("left", t), left_t.at[t % 2, :, other_rows])
        block = flip(z, s)
        left = left_t.at[t % 2]

        def multiply(right, first, step):
            def piece(at, carry):
                here = pl.multiple_of(at * step, step)
                there = pl.ds(pl.multiple_of(block * cols[t] + here, step), step)
                values = dot(left[...], right[:, pl.ds(pl.multiple_of(first + here, step), step)])
                out[:, there] = values.astype(bf16)
                return carry

            lax.fori_loop(0, cols[t] // step, piece, 0)

        if slab < 2:
            if slab == 0:
                loads[layer, "block", s].wait()
            else:
                arrived((layer, "grads", s), blocks.at[s % 2, other_rows, :])
            multiply(blocks.at[s % 2], 0, TILE)
            if slab == 0 and s < 2:
                fetch_block(layer, s + 2)
            elif slab == 0:
                give(block_credit.at[s - 2])
            elif s < 2:
                give(block_credit.at[s + 2])
        else:
            if slab == 2 and s == 0:
                loads[layer, "mixed"].wait()
                arrived((layer, "mixed"), mixed_other)
            ours = block // slots == core
            within = pl.multiple_of((block % slots) * cols[t], cols[t])
            near, far = ((mixed, mixed_other), (qkv, row_other))[slab - 2]
            pl.when(ours)(lambda: multiply(near, within, TILE))
            pl.when(jnp.logical_not(ours))(lambda: multiply(far, within, TILE))
        if s == mp_size - 1 and t < 6:
            give(left_credit.at[t % 2])
        work.advance(t, 1, block, s)

    def finish(t):
        final = work.part(t, 0, 1, z)
        copy = pltpu.make_async_copy(final, outs[t], out_sems.at[t])
        copy.start()
        loads["out", t] = copy
        step = 16

        def some_rows(at, carry):
            rows = pl.ds(pl.multiple_of(at * step, step), step)
            part = final[rows, :].astype(f32)
            part = part * part
            if t == 8:
                row = at * step + lax.broadcasted_iota(jnp.int32, part.shape, 0)
                part = jnp.where(row < vector_count, part * (1.0 / mp_size), part)
            total = carry
            for top in range(0, step, 8):
                for side in range(0, cols[t], HD):
                    total = total + part[top : top + 8, side : side + HD]
            return total

        tiles[0] += lax.fori_loop(0, wides[t] // step, some_rows, jnp.zeros((8, HD), f32))

    tiles[0] = jnp.zeros(tiles.shape[1:], f32)
    for step in order:
        if step[0] == "weight":
            weight(*step[1:])
        elif isinstance(step[1], str):
            compute(*step)
        else:
            work.step(*step, finish)

    pairs = [{DP: flip(d, bit)} for bit in [1] + upper]
    pairs += [{MP: flip(z, bit)} for bit in mp_bits]
    for at, to in enumerate(pairs):
        exchange = pltpu.make_async_remote_copy(
            src_ref=tiles.at[2 * at],
            dst_ref=tiles.at[2 * at + 1],
            send_sem=tile_sems.at[2 * at],
            recv_sem=tile_sems.at[2 * at + 1],
            device_id=to,
            device_id_type=MESH,
        )
        exchange.start()
        exchange.wait()
        tiles[2 * at + 2] = tiles[2 * at] + tiles[2 * at + 1]
    norm_ref[...] = tiles[2 * len(pairs)]

    for s in (2, 3):
        pushed((0, "grads", s))
    for key in ((0, "mixed"), (0, "share"), (0, "back"), ("left", 6), ("left", 7)):
        pushed(key)
    for t in range(n):
        work.settle(t)
        if t >= 4:
            loads["out", t].wait()
    loads["input_grad"].wait()
    loads["input_low"].wait()


def backward_chain(plans, layers):
    chain = []
    for done, layer in enumerate(reversed(range(layers))):
        turns = {"turn_down": 0, "turn_up": 1, "turn_proj": 2, "back": 3}
        t = None
        for name in BACKWARD_STEPS:
            if name.startswith("W"):
                chain.append(("weight", t, int(name[1:])))
                continue
            chain.append((layer, name))
            if name in turns:
                t = 4 * done + turns[name]
            if name == "norm_one" and layer == 0:
                chain.append(("weight", len(plans) - 1, 0))
    return chain


def backward_order(plans, layers, table):
    chain = backward_chain(plans, layers)
    if not table:
        out = []
        for at, step in enumerate(chain):
            out.append(step)
            if step[0] == "weight" and (step[1] == 8 or step[2] == 3):
                out += [(step[1], event) for event in plans[step[1]].events]
        return out
    steps = chain + [(t, event) for t, plan in enumerate(plans) for event in plan.events]
    return [steps[at] for at in table]


def backward_all(
    full, cotangent, vectors, docs, stored, plans, order, dp_size, mp_size, layers, vector_count,
    gain_rows, shift_rows,
):
    n = len(plans)
    _, total = number_rows(plans, mp_size)
    tokens, features = cotangent.shape
    length = docs.shape[0]
    units = full[2].shape[1]
    wides = [features // dp_size] * 8 + [vectors.shape[0]]
    cols = [
        full[4 * layer + kind].shape[1] // mp_size
        for layer in reversed(range(layers))
        for kind in (3, 2, 1, 0)
    ] + [max(HD, features // dp_size)]
    rounds = len(bits_of(dp_size)) + len(bits_of(mp_size))
    half_qkv = full[0].shape[1] // 2
    any_place = pl.BlockSpec(memory_space=pl.ANY)
    vmem = pl.BlockSpec(memory_space=pltpu.VMEM)
    out_shape = [jax.ShapeDtypeStruct((wide, each), bf16) for wide, each in zip(wides, cols)]
    out_shape += [
        jax.ShapeDtypeStruct((8, HD), f32),
        jax.ShapeDtypeStruct((tokens, features), f32),
        jax.ShapeDtypeStruct((tokens, features), bf16),
    ]
    slabs = (0, 1, 2, 3, 8)
    scratch = [
        pltpu.VMEM((plans[t].kept[0] * wides[t], mp_size * cols[t]), bf16) for t in slabs
    ]
    for t in slabs:
        plan = plans[t]
        for stage, dim in enumerate(plan.dims, 1):
            rows = plan.kept[stage] * wides[t]
            if dim == MP:
                shape = (mp_size + 1, rows, cols[t])
            elif not plan.full(stage):
                shape = (1, rows, cols[t])
            elif plan.merged:
                shape = (1, rows, mp_size * cols[t])
            else:
                shape = (mp_size, rows, cols[t])
            scratch.append(pltpu.VMEM(shape, bf16))
    wide = 512
    scratch += [
        pltpu.VMEM((2, length, cols[0]), bf16),
        pltpu.VMEM((2, features // 2, length), bf16),
        pltpu.VMEM((2, features // 2, tokens), bf16),
        pltpu.VMEM((tokens, features), f32),
        pltpu.VMEM((tokens, features), f32),
        pltpu.VMEM((tokens, features), bf16),
        pltpu.VMEM((2, tokens, wide), bf16),
        pltpu.VMEM((2, features, wide), bf16),
        pltpu.VMEM((2, features, wide), bf16),
        pltpu.VMEM((tokens, features), bf16),
        pltpu.VMEM((tokens, features), bf16),
        pltpu.VMEM((length, half_qkv), bf16),
        pltpu.VMEM((length, features // 2), bf16),
        pltpu.VMEM((length, features // 2), bf16),
        pltpu.VMEM((length, HD), f32),
        pltpu.VMEM((length, features // 2), bf16),
        pltpu.VMEM((tokens, features // 2), bf16),
        pltpu.VMEM((length, half_qkv), bf16),
        pltpu.VMEM((length, HD), f32),
        pltpu.VMEM((length, HD), f32),
        pltpu.VMEM((wides[8], features), f32),
        pltpu.VMEM((wides[8], units), f32),
        pltpu.VMEM((2 * rounds + 1, 8, HD), f32),
        pltpu.SemaphoreType.DMA((110,)),
        pltpu.SemaphoreType.DMA((2 * 11 * layers,)),
        pltpu.SemaphoreType.DMA((n + 2,)),
        pltpu.SemaphoreType.DMA((2 * rounds,)),
        pltpu.SemaphoreType.DMA((total,)),
        pltpu.SemaphoreType.DMA((total,)),
        pltpu.SemaphoreType.REGULAR((4, len(plans[0].dims) + 1, 2)),
        pltpu.SemaphoreType.REGULAR((mp_size,)),
        pltpu.SemaphoreType.REGULAR((2,)),
    ]
    operands = list(full[: 4 * layers]) + [cotangent, vectors]
    operands += [docs.reshape(-1, 1), docs.reshape(1, -1)]
    specs = [any_place] * (4 * layers + 1) + [vmem] * 3
    for each in stored:
        operands += each
        specs += [any_place] * SAVED
    out = pl.pallas_call(
        functools.partial(
            backward_kernel, plans, order, mp_size, layers, vector_count, gain_rows, shift_rows
        ),
        out_shape=out_shape,
        in_specs=specs,
        out_specs=[any_place] * n + [vmem, any_place, any_place],
        scratch_shapes=scratch,
        compiler_params=pltpu.CompilerParams(
            collective_id=1, has_side_effects=True, vmem_limit_bytes=63 * 2**20
        ),
    )(*operands)
    return list(out[:n]), out[n], out[n + 1], out[n + 2]


forward_table = (
    116, 1, 22, 23, 188, 0, 189, 95, 118, 117, 97, 191, 119, 24, 190, 25, 3, 121, 94, 193, 5, 192,
    194, 26, 27, 206, 2, 71, 99, 4, 195, 120, 29, 69, 11, 199, 123, 196, 96, 28, 30, 197, 122, 13,
    70, 128, 31, 127, 73, 6, 7, 8, 98, 33, 34, 9, 129, 44, 203, 72, 10, 32, 77, 202, 14, 45, 134,
    19, 125, 124, 207, 76, 18, 12, 100, 75, 204, 41, 205, 37, 126, 46, 35, 103, 74, 198, 79, 105,
    20, 200, 107, 201, 16, 208, 47, 136, 102, 36, 209, 106, 104, 42, 78, 17, 15, 210, 39, 48, 112,
    52, 38, 21, 211, 101, 51, 49, 82, 43, 83, 81, 212, 80, 135, 213, 50, 57, 54, 113, 214, 165,
    53, 132, 85, 164, 163, 131, 215, 108, 65, 55, 40, 56, 216, 138, 133, 217, 87, 60, 58, 111, 84,
    130, 91, 66, 218, 140, 61, 59, 114, 167, 90, 219, 86, 139, 171, 110, 166, 62, 88, 137, 92, 67,
    170, 146, 63, 64, 145, 89, 109, 220, 68, 221, 222, 223, 141, 142, 224, 115, 169, 225, 226, 93,
    168, 227, 228, 173, 229, 230, 172, 231, 232, 233, 143, 147, 144, 234, 148, 235, 152, 176, 236,
    237, 153, 174, 175, 180, 151, 181, 238, 177, 149, 150, 239, 157, 154, 240, 179, 182, 158, 155,
    156, 178, 184, 183, 159, 241, 242, 161, 160, 185, 243, 162, 244, 245, 246, 247, 187, 248, 249,
    250, 186, 251, 252, 253, 254, 255,
)
backward_table = (
    0, 1, 2, 3, 4, 5, 6, 7, 8, 9, 10, 11, 12, 13, 14, 15, 16, 17, 87, 18, 19, 20, 21, 85, 96, 22,
    23, 88, 24, 25, 26, 27, 28, 29, 86, 90, 108, 30, 89, 109, 31, 32, 99, 110, 107, 33, 34, 35,
    111, 98, 92, 91, 36, 97, 37, 113, 38, 100, 114, 101, 122, 93, 121, 112, 103, 102, 125, 39,
    123, 40, 126, 94, 41, 124, 127, 42, 104, 105, 95, 43, 115, 44, 45, 46, 47, 116, 106, 48, 49,
    50, 51, 52, 128, 53, 54, 55, 136, 56, 117, 129, 57, 118, 58, 130, 59, 60, 61, 62, 131, 63,
    120, 132, 119, 137, 64, 65, 66, 67, 68, 69, 138, 70, 71, 135, 146, 72, 133, 73, 74, 134, 140,
    149, 139, 157, 75, 76, 77, 148, 147, 151, 141, 171, 150, 142, 78, 79, 159, 172, 80, 175, 158,
    81, 82, 153, 83, 173, 160, 84, 161, 152, 185, 177, 174, 163, 144, 162, 164, 186, 178, 165,
    154, 187, 143, 176, 166, 167, 180, 189, 179, 168, 155, 188, 181, 182, 170, 190, 145, 191, 169,
    156, 183, 192, 184, 193,
)


def program(dp_size, mp_size, args):
    (
        inputs, documents, cotangent,
        qkv_weight, qkv_moment, qkv_square,
        proj_weight, proj_moment, proj_square,
        upper_weight, upper_moment, upper_square,
        lower_weight, lower_moment, lower_square,
        hidden_bias, bias_moment, bias_square,
        norm_gains, gains_moment, gains_square,
        shift_params, shifts_moment, shifts_square,
    ) = args
    layers = qkv_weight.shape[0]
    tokens, features = inputs.shape
    length = documents.shape[1]
    pieces = length // tokens
    slots = mp_size // pieces
    wide = features // dp_size
    z_cols = qkv_weight.shape[3]
    heads_slot = z_cols // HD
    me_dp = lax.axis_index(DP)
    me_mp = lax.axis_index(MP)
    core = me_dp % 2

    def swap(values):
        return lax.ppermute(values, DP, [(at, at ^ 1) for at in range(dp_size)])

    def by_core(own, other, axis):
        first = jnp.where(core == 0, own, other)
        second = jnp.where(core == 0, other, own)
        return jnp.concatenate([first, second], axis=axis)

    paired = pieces == 2 and dp_size % 2 == 0 and mp_size % 2 == 0
    if paired:
        moved = core != me_mp % 2
        pairs = []
        for d in range(dp_size):
            for m in range(mp_size):
                if d % 2 != m % 2:
                    pairs.append((d * mp_size + m, (d ^ 1) * mp_size + (m ^ 1)))

        def trade(values):
            other = lax.ppermute(values, (DP, MP), pairs)
            return jnp.where(moved, other, values)

        doc_rows = jnp.where(moved, swap(documents), documents)
        docs = lax.dynamic_index_in_dim(doc_rows, me_mp // 2, 0, False)

        def share_heads(values):
            half = values.shape[1] // 2
            own = lax.dynamic_slice_in_dim(values, core * half, half, 1)
            sent = lax.dynamic_slice_in_dim(values, (1 - core) * half, half, 1)
            return by_core(own, swap(sent), 0)

        def return_heads(values):
            own = lax.dynamic_slice_in_dim(values, core * tokens, tokens, 0)
            sent = lax.dynamic_slice_in_dim(values, (1 - core) * tokens, tokens, 0)
            return by_core(own, swap(sent), 1)

        first_slot = core * slots
    else:
        groups = [list(range(g * pieces, (g + 1) * pieces)) for g in range(mp_size // pieces)]

        def trade(values):
            return values

        docs = lax.dynamic_index_in_dim(documents, me_mp // pieces, 0, False)

        def share_heads(values):
            return lax.all_to_all(values, MP, 1, 0, axis_index_groups=groups, tiled=True)

        def return_heads(values):
            return lax.all_to_all(values, MP, 0, 1, axis_index_groups=groups, tiled=True)

        moved = False
        first_slot = (me_mp % pieces) * slots
    slope_table = jnp.asarray(0.5 ** (np.arange(H) + 1.0), dtype=f32)
    slopes = lax.dynamic_slice_in_dim(
        slope_table, first_slot * heads_slot, slots * heads_slot
    )

    bits = bits_of(dp_size)[1:]
    line_first = [(MP, *bits), (MP, *bits[::-1])]
    line_second = [(bits[0], MP, *bits[1:]), (bits[-1], MP, *bits[:-1][::-1])]

    gain_rows = norm_gains.shape[1]
    shift_rows = shift_params.shape[1]
    vector_count = layers * (gain_rows + shift_rows)
    bias_wide = hidden_bias.shape[1]
    lanes = max(wide, HD)
    small_rows = -(-(vector_count + layers) // 16) * 16

    def padded(values):
        return jnp.pad(values, [(0, 0)] * (values.ndim - 1) + [(0, lanes - values.shape[-1])])

    spreads = []
    for layer in range(layers):
        spreads += line_first[:: 1 if layer % 2 == 0 else -1] + line_second
    spreads.append(line_first[0])
    qkv_by_part = qkv_weight.transpose(0, 2, 1, 3)
    if paired and wide == lanes and bias_wide == lanes:
        shards = prepare_all(
            [
                qkv_by_part, proj_weight, upper_weight, lower_weight, norm_gains, shift_params,
                hidden_bias,
            ],
            small_rows,
        )
    else:
        small = jnp.concatenate(
            [
                padded(norm_gains.reshape(-1, wide)),
                padded(shift_params.reshape(-1, wide)),
                padded(hidden_bias),
                jnp.zeros((small_rows - vector_count - layers, lanes), f32),
            ],
            axis=0,
        ).astype(bf16)
        shards = []
        for layer in range(layers):
            shards += [
                qkv_weight[layer].astype(bf16).reshape(wide, 3 * z_cols),
                proj_weight[layer].astype(bf16).T,
                upper_weight[layer].astype(bf16),
                lower_weight[layer].astype(bf16).T,
            ]
        shards.append(small)
    spreads = [Spread(dims, mp_size) for dims in spreads]
    tabled = dp_size == 8 and mp_size == 4 and layers == 2
    if paired:
        spread_order = forward_order(spreads, layers, forward_table if tabled else ())
        full, stored, stream, stream_low, vectors = forward_all(
            shards, inputs, docs, spreads, spread_order, dp_size, mp_size, layers,
            vector_count, gain_rows, shift_rows,
        )
    else:
        spread_order = step_order(spreads, (), lambda t, stage: t // 2 + stage)
        full = spread_all(shards, spreads, spread_order, dp_size, mp_size)
    cotangent = trade(cotangent)
    if not paired:
        small_all = full[-1].reshape(dp_size, small_rows, mp_size, lanes).astype(f32)
        vectors = small_all[:, :vector_count, 0, :wide].transpose(1, 0, 2)
        vectors = vectors.reshape(vector_count, features)
        gains = vectors[: layers * gain_rows].reshape(layers, gain_rows, features)
        shifts = vectors[layers * gain_rows :].reshape(layers, shift_rows, features)
        biases = small_all[:, vector_count : vector_count + layers, :, :bias_wide]
        biases = biases.transpose(1, 2, 0, 3).reshape(layers, -1)
        stream = inputs.astype(f32)
        stored = []
        for layer in range(layers):
            qkv_w, proj_w, upper_w, lower_w = full[4 * layer : 4 * layer + 4]
            normed = layer_norm(stream, gains[layer, 0], shifts[layer, 0]).astype(bf16)
            qkv = share_heads(dot(normed, qkv_w).astype(bf16))
            mixed = attend(slopes, docs, qkv, slots)
            attended = return_heads(mixed)
            middle = stream + dot_cols(attended, proj_w)
            normed_two = layer_norm(middle, gains[layer, 1], shifts[layer, 1]).astype(bf16)
            hidden = dot(normed_two, upper_w) + biases[layer]
            active = gelu_tanh(hidden).astype(bf16)
            stored.append(
                (stream, middle, normed, qkv, mixed, attended, normed_two, hidden, active)
            )
            stream = middle + dot_cols(active, lower_w) + shifts[layer, 2]
    output_stream = stream
    if paired:
        stream_other = lax.ppermute(stream_low, (DP, MP), pairs)

    ways = []
    for layer in reversed(range(layers)):
        ways += fold_dims(line_first, line_second, layer)
    ways.append(line_first[0][::-1])
    if paired:
        ways[-1] = (1,) + ways[-1]
        folds = [Rows(dims, mp_size, at == 8) for at, dims in enumerate(ways)]
        fold_order = backward_order(folds, layers, backward_table if tabled else ())
        owned, norm_tile, input_grad, grad_low = backward_all(
            full, cotangent, vectors, docs, stored, folds, fold_order, dp_size, mp_size, layers,
            vector_count, gain_rows, shift_rows,
        )
        grad_other = lax.ppermute(grad_low, (DP, MP), pairs)
    else:
        grad_stream = cotangent.astype(f32)
        weight_grads = [None] * layers
        vector_grads = [None] * layers
        bias_grads = [None] * layers
        no_shift = jnp.zeros((features,), f32)
        for layer in reversed(range(layers)):
            qkv_w, proj_w, upper_w, lower_w = full[4 * layer : 4 * layer + 4]
            stream_in, middle, normed, qkv, mixed, attended, normed_two, hidden, active = stored[layer]
            out_shift_grad = jnp.sum(grad_stream, axis=0)
            grad_low = grad_stream.astype(bf16)
            active_grad = dot(grad_low, lower_w)
            _, pull_gelu = jax.vjp(gelu_tanh, hidden.astype(f32))
            hidden_grad = pull_gelu(active_grad)[0].astype(bf16)
            lower_grad = dot_rows(grad_low, active).astype(bf16)
            upper_grad = dot_rows(normed_two, hidden_grad).astype(bf16)
            bias_grads[layer] = jnp.sum(hidden_grad, axis=0, dtype=f32)
            normed_two_grad = dot_cols(hidden_grad, upper_w)
            _, pull_two = jax.vjp(layer_norm, middle, gains[layer, 1], no_shift)
            middle_part, gain_two, shift_two = pull_two(normed_two_grad)
            middle_grad = grad_stream + middle_part
            middle_low = middle_grad.astype(bf16)
            mixed_grad = share_heads(dot(middle_low, proj_w).astype(bf16))
            proj_grad = dot_rows(middle_low, attended).astype(bf16)
            qkv_grad = return_heads(attend_back(slopes, docs, qkv, mixed, mixed_grad, slots))
            normed_grad = dot_cols(qkv_grad, qkv_w)
            qkv_weight_grad = dot_rows(normed, qkv_grad).astype(bf16)
            _, pull_one = jax.vjp(layer_norm, stream_in, gains[layer, 0], no_shift)
            stream_part, gain_one, shift_one = pull_one(normed_grad)
            grad_stream = middle_grad + stream_part
            weight_grads[layer] = (lower_grad, upper_grad, proj_grad, qkv_weight_grad)
            vector_grads[layer] = (
                jnp.stack([gain_one, gain_two]),
                jnp.stack([shift_one, shift_two, out_shift_grad]),
            )
        input_grad = grad_stream

        vector_sums = jnp.concatenate(
            [jnp.concatenate([vector_grads[at][kind] for at in range(layers)]) for kind in (0, 1)]
        )
        vector_sums = padded(vector_sums.reshape(vector_count, dp_size, wide)).transpose(1, 0, 2)
        vector_sums = jnp.broadcast_to(
            vector_sums[:, :, None], (dp_size, vector_count, mp_size, lanes)
        )
        bias_sums = padded(jnp.stack(bias_grads).reshape(layers, mp_size, dp_size, bias_wide))
        bias_sums = bias_sums.transpose(2, 0, 1, 3)
        rest = jnp.zeros((dp_size, small_rows - vector_count - layers, mp_size, lanes), f32)
        small_grad = jnp.concatenate([vector_sums, bias_sums, rest], axis=1)
        small_grad = small_grad.reshape(dp_size * small_rows, mp_size * lanes).astype(bf16)

        local = []
        for layer in reversed(range(layers)):
            local += weight_grads[layer]
        local.append(small_grad)
        folds = [Fold(dims, mp_size) for dims in ways]
        fold_order = step_order(folds, (), lambda t, stage: t // 2 + stage)
        owned, norm_tile = fold_all(local, folds, fold_order, dp_size, mp_size, vector_count)
    small_owned = owned.pop().astype(f32)
    vector_owned = small_owned[:vector_count, :wide]
    bias_owned = small_owned[vector_count : vector_count + layers, :bias_wide]
    grad_norm = jnp.sqrt(jnp.sum(norm_tile))
    factor = jnp.minimum(1.0, clip_bound / grad_norm)

    states = [qkv_by_part, qkv_moment.transpose(0, 2, 1, 3), qkv_square.transpose(0, 2, 1, 3)]
    states += [
        proj_weight, proj_moment, proj_square, upper_weight, upper_moment, upper_square,
        lower_weight, lower_moment, lower_square,
    ]
    ordered = [owned[4 * layer + kind] for kind in (3, 2, 1, 0) for layer in range(layers)]
    streams = [output_stream, stream_other, input_grad, grad_other] if paired else []
    matrices = list(adam_all(factor, moved, ordered, states, streams))
    if paired:
        output_stream, input_grad = matrices[12:]
        matrices = matrices[:12]
    matrices[:3] = [each.transpose(0, 2, 1, 3) for each in matrices[:3]]
    results = [output_stream, input_grad] + matrices
    rest = (
        (hidden_bias, bias_moment, bias_square, bias_owned),
        (
            norm_gains, gains_moment, gains_square,
            vector_owned[: layers * gain_rows].reshape(layers, gain_rows, wide),
        ),
        (
            shift_params, shifts_moment, shifts_square,
            vector_owned[layers * gain_rows :].reshape(layers, shift_rows, wide),
        ),
    )
    for at, group in enumerate(rest, 4):
        results.extend(adam_update(*group, factor, group_rates[at], group_decays[at]))
    results.append(grad_norm)
    return tuple(results)


def fold_dims(line_first, line_second, layer):
    first = [dims[::-1] for dims in line_first]
    second = [dims[::-1] for dims in line_second]
    return second + (first if layer % 2 else first[::-1])


def solution(mesh):
    dp_size = mesh.shape[DP]
    mp_size = mesh.shape[MP]
    rows = P((DP, MP), None)
    split_rows = P(None, DP, None, MP)
    split_upper = P(None, DP, MP)
    split_lower = P(None, MP, DP)
    split_bias = P(None, (MP, DP))
    split_vector = P(None, None, DP)
    groups = (
        split_rows, split_lower, split_upper, split_lower, split_bias, split_vector, split_vector
    )
    placed = tuple(spec for spec in groups for _ in range(3))

    def shards(*args):
        return program(dp_size, mp_size, args)

    return jax.shard_map(
        shards,
        mesh=mesh,
        in_specs=(rows, P(DP, None), rows) + placed,
        out_specs=(rows, rows) + placed + (P(),),
        check_vma=False,
    )
```

```python
import functools
import math

import jax
import jax.numpy as jnp
import numpy as np
from jax import lax
from jax.experimental import pallas as pl
from jax.experimental.pallas import tpu as pltpu
from jax.sharding import PartitionSpec as P

DP = "dp"
MP = "mp"
H = 8
HD = 128
STEP = 5
MAX_DOC = 512

norm_eps = 1e-05
clip_bound = 1.0
beta_first = 0.9
beta_second = 0.95
adam_eps = 1e-08
masked_score = -1e30
group_rates = (0.03, 0.12, 0.03, 0.015, 0.3, 0.7, 0.3)
group_decays = (0.1, 0.1, 0.1, 0.1, 0.0, 0.0, 0.0)
contract_rows = (((0,), (0,)), ((), ()))
contract_cols = (((1,), (1,)), ((), ()))
f32 = jnp.float32
bf16 = jnp.bfloat16
score_scale = 1.0 / math.sqrt(HD)
MESH = pl.DeviceIdType.MESH


def adam_update(master, moment, square, gradient, factor, step_rate, decay_rate):
    clipped = gradient * factor
    moment_new = beta_first * moment + (1.0 - beta_first) * clipped
    square_new = beta_second * square + (1.0 - beta_second) * clipped * clipped
    first_hat = moment_new / (1.0 - beta_first**STEP)
    second_hat = square_new / (1.0 - beta_second**STEP)
    master_new = master - step_rate * (
        first_hat / (jnp.sqrt(second_hat) + adam_eps) + decay_rate * master
    )
    return (master_new, moment_new, square_new)


def gelu_tanh(values):
    return jax.nn.gelu(values, approximate=True)


def layer_norm(values, scale_vec, shift_vec):
    center = values - jnp.mean(values, axis=-1, keepdims=True)
    spread = jnp.mean(center * center, axis=-1, keepdims=True)
    return center * lax.rsqrt(spread + norm_eps) * scale_vec + shift_vec


def dot(left, right):
    return jnp.dot(left, right, preferred_element_type=f32)


def dot_rows(left, right):
    return lax.dot_general(left, right, contract_rows, preferred_element_type=f32)


def dot_cols(left, right):
    return lax.dot_general(left, right, contract_cols, preferred_element_type=f32)


def masked_scores(slope, doc_col, doc_row, query, key, first_row, first_col):
    scores = dot_cols(query, key) * score_scale
    rows = first_row + lax.broadcasted_iota(jnp.int32, scores.shape, 0)
    cols = first_col + lax.broadcasted_iota(jnp.int32, scores.shape, 1)
    distance = rows - cols
    allowed = (distance >= 0) & (doc_col == doc_row)
    return jnp.where(allowed, scores - slope * distance.astype(f32), masked_score)


def key_range(first_row, block):
    low = max(0, first_row - (MAX_DOC - 1)) // block * block
    return low, first_row + block


def attend_kernel(heads, block, slope_ref, dcol_ref, drow_ref, qkv_ref, o_ref):
    length = o_ref.shape[0]
    for head in range(heads):
        slope = slope_ref[pl.program_id(0) * heads + head]
        at = head * HD
        kat = (heads + head) * HD
        vat = (2 * heads + head) * HD
        for first_row in range(0, length, block):
            low, high = key_range(first_row, block)
            scores = masked_scores(
                slope,
                dcol_ref[first_row : first_row + block, :],
                drow_ref[:, low:high],
                qkv_ref[first_row : first_row + block, at : at + HD],
                qkv_ref[low:high, kat : kat + HD],
                first_row,
                low,
            )
            shifted = jnp.exp(scores - jnp.max(scores, axis=-1, keepdims=True))
            total = jnp.sum(shifted, axis=-1, keepdims=True)
            prob_low = (shifted * (1.0 / total)).astype(bf16)
            o_ref[first_row : first_row + block, at : at + HD] = dot(
                prob_low, qkv_ref[low:high, vat : vat + HD]
            ).astype(bf16)


def attend_back_kernel(
    heads, block, slope_ref, dcol_ref, drow_ref, qkv_ref, o_ref, do_ref,
    grad_ref, key_acc, value_acc,
):
    length = o_ref.shape[0]
    for head in range(heads):
        slope = slope_ref[pl.program_id(0) * heads + head]
        at = head * HD
        kat = (heads + head) * HD
        vat = (2 * heads + head) * HD
        key_acc[...] = jnp.zeros_like(key_acc)
        value_acc[...] = jnp.zeros_like(value_acc)
        for first_row in range(0, length, block):
            low, high = key_range(first_row, block)
            rows = slice(first_row, first_row + block)
            query = qkv_ref[rows, at : at + HD]
            key = qkv_ref[low:high, kat : kat + HD]
            scores = masked_scores(
                slope, dcol_ref[rows, :], drow_ref[:, low:high], query, key, first_row, low
            )
            shifted = jnp.exp(scores - jnp.max(scores, axis=-1, keepdims=True))
            total = jnp.sum(shifted, axis=-1, keepdims=True)
            probs = shifted * (1.0 / total)
            out_grad = do_ref[rows, at : at + HD]
            value_acc[low:high, :] += dot_rows(probs.astype(bf16), out_grad)
            prob_grad = dot_cols(out_grad, qkv_ref[low:high, vat : vat + HD])
            inner = jnp.sum(
                out_grad.astype(f32) * o_ref[rows, at : at + HD].astype(f32),
                axis=-1,
                keepdims=True,
            )
            score_grad = (probs * (prob_grad - inner)).astype(bf16)
            grad_ref[rows, at : at + HD] = (dot(score_grad, key) * score_scale).astype(bf16)
            key_acc[low:high, :] += dot_rows(score_grad, query)
        grad_ref[:, kat : kat + HD] = (key_acc[...] * score_scale).astype(bf16)
        grad_ref[:, vat : vat + HD] = value_acc[...].astype(bf16)


def attend_specs(length, width):
    def columns(each):
        return pl.BlockSpec((length, each), lambda s: (0, s))

    fixed = [
        pl.BlockSpec(memory_space=pltpu.SMEM),
        pl.BlockSpec((length, 1), lambda s: (0, 0)),
        pl.BlockSpec((1, length), lambda s: (0, 0)),
    ]
    return fixed, columns(3 * width), columns(width)


def attend(slopes, docs, qkv, slots):
    length = qkv.shape[0]
    width = qkv.shape[1] // (3 * slots)
    fixed, wide, narrow = attend_specs(length, width)
    pairs = slots * width // HD * length * length
    return pl.pallas_call(
        functools.partial(attend_kernel, width // HD, min(256, length)),
        grid=(slots,),
        in_specs=fixed + [wide],
        out_specs=narrow,
        out_shape=jax.ShapeDtypeStruct((length, slots * width), bf16),
        compiler_params=pltpu.CompilerParams(vmem_limit_bytes=32 * 2**20),
        cost_estimate=pl.CostEstimate(
            flops=4 * pairs * HD, bytes_accessed=3 * qkv.size, transcendentals=pairs
        ),
    )(slopes, docs.reshape(-1, 1), docs.reshape(1, -1), qkv)


def attend_back(slopes, docs, qkv, o, do, slots):
    length = qkv.shape[0]
    width = qkv.shape[1] // (3 * slots)
    fixed, wide, narrow = attend_specs(length, width)
    pairs = slots * width // HD * length * length
    return pl.pallas_call(
        functools.partial(attend_back_kernel, width // HD, min(256, length)),
        grid=(slots,),
        in_specs=fixed + [wide, narrow, narrow],
        out_specs=wide,
        out_shape=jax.ShapeDtypeStruct(qkv.shape, bf16),
        scratch_shapes=[pltpu.VMEM((length, HD), f32), pltpu.VMEM((length, HD), f32)],
        compiler_params=pltpu.CompilerParams(vmem_limit_bytes=32 * 2**20),
        cost_estimate=pl.CostEstimate(
            flops=10 * pairs * HD, bytes_accessed=6 * qkv.size, transcendentals=pairs
        ),
    )(slopes, docs.reshape(-1, 1), docs.reshape(1, -1), qkv, o, do)


def bits_of(size):
    return [1 << at for at in range(size.bit_length() - 1)]


def flip(value, mask):
    bit = 1
    while bit <= mask:
        if mask & bit:
            value = value + bit * (1 - 2 * ((value // bit) % 2))
        bit *= 2
    return value


def place(at, size):
    if isinstance(at, int):
        return at * size
    return pl.multiple_of(at * size, size)


class Spread:
    def __init__(self, dims, mp_size):
        self.dims = tuple(dims)
        self.events = []
        masks, spread = [0], False
        for stage, dim in enumerate(self.dims):
            for mask in masks:
                if dim == MP:
                    for hops in range(1, mp_size):
                        self.events += [(stage, mask, way, hops) for way in (1, -1)]
                else:
                    places = range(mp_size) if spread else (0,)
                    self.events += [(stage, mask | dim, 0, at) for at in places]
            if dim == MP:
                spread = True
            else:
                masks = masks + [mask | dim for mask in masks]
        self.events += [(len(self.dims), mask | 1, 0, 0) for mask in masks]

    def full(self, stage):
        return MP in self.dims[:stage]


class Fold:
    def __init__(self, dims, mp_size, halves=1):
        self.dims = tuple(dims)
        masks = [0]
        for dim in self.dims:
            if dim != MP:
                masks = masks + [mask | dim for mask in masks]
        self.masks = masks
        self.kept = {}
        sent_first = sorted(masks, key=self.leaves)
        self.events = [(0, mask, 0, half) for mask in sent_first for half in range(halves)]
        rows = list(masks)
        for stage, dim in enumerate(self.dims, 1):
            if dim != MP:
                rows = [mask for mask in rows if not mask & dim]
            self.kept[stage] = list(rows)
            if dim == MP:
                for hops in reversed(range(mp_size - 1)):
                    for mask in rows:
                        self.events += [(stage, mask, way, hops) for way in (1, -1)]
            else:
                places = reversed(range(mp_size)) if self.full(stage) else (0,)
                places = list(places)
                for mask in rows:
                    self.events += [(stage, mask, 0, at) for at in places]

    def leaves(self, mask):
        for at, dim in enumerate(self.dims):
            if dim != MP and mask & dim:
                return at
        return len(self.dims)

    def full(self, stage):
        return MP not in self.dims[: stage - 1]


def number(plans, mp_size, single):
    index, total = {}, 0
    for t, plan in enumerate(plans):
        for event in plan.events:
            stage, mask, way, at = event
            if way or single(plan, stage):
                index[(t,) + event] = total
                total += 1
            elif (t, stage, mask) not in index:
                index[t, stage, mask] = total
                total += mp_size
    return index, total


def spread_single(plan, stage):
    return stage == len(plan.dims)


def fold_single(plan, stage):
    return stage == 0


def merge_small(order, plans):
    t = len(plans) - 1
    small = [(t, event) for event in plans[t].events]
    out, used = [], 0
    for at, step in enumerate(order):
        out.append(step)
        while used < len(small) and (used + 1) * len(order) <= (at + 1) * (len(small) + 1):
            out.append(small[used])
            used += 1
    return out + small[used:]


def step_order(plans, table, by_stage):
    steps = [(t, event) for t, plan in enumerate(plans[:-1]) for event in plan.events]
    if len(table) == len(steps):
        return merge_small([steps[at] for at in table], plans)
    ranked = sorted(range(len(steps)), key=lambda at: (by_stage(steps[at][0], steps[at][1][0]), at))
    return merge_small([steps[at] for at in ranked], plans)


def forward_order(plans, layers, table):
    steps = [(t, event) for t, plan in enumerate(plans) for event in plan.events]
    compute = [(layer, name) for layer in range(layers) for name in FORWARD_STEPS]
    if len(table) == len(steps) + len(compute):
        steps += compute
        return [steps[at] for at in table]
    return steps + compute


def greet(z, d, upper, mp_size, mp_bits=(), across=None, moved=None):
    barrier = pltpu.get_barrier_semaphore()
    for bit in mp_bits:
        pl.semaphore_signal(
            barrier, inc=1, device_id={MP: flip(z, bit)}, device_id_type=MESH
        )
    for bit in [1] + upper:
        pl.semaphore_signal(
            barrier, inc=1, device_id={DP: flip(d, bit)}, device_id_type=MESH
        )
    also = 0
    if across is not None:

        @pl.when(moved)
        def _():
            pl.semaphore_signal(barrier, inc=1, device_id=across, device_id_type=MESH)

        also = jnp.where(moved, 1, 0)
    for way in (1, -1):

        @pl.when((z + way >= 0) & (z + way < mp_size))
        def _(way=way):
            pl.semaphore_signal(
                barrier, inc=1, device_id={MP: z + way}, device_id_type=MESH
            )

    around = jnp.where(z > 0, 1, 0) + jnp.where(z < mp_size - 1, 1, 0)
    pl.semaphore_wait(barrier, 1 + len(upper) + len(mp_bits) + around + also)


def greet_all(z, d, dp_size, mp_size, across, moved):
    barrier = pltpu.get_barrier_semaphore()
    for mask in range(1, dp_size):
        pl.semaphore_signal(
            barrier, inc=1, device_id={DP: flip(d, mask)}, device_id_type=MESH
        )
    for mask in range(1, mp_size):
        pl.semaphore_signal(
            barrier, inc=1, device_id={MP: flip(z, mask)}, device_id_type=MESH
        )

    @pl.when(moved)
    def _():
        pl.semaphore_signal(barrier, inc=1, device_id=across, device_id_type=MESH)

    pl.semaphore_wait(barrier, dp_size + mp_size - 2 + jnp.where(moved, 1, 0))


class SpreadWork:
    def __init__(self, plans, order, mp_size, shards, outs, send_sems, recv_sems, own_sems):
        self.plans, self.mp_size = plans, mp_size
        self.order = [step for step in order if not isinstance(step[1], str)]
        self.shards, self.outs = shards, outs
        self.sems = send_sems, recv_sems
        self.own_sems = own_sems
        self.z = lax.axis_index(MP)
        self.d = lax.axis_index(DP)
        self.upper = [dim for dim in plans[0].dims if dim != MP]
        self.index, _ = number(plans, mp_size, spread_single)
        self.owns = []
        self.left = {}
        for t, event in self.order:
            if event[0] < len(plans[t].dims):
                self.left[t, event[1]] = self.left.get((t, event[1]), 0) + 1

    def inside(self, at):
        return (at >= 0) & (at < self.mp_size)

    def region(self, t, mask, block):
        wide, cols = self.shards[t].shape
        rows = pl.ds(place(flip(self.d, mask), wide), wide)
        if block is None:
            return self.outs[t].at[rows, :]
        return self.outs[t].at[rows, pl.ds(place(block, cols), cols)]

    def remote(self, t, event, block, src, dst, to):
        stage, mask, way, at = event
        if way or stage == len(self.plans[t].dims):
            sem = self.index[(t,) + event]
        else:
            sem = self.index[t, stage, mask] + block
        return pltpu.make_async_remote_copy(
            src_ref=src,
            dst_ref=dst,
            send_sem=self.sems[0].at[sem],
            recv_sem=self.sems[1].at[sem],
            device_id=to,
            device_id_type=MESH,
        )

    def sending(self, t, event, block, to, own=False):
        stage, mask, way, at = event
        dims = self.plans[t].dims
        bit = 0 if way else 1 if stage == len(dims) else dims[stage]
        dst = self.region(t, mask ^ bit, block)
        return self.remote(t, event, block, self.shards[t] if own else dst, dst, to)

    def arrival(self, t, event, block):
        dst = self.region(t, event[1], block)
        return self.remote(t, event, block, dst, dst, {DP: self.d, MP: self.z})

    def on_line(self, t, stage, mask, block, way, hops, own):
        @pl.when(self.inside(self.z + way))
        def _():
            to = {MP: self.z + way}
            self.sending(t, (stage, mask, way, hops), block, to, own).start()

    def onward(self, t, stage, mask, block, own=False):
        dims = self.plans[t].dims
        for later in range(stage, len(dims)):
            if dims[later] == MP:
                for way in (1, -1):
                    self.on_line(t, later, mask, block, way, 1, own)
            else:
                to = {DP: flip(self.d, dims[later])}
                self.sending(t, (later, mask | dims[later], 0, None), block, to, own).start()

    def place_of(self, t, event):
        return flip(self.z, event[3]) if self.plans[t].full(event[0]) else self.z

    def begin(self):
        for t in range(len(self.plans)):
            self.onward(t, 0, 0, self.z, True)
            own = pltpu.make_async_copy(
                self.shards[t], self.region(t, 0, self.z), self.own_sems.at[t]
            )
            own.start()
            self.owns.append(own)

    def step(self, t, event):
        stage, mask, way, at = event
        last = len(self.plans[t].dims)
        if stage == last:
            self.arrival(t, event, None).wait_recv()
            return
        if way:
            block = self.z - way * at

            @pl.when(self.inside(block))
            def _():
                self.arrival(t, event, block).wait_recv()
                if at + 1 < self.mp_size:
                    self.on_line(t, stage, mask, block, way, at + 1, False)
                self.onward(t, stage + 1, mask, block)

        else:
            block = self.place_of(t, event)
            self.arrival(t, event, block).wait_recv()
            self.onward(t, stage + 1, mask, block)
        self.left[t, mask] -= 1
        if self.left[t, mask] == 0:
            if mask == 0:
                self.owns[t].wait()
            to = {DP: flip(self.d, 1)}
            self.sending(t, (last, mask | 1, 0, 0), None, to).start()

    def finish(self):
        for t, event in self.order:
            stage, mask, way, at = event
            if stage == len(self.plans[t].dims):
                self.sending(t, event, None, {DP: flip(self.d, 1)}).wait_send()
            elif way:

                @pl.when(self.inside(self.z - way * (at - 1)) & self.inside(self.z + way))
                def _():
                    to = {MP: self.z + way}
                    self.sending(t, event, self.z - way * (at - 1), to).wait_send()

            else:
                to = {DP: flip(self.d, self.plans[t].dims[stage])}
                self.sending(t, event, self.place_of(t, event), to).wait_send()


def spread_kernel(plans, order, mp_size, *refs):
    n = len(plans)
    work = SpreadWork(plans, order, mp_size, refs[:n], refs[n : 2 * n], *refs[2 * n :])
    greet(work.z, work.d, work.upper, mp_size)
    work.begin()
    for t, event in order:
        work.step(t, event)
    work.finish()


def spread_all(shards, plans, order, dp_size, mp_size):
    _, total = number(plans, mp_size, spread_single)
    return pl.pallas_call(
        functools.partial(spread_kernel, plans, order, mp_size),
        out_shape=[
            jax.ShapeDtypeStruct((s.shape[0] * dp_size, s.shape[1] * mp_size), s.dtype)
            for s in shards
        ],
        in_specs=[pl.BlockSpec(memory_space=pl.ANY)] * len(shards),
        out_specs=[pl.BlockSpec(memory_space=pl.ANY)] * len(shards),
        scratch_shapes=[
            pltpu.SemaphoreType.DMA((total,)),
            pltpu.SemaphoreType.DMA((total,)),
            pltpu.SemaphoreType.DMA((len(shards),)),
        ],
        compiler_params=pltpu.CompilerParams(collective_id=0, has_side_effects=True),
    )(*shards)


def fold_kernel(plans, order, mp_size, vector_count, *refs):
    n = len(plans)
    grads, outs = refs[:n], refs[n : 2 * n]
    norm_ref = refs[2 * n]
    landed, sums = refs[2 * n + 1 : 3 * n + 1], refs[3 * n + 1 : 4 * n + 1]
    at = 4 * n + 1
    recv = {}
    for t, plan in enumerate(plans):
        for stage in range(1, len(plan.dims) + 1):
            recv[t, stage] = refs[at]
            at += 1
    staging, tiles, load_sems, own_sems, tile_sems, send_sems, recv_sems = refs[at:]
    z = lax.axis_index(MP)
    d = lax.axis_index(DP)
    upper = [dim for dim in plans[0].dims if dim != MP]
    index, _ = number(plans, mp_size, fold_single)
    wides = [out.shape[0] for out in outs]
    cols = [out.shape[1] for out in outs]

    def inside(at):
        return (at >= 0) & (at < mp_size)

    def rows_of(t, mask):
        return pl.ds(plans[t].masks.index(mask) * wides[t], wides[t])

    def sum_at(t, mask, block):
        return sums[t].at[rows_of(t, mask), pl.ds(place(block, cols[t]), cols[t])]

    def landing(t, event, block):
        stage, mask, way, at = event
        kept = plans[t].kept[stage].index(mask)
        if way:
            return recv[t, stage].at[kept, (0 if way == 1 else mp_size - 1) + at]
        return recv[t, stage].at[kept, block if plans[t].full(stage) else 0]

    def remote(t, event, block, src, dst, to):
        stage, mask, way, at = event
        if way or stage == 0:
            sem = index[(t,) + event]
        else:
            sem = index[t, stage, mask] + block
        return pltpu.make_async_remote_copy(
            src_ref=src,
            dst_ref=dst,
            send_sem=send_sems.at[sem],
            recv_sem=recv_sems.at[sem],
            device_id=to,
            device_id_type=MESH,
        )

    def core_copy(t, mask):
        rows = pl.ds(place(flip(d, mask | 1), wides[t]), wides[t])
        dst = landed[t].at[rows_of(t, mask), :]
        return remote(t, (0, mask, 0, 0), 0, grads[t].at[rows, :], dst, {DP: flip(d, 1)})

    def own_copy(t, mask):
        rows = pl.ds(place(flip(d, mask), wides[t]), wides[t])
        return pltpu.make_async_copy(
            grads[t].at[rows, :],
            sums[t].at[rows_of(t, mask), :],
            own_sems.at[t, plans[t].masks.index(mask)],
        )

    def bit_copy(t, stage, mask, block):
        dim = plans[t].dims[stage - 1]
        event = (stage, mask & ~dim, 0, None)
        dst = landing(t, event, block)
        return remote(t, event, block, sum_at(t, mask, block), dst, {DP: flip(d, dim)})

    def line_copy(t, stage, mask, way, hops):
        event = (stage, mask, way, hops - 1)
        src = sum_at(t, mask, z + way * hops)
        return remote(t, event, None, src, landing(t, event, None), {MP: z + way})

    def arrival(t, event, block):
        dst = landing(t, event, block)
        return remote(t, event, block, dst, dst, {DP: d, MP: z})

    def add(dst, src, wide):
        step = 16

        def some_rows(at, carry):
            rows = pl.ds(pl.multiple_of(at * step, step), step)
            total = dst[rows, :].astype(f32) + src[rows, :].astype(f32)
            dst[rows, :] = total.astype(bf16)
            return carry

        lax.fori_loop(0, wide // step, some_rows, 0)

    def advance(t, stage, mask, block, other):
        if stage > len(plans[t].dims):
            return
        dim = plans[t].dims[stage - 1]
        if dim == MP:
            if other:
                for way, end in ((1, 0), (-1, mp_size - 1)):

                    @pl.when(z == end)
                    def _(way=way):
                        line_copy(t, stage, mask, way, other).start()

        elif mask & dim:
            bit_copy(t, stage, mask, block).start()

    mp_bits = bits_of(mp_size)
    greet(z, d, upper, mp_size, mp_bits)
    cores = [(t, event[1]) for t, event in order if event[0] == 0]
    for t, mask in cores:
        core_copy(t, mask).start()
        own_copy(t, mask).start()

    def load(at):
        t, mask = cores[at]
        return pltpu.make_async_copy(
            landed[t].at[rows_of(t, mask), :],
            staging.at[at % 2, pl.ds(0, wides[t]), pl.ds(0, cols[t] * mp_size)],
            load_sems.at[at % 2],
        )

    seen = 0
    brought = {}
    for t, event in order:
        stage, mask, way, at = event
        plan = plans[t]
        if stage == 0:
            for ahead in (0, 1) if seen == 0 else (seen + 1,):
                if ahead < len(cores):
                    core_copy(*cores[ahead]).wait_recv()
                    load(ahead).start()
            load(seen).wait()
            own_copy(t, mask).wait()
            part = staging.at[seen % 2, pl.ds(0, wides[t]), pl.ds(0, cols[t] * mp_size)]
            add(sums[t].at[rows_of(t, mask), :], part, wides[t])
            seen += 1
            for other in reversed(range(mp_size)):
                advance(t, 1, mask, flip(z, other), other)
        elif way:
            block = z + way * at

            @pl.when(inside(block) & inside(z - way))
            def _():
                arrival(t, event, None).wait_recv()
                add(sum_at(t, mask, block), landing(t, event, None), wides[t])
                if at > 0:
                    line_copy(t, stage, mask, way, at).start()

            if at == 0:
                brought[t, mask] = brought.get((t, mask), 0) + 1
                if brought[t, mask] == 2:
                    advance(t, stage + 1, mask, z, 0)
        else:
            block = flip(z, at) if plan.full(stage) else z
            arrival(t, event, block).wait_recv()
            add(sum_at(t, mask, block), landing(t, event, block), wides[t])
            advance(t, stage + 1, mask, block, at)

    tiles[0] = jnp.zeros(tiles.shape[1:], f32)
    for t in range(n):
        step = 16

        def some_rows(at, carry, t=t):
            rows = pl.ds(pl.multiple_of(at * step, step), step)
            part = sums[t][rows, pl.ds(place(z, cols[t]), cols[t])].astype(f32)
            outs[t][rows, :] = part
            part = part * part
            total = carry
            for low in range(0, step, 8):
                for left in range(0, cols[t], HD):
                    total = total + part[low : low + 8, left : left + HD]
            return total

        if t == n - 1:
            whole = sums[t][pl.ds(0, wides[t]), pl.ds(place(z, cols[t]), cols[t])].astype(f32)
            outs[t][...] = whole
            row = lax.broadcasted_iota(jnp.int32, whole.shape, 0)
            whole = whole * whole
            whole = jnp.where(row < vector_count, whole * (1.0 / mp_size), whole)
            for low in range(0, wides[t], 8):
                tiles[0] += whole[low : low + 8, :HD]
        else:
            zero = jnp.zeros((8, HD), f32)
            tiles[0] += lax.fori_loop(0, wides[t] // step, some_rows, zero)
    pairs = [{DP: flip(d, bit)} for bit in [1] + upper]
    pairs += [{MP: flip(z, bit)} for bit in mp_bits]
    for at, to in enumerate(pairs):
        exchange = pltpu.make_async_remote_copy(
            src_ref=tiles.at[2 * at],
            dst_ref=tiles.at[2 * at + 1],
            send_sem=tile_sems.at[2 * at],
            recv_sem=tile_sems.at[2 * at + 1],
            device_id=to,
            device_id_type=MESH,
        )
        exchange.start()
        exchange.wait()
        tiles[2 * at + 2] = tiles[2 * at] + tiles[2 * at + 1]
    norm_ref[...] = tiles[2 * len(pairs)]

    for t, event in order:
        stage, mask, way, at = event
        if stage == 0:
            core_copy(t, mask).wait_send()
        elif way:

            @pl.when(inside(z + way) & inside(z + way * (at + 1)))
            def _():
                line_copy(t, stage, mask, way, at + 1).wait_send()

        else:
            block = flip(z, at) if plans[t].full(stage) else z
            bit_copy(t, stage, mask | plans[t].dims[stage - 1], block).wait_send()


def fold_all(grads, plans, order, dp_size, mp_size, vector_count):
    n = len(grads)
    _, total = number(plans, mp_size, fold_single)
    wides = [g.shape[0] // dp_size for g in grads]
    cols = [g.shape[1] // mp_size for g in grads]
    rounds = len(bits_of(dp_size)) + len(bits_of(mp_size))
    halves = [(dp_size // 2 * wide, mp_size * each) for wide, each in zip(wides, cols)]
    scratch = [pltpu.VMEM(half, bf16) for half in halves]
    for plan, wide, each in zip(plans, wides, cols):
        for stage, dim in enumerate(plan.dims, 1):
            blocks = 2 * (mp_size - 1) if dim == MP else mp_size if plan.full(stage) else 1
            scratch.append(pltpu.VMEM((len(plan.kept[stage]), blocks, wide, each), bf16))
    scratch += [
        pltpu.VMEM((2, max(wides), mp_size * max(cols)), bf16),
        pltpu.VMEM((2 * rounds + 1, 8, HD), f32),
        pltpu.SemaphoreType.DMA((2,)),
        pltpu.SemaphoreType.DMA((n, dp_size // 2)),
        pltpu.SemaphoreType.DMA((2 * rounds,)),
        pltpu.SemaphoreType.DMA((total,)),
        pltpu.SemaphoreType.DMA((total,)),
    ]
    out = pl.pallas_call(
        functools.partial(fold_kernel, plans, order, mp_size, vector_count),
        out_shape=[jax.ShapeDtypeStruct((wide, each), f32) for wide, each in zip(wides, cols)]
        + [jax.ShapeDtypeStruct((8, HD), f32)]
        + [jax.ShapeDtypeStruct(half, bf16) for half in halves],
        in_specs=[pl.BlockSpec(memory_space=pl.ANY)] * n,
        out_specs=[pl.BlockSpec(memory_space=pltpu.VMEM)] * (n + 1)
        + [pl.BlockSpec(memory_space=pl.ANY)] * n,
        scratch_shapes=scratch,
        compiler_params=pltpu.CompilerParams(
            collective_id=1, has_side_effects=True, vmem_limit_bytes=63 * 2**20
        ),
    )(*grads)
    return list(out[:n]), out[n]


def prepare_kernel(layers, *refs):
    count = 4 * layers + 1
    states, outs = refs[:7], refs[7 : 7 + count]
    held, made = refs[7 + count : 14 + count], refs[14 + count : 14 + 2 * count]
    in_sems, out_sems = refs[14 + 2 * count :]
    loads = [pltpu.make_async_copy(a, b, in_sems.at[at]) for at, (a, b) in enumerate(zip(states, held))]
    for copy in loads:
        copy.start()
    qkv, proj, upper, lower, gains, shifts, bias = held
    stores = [pltpu.make_async_copy(a, b, out_sems.at[at]) for at, (a, b) in enumerate(zip(made, outs))]
    for kind in range(4):
        loads[kind].wait()
        for layer in range(layers):
            out = made[4 * layer + kind]
            if kind == 0:
                cols = qkv.shape[3]
                for part in range(3):
                    out[:, part * cols : (part + 1) * cols] = qkv[layer, part].astype(bf16)
            elif kind == 2:
                for low in range(0, upper.shape[2], 256):
                    out[:, low : low + 256] = upper[layer, :, low : low + 256].astype(bf16)
            else:
                from_ref = proj if kind == 1 else lower
                for low in range(0, from_ref.shape[1], HD):
                    out[:, low : low + HD] = from_ref[layer, low : low + HD, :].T.astype(bf16)
            stores[4 * layer + kind].start()
    for copy in loads[4:]:
        copy.wait()
    small = made[-1]
    rows = [gains[layer] for layer in range(layers)]
    rows += [shifts[:, layer] for layer in range(layers)] + [bias[...]]
    used = sum(each.shape[0] for each in rows)
    rows.append(jnp.zeros((small.shape[0] - used, small.shape[1]), f32))
    small[...] = jnp.concatenate(rows, axis=0).astype(bf16)
    stores[-1].start()
    for copy in stores:
        copy.wait()


def prepare_all(states, small_rows):
    qkv, proj, upper, lower = states[:4]
    layers = qkv.shape[0]
    wide = upper.shape[1]
    each = [3 * qkv.shape[3], proj.shape[1], upper.shape[2], lower.shape[1]] * layers
    shapes = [(wide, cols) for cols in each] + [(small_rows, wide)]
    any_place = pl.BlockSpec(memory_space=pl.ANY)
    return pl.pallas_call(
        functools.partial(prepare_kernel, layers),
        out_shape=[jax.ShapeDtypeStruct(shape, bf16) for shape in shapes],
        in_specs=[any_place] * 7,
        out_specs=[any_place] * len(shapes),
        scratch_shapes=[pltpu.VMEM(state.shape, f32) for state in states]
        + [pltpu.VMEM(shape, bf16) for shape in shapes]
        + [pltpu.SemaphoreType.DMA((7,)), pltpu.SemaphoreType.DMA((len(shapes),))],
        compiler_params=pltpu.CompilerParams(vmem_limit_bytes=56 * 2**20),
    )(*states)


def adam_kernel(streams, vector_count, gain_rows, *refs):
    ins = 31 + 2 * streams
    news = 22 + streams
    sources, outs = refs[:ins], refs[ins : ins + news]
    held, made = refs[ins + news : 2 * ins + news], refs[2 * ins + news : 2 * (ins + news)]
    in_sems, out_sems = refs[2 * (ins + news) :]
    loads = [
        pltpu.make_async_copy(a, b, in_sems.at[at]) for at, (a, b) in enumerate(zip(sources, held))
    ]
    stores = [pltpu.make_async_copy(a, b, out_sems.at[at]) for at, (a, b) in enumerate(zip(made, outs))]
    order = []
    for group in range(4):
        order += [2 * group, 2 * group + 1] + [8 + 3 * group + which for which in range(3)]
    for at in [21, 20] + order + list(range(22, ins)):
        loads[at].start()
    loads[21].wait()
    norm = jnp.sqrt(jnp.sum(held[21][...], keepdims=True))
    made[21][...] = jnp.broadcast_to(norm, made[21].shape)
    stores[21].start()
    factor = jnp.minimum(1.0, clip_bound / norm)

    def update(group, at, gradient):
        found = [held[8 + 3 * group + which][at] for which in range(3)]
        new = adam_update(
            *found, gradient.astype(f32), factor, group_rates[group], group_decays[group]
        )
        for which in range(3):
            made[3 * group + which][at] = new[which]

    for group in range(4):
        for at in order[5 * group : 5 * group + 5]:
            loads[at].wait()
        for layer, gradient in enumerate((held[2 * group + 1], held[2 * group])):
            if group == 0:
                wide, cols = gradient.shape[0], gradient.shape[1] // 3
                for part in range(3):
                    for low in range(0, wide, 64):
                        update(
                            0,
                            (layer, part, slice(low, low + 64)),
                            gradient[low : low + 64, part * cols : (part + 1) * cols],
                        )
            elif group == 2:
                for low in range(0, gradient.shape[0], 16):
                    update(2, (layer, slice(low, low + 16)), gradient[low : low + 16, :])
            else:
                for low in range(0, gradient.shape[1], HD):
                    part = gradient[:, low : low + HD].astype(f32).T
                    update(group, (layer, slice(low, low + HD)), part)
        for which in range(3):
            stores[3 * group + which].start()
    loads[20].wait()
    small = held[20][...].astype(f32)
    for group in range(3):
        for which in range(3):
            loads[22 + 3 * group + which].wait()
        for layer in range(2):
            if group == 0:
                at = (slice(layer, layer + 1),)
                first = vector_count + layer
            elif group == 1:
                at = (layer,)
                first = layer * gain_rows
            else:
                at = (slice(None), layer)
                first = 2 * gain_rows + layer * held[28].shape[0]
            found = [held[22 + 3 * group + which][at] for which in range(3)]
            part = small[first : first + found[0].shape[0]]
            new = adam_update(*found, part, factor, group_rates[4 + group], group_decays[4 + group])
            for which in range(3):
                made[12 + 3 * group + which][at] = new[which]
        for which in range(3):
            stores[12 + 3 * group + which].start()
    moved = lax.axis_index(DP) % 2 != lax.axis_index(MP) % 2
    for at in range(streams):
        for which in range(2):
            loads[31 + 2 * at + which].wait()
        ours, others = held[31 + 2 * at : 33 + 2 * at]
        for low in range(0, ours.shape[0], 64):
            rows = slice(low, low + 64)
            values = jnp.where(moved, others[rows, :].astype(f32), ours[rows, :])
            made[22 + at][rows, :] = values
        stores[22 + at].start()
    for copy in stores:
        copy.wait()


def adam_all(gradients, states, small, norm_tile, small_states, streams, vector_count, gain_rows):
    any_place = pl.BlockSpec(memory_space=pl.ANY)
    operands = list(gradients) + list(states) + [small, norm_tile] + list(small_states)
    operands += streams
    shapes = [each.shape for each in list(states) + list(small_states)] + [(8, HD)]
    shapes += [each.shape for each in streams[::2]]
    news = [jax.ShapeDtypeStruct(shape, f32) for shape in shapes]
    return pl.pallas_call(
        functools.partial(adam_kernel, len(streams) // 2, vector_count, gain_rows),
        out_shape=news,
        in_specs=[any_place] * len(operands),
        out_specs=[any_place] * len(news),
        scratch_shapes=[pltpu.VMEM(each.shape, each.dtype) for each in operands + news]
        + [
            pltpu.SemaphoreType.DMA((len(operands),)),
            pltpu.SemaphoreType.DMA((len(news),)),
        ],
        compiler_params=pltpu.CompilerParams(vmem_limit_bytes=60 * 2**20),
    )(*operands)


ROWS = 64
SAVED = 9
TILE = 256


def norm_rows(src, dst, low, gain, shift):
    def some_rows(at, carry):
        rows = pl.ds(pl.multiple_of(at * ROWS, ROWS), ROWS)
        values = src[rows, :]
        low[rows, :] = values.astype(bf16)
        dst[rows, :] = layer_norm(values, gain, shift).astype(bf16)
        return carry

    lax.fori_loop(0, src.shape[0] // ROWS, some_rows, 0)


def tiles_of(width, body):
    def one(at, carry):
        body(pl.multiple_of(at * TILE, TILE))
        return carry

    lax.fori_loop(0, width // TILE, one, 0)


def block_scores(query, key, slope, doc_col, doc_row, first_col, diagonal):
    cols = first_col + lax.broadcasted_iota(jnp.int32, (1, key.shape[0]), 1)
    scores = dot_cols(query, key) * score_scale + slope * cols.astype(f32)
    allowed = doc_col == doc_row
    if diagonal:
        row = lax.broadcasted_iota(jnp.int32, scores.shape, 0)
        col = lax.broadcasted_iota(jnp.int32, scores.shape, 1)
        allowed = allowed & (row >= col)
    return jnp.where(allowed, scores, masked_score)


def lane_of(values, lane):
    return lax.broadcasted_iota(jnp.int32, values.shape, 1) == lane


def head_slope(slot, inner, slots, heads_slot, core):
    slope = 0.5 ** (slot * heads_slot + 1.0)
    for later in range(1, heads_slot):
        slope = jnp.where(inner == later, 0.5 ** (slot * heads_slot + later + 1.0), slope)
    return slope * jnp.where(core == 0, 1.0, 0.5 ** (slots * heads_slot))


def attend_head(qkv, out, logs, head, at, width, slope, doc_cols, doc_rows):
    query_cols, key_cols, value_cols = (
        pl.ds(pl.multiple_of(at + part * width, HD), HD) for part in range(3)
    )
    length = qkv.shape[0]
    block = min(256, length)
    for first_row in range(0, length, block):
        rows = slice(first_row, first_row + block)
        low, high = key_range(first_row, block)
        blocks = [slice(first, first + block) for first in range(low, high, block)]
        query = qkv[rows, query_cols]
        scores = [
            block_scores(
                query, qkv[cols, key_cols], slope, doc_cols[rows, :],
                doc_rows[:, cols], cols.start, cols == rows,
            )
            for cols in blocks
        ]
        top = scores[0]
        for each in scores[1:]:
            top = jnp.maximum(top, each)
        top = jnp.max(top, axis=-1, keepdims=True)
        total, mixed = 0.0, 0.0
        for cols, each in zip(blocks, scores):
            shifted = jnp.exp(each - top)
            total = total + jnp.sum(shifted, axis=-1, keepdims=True)
            mixed = mixed + dot(shifted.astype(bf16), qkv[cols, value_cols])
        to = pl.ds(pl.multiple_of(head * HD, HD), HD)
        out[rows, to] = (mixed * (1.0 / total)).astype(bf16)
        logs[rows, :] = jnp.where(lane_of(logs[rows, :], head), top + jnp.log(total), logs[rows, :])


FORWARD_STEPS = (
    ("norm_one", "other_0", "other_1", "own_0", "own_1", "share")
    + ("head_0", "head_1")
    + ("back", "proj", "norm_two")
    + tuple(f"up_{at}" for at in range(8))
    + tuple(f"down_{at}" for at in range(4))
)


def forward_kernel(plans, order, mp_size, layers, vector_count, gain_rows, shift_rows, *refs):
    n = len(plans)
    shards = refs[:n]
    inputs, cotangent, doc_cols, doc_rows = refs[n : n + 4]
    outs = refs[n + 4 : 2 * n + 4]
    at = 2 * n + 4
    saved = [refs[at + SAVED * layer : at + SAVED * (layer + 1)] for layer in range(layers)]
    at += SAVED * layers
    last_stream, last_low, cotangent_out, vectors = refs[at : at + 4]
    (
        streams, middles, lows, normed_one, normed_two, send_buf, qkv_full, mixed, logs, attended,
        hidden, active, w_qkv, w_proj, w_up, w_down, small_buf, biases, traded,
        load_sems, save_sems, trade_sems, head_sems, send_sems, recv_sems, own_sems,
    ) = refs[at + 4 :]
    work = SpreadWork(plans, order, mp_size, shards, outs, send_sems, recv_sems, own_sems)
    z, d = work.z, work.d
    core = d % 2
    moved = core != z % 2
    partner = {DP: flip(d, 1)}
    across = {DP: flip(d, 1), MP: flip(z, 1)}
    tokens = inputs.shape[0]
    features = inputs.shape[1]
    half = attended.shape[2] // 2
    wide_small = shards[-1].shape[0]
    lanes = shards[-1].shape[1]
    third = w_qkv.shape[2] // 3
    slots = qkv_full.shape[2] // w_qkv.shape[2]
    heads_slot = third // HD

    greet(z, d, work.upper, mp_size, (), across, moved)
    trade = pltpu.make_async_remote_copy(
        src_ref=inputs, dst_ref=traded, send_sem=trade_sems.at[0], recv_sem=trade_sems.at[1],
        device_id=across, device_id_type=MESH,
    )
    keep = pltpu.make_async_copy(inputs, traded, trade_sems.at[2])
    trade_back = pltpu.make_async_remote_copy(
        src_ref=cotangent, dst_ref=cotangent_out, send_sem=trade_sems.at[3],
        recv_sem=trade_sems.at[4], device_id=across, device_id_type=MESH,
    )
    keep_back = pltpu.make_async_copy(cotangent, cotangent_out, trade_sems.at[5])

    @pl.when(moved)
    def _():
        trade.start()

    @pl.when(jnp.logical_not(moved))
    def _():
        keep.start()

    work.begin()

    saves = []

    def save(src, dst):
        copy = pltpu.make_async_copy(src, dst, save_sems.at[len(saves)])
        copy.start()
        saves.append(copy)
        return copy

    loads = {}

    def load(key, src, dst, slot):
        copy = pltpu.make_async_copy(src, dst, load_sems.at[slot])
        copy.start()
        loads[key] = copy

    def load_tile(layer, kind, at):
        full = outs[4 * layer : 4 * layer + 4]
        if kind == "qkv":
            cols = w_qkv.shape[2]
            first = (1 - core) * slots if at < slots else core * slots
            where = pl.ds(place(first + at % slots, cols), cols)
            load((layer, kind, at), full[0].at[:, where], w_qkv.at[at % 2], at % 2)
        elif kind == "proj":
            load((layer, kind, at), full[1], w_proj, 2)
        elif kind == "up":
            cols = w_up.shape[2]
            where = pl.ds(at * cols, cols)
            load((layer, kind, at), full[2].at[:, where], w_up.at[at % 2], 3 + at % 2)
        else:
            load((layer, kind, at), full[3].at[pair_of(at), :], w_down.at[at % 2], 5 + at % 2)

    def pair_of(at):
        rows = w_down.shape[1]
        return pl.ds(place(flip(d // 2, at), rows), rows)

    def tile(layer, kind, at, count):
        if (layer, kind, at) not in loads:
            load_tile(layer, kind, at)
        loads[layer, kind, at].wait()
        ready = kind != "down" or (4 * layer + 3, 2 * at + 2) in complete
        if at + 1 < count and ready:
            load_tile(layer, kind, at + 1)

    def share_copy(layer):
        rows = pl.ds(place(core, tokens), tokens)
        return pltpu.make_async_remote_copy(
            src_ref=send_buf.at[layer], dst_ref=qkv_full.at[layer, rows, :],
            send_sem=head_sems.at[4 * layer], recv_sem=head_sems.at[4 * layer + 1],
            device_id=partner, device_id_type=MESH,
        )

    def back_copy(layer):
        rows = pl.ds(place(1 - core, tokens), tokens)
        return pltpu.make_async_remote_copy(
            src_ref=mixed.at[layer, rows, :],
            dst_ref=attended.at[layer, :, pl.ds(place(core, half), half)],
            send_sem=head_sems.at[4 * layer + 2], recv_sem=head_sems.at[4 * layer + 3],
            device_id=partner, device_id_type=MESH,
        )

    def active_copy(layer):
        rows = pl.ds(place(core, tokens), tokens)
        return pltpu.make_async_remote_copy(
            src_ref=active, dst_ref=saved[layer][7].at[rows, :],
            send_sem=head_sems.at[4 * layers + 2 * layer],
            recv_sem=head_sems.at[4 * layers + 2 * layer + 1],
            device_id=partner, device_id_type=MESH,
        )

    def vector(at):
        return vectors[at : at + 1, :]

    ahead = {
        "norm_one": ("qkv", 0), "head_0": ("proj", 1), "proj": ("up", 2), "up_6": ("down", 3)
    }

    def compute(layer, name):
        kind, _, at = name.partition("_")
        if name in ahead and 4 * layer + ahead[name][1] not in missing:
            load_tile(layer, ahead[name][0], 0)
        gain = layer * gain_rows
        shift = layers * gain_rows + layer * shift_rows
        keeps = saved[layer]
        if name == "norm_one":
            if layer == 0:
                small = pltpu.make_async_copy(outs[-1], small_buf, load_sems.at[7])
                small.start()

                @pl.when(moved)
                def _():
                    trade.wait_recv()

                @pl.when(jnp.logical_not(moved))
                def _():
                    keep.wait()

                streams[0] = traded[...].astype(f32)
                small.wait()
                for b in range(outs[-1].shape[0] // wide_small):
                    rows = small_buf[b * wide_small : (b + 1) * wide_small, :].astype(f32)
                    vectors[:, b * lanes : (b + 1) * lanes] = rows[:, :lanes]
                    for m in range(mp_size):
                        first = m * (biases.shape[1] // mp_size) + b * lanes
                        biases[:, first : first + lanes] = rows[:, m * lanes : (m + 1) * lanes]
            norm_rows(
                streams.at[layer], normed_one.at[layer], lows.at[2 * layer],
                vector(gain), vector(shift),
            )
            save(lows.at[2 * layer], keeps[0])
            save(normed_one.at[layer], keeps[2])
        elif kind in ("other", "own"):
            at = int(at)
            tile(layer, "qkv", at + (slots if kind == "own" else 0), 2 * slots)
            weight = w_qkv.at[at % 2]
            cols = w_qkv.shape[2]

            def piece(first):
                values = dot(normed_one[layer], weight[:, pl.ds(first, TILE)]).astype(bf16)
                to = pl.ds(pl.multiple_of(at * cols + first, TILE), TILE)
                if kind == "own":
                    qkv_full[layer, pl.ds(place(core, tokens), tokens), to] = values
                else:
                    send_buf[layer, :, to] = values

            tiles_of(cols, piece)
            if kind == "other" and at == slots - 1:
                share_copy(layer).start()
        elif kind == "share":
            arrived = pltpu.make_async_remote_copy(
                src_ref=send_buf.at[layer],
                dst_ref=qkv_full.at[layer, pl.ds(place(1 - core, tokens), tokens), :],
                send_sem=head_sems.at[4 * layer], recv_sem=head_sems.at[4 * layer + 1],
                device_id=partner, device_id_type=MESH,
            )
            arrived.wait_recv()
            save(qkv_full.at[layer], keeps[3])
        elif kind == "head":
            slot = int(at)
            if slot == 0:
                logs[layer] = jnp.zeros(logs.shape[1:], f32)

            def one_head(inner, carry):
                attend_head(
                    qkv_full.at[layer], mixed.at[layer], logs.at[layer], slot * heads_slot + inner,
                    slot * 3 * third + inner * HD, third,
                    head_slope(slot, inner, slots, heads_slot, core), doc_cols, doc_rows,
                )
                return carry

            lax.fori_loop(0, heads_slot, one_head, 0)
            if slot == slots - 1:
                back_copy(layer).start()
                rows = pl.ds(place(core, tokens), tokens)
                attended[layer, :, pl.ds(place(core, half), half)] = mixed[layer, rows, :]
                save(mixed.at[layer], keeps[4])
                save(logs.at[layer], keeps[8])
        elif kind == "back":
            arrived = pltpu.make_async_remote_copy(
                src_ref=mixed.at[layer, pl.ds(0, tokens), :],
                dst_ref=attended.at[layer, :, pl.ds(place(1 - core, half), half)],
                send_sem=head_sems.at[4 * layer + 2], recv_sem=head_sems.at[4 * layer + 3],
                device_id=partner, device_id_type=MESH,
            )
            arrived.wait_recv()
        elif kind == "proj":
            tile(layer, "proj", 0, 1)

            def piece(first):
                cols = pl.ds(first, TILE)
                values = dot_cols(attended[layer], w_proj[cols, :])
                middles[layer, :, cols] = streams[layer, :, cols] + values

            tiles_of(features, piece)
        elif name == "norm_two":
            norm_rows(
                middles.at[layer], normed_two.at[layer], lows.at[2 * layer + 1],
                vector(gain + 1), vector(shift + 1),
            )
            save(lows.at[2 * layer + 1], keeps[1])
            save(normed_two.at[layer], keeps[5])
        elif kind == "up":
            at = int(at)
            if at == 0 and layer == layers - 1:
                pl.when(moved)(trade_back.start)
                pl.when(jnp.logical_not(moved))(keep_back.start)
            if at == 0 and layer > 0:
                for copy in big_saves[layer - 1]:
                    copy.wait()
                active_copy(layer - 1).wait_send()
            cols = w_up.shape[2]
            tile(layer, "up", at, hidden.shape[1] // cols)
            weight = w_up.at[at % 2]

            def piece(first):
                to = pl.ds(pl.multiple_of(at * cols + first, TILE), TILE)
                bias = biases[vector_count + layer : vector_count + layer + 1, to]
                values = dot(normed_two[layer], weight[:, pl.ds(first, TILE)]) + bias
                hidden[:, to] = values.astype(bf16)
                active[:, to] = gelu_tanh(values).astype(bf16)

            tiles_of(cols, piece)
            if (at + 1) * cols == hidden.shape[1]:
                rows = pl.ds(place(core, tokens), tokens)
                big_saves[layer] = [save(hidden, keeps[6]), save(active, keeps[7].at[rows, :])]
                active_copy(layer).start()
        elif kind == "down":
            at = int(at)
            tile(layer, "down", at, features // w_down.shape[1])
            weight = w_down.at[at % 2]
            out = streams.at[layer + 1]
            cols = pair_of(at)
            out[:, cols] = middles[layer, :, cols] + vectors[shift + 2 : shift + 3, cols]

            def piece(step, carry):
                inner = pl.ds(pl.multiple_of(step * 1024, 1024), 1024)
                out[:, cols] += dot_cols(active[:, inner], weight[:, inner])
                return carry

            lax.fori_loop(0, hidden.shape[1] // 1024, piece, 0)

    big_saves = {}
    missing = {}
    complete = set()
    for t, _ in work.order:
        missing[t] = missing.get(t, 0) + 1
    for step in order:
        if isinstance(step[1], str):
            compute(*step)
        else:
            work.step(*step)
            if step[1][0] == len(plans[step[0]].dims):
                complete.add((step[0], step[1][1] - 1))
            missing[step[0]] -= 1
            if missing[step[0]] == 0:
                del missing[step[0]]
    save(streams.at[layers], last_stream)
    traded[...] = streams[layers].astype(bf16)
    save(traded, last_low)
    done_already = [id(copy) for layer in range(layers - 1) for copy in big_saves[layer]]
    for copy in saves:
        if id(copy) not in done_already:
            copy.wait()
    for layer in range(layers):
        share_copy(layer).wait_send()
        back_copy(layer).wait_send()
        rows = pl.ds(place(1 - core, tokens), tokens)
        pltpu.make_async_remote_copy(
            src_ref=active, dst_ref=saved[layer][7].at[rows, :],
            send_sem=head_sems.at[4 * layers + 2 * layer],
            recv_sem=head_sems.at[4 * layers + 2 * layer + 1],
            device_id=partner, device_id_type=MESH,
        ).wait_recv()
    active_copy(layers - 1).wait_send()

    @pl.when(moved)
    def _():
        trade.wait_send()
        trade_back.wait()

    @pl.when(jnp.logical_not(moved))
    def _():
        keep_back.wait()

    work.finish()


def forward_all(
    shards, inputs, cotangent, docs, plans, order, dp_size, mp_size, layers, vector_count, gain_rows, shift_rows
):
    _, total = number(plans, mp_size, spread_single)
    tokens, features = inputs.shape
    length = docs.shape[0]
    half = features // 2
    units = shards[2].shape[1] * mp_size
    cols = shards[0].shape[1]
    slots = mp_size // 2
    any_place = pl.BlockSpec(memory_space=pl.ANY)
    vmem = pl.BlockSpec(memory_space=pltpu.VMEM)
    saved = [
        jax.ShapeDtypeStruct((tokens, features), bf16),
        jax.ShapeDtypeStruct((tokens, features), bf16),
        jax.ShapeDtypeStruct((tokens, features), bf16),
        jax.ShapeDtypeStruct((length, slots * cols), bf16),
        jax.ShapeDtypeStruct((length, half), bf16),
        jax.ShapeDtypeStruct((tokens, features), bf16),
        jax.ShapeDtypeStruct((tokens, units), bf16),
        jax.ShapeDtypeStruct((length, units), bf16),
        jax.ShapeDtypeStruct((length, HD), f32),
    ]
    small_shape = (shards[-1].shape[0] * dp_size, shards[-1].shape[1] * mp_size)
    out_shape = [
        jax.ShapeDtypeStruct((s.shape[0] * dp_size, s.shape[1] * mp_size), s.dtype)
        for s in shards
    ]
    out_shape += saved * layers + [
        jax.ShapeDtypeStruct((tokens, features), f32),
        jax.ShapeDtypeStruct((tokens, features), bf16),
        jax.ShapeDtypeStruct((tokens, features), bf16),
    ]
    out_shape.append(jax.ShapeDtypeStruct((shards[-1].shape[0], features), f32))
    out = pl.pallas_call(
        functools.partial(
            forward_kernel, plans, order, mp_size, layers, vector_count, gain_rows, shift_rows
        ),
        out_shape=out_shape,
        in_specs=[any_place] * (len(shards) + 2) + [vmem] * 2,
        out_specs=[any_place] * (len(out_shape) - 1) + [vmem],
        scratch_shapes=[
            pltpu.VMEM((layers + 1, tokens, features), f32),
            pltpu.VMEM((layers, tokens, features), f32),
            pltpu.VMEM((2 * layers, tokens, features), bf16),
            pltpu.VMEM((layers, tokens, features), bf16),
            pltpu.VMEM((layers, tokens, features), bf16),
            pltpu.VMEM((layers, tokens, slots * cols), bf16),
            pltpu.VMEM((layers, length, slots * cols), bf16),
            pltpu.VMEM((layers, length, half), bf16),
            pltpu.VMEM((layers, length, HD), f32),
            pltpu.VMEM((layers, tokens, features), bf16),
            pltpu.VMEM((tokens, units), bf16),
            pltpu.VMEM((tokens, units), bf16),
            pltpu.VMEM((2, features, cols), bf16),
            pltpu.VMEM((features, features), bf16),
            pltpu.VMEM((2, features, units // 8), bf16),
            pltpu.VMEM((2, features // 4, units), bf16),
            pltpu.VMEM(small_shape, bf16),
            pltpu.VMEM((shards[-1].shape[0], units), f32),
            pltpu.VMEM((tokens, features), bf16),
            pltpu.SemaphoreType.DMA((8,)),
            pltpu.SemaphoreType.DMA((SAVED * layers + 2,)),
            pltpu.SemaphoreType.DMA((6,)),
            pltpu.SemaphoreType.DMA((6 * layers,)),
            pltpu.SemaphoreType.DMA((total,)),
            pltpu.SemaphoreType.DMA((total,)),
            pltpu.SemaphoreType.DMA((len(shards),)),
        ],
        compiler_params=pltpu.CompilerParams(
            collective_id=2, has_side_effects=True, vmem_limit_bytes=62 * 2**20
        ),
    )(*shards, inputs, cotangent, docs.reshape(-1, 1), docs.reshape(1, -1))
    n = len(shards)
    stored = [out[n + SAVED * at : n + SAVED * (at + 1)] for at in range(layers)]
    return out[:n], stored, *out[-4:]


KINDS = ("down", "up", "proj", "qkv")
BACKWARD_STEPS = (
    "turn_down", "W0", "W1", "W2", "W3",
    "turn_up", "hidden_0", "hidden_1", "hidden_2", "hidden_3", "W0",
    "hidden_4", "hidden_5", "W1", "hidden_6", "hidden_7", "norm_two", "mixed_0", "mixed_1",
    "W2", "W3", "turn_proj", "W0", "W1", "W2", "W3", "turn_qkv",
    "share", "head_0", "head_1", "rows_0", "rows_1", "rows_2",
    "back", "W0", "W1", "W2", "W3", "rows_3", "rows_4", "rows_5", "norm_one",
)


def gelu_slope(v):
    root = math.sqrt(2.0 / math.pi)
    t = jnp.tanh(root * (v + 0.044715 * v * v * v))
    return 0.5 * (1.0 + t) + 0.5 * v * (1.0 - t * t) * root * (1.0 + 3 * 0.044715 * v * v)


def norm_back(src, upstream, total, low, gain):
    features = src.shape[1]

    def some_rows(at, carry):
        rows = pl.ds(pl.multiple_of(at * ROWS, ROWS), ROWS)
        value = src[rows, :].astype(f32)
        center = value - jnp.mean(value, axis=-1, keepdims=True)
        scale = lax.rsqrt(jnp.mean(center * center, axis=-1, keepdims=True) + norm_eps)
        normal = center * scale
        grad = upstream[rows, :]
        inner = grad * gain
        mean_inner = jnp.mean(inner, axis=-1, keepdims=True)
        mean_both = jnp.mean(inner * normal, axis=-1, keepdims=True)
        new = total[rows, :] + scale * (inner - mean_inner - normal * mean_both)
        total[rows, :] = new
        low[rows, :] = new.astype(bf16)
        return (
            carry[0] + jnp.sum(grad * normal, axis=0, keepdims=True),
            carry[1] + jnp.sum(grad, axis=0, keepdims=True),
            carry[2] + jnp.sum(new, axis=0, keepdims=True),
        )

    zero = jnp.zeros((1, features), f32)
    return lax.fori_loop(0, src.shape[0] // ROWS, some_rows, (zero, zero, zero))


def attend_back_head(
    qkv, mixed, mixed_grad, logs, key_acc, value_acc, head, at, width, slope, doc_cols, doc_rows
):
    length = qkv.shape[0]
    block = min(256, length)
    key_acc[...] = jnp.zeros_like(key_acc)
    value_acc[...] = jnp.zeros_like(value_acc)
    query_cols, key_cols, value_cols = (
        pl.ds(pl.multiple_of(at + part * width, HD), HD) for part in range(3)
    )
    mine = pl.ds(pl.multiple_of(head * HD, HD), HD)
    for first_row in range(0, length, block):
        rows = slice(first_row, first_row + block)
        low, high = key_range(first_row, block)
        query = qkv[rows, query_cols]
        out_grad = mixed_grad[rows, mine]
        values = mixed[rows, mine]
        inner = jnp.sum(out_grad.astype(f32) * values.astype(f32), axis=-1, keepdims=True)
        log = logs[rows, :]
        log = jnp.sum(jnp.where(lane_of(log, head), log, 0.0), axis=-1, keepdims=True)
        query_grad = 0.0
        for first in range(low, high, block):
            cols = slice(first, first + block)
            key = qkv[cols, key_cols]
            scores = block_scores(
                query, key, slope, doc_cols[rows, :], doc_rows[:, cols], first, first == first_row
            )
            probs = jnp.exp(scores - log)
            value_acc[cols, :] += dot_rows(probs.astype(bf16), out_grad)
            prob_grad = dot_cols(out_grad, qkv[cols, value_cols])
            score_grad = (probs * (prob_grad - inner)).astype(bf16)
            query_grad = query_grad + dot(score_grad, key)
            key_acc[cols, :] += dot_rows(score_grad, query)
        qkv[rows, query_cols] = (query_grad * score_scale).astype(bf16)
    qkv[:, key_cols] = (key_acc[...] * score_scale).astype(bf16)
    qkv[:, value_cols] = value_acc[...].astype(bf16)


def flip_by(value, at, size):
    out = 0
    for bit in bits_of(size):
        one = (value // bit) % 2
        out = out + bit * (1 - one if at & bit else one)
    return out


class Rows:
    def __init__(self, dims, mp_size, merged=False):
        self.dims = tuple(dims)
        self.merged = merged
        self.masks = [0]
        for dim in reversed([dim for dim in self.dims if dim != MP]):
            self.masks = self.masks + [mask | dim for mask in self.masks]
        self.kept = {0: len(self.masks)}
        self.events = []
        for stage, dim in enumerate(self.dims, 1):
            self.kept[stage] = self.kept[stage - 1] // (1 if dim == MP else 2)
            if dim == MP:
                for hops in reversed(range(mp_size - 1)):
                    self.events += [(stage, way, hops) for way in (1, -1)]
            else:
                count = mp_size if self.full(stage) and not merged else 1
                self.events += [(stage, 0, at) for at in range(count)]

    def full(self, stage):
        return MP not in self.dims[: stage - 1]


def number_rows(plans, mp_size):
    index, total = {}, 0
    for t, plan in enumerate(plans):
        for stage, way, at in plan.events:
            if way:
                index[t, stage, way, at] = total
                total += 1
            elif (t, stage) not in index:
                index[t, stage] = total
                total += mp_size
    return index, total


class RowsWork:
    def __init__(self, plans, mp_size, wides, cols, sums, recv, sems):
        self.plans, self.mp_size = plans, mp_size
        self.wides, self.cols = wides, cols
        self.sums, self.recv = sums, recv
        self.send_sems, self.recv_sems, self.credit_sems = sems
        self.z = lax.axis_index(MP)
        self.d = lax.axis_index(DP)
        self.index, _ = number_rows(plans, mp_size)
        self.brought = {}
        self.credited = set()
        self.outgoing = {}
        self.left, self.left_stage = {}, {}
        for t, plan in enumerate(plans):
            self.left[t] = len(plan.events)
            for event in plan.events:
                key = t, event[0]
                self.left_stage[key] = self.left_stage.get(key, 0) + 1

    def inside(self, at):
        return (at >= 0) & (at < self.mp_size)

    def slab(self, t):
        return t % 4 if t < 8 else 4

    def part(self, t, low, high, block):
        wide, cols = self.wides[t], self.cols[t]
        where = pl.ds(0, cols * self.mp_size) if block is None else pl.ds(place(block, cols), cols)
        return self.sums[self.slab(t)].at[pl.ds(low * wide, (high - low) * wide), where]

    def landing(self, t, event, block):
        stage, way, at = event
        ref = self.recv[self.slab(t), stage]
        if way:
            return ref.at[block if way == 1 or at > 0 else self.mp_size]
        if block is None:
            return ref.at[0]
        return ref.at[block if self.plans[t].full(stage) else 0]

    def remote(self, t, event, block, src, dst, to):
        stage, way, at = event
        if way:
            sem = self.index[(t,) + event]
        else:
            sem = self.index[t, stage] + (0 if block is None else block)
        return pltpu.make_async_remote_copy(
            src_ref=src,
            dst_ref=dst,
            send_sem=self.send_sems.at[sem],
            recv_sem=self.recv_sems.at[sem],
            device_id=to,
            device_id_type=MESH,
        )

    def launch(self, t, copy, when=None):
        if when is None:
            copy.start()
        else:
            pl.when(when)(copy.start)
        self.outgoing.setdefault(t, []).append((copy, when))

    def settle(self, t):
        for copy, when in self.outgoing.pop(t, []):
            if when is None:
                copy.wait_send()
            else:
                pl.when(when)(copy.wait_send)

    def take_credit(self, t, stage, way=0):
        if not 4 <= t < 8 or (t, stage, way) in self.credited:
            return
        self.credited.add((t, stage, way))
        sem = self.credit_sems.at[t - 4, stage, 1 if way == -1 else 0]
        if way:
            pl.when(self.inside(self.z + way))(lambda: pl.semaphore_wait(sem, 1))
        else:
            pl.semaphore_wait(sem, 1)

    def give_credit(self, t, stage):
        dim = self.plans[t + 4].dims[stage - 1]
        if dim != MP:
            pl.semaphore_signal(
                self.credit_sems.at[t, stage, 0], inc=1,
                device_id={DP: flip(self.d, dim)}, device_id_type=MESH,
            )
            return
        for way in (1, -1):

            @pl.when(self.inside(self.z - way))
            def _(way=way):
                pl.semaphore_signal(
                    self.credit_sems.at[t, stage, 1 if way == -1 else 0], inc=1,
                    device_id={MP: self.z - way}, device_id_type=MESH,
                )

    def line_copy(self, t, stage, way, hops):
        event = (stage, way, hops - 1)
        block = self.z + way * hops
        dst = self.landing(t, event, block)
        src = self.part(t, 0, self.plans[t].kept[stage], block)
        return self.remote(t, event, block, src, dst, {MP: self.z + way})

    def arrival(self, t, event, block):
        dst = self.landing(t, event, block)
        return self.remote(t, event, block, dst, dst, {DP: self.d, MP: self.z})

    def add(self, dst, src, rows_count):
        step = 16

        def some_rows(at, carry):
            rows = pl.ds(pl.multiple_of(at * step, step), step)
            dst[rows, :] += src[rows, :]
            return carry

        lax.fori_loop(0, rows_count // step, some_rows, 0)

    def advance(self, t, stage, block, other):
        plan = self.plans[t]
        if stage > len(plan.dims):
            return
        dim = plan.dims[stage - 1]
        if dim == MP:
            for way, end in ((1, 0), (-1, self.mp_size - 1)):
                self.take_credit(t, stage, way)
                for hops in range(1, self.mp_size) if block is None else (other,) * (other > 0):
                    copy = self.line_copy(t, stage, way, hops)
                    self.launch(t, copy, self.z == end)
            return
        self.take_credit(t, stage)
        event = (stage, 0, None)
        src = self.part(t, plan.kept[stage], plan.kept[stage - 1], block)
        dst = self.landing(t, event, block)
        self.launch(t, self.remote(t, event, block, src, dst, {DP: flip(self.d, dim)}))

    def step(self, t, event, finish):
        stage, way, at = event
        plan = self.plans[t]
        kept = plan.kept[stage]
        if way:
            block = self.z + way * at
            here = self.inside(block) & self.inside(self.z - way)
            if at > 0:
                self.take_credit(t, stage, way)

            @pl.when(here)
            def _():
                self.arrival(t, event, block).wait_recv()
                self.add(
                    self.part(t, 0, kept, block), self.landing(t, event, block),
                    kept * self.wides[t],
                )

            if at > 0:
                self.launch(t, self.line_copy(t, stage, way, at), here)
            else:
                self.brought[t] = self.brought.get(t, 0) + 1
                if self.brought[t] == 2:
                    self.advance(t, stage + 1, self.z, 0)
        else:
            if plan.full(stage):
                block = None if plan.merged else flip(self.z, at)
            else:
                block = self.z
            self.arrival(t, event, block).wait_recv()
            self.add(
                self.part(t, 0, kept, block), self.landing(t, event, block), kept * self.wides[t]
            )
            self.advance(t, stage + 1, block, at)
        self.left[t] -= 1
        self.left_stage[t, stage] -= 1
        if t < 4 and self.left_stage[t, stage] == 0:
            self.give_credit(t, stage)
        if self.left[t] == 0:
            finish(t)


def backward_kernel(
    plans, order, mp_size, layers, vector_count, gain_rows, shift_rows, *refs
):
    n = len(plans)
    full = [refs[4 * layer : 4 * layer + 4] for layer in range(layers)]
    at = 4 * layers
    cotangent, stream_low, vectors, doc_cols, doc_rows = refs[at : at + 5]
    at += 5
    saved = [refs[at + SAVED * layer : at + SAVED * (layer + 1)] for layer in range(layers)]
    at += SAVED * layers
    outs, (norm_ref, input_grad) = refs[at : at + n], refs[at + n : at + n + 2]
    stream_other, grad_other = refs[at + n + 2 : at + n + 4]
    at += n + 4
    sums = refs[at : at + 5]
    at += 5
    recv = {}
    for slab, plan in zip((0, 1, 2, 3, 4), plans[:4] + plans[8:]):
        for stage in range(1, len(plan.dims) + 1):
            recv[slab, stage] = refs[at]
            at += 1
    (
        blocks, left_t, turn_send, grad, acc, low, hidden_buf, w_a, w_b, normed,
        source, qkv, mixed, mixed_other, logs, mixed_grad, mixed_send, row_other, key_acc,
        value_acc, vector_sums, bias_sums, tiles,
        load_sems, core_sems, out_sems, tile_sems, send_sems, recv_sems, credit_sems,
        block_credit, left_credit,
    ) = refs[at:]
    cols = [out.shape[1] for out in outs]
    wides = [out.shape[0] for out in outs]
    work = RowsWork(plans, mp_size, wides, cols, sums, recv, (send_sems, recv_sems, credit_sems))
    z, d = work.z, work.d
    core = d % 2
    partner = {DP: flip(d, 1)}
    upper = [dim for dim in plans[0].dims if dim != MP]
    tokens, features = low.shape
    half = features // 2
    own_rows = pl.ds(place(core, tokens), tokens)
    other_rows = pl.ds(place(1 - core, tokens), tokens)
    half_qkv = qkv.shape[1]
    slots = mp_size // 2
    third = half_qkv // slots // 3
    heads_slot = third // HD
    wide = w_a.shape[2]
    per_block = cols[0] // wide

    across = {DP: flip(d, 1), MP: flip(z, 1)}
    moved = core != z % 2
    dp_size = 2 ** (len(upper) + 1)
    greet_all(z, d, dp_size, mp_size, across, moved)

    def trade(src, dst, at):
        return pltpu.make_async_remote_copy(
            src_ref=src, dst_ref=dst, send_sem=tile_sems.at[at], recv_sem=tile_sems.at[at + 1],
            device_id=across, device_id_type=MESH,
        )

    trades = [
        trade(stream_low, stream_other, 2 * (dp_size + mp_size) - 4),
        trade(low, grad_other, 2 * (dp_size + mp_size) - 2),
    ]
    pl.when(moved)(trades[0].start)

    loads = {}

    def fetch(key, src, dst):
        copy = pltpu.make_async_copy(src, dst, load_sems.at[len(loads)])
        copy.start()
        loads[key] = copy

    pushes = {}

    def push(key, src, dst):
        at = 2 * len(pushes)
        copy = pltpu.make_async_remote_copy(
            src_ref=src, dst_ref=dst, send_sem=core_sems.at[at], recv_sem=core_sems.at[at + 1],
            device_id=partner, device_id_type=MESH,
        )
        copy.start()
        pushes[key] = at, copy

    def pushed(key):
        pushes[key][1].wait_send()

    def arrived(key, dst):
        at = pushes[key][0]
        pltpu.make_async_remote_copy(
            src_ref=dst, dst_ref=dst, send_sem=core_sems.at[at], recv_sem=core_sems.at[at + 1],
            device_id=partner, device_id_type=MESH,
        ).wait_recv()

    def give(sem):
        pl.semaphore_signal(sem, inc=1, device_id=partner, device_id_type=MESH)

    fetch("cotangent", cotangent, low)
    vector_sums[...] = jnp.zeros_like(vector_sums)
    bias_sums[...] = jnp.zeros_like(bias_sums)

    def block_cols(at):
        block = flip(z, at // per_block)
        return pl.ds(pl.multiple_of(block * cols[0] + (at % per_block) * wide, wide), wide)

    def row_cols(at):
        count = half_qkv // wide
        part = core if at < count else 1 - core
        return pl.ds(pl.multiple_of(part * half_qkv + (at % count) * wide, wide), wide)

    def fetch_tile(layer, name, at):
        qkv_w, proj, up, down = full[layer]
        slot = at % 2
        if name == "hidden":
            where = block_cols(at)
            fetch((layer, "w_a", name, at), down.at[:, where], w_a.at[slot])
            fetch((layer, "w_b", name, at), up.at[:, where], w_b.at[slot])
            fetch((layer, "z", name, at), saved[layer][6].at[:, where], hidden_buf.at[slot])
        elif name == "mixed":
            first = place(1 - core if at == 0 else core, half)
            fetch((layer, "w_a", name, at), proj.at[:, pl.ds(first, half)], w_a.at[slot])
        else:
            fetch((layer, "w_b", name, at), qkv_w.at[:, row_cols(at)], w_b.at[slot])

    counts = {"hidden": mp_size * per_block, "mixed": 2, "rows": 2 * half_qkv // wide}

    def use_tile(layer, name, at):
        for which in ("w_a", "w_b", "z"):
            if (layer, which, name, at) in loads:
                loads[layer, which, name, at].wait()
        if at + 1 < counts[name]:
            fetch_tile(layer, name, at + 1)

    def fetch_block(layer, s):
        where = pl.ds(place(flip(z, s), cols[0]), cols[0])
        fetch((layer, "block", s), saved[layer][7].at[:, where], blocks.at[s % 2])

    def accumulate(left, weight, first):
        def piece(at, carry):
            rows = pl.ds(pl.multiple_of(at * TILE, TILE), TILE)
            values = dot_cols(left[...], weight[rows, :])
            if first:
                acc[:, rows] = values
            else:
                acc[:, rows] += values
            return carry

        lax.fori_loop(0, features // TILE, piece, 0)

    def put_vector(row, values):
        vector_sums[row : row + 1, :] = values

    def turn(use, src):
        slot = use % 2
        masks = plans[use].masks
        if use >= 2:
            pushed(("left", use - 2))
            pl.semaphore_wait(left_credit.at[slot], 1)
        for row, mask in enumerate(masks):
            there = pl.ds(row * wides[use], wides[use])
            theirs = pl.ds(place(flip(d, mask | 1), wides[use]), wides[use])
            mine = pl.ds(place(flip(d, mask), wides[use]), wides[use])
            turn_send[slot, there, :] = src[:, theirs].astype(f32).T.astype(bf16)
            left_t[slot, there, own_rows] = src[:, mine].astype(f32).T.astype(bf16)
        push(("left", use), turn_send.at[slot], left_t.at[slot, :, own_rows])

    def compute(layer, name):
        kind, _, at = name.partition("_")
        keeps = saved[layer]
        gain = layer * gain_rows
        shift = layers * gain_rows + layer * shift_rows
        last = layer == layers - 1
        use = 4 * (layers - 1 - layer)
        if name == "turn_down":
            if last:
                fetch_block(layer, 0)
                fetch_block(layer, 1)
                loads["cotangent"].wait()

                def some_rows(at, carry):
                    rows = pl.ds(pl.multiple_of(at * ROWS, ROWS), ROWS)
                    values = low[rows, :].astype(f32)
                    grad[rows, :] = values
                    return carry + jnp.sum(values, axis=0, keepdims=True)

                total = lax.fori_loop(
                    0, tokens // ROWS, some_rows, jnp.zeros((1, features), f32)
                )
                put_vector(shift + 2, total)
            else:
                pushed((layer + 1, "back"))
                pushed((layer + 1, "mixed"))
            fetch_tile(layer, "hidden", 0)
            fetch((layer, "normed_two"), keeps[5], normed)
            fetch((layer, "middle"), keeps[1], source)
            fetch((layer, "qkv"), keeps[3], qkv)
            fetch((layer, "mixed"), keeps[4], mixed)
            fetch((layer, "logs"), keeps[8], logs)
            push((layer, "mixed"), keeps[4], mixed_other)
            turn(use, low)
        elif name == "turn_up":
            loads[layer, "normed_two"].wait()
            turn(use + 1, normed)
            fetch((layer, "normed_one"), keeps[2], normed)
        elif name == "turn_proj":
            turn(use + 2, low)
        elif name == "turn_qkv":
            loads[layer, "normed_one"].wait()
            turn(use + 3, normed)
        elif kind == "hidden":
            at = int(at)
            use_tile(layer, "hidden", at)
            slot = at % 2
            s, inner = at // per_block, at % per_block
            to_block = s % 2
            if inner == 0 and s >= 2:
                pushed((layer, "grads", s - 2))

            def piece(first):
                here = pl.ds(first, TILE)
                values = dot(low[...], w_a[slot, :, here])
                values = values * gelu_slope(hidden_buf[slot, :, here].astype(f32))
                to = pl.multiple_of(flip(z, s) * cols[0] + inner * wide + first, TILE)
                bias_sums[vector_count + layer : vector_count + layer + 1, pl.ds(to, TILE)] = (
                    jnp.sum(values, axis=0, keepdims=True)
                )
                to = pl.ds(pl.multiple_of(inner * wide + first, TILE), TILE)
                blocks[to_block, own_rows, to] = values.astype(bf16)

            tiles_of(wide, piece)
            left = blocks.at[to_block, own_rows, pl.ds(inner * wide, wide)]
            accumulate(left, w_b.at[slot], at == 0)
            if inner == per_block - 1:
                pl.semaphore_wait(block_credit.at[s], 1)
                part = blocks.at[to_block, own_rows, :]
                push((layer, "grads", s), part, part)
        elif name == "norm_two":
            loads[layer, "middle"].wait()
            sums_of = norm_back(source, acc, grad, low, vectors[gain + 1 : gain + 2, :])
            put_vector(gain + 1, sums_of[0])
            put_vector(shift + 1, sums_of[1])
            fetch((layer, "stream"), keeps[0], source)
            fetch_tile(layer, "mixed", 0)
        elif kind == "mixed":
            at = int(at)
            use_tile(layer, "mixed", at)
            if at == 0 and not last:
                pushed((layer + 1, "share"))

            def piece(first):
                here = pl.ds(first, TILE)
                values = dot(low[...], w_a[at % 2, :, here]).astype(bf16)
                if at == 0:
                    mixed_send[:, here] = values
                else:
                    mixed_grad[own_rows, here] = values

            tiles_of(half, piece)
            if at == 0:
                push((layer, "share"), mixed_send, mixed_grad.at[own_rows, :])
        elif name == "share":
            arrived((layer, "share"), mixed_grad.at[other_rows, :])
            loads[layer, "qkv"].wait()
            loads[layer, "logs"].wait()
            fetch_tile(layer, "rows", 0)
        elif kind == "head":
            slot = int(at)
            if slot == 0 and layer > 0:
                pushed((layer, "grads", 2))
                pushed((layer, "grads", 3))
                fetch_block(layer - 1, 0)
                fetch_block(layer - 1, 1)

            def one_head(inner, carry):
                attend_back_head(
                    qkv, mixed, mixed_grad, logs, key_acc, value_acc, slot * heads_slot + inner,
                    slot * 3 * third + inner * HD, third,
                    head_slope(slot, inner, slots, heads_slot, core), doc_cols, doc_rows,
                )
                return carry

            lax.fori_loop(0, heads_slot, one_head, 0)
            if slot == slots - 1:
                push((layer, "back"), qkv, row_other)
        elif name == "back":
            arrived((layer, "back"), row_other)
        elif kind == "rows":
            at = int(at)
            use_tile(layer, "rows", at)
            count = half_qkv // wide
            here = pl.ds(at % count * wide, wide)
            left = (qkv if at < count else row_other).at[own_rows, here]
            accumulate(left, w_b.at[at % 2], at == 0)
        elif name == "norm_one":
            loads[layer, "stream"].wait()
            sums_of = norm_back(source, acc, grad, low, vectors[gain : gain + 1, :])
            put_vector(gain, sums_of[0])
            put_vector(shift, sums_of[1])
            if layer > 0:
                put_vector(shift - shift_rows + 2, sums_of[2])
            else:
                copy = pltpu.make_async_copy(grad, input_grad, out_sems.at[n])
                copy.start()
                loads["input_grad"] = copy
                pl.when(moved)(trades[1].start)

    def weight(t, s):
        slab = work.slab(t)
        out = sums[slab]
        if t == 8:
            for row, mask in enumerate(plans[t].masks):
                block = flip(d, mask)
                part = vector_sums[:, pl.ds(place(block, cols[t]), cols[t])]
                for m in range(mp_size):
                    first = pl.multiple_of(m * (bias_sums.shape[1] // mp_size) + block * cols[t], cols[t])
                    values = part + bias_sums[:, pl.ds(first, cols[t])]
                    rows = slice(row * wides[t], (row + 1) * wides[t])
                    out[rows, m * cols[t] : (m + 1) * cols[t]] = values.astype(bf16)
            work.advance(t, 1, None, 0)
            return
        layer = layers - 1 - t // 4
        if s == 0:
            if t >= 4:
                work.settle(t - 4)
                loads["out", t - 4].wait()
            arrived(("left", t), left_t.at[t % 2, :, other_rows])
        block = flip(z, s)
        left = left_t.at[t % 2]

        def multiply(right, first, step):
            step = 2 * step if cols[t] % (2 * step) == 0 else step

            def piece(at, carry):
                here = pl.multiple_of(at * step, step)
                there = pl.ds(pl.multiple_of(block * cols[t] + here, step), step)
                values = dot(left[...], right[:, pl.ds(pl.multiple_of(first + here, step), step)])
                out[:, there] = values.astype(bf16)
                return carry

            lax.fori_loop(0, cols[t] // step, piece, 0)

        if slab < 2:
            if slab == 0:
                loads[layer, "block", s].wait()
            else:
                arrived((layer, "grads", s), blocks.at[s % 2, other_rows, :])
            multiply(blocks.at[s % 2], 0, TILE)
            if slab == 0 and s < 2:
                fetch_block(layer, s + 2)
            elif slab == 0:
                give(block_credit.at[s - 2])
            elif s < 2:
                give(block_credit.at[s + 2])
        else:
            if slab == 2 and s == 0:
                loads[layer, "mixed"].wait()
                arrived((layer, "mixed"), mixed_other)
            ours = block // slots == core
            within = pl.multiple_of((block % slots) * cols[t], cols[t])
            near, far = ((mixed, mixed_other), (qkv, row_other))[slab - 2]
            pl.when(ours)(lambda: multiply(near, within, TILE))
            pl.when(jnp.logical_not(ours))(lambda: multiply(far, within, TILE))
        if s == mp_size - 1 and t < 6:
            give(left_credit.at[t % 2])
        work.advance(t, 1, block, s)

    def finish(t):
        final = work.part(t, 0, 1, z)
        copy = pltpu.make_async_copy(final, outs[t], out_sems.at[t])
        copy.start()
        loads["out", t] = copy
        step = 16

        def some_rows(at, carry):
            rows = pl.ds(pl.multiple_of(at * step, step), step)
            part = final[rows, :].astype(f32)
            part = part * part
            if t == 8:
                row = at * step + lax.broadcasted_iota(jnp.int32, part.shape, 0)
                part = jnp.where(row < vector_count, part * (1.0 / mp_size), part)
            total = carry
            for top in range(0, step, 8):
                for side in range(0, cols[t], HD):
                    total = total + part[top : top + 8, side : side + HD]
            return total

        tiles[0] += lax.fori_loop(0, wides[t] // step, some_rows, jnp.zeros((8, HD), f32))

    tiles[0] = jnp.zeros(tiles.shape[1:], f32)
    for step in order:
        if step[0] == "weight":
            weight(*step[1:])
        elif isinstance(step[1], str):
            compute(*step)
        else:
            work.step(*step, finish)

    first = 0
    sem = 0
    for axis, me, size in ((DP, d, dp_size), (MP, z, mp_size)):
        copies = []
        for mask in range(1, size):
            copies.append(
                pltpu.make_async_remote_copy(
                    src_ref=tiles.at[first],
                    dst_ref=tiles.at[first + mask],
                    send_sem=tile_sems.at[sem],
                    recv_sem=tile_sems.at[sem + 1],
                    device_id={axis: flip(me, mask)},
                    device_id_type=MESH,
                )
            )
            sem += 2
        for copy in copies:
            copy.start()
        for copy in copies:
            copy.wait()
        total = tiles[first + flip_by(me, 0, size)]
        for at in range(1, size):
            total = total + tiles[first + flip_by(me, at, size)]
        first += size
        tiles[first] = total
    norm_ref[...] = tiles[first]

    for s in (2, 3):
        pushed((0, "grads", s))
    for key in ((0, "mixed"), (0, "share"), (0, "back"), ("left", 6), ("left", 7)):
        pushed(key)
    for t in range(n):
        work.settle(t)
        if t >= 4:
            loads["out", t].wait()
    loads["input_grad"].wait()
    for copy in trades:
        pl.when(moved)(copy.wait)


def backward_chain(plans, layers):
    chain = []
    for done, layer in enumerate(reversed(range(layers))):
        turns = {"turn_down": 0, "turn_up": 1, "turn_proj": 2, "back": 3}
        t = None
        for name in BACKWARD_STEPS:
            if name.startswith("W"):
                chain.append(("weight", t, int(name[1:])))
                continue
            chain.append((layer, name))
            if name in turns:
                t = 4 * done + turns[name]
            if name == "norm_one" and layer == 0:
                chain.append(("weight", len(plans) - 1, 0))
    return chain


def backward_order(plans, layers, table):
    chain = backward_chain(plans, layers)
    if not table:
        out = []
        for at, step in enumerate(chain):
            out.append(step)
            if step[0] == "weight" and (step[1] == 8 or step[2] == 3):
                out += [(step[1], event) for event in plans[step[1]].events]
        return out
    steps = chain + [(t, event) for t, plan in enumerate(plans) for event in plan.events]
    return [steps[at] for at in table]


def backward_all(
    full, cotangent, stream_low, vectors, docs, stored, plans, order, dp_size, mp_size, layers, vector_count,
    gain_rows, shift_rows,
):
    n = len(plans)
    _, total = number_rows(plans, mp_size)
    tokens, features = cotangent.shape
    length = docs.shape[0]
    units = full[2].shape[1]
    wides = [features // dp_size] * 8 + [vectors.shape[0]]
    cols = [
        full[4 * layer + kind].shape[1] // mp_size
        for layer in reversed(range(layers))
        for kind in (3, 2, 1, 0)
    ] + [max(HD, features // dp_size)]
    half_qkv = full[0].shape[1] // 2
    any_place = pl.BlockSpec(memory_space=pl.ANY)
    vmem = pl.BlockSpec(memory_space=pltpu.VMEM)
    out_shape = [jax.ShapeDtypeStruct((wide, each), bf16) for wide, each in zip(wides, cols)]
    out_shape += [
        jax.ShapeDtypeStruct((8, HD), f32),
        jax.ShapeDtypeStruct((tokens, features), f32),
        jax.ShapeDtypeStruct((tokens, features), bf16),
        jax.ShapeDtypeStruct((tokens, features), bf16),
    ]
    slabs = (0, 1, 2, 3, 8)
    scratch = [
        pltpu.VMEM((plans[t].kept[0] * wides[t], mp_size * cols[t]), bf16) for t in slabs
    ]
    for t in slabs:
        plan = plans[t]
        for stage, dim in enumerate(plan.dims, 1):
            rows = plan.kept[stage] * wides[t]
            if dim == MP:
                shape = (mp_size + 1, rows, cols[t])
            elif not plan.full(stage):
                shape = (1, rows, cols[t])
            elif plan.merged:
                shape = (1, rows, mp_size * cols[t])
            else:
                shape = (mp_size, rows, cols[t])
            scratch.append(pltpu.VMEM(shape, bf16))
    wide = 512
    scratch += [
        pltpu.VMEM((2, length, cols[0]), bf16),
        pltpu.VMEM((2, features // 2, length), bf16),
        pltpu.VMEM((2, features // 2, tokens), bf16),
        pltpu.VMEM((tokens, features), f32),
        pltpu.VMEM((tokens, features), f32),
        pltpu.VMEM((tokens, features), bf16),
        pltpu.VMEM((2, tokens, wide), bf16),
        pltpu.VMEM((2, features, wide), bf16),
        pltpu.VMEM((2, features, wide), bf16),
        pltpu.VMEM((tokens, features), bf16),
        pltpu.VMEM((tokens, features), bf16),
        pltpu.VMEM((length, half_qkv), bf16),
        pltpu.VMEM((length, features // 2), bf16),
        pltpu.VMEM((length, features // 2), bf16),
        pltpu.VMEM((length, HD), f32),
        pltpu.VMEM((length, features // 2), bf16),
        pltpu.VMEM((tokens, features // 2), bf16),
        pltpu.VMEM((length, half_qkv), bf16),
        pltpu.VMEM((length, HD), f32),
        pltpu.VMEM((length, HD), f32),
        pltpu.VMEM((wides[8], features), f32),
        pltpu.VMEM((wides[8], units), f32),
        pltpu.VMEM((dp_size + mp_size + 1, 8, HD), f32),
        pltpu.SemaphoreType.DMA((110,)),
        pltpu.SemaphoreType.DMA((2 * 11 * layers,)),
        pltpu.SemaphoreType.DMA((n + 1,)),
        pltpu.SemaphoreType.DMA((2 * (dp_size + mp_size),)),
        pltpu.SemaphoreType.DMA((total,)),
        pltpu.SemaphoreType.DMA((total,)),
        pltpu.SemaphoreType.REGULAR((4, len(plans[0].dims) + 1, 2)),
        pltpu.SemaphoreType.REGULAR((mp_size,)),
        pltpu.SemaphoreType.REGULAR((2,)),
    ]
    operands = list(full[: 4 * layers]) + [cotangent, stream_low, vectors]
    operands += [docs.reshape(-1, 1), docs.reshape(1, -1)]
    specs = [any_place] * (4 * layers + 2) + [vmem] * 3
    for each in stored:
        operands += each
        specs += [any_place] * SAVED
    out = pl.pallas_call(
        functools.partial(
            backward_kernel, plans, order, mp_size, layers, vector_count, gain_rows, shift_rows
        ),
        out_shape=out_shape,
        in_specs=specs,
        out_specs=[any_place] * n + [vmem] + [any_place] * 3,
        scratch_shapes=scratch,
        compiler_params=pltpu.CompilerParams(
            collective_id=1, has_side_effects=True, vmem_limit_bytes=63 * 2**20
        ),
    )(*operands)
    return list(out[:n]), *out[n:]


forward_table = (
    22, 23, 0, 1, 188, 116, 24, 25, 2, 189, 3, 117, 27, 191, 26, 190, 94, 118, 4, 70, 95, 119, 71,
    5, 192, 193, 121, 200, 97, 8, 96, 31, 195, 197, 194, 28, 9, 198, 99, 120, 98, 30, 100, 72, 73,
    69, 196, 32, 6, 207, 127, 7, 104, 12, 74, 44, 16, 10, 199, 201, 128, 33, 105, 18, 13, 46, 208,
    29, 112, 45, 40, 17, 11, 107, 203, 202, 75, 76, 83, 19, 77, 34, 125, 205, 47, 206, 122, 204,
    39, 209, 52, 48, 20, 14, 103, 36, 15, 38, 79, 210, 106, 21, 78, 211, 212, 213, 126, 49, 41,
    51, 35, 101, 214, 102, 54, 37, 80, 114, 81, 53, 129, 215, 50, 216, 82, 86, 164, 56, 165, 55,
    123, 163, 124, 84, 87, 217, 42, 136, 65, 57, 91, 59, 61, 133, 111, 58, 85, 166, 138, 113, 139,
    134, 66, 130, 43, 108, 60, 218, 90, 219, 88, 140, 62, 170, 135, 167, 171, 64, 109, 67, 92, 63,
    220, 146, 110, 132, 131, 68, 168, 221, 89, 222, 223, 224, 225, 145, 226, 115, 227, 228, 229,
    141, 142, 93, 173, 230, 231, 169, 148, 232, 233, 172, 147, 176, 234, 143, 144, 152, 151, 137,
    235, 236, 237, 159, 177, 178, 175, 174, 181, 153, 180, 184, 238, 149, 150, 239, 240, 155, 157,
    156, 182, 154, 160, 158, 185, 179, 241, 242, 243, 161, 183, 162, 244, 245, 246, 247, 248, 249,
    186, 250, 251, 252, 187, 253, 254, 255,
)
backward_table = (
    0, 1, 2, 3, 4, 5, 6, 7, 8, 9, 10, 11, 12, 13, 14, 15, 16, 17, 87, 18, 19, 20, 21, 85, 96, 22,
    23, 88, 24, 25, 26, 27, 28, 29, 86, 90, 108, 30, 89, 109, 31, 32, 99, 110, 107, 33, 34, 35,
    111, 98, 92, 91, 36, 97, 37, 113, 38, 100, 114, 101, 122, 93, 121, 112, 103, 102, 125, 39,
    123, 40, 126, 94, 41, 124, 127, 42, 104, 105, 95, 43, 115, 44, 45, 46, 47, 116, 106, 48, 49,
    50, 51, 52, 128, 53, 54, 55, 136, 56, 117, 129, 57, 118, 58, 130, 59, 60, 61, 62, 131, 63,
    120, 132, 119, 137, 64, 65, 66, 67, 68, 69, 138, 70, 71, 135, 146, 72, 133, 73, 74, 134, 140,
    149, 139, 157, 75, 76, 77, 148, 147, 151, 141, 171, 150, 142, 78, 79, 159, 172, 80, 175, 158,
    81, 82, 153, 83, 173, 160, 84, 161, 152, 185, 177, 174, 163, 144, 162, 164, 186, 178, 165,
    154, 187, 143, 176, 166, 167, 180, 189, 179, 168, 155, 188, 181, 182, 170, 190, 145, 191, 169,
    156, 183, 192, 184, 193,
)


def program(dp_size, mp_size, args):
    (
        inputs, documents, cotangent,
        qkv_weight, qkv_moment, qkv_square,
        proj_weight, proj_moment, proj_square,
        upper_weight, upper_moment, upper_square,
        lower_weight, lower_moment, lower_square,
        hidden_bias, bias_moment, bias_square,
        norm_gains, gains_moment, gains_square,
        shift_params, shifts_moment, shifts_square,
    ) = args
    layers = qkv_weight.shape[0]
    tokens, features = inputs.shape
    length = documents.shape[1]
    pieces = length // tokens
    slots = mp_size // pieces
    wide = features // dp_size
    z_cols = qkv_weight.shape[3]
    heads_slot = z_cols // HD
    me_dp = lax.axis_index(DP)
    me_mp = lax.axis_index(MP)
    core = me_dp % 2

    def swap(values):
        return lax.ppermute(values, DP, [(at, at ^ 1) for at in range(dp_size)])

    def by_core(own, other, axis):
        first = jnp.where(core == 0, own, other)
        second = jnp.where(core == 0, other, own)
        return jnp.concatenate([first, second], axis=axis)

    paired = pieces == 2 and dp_size % 2 == 0 and mp_size % 2 == 0
    if paired:
        moved = core != me_mp % 2
        doc_rows = jnp.where(moved, swap(documents), documents)
        docs = lax.dynamic_index_in_dim(doc_rows, me_mp // 2, 0, False)

        def share_heads(values):
            half = values.shape[1] // 2
            own = lax.dynamic_slice_in_dim(values, core * half, half, 1)
            sent = lax.dynamic_slice_in_dim(values, (1 - core) * half, half, 1)
            return by_core(own, swap(sent), 0)

        def return_heads(values):
            own = lax.dynamic_slice_in_dim(values, core * tokens, tokens, 0)
            sent = lax.dynamic_slice_in_dim(values, (1 - core) * tokens, tokens, 0)
            return by_core(own, swap(sent), 1)

        first_slot = core * slots
    else:
        groups = [list(range(g * pieces, (g + 1) * pieces)) for g in range(mp_size // pieces)]

        docs = lax.dynamic_index_in_dim(documents, me_mp // pieces, 0, False)

        def share_heads(values):
            return lax.all_to_all(values, MP, 1, 0, axis_index_groups=groups, tiled=True)

        def return_heads(values):
            return lax.all_to_all(values, MP, 0, 1, axis_index_groups=groups, tiled=True)

        moved = False
        first_slot = (me_mp % pieces) * slots
    slope_table = jnp.asarray(0.5 ** (np.arange(H) + 1.0), dtype=f32)
    slopes = lax.dynamic_slice_in_dim(
        slope_table, first_slot * heads_slot, slots * heads_slot
    )

    bits = bits_of(dp_size)[1:]
    line_first = [(MP, *bits), (MP, *bits[::-1])]
    line_second = [(bits[0], MP, *bits[1:]), (bits[-1], MP, *bits[:-1][::-1])]

    gain_rows = norm_gains.shape[1]
    shift_rows = shift_params.shape[1]
    vector_count = layers * (gain_rows + shift_rows)
    bias_wide = hidden_bias.shape[1]
    lanes = max(wide, HD)
    small_rows = -(-(vector_count + layers) // 16) * 16

    def padded(values):
        return jnp.pad(values, [(0, 0)] * (values.ndim - 1) + [(0, lanes - values.shape[-1])])

    spreads = []
    for layer in range(layers):
        spreads += line_first[:: 1 if layer % 2 == 0 else -1] + line_second
    spreads.append(line_first[0])
    qkv_by_part = qkv_weight.transpose(0, 2, 1, 3)
    if paired and wide == lanes and bias_wide == lanes:
        shards = prepare_all(
            [
                qkv_by_part, proj_weight, upper_weight, lower_weight, norm_gains,
                shift_params.transpose(1, 0, 2), hidden_bias,
            ],
            small_rows,
        )
    else:
        small = jnp.concatenate(
            [
                padded(norm_gains.reshape(-1, wide)),
                padded(shift_params.reshape(-1, wide)),
                padded(hidden_bias),
                jnp.zeros((small_rows - vector_count - layers, lanes), f32),
            ],
            axis=0,
        ).astype(bf16)
        shards = []
        for layer in range(layers):
            shards += [
                qkv_weight[layer].astype(bf16).reshape(wide, 3 * z_cols),
                proj_weight[layer].astype(bf16).T,
                upper_weight[layer].astype(bf16),
                lower_weight[layer].astype(bf16).T,
            ]
        shards.append(small)
    spreads = [Spread(dims, mp_size) for dims in spreads]
    tabled = dp_size == 8 and mp_size == 4 and layers == 2
    if paired:
        spread_order = forward_order(spreads, layers, forward_table if tabled else ())
        full, stored, stream, stream_low, cotangent, vectors = forward_all(
            shards, inputs, cotangent, docs, spreads, spread_order, dp_size, mp_size, layers,
            vector_count, gain_rows, shift_rows,
        )
    else:
        spread_order = step_order(spreads, (), lambda t, stage: t // 2 + stage)
        full = spread_all(shards, spreads, spread_order, dp_size, mp_size)
    if not paired:
        small_all = full[-1].reshape(dp_size, small_rows, mp_size, lanes).astype(f32)
        vectors = small_all[:, :vector_count, 0, :wide].transpose(1, 0, 2)
        vectors = vectors.reshape(vector_count, features)
        gains = vectors[: layers * gain_rows].reshape(layers, gain_rows, features)
        shifts = vectors[layers * gain_rows :].reshape(layers, shift_rows, features)
        biases = small_all[:, vector_count : vector_count + layers, :, :bias_wide]
        biases = biases.transpose(1, 2, 0, 3).reshape(layers, -1)
        stream = inputs.astype(f32)
        stored = []
        for layer in range(layers):
            qkv_w, proj_w, upper_w, lower_w = full[4 * layer : 4 * layer + 4]
            normed = layer_norm(stream, gains[layer, 0], shifts[layer, 0]).astype(bf16)
            qkv = share_heads(dot(normed, qkv_w).astype(bf16))
            mixed = attend(slopes, docs, qkv, slots)
            attended = return_heads(mixed)
            middle = stream + dot_cols(attended, proj_w)
            normed_two = layer_norm(middle, gains[layer, 1], shifts[layer, 1]).astype(bf16)
            hidden = dot(normed_two, upper_w) + biases[layer]
            active = gelu_tanh(hidden).astype(bf16)
            stored.append(
                (stream, middle, normed, qkv, mixed, attended, normed_two, hidden, active)
            )
            stream = middle + dot_cols(active, lower_w) + shifts[layer, 2]
    output_stream = stream

    ways = []
    for layer in reversed(range(layers)):
        ways += fold_dims(line_first, line_second, layer)
    ways.append(line_first[0][::-1])
    if paired:
        ways[-1] = (1,) + ways[-1]
        folds = [Rows(dims, mp_size, at == 8) for at, dims in enumerate(ways)]
        fold_order = backward_order(folds, layers, backward_table if tabled else ())
        owned, norm_tile, input_grad, stream_other, grad_other = backward_all(
            full, cotangent, stream_low, vectors, docs, stored, folds, fold_order, dp_size, mp_size, layers,
            vector_count, gain_rows, shift_rows,
        )
    else:
        grad_stream = cotangent.astype(f32)
        weight_grads = [None] * layers
        vector_grads = [None] * layers
        bias_grads = [None] * layers
        no_shift = jnp.zeros((features,), f32)
        for layer in reversed(range(layers)):
            qkv_w, proj_w, upper_w, lower_w = full[4 * layer : 4 * layer + 4]
            stream_in, middle, normed, qkv, mixed, attended, normed_two, hidden, active = stored[layer]
            out_shift_grad = jnp.sum(grad_stream, axis=0)
            grad_low = grad_stream.astype(bf16)
            active_grad = dot(grad_low, lower_w)
            _, pull_gelu = jax.vjp(gelu_tanh, hidden.astype(f32))
            hidden_grad = pull_gelu(active_grad)[0].astype(bf16)
            lower_grad = dot_rows(grad_low, active).astype(bf16)
            upper_grad = dot_rows(normed_two, hidden_grad).astype(bf16)
            bias_grads[layer] = jnp.sum(hidden_grad, axis=0, dtype=f32)
            normed_two_grad = dot_cols(hidden_grad, upper_w)
            _, pull_two = jax.vjp(layer_norm, middle, gains[layer, 1], no_shift)
            middle_part, gain_two, shift_two = pull_two(normed_two_grad)
            middle_grad = grad_stream + middle_part
            middle_low = middle_grad.astype(bf16)
            mixed_grad = share_heads(dot(middle_low, proj_w).astype(bf16))
            proj_grad = dot_rows(middle_low, attended).astype(bf16)
            qkv_grad = return_heads(attend_back(slopes, docs, qkv, mixed, mixed_grad, slots))
            normed_grad = dot_cols(qkv_grad, qkv_w)
            qkv_weight_grad = dot_rows(normed, qkv_grad).astype(bf16)
            _, pull_one = jax.vjp(layer_norm, stream_in, gains[layer, 0], no_shift)
            stream_part, gain_one, shift_one = pull_one(normed_grad)
            grad_stream = middle_grad + stream_part
            weight_grads[layer] = (lower_grad, upper_grad, proj_grad, qkv_weight_grad)
            vector_grads[layer] = (
                jnp.stack([gain_one, gain_two]),
                jnp.stack([shift_one, shift_two, out_shift_grad]),
            )
        input_grad = grad_stream

        vector_sums = jnp.concatenate(
            [jnp.concatenate([vector_grads[at][kind] for at in range(layers)]) for kind in (0, 1)]
        )
        vector_sums = padded(vector_sums.reshape(vector_count, dp_size, wide)).transpose(1, 0, 2)
        vector_sums = jnp.broadcast_to(
            vector_sums[:, :, None], (dp_size, vector_count, mp_size, lanes)
        )
        bias_sums = padded(jnp.stack(bias_grads).reshape(layers, mp_size, dp_size, bias_wide))
        bias_sums = bias_sums.transpose(2, 0, 1, 3)
        rest = jnp.zeros((dp_size, small_rows - vector_count - layers, mp_size, lanes), f32)
        small_grad = jnp.concatenate([vector_sums, bias_sums, rest], axis=1)
        small_grad = small_grad.reshape(dp_size * small_rows, mp_size * lanes).astype(bf16)

        local = []
        for layer in reversed(range(layers)):
            local += weight_grads[layer]
        local.append(small_grad)
        folds = [Fold(dims, mp_size) for dims in ways]
        fold_order = step_order(folds, (), lambda t, stage: t // 2 + stage)
        owned, norm_tile = fold_all(local, folds, fold_order, dp_size, mp_size, vector_count)
    small_owned = owned.pop()

    def by_row(values):
        return values.transpose(1, 0, 2)

    states = [qkv_by_part, qkv_moment.transpose(0, 2, 1, 3), qkv_square.transpose(0, 2, 1, 3)]
    states += [
        proj_weight, proj_moment, proj_square, upper_weight, upper_moment, upper_square,
        lower_weight, lower_moment, lower_square,
    ]
    ordered = [owned[4 * layer + kind] for kind in (3, 2, 1, 0) for layer in range(layers)]
    small_states = [
        hidden_bias, bias_moment, bias_square, norm_gains, gains_moment, gains_square,
        by_row(shift_params), by_row(shifts_moment), by_row(shifts_square),
    ]
    if wide < lanes or bias_wide < lanes:
        small_states = [padded(each) for each in small_states]
    streams = [output_stream, stream_other, input_grad, grad_other] if paired else []
    results = list(
        adam_all(
            ordered, states, small_owned, norm_tile, small_states, streams, vector_count, gain_rows
        )
    )
    if paired:
        output_stream, input_grad = results[22:]
    grad_norm = results[21][0, 0]
    results[:3] = [each.transpose(0, 2, 1, 3) for each in results[:3]]
    results[18:21] = [by_row(each) for each in results[18:21]]
    results[12:15] = [each[:, :bias_wide] for each in results[12:15]]
    results[15:21] = [each[:, :, :wide] for each in results[15:21]]
    return (output_stream, input_grad, *results[:21], grad_norm)


def fold_dims(line_first, line_second, layer):
    first = [dims[::-1] for dims in line_first]
    second = [dims[::-1] for dims in line_second]
    return second + (first if layer % 2 else first[::-1])


def solution(mesh):
    dp_size = mesh.shape[DP]
    mp_size = mesh.shape[MP]
    rows = P((DP, MP), None)
    split_rows = P(None, DP, None, MP)
    split_upper = P(None, DP, MP)
    split_lower = P(None, MP, DP)
    split_bias = P(None, (MP, DP))
    split_vector = P(None, None, DP)
    groups = (
        split_rows, split_lower, split_upper, split_lower, split_bias, split_vector, split_vector
    )
    placed = tuple(spec for spec in groups for _ in range(3))

    def shards(*args):
        return program(dp_size, mp_size, args)

    return jax.shard_map(
        shards,
        mesh=mesh,
        in_specs=(rows, P(DP, None), rows) + placed,
        out_specs=(rows, rows) + placed + (P(),),
        check_vma=False,
    )
```

```python
import functools
import math

import jax
import jax.numpy as jnp
import numpy as np
from jax import lax
from jax.experimental import pallas as pl
from jax.experimental.pallas import tpu as pltpu
from jax.sharding import PartitionSpec as P

DP = "dp"
MP = "mp"
H = 8
HD = 128
STEP = 5
MAX_DOC = 512

norm_eps = 1e-05
clip_bound = 1.0
beta_first = 0.9
beta_second = 0.95
adam_eps = 1e-08
masked_score = -1e30
group_rates = (0.03, 0.12, 0.03, 0.015, 0.3, 0.7, 0.3)
group_decays = (0.1, 0.1, 0.1, 0.1, 0.0, 0.0, 0.0)
contract_rows = (((0,), (0,)), ((), ()))
contract_cols = (((1,), (1,)), ((), ()))
f32 = jnp.float32
bf16 = jnp.bfloat16
score_scale = 1.0 / math.sqrt(HD)
MESH = pl.DeviceIdType.MESH


def adam_update(master, moment, square, gradient, factor, step_rate, decay_rate):
    clipped = gradient * factor
    moment_new = beta_first * moment + (1.0 - beta_first) * clipped
    square_new = beta_second * square + (1.0 - beta_second) * clipped * clipped
    first_hat = moment_new / (1.0 - beta_first**STEP)
    second_hat = square_new / (1.0 - beta_second**STEP)
    master_new = master - step_rate * (
        first_hat / (jnp.sqrt(second_hat) + adam_eps) + decay_rate * master
    )
    return (master_new, moment_new, square_new)


def gelu_tanh(values):
    return jax.nn.gelu(values, approximate=True)


def layer_norm(values, scale_vec, shift_vec):
    center = values - jnp.mean(values, axis=-1, keepdims=True)
    spread = jnp.mean(center * center, axis=-1, keepdims=True)
    return center * lax.rsqrt(spread + norm_eps) * scale_vec + shift_vec


def dot(left, right):
    return jnp.dot(left, right, preferred_element_type=f32)


def dot_rows(left, right):
    return lax.dot_general(left, right, contract_rows, preferred_element_type=f32)


def dot_cols(left, right):
    return lax.dot_general(left, right, contract_cols, preferred_element_type=f32)


def masked_scores(slope, doc_col, doc_row, query, key, first_row, first_col):
    scores = dot_cols(query, key) * score_scale
    rows = first_row + lax.broadcasted_iota(jnp.int32, scores.shape, 0)
    cols = first_col + lax.broadcasted_iota(jnp.int32, scores.shape, 1)
    distance = rows - cols
    allowed = (distance >= 0) & (doc_col == doc_row)
    return jnp.where(allowed, scores - slope * distance.astype(f32), masked_score)


def key_range(first_row, block):
    low = max(0, first_row - (MAX_DOC - 1)) // block * block
    return low, first_row + block


def attend_kernel(heads, block, slope_ref, dcol_ref, drow_ref, qkv_ref, o_ref):
    length = o_ref.shape[0]
    for head in range(heads):
        slope = slope_ref[pl.program_id(0) * heads + head]
        at = head * HD
        kat = (heads + head) * HD
        vat = (2 * heads + head) * HD
        for first_row in range(0, length, block):
            low, high = key_range(first_row, block)
            scores = masked_scores(
                slope,
                dcol_ref[first_row : first_row + block, :],
                drow_ref[:, low:high],
                qkv_ref[first_row : first_row + block, at : at + HD],
                qkv_ref[low:high, kat : kat + HD],
                first_row,
                low,
            )
            shifted = jnp.exp(scores - jnp.max(scores, axis=-1, keepdims=True))
            total = jnp.sum(shifted, axis=-1, keepdims=True)
            prob_low = (shifted * (1.0 / total)).astype(bf16)
            o_ref[first_row : first_row + block, at : at + HD] = dot(
                prob_low, qkv_ref[low:high, vat : vat + HD]
            ).astype(bf16)


def attend_back_kernel(
    heads, block, slope_ref, dcol_ref, drow_ref, qkv_ref, o_ref, do_ref,
    grad_ref, key_acc, value_acc,
):
    length = o_ref.shape[0]
    for head in range(heads):
        slope = slope_ref[pl.program_id(0) * heads + head]
        at = head * HD
        kat = (heads + head) * HD
        vat = (2 * heads + head) * HD
        key_acc[...] = jnp.zeros_like(key_acc)
        value_acc[...] = jnp.zeros_like(value_acc)
        for first_row in range(0, length, block):
            low, high = key_range(first_row, block)
            rows = slice(first_row, first_row + block)
            query = qkv_ref[rows, at : at + HD]
            key = qkv_ref[low:high, kat : kat + HD]
            scores = masked_scores(
                slope, dcol_ref[rows, :], drow_ref[:, low:high], query, key, first_row, low
            )
            shifted = jnp.exp(scores - jnp.max(scores, axis=-1, keepdims=True))
            total = jnp.sum(shifted, axis=-1, keepdims=True)
            probs = shifted * (1.0 / total)
            out_grad = do_ref[rows, at : at + HD]
            value_acc[low:high, :] += dot_rows(probs.astype(bf16), out_grad)
            prob_grad = dot_cols(out_grad, qkv_ref[low:high, vat : vat + HD])
            inner = jnp.sum(
                out_grad.astype(f32) * o_ref[rows, at : at + HD].astype(f32),
                axis=-1,
                keepdims=True,
            )
            score_grad = (probs * (prob_grad - inner)).astype(bf16)
            grad_ref[rows, at : at + HD] = (dot(score_grad, key) * score_scale).astype(bf16)
            key_acc[low:high, :] += dot_rows(score_grad, query)
        grad_ref[:, kat : kat + HD] = (key_acc[...] * score_scale).astype(bf16)
        grad_ref[:, vat : vat + HD] = value_acc[...].astype(bf16)


def attend_specs(length, width):
    def columns(each):
        return pl.BlockSpec((length, each), lambda s: (0, s))

    fixed = [
        pl.BlockSpec(memory_space=pltpu.SMEM),
        pl.BlockSpec((length, 1), lambda s: (0, 0)),
        pl.BlockSpec((1, length), lambda s: (0, 0)),
    ]
    return fixed, columns(3 * width), columns(width)


def attend(slopes, docs, qkv, slots):
    length = qkv.shape[0]
    width = qkv.shape[1] // (3 * slots)
    fixed, wide, narrow = attend_specs(length, width)
    pairs = slots * width // HD * length * length
    return pl.pallas_call(
        functools.partial(attend_kernel, width // HD, min(256, length)),
        grid=(slots,),
        in_specs=fixed + [wide],
        out_specs=narrow,
        out_shape=jax.ShapeDtypeStruct((length, slots * width), bf16),
        compiler_params=pltpu.CompilerParams(vmem_limit_bytes=32 * 2**20),
        cost_estimate=pl.CostEstimate(
            flops=4 * pairs * HD, bytes_accessed=3 * qkv.size, transcendentals=pairs
        ),
    )(slopes, docs.reshape(-1, 1), docs.reshape(1, -1), qkv)


def attend_back(slopes, docs, qkv, o, do, slots):
    length = qkv.shape[0]
    width = qkv.shape[1] // (3 * slots)
    fixed, wide, narrow = attend_specs(length, width)
    pairs = slots * width // HD * length * length
    return pl.pallas_call(
        functools.partial(attend_back_kernel, width // HD, min(256, length)),
        grid=(slots,),
        in_specs=fixed + [wide, narrow, narrow],
        out_specs=wide,
        out_shape=jax.ShapeDtypeStruct(qkv.shape, bf16),
        scratch_shapes=[pltpu.VMEM((length, HD), f32), pltpu.VMEM((length, HD), f32)],
        compiler_params=pltpu.CompilerParams(vmem_limit_bytes=32 * 2**20),
        cost_estimate=pl.CostEstimate(
            flops=10 * pairs * HD, bytes_accessed=6 * qkv.size, transcendentals=pairs
        ),
    )(slopes, docs.reshape(-1, 1), docs.reshape(1, -1), qkv, o, do)


def bits_of(size):
    return [1 << at for at in range(size.bit_length() - 1)]


def flip(value, mask):
    bit = 1
    while bit <= mask:
        if mask & bit:
            value = value + bit * (1 - 2 * ((value // bit) % 2))
        bit *= 2
    return value


def place(at, size):
    if isinstance(at, int):
        return at * size
    return pl.multiple_of(at * size, size)


class Spread:
    def __init__(self, dims, mp_size):
        self.dims = tuple(dims)
        self.events = []
        masks, spread = [0], False
        for stage, dim in enumerate(self.dims):
            for mask in masks:
                if dim == MP:
                    for hops in range(1, mp_size):
                        self.events += [(stage, mask, way, hops) for way in (1, -1)]
                else:
                    places = range(mp_size) if spread else (0,)
                    self.events += [(stage, mask | dim, 0, at) for at in places]
            if dim == MP:
                spread = True
            else:
                masks = masks + [mask | dim for mask in masks]
        self.events += [(len(self.dims), mask | 1, 0, 0) for mask in masks]

    def full(self, stage):
        return MP in self.dims[:stage]


class Fold:
    def __init__(self, dims, mp_size, halves=1):
        self.dims = tuple(dims)
        masks = [0]
        for dim in self.dims:
            if dim != MP:
                masks = masks + [mask | dim for mask in masks]
        self.masks = masks
        self.kept = {}
        sent_first = sorted(masks, key=self.leaves)
        self.events = [(0, mask, 0, half) for mask in sent_first for half in range(halves)]
        rows = list(masks)
        for stage, dim in enumerate(self.dims, 1):
            if dim != MP:
                rows = [mask for mask in rows if not mask & dim]
            self.kept[stage] = list(rows)
            if dim == MP:
                for hops in reversed(range(mp_size - 1)):
                    for mask in rows:
                        self.events += [(stage, mask, way, hops) for way in (1, -1)]
            else:
                places = reversed(range(mp_size)) if self.full(stage) else (0,)
                places = list(places)
                for mask in rows:
                    self.events += [(stage, mask, 0, at) for at in places]

    def leaves(self, mask):
        for at, dim in enumerate(self.dims):
            if dim != MP and mask & dim:
                return at
        return len(self.dims)

    def full(self, stage):
        return MP not in self.dims[: stage - 1]


def number(plans, mp_size, single):
    index, total = {}, 0
    for t, plan in enumerate(plans):
        for event in plan.events:
            stage, mask, way, at = event
            if way or single(plan, stage):
                index[(t,) + event] = total
                total += 1
            elif (t, stage, mask) not in index:
                index[t, stage, mask] = total
                total += mp_size
    return index, total


def spread_single(plan, stage):
    return stage == len(plan.dims)


def fold_single(plan, stage):
    return stage == 0


def merge_small(order, plans):
    t = len(plans) - 1
    small = [(t, event) for event in plans[t].events]
    out, used = [], 0
    for at, step in enumerate(order):
        out.append(step)
        while used < len(small) and (used + 1) * len(order) <= (at + 1) * (len(small) + 1):
            out.append(small[used])
            used += 1
    return out + small[used:]


def step_order(plans, table, by_stage):
    steps = [(t, event) for t, plan in enumerate(plans[:-1]) for event in plan.events]
    if len(table) == len(steps):
        return merge_small([steps[at] for at in table], plans)
    ranked = sorted(range(len(steps)), key=lambda at: (by_stage(steps[at][0], steps[at][1][0]), at))
    return merge_small([steps[at] for at in ranked], plans)


def forward_order(plans, layers, table):
    steps = [(t, event) for t, plan in enumerate(plans) for event in plan.events]
    compute = [(layer, name) for layer in range(layers) for name in FORWARD_STEPS]
    if len(table) == len(steps) + len(compute):
        steps += compute
        return [steps[at] for at in table]
    return steps + compute


def greet(z, d, upper, mp_size, mp_bits=(), across=None, moved=None):
    barrier = pltpu.get_barrier_semaphore()
    for bit in mp_bits:
        pl.semaphore_signal(
            barrier, inc=1, device_id={MP: flip(z, bit)}, device_id_type=MESH
        )
    for bit in [1] + upper:
        pl.semaphore_signal(
            barrier, inc=1, device_id={DP: flip(d, bit)}, device_id_type=MESH
        )
    also = 0
    if across is not None:

        @pl.when(moved)
        def _():
            pl.semaphore_signal(barrier, inc=1, device_id=across, device_id_type=MESH)

        also = jnp.where(moved, 1, 0)
    for way in (1, -1):

        @pl.when((z + way >= 0) & (z + way < mp_size))
        def _(way=way):
            pl.semaphore_signal(
                barrier, inc=1, device_id={MP: z + way}, device_id_type=MESH
            )

    around = jnp.where(z > 0, 1, 0) + jnp.where(z < mp_size - 1, 1, 0)
    pl.semaphore_wait(barrier, 1 + len(upper) + len(mp_bits) + around + also)


def greet_all(z, d, dp_size, mp_size, across, moved):
    barrier = pltpu.get_barrier_semaphore()
    for mask in range(1, dp_size):
        pl.semaphore_signal(
            barrier, inc=1, device_id={DP: flip(d, mask)}, device_id_type=MESH
        )
    for mask in range(1, mp_size):
        pl.semaphore_signal(
            barrier, inc=1, device_id={MP: flip(z, mask)}, device_id_type=MESH
        )

    @pl.when(moved)
    def _():
        pl.semaphore_signal(barrier, inc=1, device_id=across, device_id_type=MESH)

    pl.semaphore_wait(barrier, dp_size + mp_size - 2 + jnp.where(moved, 1, 0))


class SpreadWork:
    def __init__(self, plans, order, mp_size, shards, outs, send_sems, recv_sems, own_sems):
        self.plans, self.mp_size = plans, mp_size
        self.order = [step for step in order if not isinstance(step[1], str)]
        self.shards, self.outs = shards, outs
        self.sems = send_sems, recv_sems
        self.own_sems = own_sems
        self.z = lax.axis_index(MP)
        self.d = lax.axis_index(DP)
        self.upper = [dim for dim in plans[0].dims if dim != MP]
        self.index, _ = number(plans, mp_size, spread_single)
        self.owns = []
        self.left = {}
        for t, event in self.order:
            if event[0] < len(plans[t].dims):
                self.left[t, event[1]] = self.left.get((t, event[1]), 0) + 1

    def inside(self, at):
        return (at >= 0) & (at < self.mp_size)

    def region(self, t, mask, block):
        wide, cols = self.shards[t].shape
        rows = pl.ds(place(flip(self.d, mask), wide), wide)
        if block is None:
            return self.outs[t].at[rows, :]
        return self.outs[t].at[rows, pl.ds(place(block, cols), cols)]

    def remote(self, t, event, block, src, dst, to):
        stage, mask, way, at = event
        if way or stage == len(self.plans[t].dims):
            sem = self.index[(t,) + event]
        else:
            sem = self.index[t, stage, mask] + block
        return pltpu.make_async_remote_copy(
            src_ref=src,
            dst_ref=dst,
            send_sem=self.sems[0].at[sem],
            recv_sem=self.sems[1].at[sem],
            device_id=to,
            device_id_type=MESH,
        )

    def sending(self, t, event, block, to, own=False):
        stage, mask, way, at = event
        dims = self.plans[t].dims
        bit = 0 if way else 1 if stage == len(dims) else dims[stage]
        dst = self.region(t, mask ^ bit, block)
        return self.remote(t, event, block, self.shards[t] if own else dst, dst, to)

    def arrival(self, t, event, block):
        dst = self.region(t, event[1], block)
        return self.remote(t, event, block, dst, dst, {DP: self.d, MP: self.z})

    def on_line(self, t, stage, mask, block, way, hops, own):
        @pl.when(self.inside(self.z + way))
        def _():
            to = {MP: self.z + way}
            self.sending(t, (stage, mask, way, hops), block, to, own).start()

    def onward(self, t, stage, mask, block, own=False):
        dims = self.plans[t].dims
        for later in range(stage, len(dims)):
            if dims[later] == MP:
                for way in (1, -1):
                    self.on_line(t, later, mask, block, way, 1, own)
            else:
                to = {DP: flip(self.d, dims[later])}
                self.sending(t, (later, mask | dims[later], 0, None), block, to, own).start()

    def place_of(self, t, event):
        return flip(self.z, event[3]) if self.plans[t].full(event[0]) else self.z

    def begin(self):
        for t in range(len(self.plans)):
            self.onward(t, 0, 0, self.z, True)
            own = pltpu.make_async_copy(
                self.shards[t], self.region(t, 0, self.z), self.own_sems.at[t]
            )
            own.start()
            self.owns.append(own)

    def step(self, t, event):
        stage, mask, way, at = event
        last = len(self.plans[t].dims)
        if stage == last:
            self.arrival(t, event, None).wait_recv()
            return
        if way:
            block = self.z - way * at

            @pl.when(self.inside(block))
            def _():
                self.arrival(t, event, block).wait_recv()
                if at + 1 < self.mp_size:
                    self.on_line(t, stage, mask, block, way, at + 1, False)
                self.onward(t, stage + 1, mask, block)

        else:
            block = self.place_of(t, event)
            self.arrival(t, event, block).wait_recv()
            self.onward(t, stage + 1, mask, block)
        self.left[t, mask] -= 1
        if self.left[t, mask] == 0:
            if mask == 0:
                self.owns[t].wait()
            to = {DP: flip(self.d, 1)}
            self.sending(t, (last, mask | 1, 0, 0), None, to).start()

    def finish(self):
        for t, event in self.order:
            stage, mask, way, at = event
            if stage == len(self.plans[t].dims):
                self.sending(t, event, None, {DP: flip(self.d, 1)}).wait_send()
            elif way:

                @pl.when(self.inside(self.z - way * (at - 1)) & self.inside(self.z + way))
                def _():
                    to = {MP: self.z + way}
                    self.sending(t, event, self.z - way * (at - 1), to).wait_send()

            else:
                to = {DP: flip(self.d, self.plans[t].dims[stage])}
                self.sending(t, event, self.place_of(t, event), to).wait_send()


def spread_kernel(plans, order, mp_size, *refs):
    n = len(plans)
    work = SpreadWork(plans, order, mp_size, refs[:n], refs[n : 2 * n], *refs[2 * n :])
    greet(work.z, work.d, work.upper, mp_size)
    work.begin()
    for t, event in order:
        work.step(t, event)
    work.finish()


def spread_all(shards, plans, order, dp_size, mp_size):
    _, total = number(plans, mp_size, spread_single)
    return pl.pallas_call(
        functools.partial(spread_kernel, plans, order, mp_size),
        out_shape=[
            jax.ShapeDtypeStruct((s.shape[0] * dp_size, s.shape[1] * mp_size), s.dtype)
            for s in shards
        ],
        in_specs=[pl.BlockSpec(memory_space=pl.ANY)] * len(shards),
        out_specs=[pl.BlockSpec(memory_space=pl.ANY)] * len(shards),
        scratch_shapes=[
            pltpu.SemaphoreType.DMA((total,)),
            pltpu.SemaphoreType.DMA((total,)),
            pltpu.SemaphoreType.DMA((len(shards),)),
        ],
        compiler_params=pltpu.CompilerParams(collective_id=0, has_side_effects=True),
    )(*shards)


def fold_kernel(plans, order, mp_size, vector_count, *refs):
    n = len(plans)
    grads, outs = refs[:n], refs[n : 2 * n]
    norm_ref = refs[2 * n]
    landed, sums = refs[2 * n + 1 : 3 * n + 1], refs[3 * n + 1 : 4 * n + 1]
    at = 4 * n + 1
    recv = {}
    for t, plan in enumerate(plans):
        for stage in range(1, len(plan.dims) + 1):
            recv[t, stage] = refs[at]
            at += 1
    staging, tiles, load_sems, own_sems, tile_sems, send_sems, recv_sems = refs[at:]
    z = lax.axis_index(MP)
    d = lax.axis_index(DP)
    upper = [dim for dim in plans[0].dims if dim != MP]
    index, _ = number(plans, mp_size, fold_single)
    wides = [out.shape[0] for out in outs]
    cols = [out.shape[1] for out in outs]

    def inside(at):
        return (at >= 0) & (at < mp_size)

    def rows_of(t, mask):
        return pl.ds(plans[t].masks.index(mask) * wides[t], wides[t])

    def sum_at(t, mask, block):
        return sums[t].at[rows_of(t, mask), pl.ds(place(block, cols[t]), cols[t])]

    def landing(t, event, block):
        stage, mask, way, at = event
        kept = plans[t].kept[stage].index(mask)
        if way:
            return recv[t, stage].at[kept, (0 if way == 1 else mp_size - 1) + at]
        return recv[t, stage].at[kept, block if plans[t].full(stage) else 0]

    def remote(t, event, block, src, dst, to):
        stage, mask, way, at = event
        if way or stage == 0:
            sem = index[(t,) + event]
        else:
            sem = index[t, stage, mask] + block
        return pltpu.make_async_remote_copy(
            src_ref=src,
            dst_ref=dst,
            send_sem=send_sems.at[sem],
            recv_sem=recv_sems.at[sem],
            device_id=to,
            device_id_type=MESH,
        )

    def core_copy(t, mask):
        rows = pl.ds(place(flip(d, mask | 1), wides[t]), wides[t])
        dst = landed[t].at[rows_of(t, mask), :]
        return remote(t, (0, mask, 0, 0), 0, grads[t].at[rows, :], dst, {DP: flip(d, 1)})

    def own_copy(t, mask):
        rows = pl.ds(place(flip(d, mask), wides[t]), wides[t])
        return pltpu.make_async_copy(
            grads[t].at[rows, :],
            sums[t].at[rows_of(t, mask), :],
            own_sems.at[t, plans[t].masks.index(mask)],
        )

    def bit_copy(t, stage, mask, block):
        dim = plans[t].dims[stage - 1]
        event = (stage, mask & ~dim, 0, None)
        dst = landing(t, event, block)
        return remote(t, event, block, sum_at(t, mask, block), dst, {DP: flip(d, dim)})

    def line_copy(t, stage, mask, way, hops):
        event = (stage, mask, way, hops - 1)
        src = sum_at(t, mask, z + way * hops)
        return remote(t, event, None, src, landing(t, event, None), {MP: z + way})

    def arrival(t, event, block):
        dst = landing(t, event, block)
        return remote(t, event, block, dst, dst, {DP: d, MP: z})

    def add(dst, src, wide):
        step = 16

        def some_rows(at, carry):
            rows = pl.ds(pl.multiple_of(at * step, step), step)
            total = dst[rows, :].astype(f32) + src[rows, :].astype(f32)
            dst[rows, :] = total.astype(bf16)
            return carry

        lax.fori_loop(0, wide // step, some_rows, 0)

    def advance(t, stage, mask, block, other):
        if stage > len(plans[t].dims):
            return
        dim = plans[t].dims[stage - 1]
        if dim == MP:
            if other:
                for way, end in ((1, 0), (-1, mp_size - 1)):

                    @pl.when(z == end)
                    def _(way=way):
                        line_copy(t, stage, mask, way, other).start()

        elif mask & dim:
            bit_copy(t, stage, mask, block).start()

    mp_bits = bits_of(mp_size)
    greet(z, d, upper, mp_size, mp_bits)
    cores = [(t, event[1]) for t, event in order if event[0] == 0]
    for t, mask in cores:
        core_copy(t, mask).start()
        own_copy(t, mask).start()

    def load(at):
        t, mask = cores[at]
        return pltpu.make_async_copy(
            landed[t].at[rows_of(t, mask), :],
            staging.at[at % 2, pl.ds(0, wides[t]), pl.ds(0, cols[t] * mp_size)],
            load_sems.at[at % 2],
        )

    seen = 0
    brought = {}
    for t, event in order:
        stage, mask, way, at = event
        plan = plans[t]
        if stage == 0:
            for ahead in (0, 1) if seen == 0 else (seen + 1,):
                if ahead < len(cores):
                    core_copy(*cores[ahead]).wait_recv()
                    load(ahead).start()
            load(seen).wait()
            own_copy(t, mask).wait()
            part = staging.at[seen % 2, pl.ds(0, wides[t]), pl.ds(0, cols[t] * mp_size)]
            add(sums[t].at[rows_of(t, mask), :], part, wides[t])
            seen += 1
            for other in reversed(range(mp_size)):
                advance(t, 1, mask, flip(z, other), other)
        elif way:
            block = z + way * at

            @pl.when(inside(block) & inside(z - way))
            def _():
                arrival(t, event, None).wait_recv()
                add(sum_at(t, mask, block), landing(t, event, None), wides[t])
                if at > 0:
                    line_copy(t, stage, mask, way, at).start()

            if at == 0:
                brought[t, mask] = brought.get((t, mask), 0) + 1
                if brought[t, mask] == 2:
                    advance(t, stage + 1, mask, z, 0)
        else:
            block = flip(z, at) if plan.full(stage) else z
            arrival(t, event, block).wait_recv()
            add(sum_at(t, mask, block), landing(t, event, block), wides[t])
            advance(t, stage + 1, mask, block, at)

    tiles[0] = jnp.zeros(tiles.shape[1:], f32)
    for t in range(n):
        step = 16

        def some_rows(at, carry, t=t):
            rows = pl.ds(pl.multiple_of(at * step, step), step)
            part = sums[t][rows, pl.ds(place(z, cols[t]), cols[t])].astype(f32)
            outs[t][rows, :] = part
            part = part * part
            total = carry
            for low in range(0, step, 8):
                for left in range(0, cols[t], HD):
                    total = total + part[low : low + 8, left : left + HD]
            return total

        if t == n - 1:
            whole = sums[t][pl.ds(0, wides[t]), pl.ds(place(z, cols[t]), cols[t])].astype(f32)
            outs[t][...] = whole
            row = lax.broadcasted_iota(jnp.int32, whole.shape, 0)
            whole = whole * whole
            whole = jnp.where(row < vector_count, whole * (1.0 / mp_size), whole)
            for low in range(0, wides[t], 8):
                tiles[0] += whole[low : low + 8, :HD]
        else:
            zero = jnp.zeros((8, HD), f32)
            tiles[0] += lax.fori_loop(0, wides[t] // step, some_rows, zero)
    pairs = [{DP: flip(d, bit)} for bit in [1] + upper]
    pairs += [{MP: flip(z, bit)} for bit in mp_bits]
    for at, to in enumerate(pairs):
        exchange = pltpu.make_async_remote_copy(
            src_ref=tiles.at[2 * at],
            dst_ref=tiles.at[2 * at + 1],
            send_sem=tile_sems.at[2 * at],
            recv_sem=tile_sems.at[2 * at + 1],
            device_id=to,
            device_id_type=MESH,
        )
        exchange.start()
        exchange.wait()
        tiles[2 * at + 2] = tiles[2 * at] + tiles[2 * at + 1]
    norm_ref[...] = tiles[2 * len(pairs)]

    for t, event in order:
        stage, mask, way, at = event
        if stage == 0:
            core_copy(t, mask).wait_send()
        elif way:

            @pl.when(inside(z + way) & inside(z + way * (at + 1)))
            def _():
                line_copy(t, stage, mask, way, at + 1).wait_send()

        else:
            block = flip(z, at) if plans[t].full(stage) else z
            bit_copy(t, stage, mask | plans[t].dims[stage - 1], block).wait_send()


def fold_all(grads, plans, order, dp_size, mp_size, vector_count):
    n = len(grads)
    _, total = number(plans, mp_size, fold_single)
    wides = [g.shape[0] // dp_size for g in grads]
    cols = [g.shape[1] // mp_size for g in grads]
    rounds = len(bits_of(dp_size)) + len(bits_of(mp_size))
    halves = [(dp_size // 2 * wide, mp_size * each) for wide, each in zip(wides, cols)]
    scratch = [pltpu.VMEM(half, bf16) for half in halves]
    for plan, wide, each in zip(plans, wides, cols):
        for stage, dim in enumerate(plan.dims, 1):
            blocks = 2 * (mp_size - 1) if dim == MP else mp_size if plan.full(stage) else 1
            scratch.append(pltpu.VMEM((len(plan.kept[stage]), blocks, wide, each), bf16))
    scratch += [
        pltpu.VMEM((2, max(wides), mp_size * max(cols)), bf16),
        pltpu.VMEM((2 * rounds + 1, 8, HD), f32),
        pltpu.SemaphoreType.DMA((2,)),
        pltpu.SemaphoreType.DMA((n, dp_size // 2)),
        pltpu.SemaphoreType.DMA((2 * rounds,)),
        pltpu.SemaphoreType.DMA((total,)),
        pltpu.SemaphoreType.DMA((total,)),
    ]
    out = pl.pallas_call(
        functools.partial(fold_kernel, plans, order, mp_size, vector_count),
        out_shape=[jax.ShapeDtypeStruct((wide, each), f32) for wide, each in zip(wides, cols)]
        + [jax.ShapeDtypeStruct((8, HD), f32)]
        + [jax.ShapeDtypeStruct(half, bf16) for half in halves],
        in_specs=[pl.BlockSpec(memory_space=pl.ANY)] * n,
        out_specs=[pl.BlockSpec(memory_space=pltpu.VMEM)] * (n + 1)
        + [pl.BlockSpec(memory_space=pl.ANY)] * n,
        scratch_shapes=scratch,
        compiler_params=pltpu.CompilerParams(
            collective_id=1, has_side_effects=True, vmem_limit_bytes=63 * 2**20
        ),
    )(*grads)
    return list(out[:n]), out[n]


def prepare_kernel(layers, *refs):
    count = 4 * layers + 1
    states, outs = refs[:7], refs[7 : 7 + count]
    held, made = refs[7 + count : 14 + count], refs[14 + count : 14 + 2 * count]
    in_sems, out_sems = refs[14 + 2 * count :]
    loads = [pltpu.make_async_copy(a, b, in_sems.at[at]) for at, (a, b) in enumerate(zip(states, held))]
    for copy in loads:
        copy.start()
    qkv, proj, upper, lower, gains, shifts, bias = held
    stores = [pltpu.make_async_copy(a, b, out_sems.at[at]) for at, (a, b) in enumerate(zip(made, outs))]
    for kind in range(4):
        loads[kind].wait()
        for layer in range(layers):
            out = made[4 * layer + kind]
            if kind == 0:
                cols = qkv.shape[3]
                for part in range(3):
                    out[:, part * cols : (part + 1) * cols] = qkv[layer, part].astype(bf16)
            elif kind == 2:
                for low in range(0, upper.shape[2], 256):
                    out[:, low : low + 256] = upper[layer, :, low : low + 256].astype(bf16)
            else:
                from_ref = proj if kind == 1 else lower
                for low in range(0, from_ref.shape[1], HD):
                    out[:, low : low + HD] = from_ref[layer, low : low + HD, :].T.astype(bf16)
            stores[4 * layer + kind].start()
    for copy in loads[4:]:
        copy.wait()
    small = made[-1]
    rows = [gains[layer] for layer in range(layers)]
    rows += [shifts[:, layer] for layer in range(layers)] + [bias[...]]
    used = sum(each.shape[0] for each in rows)
    rows.append(jnp.zeros((small.shape[0] - used, small.shape[1]), f32))
    small[...] = jnp.concatenate(rows, axis=0).astype(bf16)
    stores[-1].start()
    for copy in stores:
        copy.wait()


def prepare_all(states, small_rows):
    qkv, proj, upper, lower = states[:4]
    layers = qkv.shape[0]
    wide = upper.shape[1]
    each = [3 * qkv.shape[3], proj.shape[1], upper.shape[2], lower.shape[1]] * layers
    shapes = [(wide, cols) for cols in each] + [(small_rows, wide)]
    any_place = pl.BlockSpec(memory_space=pl.ANY)
    return pl.pallas_call(
        functools.partial(prepare_kernel, layers),
        out_shape=[jax.ShapeDtypeStruct(shape, bf16) for shape in shapes],
        in_specs=[any_place] * 7,
        out_specs=[any_place] * len(shapes),
        scratch_shapes=[pltpu.VMEM(state.shape, f32) for state in states]
        + [pltpu.VMEM(shape, bf16) for shape in shapes]
        + [pltpu.SemaphoreType.DMA((7,)), pltpu.SemaphoreType.DMA((len(shapes),))],
        compiler_params=pltpu.CompilerParams(vmem_limit_bytes=56 * 2**20),
    )(*states)


def adam_kernel(streams, vector_count, gain_rows, *refs):
    ins = 31 + 2 * streams
    news = 22 + streams
    sources, outs = refs[:ins], refs[ins : ins + news]
    held, made = refs[ins + news : 2 * ins + news], refs[2 * ins + news : 2 * (ins + news)]
    in_sems, out_sems = refs[2 * (ins + news) :]
    loads = [
        pltpu.make_async_copy(a, b, in_sems.at[at]) for at, (a, b) in enumerate(zip(sources, held))
    ]
    stores = [pltpu.make_async_copy(a, b, out_sems.at[at]) for at, (a, b) in enumerate(zip(made, outs))]
    order = []
    for group in range(4):
        order += [2 * group, 2 * group + 1] + [8 + 3 * group + which for which in range(3)]
    for at in [21, 20] + order + list(range(22, ins)):
        loads[at].start()
    loads[21].wait()
    norm = jnp.sqrt(jnp.sum(held[21][...], keepdims=True))
    made[21][...] = jnp.broadcast_to(norm, made[21].shape)
    stores[21].start()
    factor = jnp.minimum(1.0, clip_bound / norm)

    def update(group, at, gradient):
        found = [held[8 + 3 * group + which][at] for which in range(3)]
        new = adam_update(
            *found, gradient.astype(f32), factor, group_rates[group], group_decays[group]
        )
        for which in range(3):
            made[3 * group + which][at] = new[which]

    for group in range(4):
        for at in order[5 * group : 5 * group + 5]:
            loads[at].wait()
        for layer, gradient in enumerate((held[2 * group + 1], held[2 * group])):
            if group == 0:
                wide, cols = gradient.shape[0], gradient.shape[1] // 3
                for part in range(3):
                    for low in range(0, wide, 64):
                        update(
                            0,
                            (layer, part, slice(low, low + 64)),
                            gradient[low : low + 64, part * cols : (part + 1) * cols],
                        )
            elif group == 2:
                for low in range(0, gradient.shape[0], 16):
                    update(2, (layer, slice(low, low + 16)), gradient[low : low + 16, :])
            else:
                for low in range(0, gradient.shape[1], HD):
                    part = gradient[:, low : low + HD].astype(f32).T
                    update(group, (layer, slice(low, low + HD)), part)
        for which in range(3):
            stores[3 * group + which].start()
    loads[20].wait()
    small = held[20][...].astype(f32)
    for group in range(3):
        for which in range(3):
            loads[22 + 3 * group + which].wait()
        for layer in range(2):
            if group == 0:
                at = (slice(layer, layer + 1),)
                first = vector_count + layer
            elif group == 1:
                at = (layer,)
                first = layer * gain_rows
            else:
                at = (slice(None), layer)
                first = 2 * gain_rows + layer * held[28].shape[0]
            found = [held[22 + 3 * group + which][at] for which in range(3)]
            part = small[first : first + found[0].shape[0]]
            new = adam_update(*found, part, factor, group_rates[4 + group], group_decays[4 + group])
            for which in range(3):
                made[12 + 3 * group + which][at] = new[which]
        for which in range(3):
            stores[12 + 3 * group + which].start()
    moved = lax.axis_index(DP) % 2 != lax.axis_index(MP) % 2
    for at in range(streams):
        for which in range(2):
            loads[31 + 2 * at + which].wait()
        ours, others = held[31 + 2 * at : 33 + 2 * at]
        for low in range(0, ours.shape[0], 64):
            rows = slice(low, low + 64)
            values = jnp.where(moved, others[rows, :].astype(f32), ours[rows, :])
            made[22 + at][rows, :] = values
        stores[22 + at].start()
    for copy in stores:
        copy.wait()


def adam_all(gradients, states, small, norm_tile, small_states, streams, vector_count, gain_rows):
    any_place = pl.BlockSpec(memory_space=pl.ANY)
    operands = list(gradients) + list(states) + [small, norm_tile] + list(small_states)
    operands += streams
    shapes = [each.shape for each in list(states) + list(small_states)] + [(8, HD)]
    shapes += [each.shape for each in streams[::2]]
    news = [jax.ShapeDtypeStruct(shape, f32) for shape in shapes]
    return pl.pallas_call(
        functools.partial(adam_kernel, len(streams) // 2, vector_count, gain_rows),
        out_shape=news,
        in_specs=[any_place] * len(operands),
        out_specs=[any_place] * len(news),
        scratch_shapes=[pltpu.VMEM(each.shape, each.dtype) for each in operands + news]
        + [
            pltpu.SemaphoreType.DMA((len(operands),)),
            pltpu.SemaphoreType.DMA((len(news),)),
        ],
        compiler_params=pltpu.CompilerParams(vmem_limit_bytes=60 * 2**20),
    )(*operands)


ROWS = 64
SAVED = 9
TILE = 256


def norm_rows(src, dst, low, gain, shift):
    def some_rows(at, carry):
        rows = pl.ds(pl.multiple_of(at * ROWS, ROWS), ROWS)
        values = src[rows, :]
        low[rows, :] = values.astype(bf16)
        dst[rows, :] = layer_norm(values, gain, shift).astype(bf16)
        return carry

    lax.fori_loop(0, src.shape[0] // ROWS, some_rows, 0)


def tiles_of(width, body):
    def one(at, carry):
        body(pl.multiple_of(at * TILE, TILE))
        return carry

    lax.fori_loop(0, width // TILE, one, 0)


def block_scores(query, key, slope, doc_col, doc_row, first_col, diagonal):
    cols = first_col + lax.broadcasted_iota(jnp.int32, (1, key.shape[0]), 1)
    scores = dot_cols(query, key) * score_scale + slope * cols.astype(f32)
    allowed = doc_col == doc_row
    if diagonal:
        row = lax.broadcasted_iota(jnp.int32, scores.shape, 0)
        col = lax.broadcasted_iota(jnp.int32, scores.shape, 1)
        allowed = allowed & (row >= col)
    return jnp.where(allowed, scores, masked_score)


def lane_of(values, lane):
    return lax.broadcasted_iota(jnp.int32, values.shape, 1) == lane


def head_slope(slot, inner, slots, heads_slot, core):
    slope = 0.5 ** (slot * heads_slot + 1.0)
    for later in range(1, heads_slot):
        slope = jnp.where(inner == later, 0.5 ** (slot * heads_slot + later + 1.0), slope)
    return slope * jnp.where(core == 0, 1.0, 0.5 ** (slots * heads_slot))


def attend_head(qkv, out, logs, head, at, width, slope, doc_cols, doc_rows):
    query_cols, key_cols, value_cols = (
        pl.ds(pl.multiple_of(at + part * width, HD), HD) for part in range(3)
    )
    length = qkv.shape[0]
    block = min(256, length)
    for first_row in range(0, length, block):
        rows = slice(first_row, first_row + block)
        low, high = key_range(first_row, block)
        blocks = [slice(first, first + block) for first in range(low, high, block)]
        query = qkv[rows, query_cols]
        scores = [
            block_scores(
                query, qkv[cols, key_cols], slope, doc_cols[rows, :],
                doc_rows[:, cols], cols.start, cols == rows,
            )
            for cols in blocks
        ]
        top = scores[0]
        for each in scores[1:]:
            top = jnp.maximum(top, each)
        top = jnp.max(top, axis=-1, keepdims=True)
        total, mixed = 0.0, 0.0
        for cols, each in zip(blocks, scores):
            shifted = jnp.exp(each - top)
            total = total + jnp.sum(shifted, axis=-1, keepdims=True)
            mixed = mixed + dot(shifted.astype(bf16), qkv[cols, value_cols])
        to = pl.ds(pl.multiple_of(head * HD, HD), HD)
        out[rows, to] = (mixed * (1.0 / total)).astype(bf16)
        logs[rows, :] = jnp.where(lane_of(logs[rows, :], head), top + jnp.log(total), logs[rows, :])


FORWARD_STEPS = (
    ("norm_one", "other_0", "other_1", "own_0", "own_1", "share")
    + ("head_0", "head_1")
    + ("back", "proj", "norm_two")
    + tuple(f"up_{at}" for at in range(8))
    + tuple(f"down_{at}" for at in range(4))
)


def forward_kernel(plans, order, mp_size, layers, vector_count, gain_rows, shift_rows, *refs):
    n = len(plans)
    shards = refs[:n]
    inputs, cotangent, doc_cols, doc_rows = refs[n : n + 4]
    outs = refs[n + 4 : 2 * n + 4]
    at = 2 * n + 4
    saved = [refs[at + SAVED * layer : at + SAVED * (layer + 1)] for layer in range(layers)]
    at += SAVED * layers
    last_stream, last_low, cotangent_out, vectors = refs[at : at + 4]
    (
        streams, middles, lows, normed_one, normed_two, send_buf, qkv_full, mixed, logs, attended,
        hidden, active, w_qkv, w_proj, w_up, w_down, small_buf, biases, traded,
        load_sems, save_sems, trade_sems, head_sems, send_sems, recv_sems, own_sems,
    ) = refs[at + 4 :]
    work = SpreadWork(plans, order, mp_size, shards, outs, send_sems, recv_sems, own_sems)
    z, d = work.z, work.d
    core = d % 2
    moved = core != z % 2
    partner = {DP: flip(d, 1)}
    across = {DP: flip(d, 1), MP: flip(z, 1)}
    tokens = inputs.shape[0]
    features = inputs.shape[1]
    half = attended.shape[2] // 2
    wide_small = shards[-1].shape[0]
    lanes = shards[-1].shape[1]
    third = w_qkv.shape[2] // 3
    slots = qkv_full.shape[2] // w_qkv.shape[2]
    heads_slot = third // HD

    greet(z, d, work.upper, mp_size, (), across, moved)
    trade = pltpu.make_async_remote_copy(
        src_ref=inputs, dst_ref=traded, send_sem=trade_sems.at[0], recv_sem=trade_sems.at[1],
        device_id=across, device_id_type=MESH,
    )
    keep = pltpu.make_async_copy(inputs, traded, trade_sems.at[2])
    trade_back = pltpu.make_async_remote_copy(
        src_ref=cotangent, dst_ref=cotangent_out, send_sem=trade_sems.at[3],
        recv_sem=trade_sems.at[4], device_id=across, device_id_type=MESH,
    )
    keep_back = pltpu.make_async_copy(cotangent, cotangent_out, trade_sems.at[5])

    work.begin()

    @pl.when(moved)
    def _():
        trade.start()

    @pl.when(jnp.logical_not(moved))
    def _():
        keep.start()

    saves = []

    def save(src, dst):
        copy = pltpu.make_async_copy(src, dst, save_sems.at[len(saves)])
        copy.start()
        saves.append(copy)
        return copy

    loads = {}

    def load(key, src, dst, slot):
        copy = pltpu.make_async_copy(src, dst, load_sems.at[slot])
        copy.start()
        loads[key] = copy

    def load_tile(layer, kind, at):
        full = outs[4 * layer : 4 * layer + 4]
        if kind == "qkv":
            cols = w_qkv.shape[2]
            first = (1 - core) * slots if at < slots else core * slots
            where = pl.ds(place(first + at % slots, cols), cols)
            load((layer, kind, at), full[0].at[:, where], w_qkv.at[at % 2], at % 2)
        elif kind == "proj":
            load((layer, kind, at), full[1], w_proj, 2)
        elif kind == "up":
            cols = w_up.shape[2]
            where = pl.ds(at * cols, cols)
            load((layer, kind, at), full[2].at[:, where], w_up.at[at % 2], 3 + at % 2)
        else:
            load((layer, kind, at), full[3].at[pair_of(at), :], w_down.at[at % 2], 5 + at % 2)

    def pair_of(at):
        rows = w_down.shape[1]
        return pl.ds(place(flip(d // 2, at), rows), rows)

    def tile(layer, kind, at, count):
        if (layer, kind, at) not in loads:
            load_tile(layer, kind, at)
        loads[layer, kind, at].wait()
        ready = kind != "down" or (4 * layer + 3, 2 * at + 2) in complete
        if at + 1 < count and ready:
            load_tile(layer, kind, at + 1)

    def share_copy(layer):
        rows = pl.ds(place(core, tokens), tokens)
        return pltpu.make_async_remote_copy(
            src_ref=send_buf.at[layer], dst_ref=qkv_full.at[layer, rows, :],
            send_sem=head_sems.at[4 * layer], recv_sem=head_sems.at[4 * layer + 1],
            device_id=partner, device_id_type=MESH,
        )

    def back_copy(layer):
        rows = pl.ds(place(1 - core, tokens), tokens)
        return pltpu.make_async_remote_copy(
            src_ref=mixed.at[layer, rows, :],
            dst_ref=attended.at[layer, :, pl.ds(place(core, half), half)],
            send_sem=head_sems.at[4 * layer + 2], recv_sem=head_sems.at[4 * layer + 3],
            device_id=partner, device_id_type=MESH,
        )

    def active_copy(layer):
        rows = pl.ds(place(core, tokens), tokens)
        return pltpu.make_async_remote_copy(
            src_ref=active, dst_ref=saved[layer][7].at[rows, :],
            send_sem=head_sems.at[4 * layers + 2 * layer],
            recv_sem=head_sems.at[4 * layers + 2 * layer + 1],
            device_id=partner, device_id_type=MESH,
        )

    def vector(at):
        return vectors[at : at + 1, :]

    ahead = {
        "norm_one": ("qkv", 0), "head_0": ("proj", 1), "proj": ("up", 2), "up_6": ("down", 3)
    }

    def compute(layer, name):
        kind, _, at = name.partition("_")
        if name in ahead and 4 * layer + ahead[name][1] not in missing:
            load_tile(layer, ahead[name][0], 0)
        gain = layer * gain_rows
        shift = layers * gain_rows + layer * shift_rows
        keeps = saved[layer]
        if name == "norm_one":
            if layer == 0:
                small = pltpu.make_async_copy(outs[-1], small_buf, load_sems.at[7])
                small.start()

                @pl.when(moved)
                def _():
                    trade.wait_recv()

                @pl.when(jnp.logical_not(moved))
                def _():
                    keep.wait()

                streams[0] = traded[...].astype(f32)
                small.wait()
                for b in range(outs[-1].shape[0] // wide_small):
                    rows = small_buf[b * wide_small : (b + 1) * wide_small, :].astype(f32)
                    vectors[:, b * lanes : (b + 1) * lanes] = rows[:, :lanes]
                    for m in range(mp_size):
                        first = m * (biases.shape[1] // mp_size) + b * lanes
                        biases[:, first : first + lanes] = rows[:, m * lanes : (m + 1) * lanes]
            norm_rows(
                streams.at[layer], normed_one.at[layer], lows.at[2 * layer],
                vector(gain), vector(shift),
            )
            save(lows.at[2 * layer], keeps[0])
            save(normed_one.at[layer], keeps[2])
        elif kind in ("other", "own"):
            at = int(at)
            tile(layer, "qkv", at + (slots if kind == "own" else 0), 2 * slots)
            weight = w_qkv.at[at % 2]
            cols = w_qkv.shape[2]

            def piece(first):
                values = dot(normed_one[layer], weight[:, pl.ds(first, TILE)]).astype(bf16)
                to = pl.ds(pl.multiple_of(at * cols + first, TILE), TILE)
                if kind == "own":
                    qkv_full[layer, pl.ds(place(core, tokens), tokens), to] = values
                else:
                    send_buf[layer, :, to] = values

            tiles_of(cols, piece)
            if kind == "other" and at == slots - 1:
                share_copy(layer).start()
        elif kind == "share":
            arrived = pltpu.make_async_remote_copy(
                src_ref=send_buf.at[layer],
                dst_ref=qkv_full.at[layer, pl.ds(place(1 - core, tokens), tokens), :],
                send_sem=head_sems.at[4 * layer], recv_sem=head_sems.at[4 * layer + 1],
                device_id=partner, device_id_type=MESH,
            )
            arrived.wait_recv()
            save(qkv_full.at[layer], keeps[3])
        elif kind == "head":
            slot = int(at)
            if slot == 0:
                logs[layer] = jnp.zeros(logs.shape[1:], f32)

            def one_head(inner, carry):
                attend_head(
                    qkv_full.at[layer], mixed.at[layer], logs.at[layer], slot * heads_slot + inner,
                    slot * 3 * third + inner * HD, third,
                    head_slope(slot, inner, slots, heads_slot, core), doc_cols, doc_rows,
                )
                return carry

            lax.fori_loop(0, heads_slot, one_head, 0)
            if slot == slots - 1:
                back_copy(layer).start()
                rows = pl.ds(place(core, tokens), tokens)
                attended[layer, :, pl.ds(place(core, half), half)] = mixed[layer, rows, :]
                save(mixed.at[layer], keeps[4])
                save(logs.at[layer], keeps[8])
        elif kind == "back":
            arrived = pltpu.make_async_remote_copy(
                src_ref=mixed.at[layer, pl.ds(0, tokens), :],
                dst_ref=attended.at[layer, :, pl.ds(place(1 - core, half), half)],
                send_sem=head_sems.at[4 * layer + 2], recv_sem=head_sems.at[4 * layer + 3],
                device_id=partner, device_id_type=MESH,
            )
            arrived.wait_recv()
        elif kind == "proj":
            tile(layer, "proj", 0, 1)

            def piece(first):
                cols = pl.ds(first, TILE)
                values = dot_cols(attended[layer], w_proj[cols, :])
                middles[layer, :, cols] = streams[layer, :, cols] + values

            tiles_of(features, piece)
        elif name == "norm_two":
            norm_rows(
                middles.at[layer], normed_two.at[layer], lows.at[2 * layer + 1],
                vector(gain + 1), vector(shift + 1),
            )
            save(lows.at[2 * layer + 1], keeps[1])
            save(normed_two.at[layer], keeps[5])
        elif kind == "up":
            at = int(at)
            if at == 0 and layer == layers - 1:
                pl.when(moved)(trade_back.start)
                pl.when(jnp.logical_not(moved))(keep_back.start)
            if at == 0 and layer > 0:
                for copy in big_saves[layer - 1]:
                    copy.wait()
                active_copy(layer - 1).wait_send()
            cols = w_up.shape[2]
            tile(layer, "up", at, hidden.shape[1] // cols)
            weight = w_up.at[at % 2]

            def piece(first):
                to = pl.ds(pl.multiple_of(at * cols + first, TILE), TILE)
                bias = biases[vector_count + layer : vector_count + layer + 1, to]
                values = dot(normed_two[layer], weight[:, pl.ds(first, TILE)]) + bias
                hidden[:, to] = values.astype(bf16)
                active[:, to] = gelu_tanh(values).astype(bf16)

            tiles_of(cols, piece)
            if (at + 1) * cols == hidden.shape[1]:
                rows = pl.ds(place(core, tokens), tokens)
                big_saves[layer] = [save(hidden, keeps[6]), save(active, keeps[7].at[rows, :])]
                active_copy(layer).start()
        elif kind == "down":
            at = int(at)
            tile(layer, "down", at, features // w_down.shape[1])
            weight = w_down.at[at % 2]
            out = streams.at[layer + 1]
            cols = pair_of(at)
            out[:, cols] = middles[layer, :, cols] + vectors[shift + 2 : shift + 3, cols]

            def piece(step, carry):
                inner = pl.ds(pl.multiple_of(step * 1024, 1024), 1024)
                out[:, cols] += dot_cols(active[:, inner], weight[:, inner])
                return carry

            lax.fori_loop(0, hidden.shape[1] // 1024, piece, 0)

    big_saves = {}
    missing = {}
    complete = set()
    for t, _ in work.order:
        missing[t] = missing.get(t, 0) + 1
    for step in order:
        if isinstance(step[1], str):
            compute(*step)
        else:
            work.step(*step)
            if step[1][0] == len(plans[step[0]].dims):
                complete.add((step[0], step[1][1] - 1))
            missing[step[0]] -= 1
            if missing[step[0]] == 0:
                del missing[step[0]]
    save(streams.at[layers], last_stream)
    traded[...] = streams[layers].astype(bf16)
    save(traded, last_low)
    done_already = [id(copy) for layer in range(layers - 1) for copy in big_saves[layer]]
    for copy in saves:
        if id(copy) not in done_already:
            copy.wait()
    for layer in range(layers):
        share_copy(layer).wait_send()
        back_copy(layer).wait_send()
        rows = pl.ds(place(1 - core, tokens), tokens)
        pltpu.make_async_remote_copy(
            src_ref=active, dst_ref=saved[layer][7].at[rows, :],
            send_sem=head_sems.at[4 * layers + 2 * layer],
            recv_sem=head_sems.at[4 * layers + 2 * layer + 1],
            device_id=partner, device_id_type=MESH,
        ).wait_recv()
    active_copy(layers - 1).wait_send()

    @pl.when(moved)
    def _():
        trade.wait_send()
        trade_back.wait()

    @pl.when(jnp.logical_not(moved))
    def _():
        keep_back.wait()

    work.finish()


def forward_all(
    shards, inputs, cotangent, docs, plans, order, dp_size, mp_size, layers, vector_count, gain_rows, shift_rows
):
    _, total = number(plans, mp_size, spread_single)
    tokens, features = inputs.shape
    length = docs.shape[0]
    half = features // 2
    units = shards[2].shape[1] * mp_size
    cols = shards[0].shape[1]
    slots = mp_size // 2
    any_place = pl.BlockSpec(memory_space=pl.ANY)
    vmem = pl.BlockSpec(memory_space=pltpu.VMEM)
    saved = [
        jax.ShapeDtypeStruct((tokens, features), bf16),
        jax.ShapeDtypeStruct((tokens, features), bf16),
        jax.ShapeDtypeStruct((tokens, features), bf16),
        jax.ShapeDtypeStruct((length, slots * cols), bf16),
        jax.ShapeDtypeStruct((length, half), bf16),
        jax.ShapeDtypeStruct((tokens, features), bf16),
        jax.ShapeDtypeStruct((tokens, units), bf16),
        jax.ShapeDtypeStruct((length, units), bf16),
        jax.ShapeDtypeStruct((length, HD), f32),
    ]
    small_shape = (shards[-1].shape[0] * dp_size, shards[-1].shape[1] * mp_size)
    out_shape = [
        jax.ShapeDtypeStruct((s.shape[0] * dp_size, s.shape[1] * mp_size), s.dtype)
        for s in shards
    ]
    out_shape += saved * layers + [
        jax.ShapeDtypeStruct((tokens, features), f32),
        jax.ShapeDtypeStruct((tokens, features), bf16),
        jax.ShapeDtypeStruct((tokens, features), bf16),
    ]
    out_shape.append(jax.ShapeDtypeStruct((shards[-1].shape[0], features), f32))
    out = pl.pallas_call(
        functools.partial(
            forward_kernel, plans, order, mp_size, layers, vector_count, gain_rows, shift_rows
        ),
        out_shape=out_shape,
        in_specs=[any_place] * (len(shards) + 2) + [vmem] * 2,
        out_specs=[any_place] * (len(out_shape) - 1) + [vmem],
        scratch_shapes=[
            pltpu.VMEM((layers + 1, tokens, features), f32),
            pltpu.VMEM((layers, tokens, features), f32),
            pltpu.VMEM((2 * layers, tokens, features), bf16),
            pltpu.VMEM((layers, tokens, features), bf16),
            pltpu.VMEM((layers, tokens, features), bf16),
            pltpu.VMEM((layers, tokens, slots * cols), bf16),
            pltpu.VMEM((layers, length, slots * cols), bf16),
            pltpu.VMEM((layers, length, half), bf16),
            pltpu.VMEM((layers, length, HD), f32),
            pltpu.VMEM((layers, tokens, features), bf16),
            pltpu.VMEM((tokens, units), bf16),
            pltpu.VMEM((tokens, units), bf16),
            pltpu.VMEM((2, features, cols), bf16),
            pltpu.VMEM((features, features), bf16),
            pltpu.VMEM((2, features, units // 8), bf16),
            pltpu.VMEM((2, features // 4, units), bf16),
            pltpu.VMEM(small_shape, bf16),
            pltpu.VMEM((shards[-1].shape[0], units), f32),
            pltpu.VMEM((tokens, features), bf16),
            pltpu.SemaphoreType.DMA((8,)),
            pltpu.SemaphoreType.DMA((SAVED * layers + 2,)),
            pltpu.SemaphoreType.DMA((6,)),
            pltpu.SemaphoreType.DMA((6 * layers,)),
            pltpu.SemaphoreType.DMA((total,)),
            pltpu.SemaphoreType.DMA((total,)),
            pltpu.SemaphoreType.DMA((len(shards),)),
        ],
        compiler_params=pltpu.CompilerParams(
            collective_id=2, has_side_effects=True, vmem_limit_bytes=62 * 2**20
        ),
    )(*shards, inputs, cotangent, docs.reshape(-1, 1), docs.reshape(1, -1))
    n = len(shards)
    stored = [out[n + SAVED * at : n + SAVED * (at + 1)] for at in range(layers)]
    return out[:n], stored, *out[-4:]


KINDS = ("down", "up", "proj", "qkv")
BACKWARD_STEPS = (
    "turn_down", "W0", "W1", "W2", "W3",
    "turn_up", "hidden_0", "hidden_1", "hidden_2", "hidden_3", "W0",
    "hidden_4", "hidden_5", "W1", "hidden_6", "hidden_7", "norm_two", "mixed_0", "mixed_1",
    "W2", "W3", "turn_proj", "W0", "W1", "W2", "W3", "turn_qkv",
    "share", "head_0", "head_1", "rows_0", "rows_1", "rows_2",
    "back", "W0", "W1", "W2", "W3", "rows_3", "rows_4", "rows_5", "norm_one",
)


def gelu_slope(v):
    root = math.sqrt(2.0 / math.pi)
    t = jnp.tanh(root * (v + 0.044715 * v * v * v))
    return 0.5 * (1.0 + t) + 0.5 * v * (1.0 - t * t) * root * (1.0 + 3 * 0.044715 * v * v)


def norm_back(src, upstream, total, low, gain):
    features = src.shape[1]

    def some_rows(at, carry):
        rows = pl.ds(pl.multiple_of(at * ROWS, ROWS), ROWS)
        value = src[rows, :].astype(f32)
        center = value - jnp.mean(value, axis=-1, keepdims=True)
        scale = lax.rsqrt(jnp.mean(center * center, axis=-1, keepdims=True) + norm_eps)
        normal = center * scale
        grad = upstream[rows, :]
        inner = grad * gain
        mean_inner = jnp.mean(inner, axis=-1, keepdims=True)
        mean_both = jnp.mean(inner * normal, axis=-1, keepdims=True)
        new = total[rows, :] + scale * (inner - mean_inner - normal * mean_both)
        total[rows, :] = new
        low[rows, :] = new.astype(bf16)
        return (
            carry[0] + jnp.sum(grad * normal, axis=0, keepdims=True),
            carry[1] + jnp.sum(grad, axis=0, keepdims=True),
            carry[2] + jnp.sum(new, axis=0, keepdims=True),
        )

    zero = jnp.zeros((1, features), f32)
    return lax.fori_loop(0, src.shape[0] // ROWS, some_rows, (zero, zero, zero))


def attend_back_head(
    qkv, mixed, mixed_grad, logs, key_acc, value_acc, head, at, width, slope, doc_cols, doc_rows
):
    length = qkv.shape[0]
    block = min(256, length)
    key_acc[...] = jnp.zeros_like(key_acc)
    value_acc[...] = jnp.zeros_like(value_acc)
    query_cols, key_cols, value_cols = (
        pl.ds(pl.multiple_of(at + part * width, HD), HD) for part in range(3)
    )
    mine = pl.ds(pl.multiple_of(head * HD, HD), HD)
    for first_row in range(0, length, block):
        rows = slice(first_row, first_row + block)
        low, high = key_range(first_row, block)
        query = qkv[rows, query_cols]
        out_grad = mixed_grad[rows, mine]
        values = mixed[rows, mine]
        inner = jnp.sum(out_grad.astype(f32) * values.astype(f32), axis=-1, keepdims=True)
        log = logs[rows, :]
        log = jnp.sum(jnp.where(lane_of(log, head), log, 0.0), axis=-1, keepdims=True)
        query_grad = 0.0
        for first in range(low, high, block):
            cols = slice(first, first + block)
            key = qkv[cols, key_cols]
            scores = block_scores(
                query, key, slope, doc_cols[rows, :], doc_rows[:, cols], first, first == first_row
            )
            probs = jnp.exp(scores - log)
            value_acc[cols, :] += dot_rows(probs.astype(bf16), out_grad)
            prob_grad = dot_cols(out_grad, qkv[cols, value_cols])
            score_grad = (probs * (prob_grad - inner)).astype(bf16)
            query_grad = query_grad + dot(score_grad, key)
            key_acc[cols, :] += dot_rows(score_grad, query)
        qkv[rows, query_cols] = (query_grad * score_scale).astype(bf16)
    qkv[:, key_cols] = (key_acc[...] * score_scale).astype(bf16)
    qkv[:, value_cols] = value_acc[...].astype(bf16)


def flip_by(value, at, size):
    out = 0
    for bit in bits_of(size):
        one = (value // bit) % 2
        out = out + bit * (1 - one if at & bit else one)
    return out


class Rows:
    def __init__(self, dims, mp_size, merged=False):
        self.dims = tuple(dims)
        self.merged = merged
        self.masks = [0]
        for dim in reversed([dim for dim in self.dims if dim != MP]):
            self.masks = self.masks + [mask | dim for mask in self.masks]
        self.kept = {0: len(self.masks)}
        self.events = []
        for stage, dim in enumerate(self.dims, 1):
            self.kept[stage] = self.kept[stage - 1] // (1 if dim == MP else 2)
            if dim == MP:
                for hops in reversed(range(mp_size - 1)):
                    self.events += [(stage, way, hops) for way in (1, -1)]
            else:
                count = mp_size if self.full(stage) and not merged else 1
                self.events += [(stage, 0, at) for at in range(count)]

    def full(self, stage):
        return MP not in self.dims[: stage - 1]


def number_rows(plans, mp_size):
    index, total = {}, 0
    for t, plan in enumerate(plans):
        for stage, way, at in plan.events:
            if way:
                index[t, stage, way, at] = total
                total += 1
            elif (t, stage) not in index:
                index[t, stage] = total
                total += mp_size
    return index, total


class RowsWork:
    def __init__(self, plans, mp_size, wides, cols, sums, recv, sems):
        self.plans, self.mp_size = plans, mp_size
        self.wides, self.cols = wides, cols
        self.sums, self.recv = sums, recv
        self.send_sems, self.recv_sems, self.credit_sems = sems
        self.z = lax.axis_index(MP)
        self.d = lax.axis_index(DP)
        self.index, _ = number_rows(plans, mp_size)
        self.brought = {}
        self.credited = set()
        self.outgoing = {}
        self.left, self.left_stage = {}, {}
        for t, plan in enumerate(plans):
            self.left[t] = len(plan.events)
            for event in plan.events:
                key = t, event[0]
                self.left_stage[key] = self.left_stage.get(key, 0) + 1

    def inside(self, at):
        return (at >= 0) & (at < self.mp_size)

    def slab(self, t):
        return t % 4 if t < 8 else 4

    def part(self, t, low, high, block):
        wide, cols = self.wides[t], self.cols[t]
        where = pl.ds(0, cols * self.mp_size) if block is None else pl.ds(place(block, cols), cols)
        return self.sums[self.slab(t)].at[pl.ds(low * wide, (high - low) * wide), where]

    def landing(self, t, event, block):
        stage, way, at = event
        ref = self.recv[self.slab(t), stage]
        if way:
            return ref.at[block if way == 1 or at > 0 else self.mp_size]
        if block is None:
            return ref.at[0]
        return ref.at[block if self.plans[t].full(stage) else 0]

    def remote(self, t, event, block, src, dst, to):
        stage, way, at = event
        if way:
            sem = self.index[(t,) + event]
        else:
            sem = self.index[t, stage] + (0 if block is None else block)
        return pltpu.make_async_remote_copy(
            src_ref=src,
            dst_ref=dst,
            send_sem=self.send_sems.at[sem],
            recv_sem=self.recv_sems.at[sem],
            device_id=to,
            device_id_type=MESH,
        )

    def launch(self, t, copy, when=None):
        if when is None:
            copy.start()
        else:
            pl.when(when)(copy.start)
        self.outgoing.setdefault(t, []).append((copy, when))

    def settle(self, t):
        for copy, when in self.outgoing.pop(t, []):
            if when is None:
                copy.wait_send()
            else:
                pl.when(when)(copy.wait_send)

    def take_credit(self, t, stage, way=0):
        if not 4 <= t < 8 or (t, stage, way) in self.credited:
            return
        self.credited.add((t, stage, way))
        sem = self.credit_sems.at[t - 4, stage, 1 if way == -1 else 0]
        if way:
            pl.when(self.inside(self.z + way))(lambda: pl.semaphore_wait(sem, 1))
        else:
            pl.semaphore_wait(sem, 1)

    def give_credit(self, t, stage):
        dim = self.plans[t + 4].dims[stage - 1]
        if dim != MP:
            pl.semaphore_signal(
                self.credit_sems.at[t, stage, 0], inc=1,
                device_id={DP: flip(self.d, dim)}, device_id_type=MESH,
            )
            return
        for way in (1, -1):

            @pl.when(self.inside(self.z - way))
            def _(way=way):
                pl.semaphore_signal(
                    self.credit_sems.at[t, stage, 1 if way == -1 else 0], inc=1,
                    device_id={MP: self.z - way}, device_id_type=MESH,
                )

    def line_copy(self, t, stage, way, hops):
        event = (stage, way, hops - 1)
        block = self.z + way * hops
        dst = self.landing(t, event, block)
        src = self.part(t, 0, self.plans[t].kept[stage], block)
        return self.remote(t, event, block, src, dst, {MP: self.z + way})

    def arrival(self, t, event, block):
        dst = self.landing(t, event, block)
        return self.remote(t, event, block, dst, dst, {DP: self.d, MP: self.z})

    def add(self, dst, src, rows_count):
        step = 16

        def some_rows(at, carry):
            rows = pl.ds(pl.multiple_of(at * step, step), step)
            dst[rows, :] += src[rows, :]
            return carry

        lax.fori_loop(0, rows_count // step, some_rows, 0)

    def advance(self, t, stage, block, other):
        plan = self.plans[t]
        if stage > len(plan.dims):
            return
        dim = plan.dims[stage - 1]
        if dim == MP:
            for way, end in ((1, 0), (-1, self.mp_size - 1)):
                self.take_credit(t, stage, way)
                for hops in range(1, self.mp_size) if block is None else (other,) * (other > 0):
                    copy = self.line_copy(t, stage, way, hops)
                    self.launch(t, copy, self.z == end)
            return
        self.take_credit(t, stage)
        event = (stage, 0, None)
        src = self.part(t, plan.kept[stage], plan.kept[stage - 1], block)
        dst = self.landing(t, event, block)
        self.launch(t, self.remote(t, event, block, src, dst, {DP: flip(self.d, dim)}))

    def step(self, t, event, finish):
        stage, way, at = event
        plan = self.plans[t]
        kept = plan.kept[stage]
        if way:
            block = self.z + way * at
            here = self.inside(block) & self.inside(self.z - way)
            if at > 0:
                self.take_credit(t, stage, way)

            @pl.when(here)
            def _():
                self.arrival(t, event, block).wait_recv()
                self.add(
                    self.part(t, 0, kept, block), self.landing(t, event, block),
                    kept * self.wides[t],
                )

            if at > 0:
                self.launch(t, self.line_copy(t, stage, way, at), here)
            else:
                self.brought[t] = self.brought.get(t, 0) + 1
                if self.brought[t] == 2:
                    self.advance(t, stage + 1, self.z, 0)
        else:
            if plan.full(stage):
                block = None if plan.merged else flip(self.z, at)
            else:
                block = self.z
            self.arrival(t, event, block).wait_recv()
            self.add(
                self.part(t, 0, kept, block), self.landing(t, event, block), kept * self.wides[t]
            )
            self.advance(t, stage + 1, block, at)
        self.left[t] -= 1
        self.left_stage[t, stage] -= 1
        if t < 4 and self.left_stage[t, stage] == 0:
            self.give_credit(t, stage)
        if self.left[t] == 0:
            finish(t)


def backward_kernel(
    plans, order, mp_size, layers, vector_count, gain_rows, shift_rows, *refs
):
    n = len(plans)
    full = [refs[4 * layer : 4 * layer + 4] for layer in range(layers)]
    at = 4 * layers
    cotangent, stream_low, vectors, doc_cols, doc_rows = refs[at : at + 5]
    at += 5
    saved = [refs[at + SAVED * layer : at + SAVED * (layer + 1)] for layer in range(layers)]
    at += SAVED * layers
    outs, (norm_ref, input_grad) = refs[at : at + n], refs[at + n : at + n + 2]
    stream_other, grad_other = refs[at + n + 2 : at + n + 4]
    at += n + 4
    sums = refs[at : at + 5]
    at += 5
    recv = {}
    for slab, plan in zip((0, 1, 2, 3, 4), plans[:4] + plans[8:]):
        for stage in range(1, len(plan.dims) + 1):
            recv[slab, stage] = refs[at]
            at += 1
    (
        blocks, left_t, turn_send, grad, acc, low, hidden_buf, w_a, w_b, normed,
        source, qkv, mixed, mixed_other, logs, mixed_grad, mixed_send, row_other, key_acc,
        value_acc, vector_sums, bias_sums, tiles,
        load_sems, core_sems, out_sems, tile_sems, send_sems, recv_sems, credit_sems,
        block_credit, left_credit,
    ) = refs[at:]
    cols = [out.shape[1] for out in outs]
    wides = [out.shape[0] for out in outs]
    work = RowsWork(plans, mp_size, wides, cols, sums, recv, (send_sems, recv_sems, credit_sems))
    z, d = work.z, work.d
    core = d % 2
    partner = {DP: flip(d, 1)}
    upper = [dim for dim in plans[0].dims if dim != MP]
    tokens, features = low.shape
    half = features // 2
    own_rows = pl.ds(place(core, tokens), tokens)
    other_rows = pl.ds(place(1 - core, tokens), tokens)
    half_qkv = qkv.shape[1]
    slots = mp_size // 2
    third = half_qkv // slots // 3
    heads_slot = third // HD
    wide = w_a.shape[2]
    per_block = cols[0] // wide

    across = {DP: flip(d, 1), MP: flip(z, 1)}
    moved = core != z % 2
    dp_size = 2 ** (len(upper) + 1)
    greet_all(z, d, dp_size, mp_size, across, moved)

    def trade(src, dst, at):
        return pltpu.make_async_remote_copy(
            src_ref=src, dst_ref=dst, send_sem=tile_sems.at[at], recv_sem=tile_sems.at[at + 1],
            device_id=across, device_id_type=MESH,
        )

    trades = [
        trade(stream_low, stream_other, 2 * (dp_size + mp_size) - 4),
        trade(low, grad_other, 2 * (dp_size + mp_size) - 2),
    ]
    pl.when(moved)(trades[0].start)

    loads = {}

    def fetch(key, src, dst):
        copy = pltpu.make_async_copy(src, dst, load_sems.at[len(loads)])
        copy.start()
        loads[key] = copy

    pushes = {}

    def push(key, src, dst):
        at = 2 * len(pushes)
        copy = pltpu.make_async_remote_copy(
            src_ref=src, dst_ref=dst, send_sem=core_sems.at[at], recv_sem=core_sems.at[at + 1],
            device_id=partner, device_id_type=MESH,
        )
        copy.start()
        pushes[key] = at, copy

    def pushed(key):
        pushes[key][1].wait_send()

    def arrived(key, dst):
        at = pushes[key][0]
        pltpu.make_async_remote_copy(
            src_ref=dst, dst_ref=dst, send_sem=core_sems.at[at], recv_sem=core_sems.at[at + 1],
            device_id=partner, device_id_type=MESH,
        ).wait_recv()

    def give(sem):
        pl.semaphore_signal(sem, inc=1, device_id=partner, device_id_type=MESH)

    fetch("cotangent", cotangent, low)
    vector_sums[...] = jnp.zeros_like(vector_sums)
    bias_sums[...] = jnp.zeros_like(bias_sums)

    def block_cols(at):
        block = flip(z, at // per_block)
        return pl.ds(pl.multiple_of(block * cols[0] + (at % per_block) * wide, wide), wide)

    def row_cols(at):
        count = half_qkv // wide
        part = core if at < count else 1 - core
        return pl.ds(pl.multiple_of(part * half_qkv + (at % count) * wide, wide), wide)

    def fetch_tile(layer, name, at):
        qkv_w, proj, up, down = full[layer]
        slot = at % 2
        if name == "hidden":
            where = block_cols(at)
            fetch((layer, "w_a", name, at), down.at[:, where], w_a.at[slot])
            fetch((layer, "w_b", name, at), up.at[:, where], w_b.at[slot])
            fetch((layer, "z", name, at), saved[layer][6].at[:, where], hidden_buf.at[slot])
        elif name == "mixed":
            first = place(1 - core if at == 0 else core, half)
            fetch((layer, "w_a", name, at), proj.at[:, pl.ds(first, half)], w_a.at[slot])
        else:
            fetch((layer, "w_b", name, at), qkv_w.at[:, row_cols(at)], w_b.at[slot])

    counts = {"hidden": mp_size * per_block, "mixed": 2, "rows": 2 * half_qkv // wide}

    def use_tile(layer, name, at):
        for which in ("w_a", "w_b", "z"):
            if (layer, which, name, at) in loads:
                loads[layer, which, name, at].wait()
        if at + 1 < counts[name]:
            fetch_tile(layer, name, at + 1)

    def fetch_block(layer, s):
        where = pl.ds(place(flip(z, s), cols[0]), cols[0])
        fetch((layer, "block", s), saved[layer][7].at[:, where], blocks.at[s % 2])

    def accumulate(left, weight, first):
        def piece(at, carry):
            rows = pl.ds(pl.multiple_of(at * TILE, TILE), TILE)
            values = dot_cols(left[...], weight[rows, :])
            if first:
                acc[:, rows] = values
            else:
                acc[:, rows] += values
            return carry

        lax.fori_loop(0, features // TILE, piece, 0)

    def put_vector(row, values):
        vector_sums[row : row + 1, :] = values

    def turn(use, src):
        slot = use % 2
        masks = plans[use].masks
        if use >= 2:
            pushed(("left", use - 2))
            pl.semaphore_wait(left_credit.at[slot], 1)
        for row, mask in enumerate(masks):
            there = pl.ds(row * wides[use], wides[use])
            theirs = pl.ds(place(flip(d, mask | 1), wides[use]), wides[use])
            mine = pl.ds(place(flip(d, mask), wides[use]), wides[use])
            turn_send[slot, there, :] = src[:, theirs].astype(f32).T.astype(bf16)
            left_t[slot, there, own_rows] = src[:, mine].astype(f32).T.astype(bf16)
        push(("left", use), turn_send.at[slot], left_t.at[slot, :, own_rows])

    def compute(layer, name):
        kind, _, at = name.partition("_")
        keeps = saved[layer]
        gain = layer * gain_rows
        shift = layers * gain_rows + layer * shift_rows
        last = layer == layers - 1
        use = 4 * (layers - 1 - layer)
        if name == "turn_down":
            if last:
                fetch_block(layer, 0)
                fetch_block(layer, 1)
                loads["cotangent"].wait()

                def some_rows(at, carry):
                    rows = pl.ds(pl.multiple_of(at * ROWS, ROWS), ROWS)
                    values = low[rows, :].astype(f32)
                    grad[rows, :] = values
                    return carry + jnp.sum(values, axis=0, keepdims=True)

                total = lax.fori_loop(
                    0, tokens // ROWS, some_rows, jnp.zeros((1, features), f32)
                )
                put_vector(shift + 2, total)
            else:
                pushed((layer + 1, "back"))
                pushed((layer + 1, "mixed"))
            fetch_tile(layer, "hidden", 0)
            fetch((layer, "normed_two"), keeps[5], normed)
            fetch((layer, "middle"), keeps[1], source)
            fetch((layer, "qkv"), keeps[3], qkv)
            fetch((layer, "mixed"), keeps[4], mixed)
            fetch((layer, "logs"), keeps[8], logs)
            push((layer, "mixed"), keeps[4], mixed_other)
            turn(use, low)
        elif name == "turn_up":
            loads[layer, "normed_two"].wait()
            turn(use + 1, normed)
            fetch((layer, "normed_one"), keeps[2], normed)
        elif name == "turn_proj":
            turn(use + 2, low)
        elif name == "turn_qkv":
            loads[layer, "normed_one"].wait()
            turn(use + 3, normed)
        elif kind == "hidden":
            at = int(at)
            use_tile(layer, "hidden", at)
            slot = at % 2
            s, inner = at // per_block, at % per_block
            to_block = s % 2
            if inner == 0 and s >= 2:
                pushed((layer, "grads", s - 2))

            def piece(first):
                here = pl.ds(first, TILE)
                values = dot(low[...], w_a[slot, :, here])
                values = values * gelu_slope(hidden_buf[slot, :, here].astype(f32))
                to = pl.multiple_of(flip(z, s) * cols[0] + inner * wide + first, TILE)
                bias_sums[vector_count + layer : vector_count + layer + 1, pl.ds(to, TILE)] = (
                    jnp.sum(values, axis=0, keepdims=True)
                )
                to = pl.ds(pl.multiple_of(inner * wide + first, TILE), TILE)
                blocks[to_block, own_rows, to] = values.astype(bf16)

            tiles_of(wide, piece)
            left = blocks.at[to_block, own_rows, pl.ds(inner * wide, wide)]
            accumulate(left, w_b.at[slot], at == 0)
            if inner == per_block - 1:
                pl.semaphore_wait(block_credit.at[s], 1)
                part = blocks.at[to_block, own_rows, :]
                push((layer, "grads", s), part, part)
        elif name == "norm_two":
            loads[layer, "middle"].wait()
            sums_of = norm_back(source, acc, grad, low, vectors[gain + 1 : gain + 2, :])
            put_vector(gain + 1, sums_of[0])
            put_vector(shift + 1, sums_of[1])
            fetch((layer, "stream"), keeps[0], source)
            fetch_tile(layer, "mixed", 0)
        elif kind == "mixed":
            at = int(at)
            use_tile(layer, "mixed", at)
            if at == 0 and not last:
                pushed((layer + 1, "share"))

            def piece(first):
                here = pl.ds(first, TILE)
                values = dot(low[...], w_a[at % 2, :, here]).astype(bf16)
                if at == 0:
                    mixed_send[:, here] = values
                else:
                    mixed_grad[own_rows, here] = values

            tiles_of(half, piece)
            if at == 0:
                push((layer, "share"), mixed_send, mixed_grad.at[own_rows, :])
        elif name == "share":
            arrived((layer, "share"), mixed_grad.at[other_rows, :])
            loads[layer, "qkv"].wait()
            loads[layer, "logs"].wait()
            fetch_tile(layer, "rows", 0)
        elif kind == "head":
            slot = int(at)
            if slot == 0 and layer > 0:
                pushed((layer, "grads", 2))
                pushed((layer, "grads", 3))
                fetch_block(layer - 1, 0)
                fetch_block(layer - 1, 1)

            def one_head(inner, carry):
                attend_back_head(
                    qkv, mixed, mixed_grad, logs, key_acc, value_acc, slot * heads_slot + inner,
                    slot * 3 * third + inner * HD, third,
                    head_slope(slot, inner, slots, heads_slot, core), doc_cols, doc_rows,
                )
                return carry

            lax.fori_loop(0, heads_slot, one_head, 0)
            if slot == slots - 1:
                push((layer, "back"), qkv, row_other)
        elif name == "back":
            arrived((layer, "back"), row_other)
        elif kind == "rows":
            at = int(at)
            use_tile(layer, "rows", at)
            count = half_qkv // wide
            here = pl.ds(at % count * wide, wide)
            left = (qkv if at < count else row_other).at[own_rows, here]
            accumulate(left, w_b.at[at % 2], at == 0)
        elif name == "norm_one":
            loads[layer, "stream"].wait()
            sums_of = norm_back(source, acc, grad, low, vectors[gain : gain + 1, :])
            put_vector(gain, sums_of[0])
            put_vector(shift, sums_of[1])
            if layer > 0:
                put_vector(shift - shift_rows + 2, sums_of[2])
            else:
                copy = pltpu.make_async_copy(grad, input_grad, out_sems.at[n])
                copy.start()
                loads["input_grad"] = copy
                pl.when(moved)(trades[1].start)

    def weight(t, s):
        slab = work.slab(t)
        out = sums[slab]
        if t == 8:
            for row, mask in enumerate(plans[t].masks):
                block = flip(d, mask)
                part = vector_sums[:, pl.ds(place(block, cols[t]), cols[t])]
                for m in range(mp_size):
                    first = pl.multiple_of(m * (bias_sums.shape[1] // mp_size) + block * cols[t], cols[t])
                    values = part + bias_sums[:, pl.ds(first, cols[t])]
                    rows = slice(row * wides[t], (row + 1) * wides[t])
                    out[rows, m * cols[t] : (m + 1) * cols[t]] = values.astype(bf16)
            work.advance(t, 1, None, 0)
            return
        layer = layers - 1 - t // 4
        if s == 0:
            if t >= 4:
                work.settle(t - 4)
                loads["out", t - 4].wait()
            arrived(("left", t), left_t.at[t % 2, :, other_rows])
        block = flip(z, s)
        left = left_t.at[t % 2]

        def multiply(right, first, step):
            step = 2 * step if cols[t] % (2 * step) == 0 else step

            def piece(at, carry):
                here = pl.multiple_of(at * step, step)
                there = pl.ds(pl.multiple_of(block * cols[t] + here, step), step)
                values = dot(left[...], right[:, pl.ds(pl.multiple_of(first + here, step), step)])
                out[:, there] = values.astype(bf16)
                return carry

            lax.fori_loop(0, cols[t] // step, piece, 0)

        if slab < 2:
            if slab == 0:
                loads[layer, "block", s].wait()
            else:
                arrived((layer, "grads", s), blocks.at[s % 2, other_rows, :])
            multiply(blocks.at[s % 2], 0, TILE)
            if slab == 0 and s < 2:
                fetch_block(layer, s + 2)
            elif slab == 0:
                give(block_credit.at[s - 2])
            elif s < 2:
                give(block_credit.at[s + 2])
        else:
            if slab == 2 and s == 0:
                loads[layer, "mixed"].wait()
                arrived((layer, "mixed"), mixed_other)
            ours = block // slots == core
            within = pl.multiple_of((block % slots) * cols[t], cols[t])
            near, far = ((mixed, mixed_other), (qkv, row_other))[slab - 2]
            pl.when(ours)(lambda: multiply(near, within, TILE))
            pl.when(jnp.logical_not(ours))(lambda: multiply(far, within, TILE))
        if s == mp_size - 1 and t < 6:
            give(left_credit.at[t % 2])
        work.advance(t, 1, block, s)

    def finish(t):
        final = work.part(t, 0, 1, z)
        copy = pltpu.make_async_copy(final, outs[t], out_sems.at[t])
        copy.start()
        loads["out", t] = copy
        step = 16

        def some_rows(at, carry):
            rows = pl.ds(pl.multiple_of(at * step, step), step)
            part = final[rows, :].astype(f32)
            part = part * part
            if t == 8:
                row = at * step + lax.broadcasted_iota(jnp.int32, part.shape, 0)
                part = jnp.where(row < vector_count, part * (1.0 / mp_size), part)
            total = carry
            for top in range(0, step, 8):
                for side in range(0, cols[t], HD):
                    total = total + part[top : top + 8, side : side + HD]
            return total

        tiles[0] += lax.fori_loop(0, wides[t] // step, some_rows, jnp.zeros((8, HD), f32))

    tiles[0] = jnp.zeros(tiles.shape[1:], f32)
    for step in order:
        if step[0] == "weight":
            weight(*step[1:])
        elif isinstance(step[1], str):
            compute(*step)
        else:
            work.step(*step, finish)

    first = 0
    sem = 0
    for axis, me, size in ((DP, d, dp_size), (MP, z, mp_size)):
        copies = []
        for mask in range(1, size):
            copies.append(
                pltpu.make_async_remote_copy(
                    src_ref=tiles.at[first],
                    dst_ref=tiles.at[first + mask],
                    send_sem=tile_sems.at[sem],
                    recv_sem=tile_sems.at[sem + 1],
                    device_id={axis: flip(me, mask)},
                    device_id_type=MESH,
                )
            )
            sem += 2
        for copy in copies:
            copy.start()
        for copy in copies:
            copy.wait()
        total = tiles[first + flip_by(me, 0, size)]
        for at in range(1, size):
            total = total + tiles[first + flip_by(me, at, size)]
        first += size
        tiles[first] = total
    norm_ref[...] = tiles[first]

    for s in (2, 3):
        pushed((0, "grads", s))
    for key in ((0, "mixed"), (0, "share"), (0, "back"), ("left", 6), ("left", 7)):
        pushed(key)
    for t in range(n):
        work.settle(t)
        if t >= 4:
            loads["out", t].wait()
    loads["input_grad"].wait()
    for copy in trades:
        pl.when(moved)(copy.wait)


def backward_chain(plans, layers):
    chain = []
    for done, layer in enumerate(reversed(range(layers))):
        turns = {"turn_down": 0, "turn_up": 1, "turn_proj": 2, "back": 3}
        t = None
        for name in BACKWARD_STEPS:
            if name.startswith("W"):
                chain.append(("weight", t, int(name[1:])))
                continue
            chain.append((layer, name))
            if name in turns:
                t = 4 * done + turns[name]
            if name == "norm_one" and layer == 0:
                chain.append(("weight", len(plans) - 1, 0))
    return chain


def backward_order(plans, layers, table):
    chain = backward_chain(plans, layers)
    if not table:
        out = []
        for at, step in enumerate(chain):
            out.append(step)
            if step[0] == "weight" and (step[1] == 8 or step[2] == 3):
                out += [(step[1], event) for event in plans[step[1]].events]
        return out
    steps = chain + [(t, event) for t, plan in enumerate(plans) for event in plan.events]
    return [steps[at] for at in table]


def backward_all(
    full, cotangent, stream_low, vectors, docs, stored, plans, order, dp_size, mp_size, layers, vector_count,
    gain_rows, shift_rows,
):
    n = len(plans)
    _, total = number_rows(plans, mp_size)
    tokens, features = cotangent.shape
    length = docs.shape[0]
    units = full[2].shape[1]
    wides = [features // dp_size] * 8 + [vectors.shape[0]]
    cols = [
        full[4 * layer + kind].shape[1] // mp_size
        for layer in reversed(range(layers))
        for kind in (3, 2, 1, 0)
    ] + [max(HD, features // dp_size)]
    half_qkv = full[0].shape[1] // 2
    any_place = pl.BlockSpec(memory_space=pl.ANY)
    vmem = pl.BlockSpec(memory_space=pltpu.VMEM)
    out_shape = [jax.ShapeDtypeStruct((wide, each), bf16) for wide, each in zip(wides, cols)]
    out_shape += [
        jax.ShapeDtypeStruct((8, HD), f32),
        jax.ShapeDtypeStruct((tokens, features), f32),
        jax.ShapeDtypeStruct((tokens, features), bf16),
        jax.ShapeDtypeStruct((tokens, features), bf16),
    ]
    slabs = (0, 1, 2, 3, 8)
    scratch = [
        pltpu.VMEM((plans[t].kept[0] * wides[t], mp_size * cols[t]), bf16) for t in slabs
    ]
    for t in slabs:
        plan = plans[t]
        for stage, dim in enumerate(plan.dims, 1):
            rows = plan.kept[stage] * wides[t]
            if dim == MP:
                shape = (mp_size + 1, rows, cols[t])
            elif not plan.full(stage):
                shape = (1, rows, cols[t])
            elif plan.merged:
                shape = (1, rows, mp_size * cols[t])
            else:
                shape = (mp_size, rows, cols[t])
            scratch.append(pltpu.VMEM(shape, bf16))
    wide = 512
    scratch += [
        pltpu.VMEM((2, length, cols[0]), bf16),
        pltpu.VMEM((2, features // 2, length), bf16),
        pltpu.VMEM((2, features // 2, tokens), bf16),
        pltpu.VMEM((tokens, features), f32),
        pltpu.VMEM((tokens, features), f32),
        pltpu.VMEM((tokens, features), bf16),
        pltpu.VMEM((2, tokens, wide), bf16),
        pltpu.VMEM((2, features, wide), bf16),
        pltpu.VMEM((2, features, wide), bf16),
        pltpu.VMEM((tokens, features), bf16),
        pltpu.VMEM((tokens, features), bf16),
        pltpu.VMEM((length, half_qkv), bf16),
        pltpu.VMEM((length, features // 2), bf16),
        pltpu.VMEM((length, features // 2), bf16),
        pltpu.VMEM((length, HD), f32),
        pltpu.VMEM((length, features // 2), bf16),
        pltpu.VMEM((tokens, features // 2), bf16),
        pltpu.VMEM((length, half_qkv), bf16),
        pltpu.VMEM((length, HD), f32),
        pltpu.VMEM((length, HD), f32),
        pltpu.VMEM((wides[8], features), f32),
        pltpu.VMEM((wides[8], units), f32),
        pltpu.VMEM((dp_size + mp_size + 1, 8, HD), f32),
        pltpu.SemaphoreType.DMA((110,)),
        pltpu.SemaphoreType.DMA((2 * 11 * layers,)),
        pltpu.SemaphoreType.DMA((n + 1,)),
        pltpu.SemaphoreType.DMA((2 * (dp_size + mp_size),)),
        pltpu.SemaphoreType.DMA((total,)),
        pltpu.SemaphoreType.DMA((total,)),
        pltpu.SemaphoreType.REGULAR((4, len(plans[0].dims) + 1, 2)),
        pltpu.SemaphoreType.REGULAR((mp_size,)),
        pltpu.SemaphoreType.REGULAR((2,)),
    ]
    operands = list(full[: 4 * layers]) + [cotangent, stream_low, vectors]
    operands += [docs.reshape(-1, 1), docs.reshape(1, -1)]
    specs = [any_place] * (4 * layers + 2) + [vmem] * 3
    for each in stored:
        operands += each
        specs += [any_place] * SAVED
    out = pl.pallas_call(
        functools.partial(
            backward_kernel, plans, order, mp_size, layers, vector_count, gain_rows, shift_rows
        ),
        out_shape=out_shape,
        in_specs=specs,
        out_specs=[any_place] * n + [vmem] + [any_place] * 3,
        scratch_shapes=scratch,
        compiler_params=pltpu.CompilerParams(
            collective_id=1, has_side_effects=True, vmem_limit_bytes=63 * 2**20
        ),
    )(*operands)
    return list(out[:n]), *out[n:]


forward_table = (
    95, 1, 23, 116, 0, 22, 188, 189, 3, 191, 71, 94, 97, 24, 25, 190, 2, 70, 192, 26, 193, 198, 5,
    73, 96, 4, 11, 10, 118, 117, 99, 27, 7, 199, 98, 197, 194, 6, 72, 29, 69, 196, 195, 201, 119,
    9, 8, 200, 101, 28, 75, 46, 45, 13, 207, 44, 32, 12, 107, 120, 202, 74, 30, 100, 105, 103, 47,
    112, 206, 208, 19, 14, 203, 104, 31, 106, 34, 35, 121, 83, 51, 48, 205, 204, 77, 17, 128, 76,
    15, 41, 20, 18, 16, 209, 49, 210, 21, 33, 52, 50, 57, 102, 84, 42, 82, 211, 212, 53, 213, 126,
    78, 214, 37, 54, 129, 215, 36, 216, 79, 38, 55, 58, 108, 56, 40, 164, 114, 217, 66, 134, 127,
    122, 80, 140, 39, 61, 165, 139, 81, 218, 124, 123, 85, 136, 43, 59, 109, 219, 60, 111, 138,
    86, 163, 62, 113, 91, 90, 65, 142, 125, 141, 92, 167, 166, 87, 64, 63, 220, 135, 110, 130, 67,
    145, 68, 221, 222, 223, 88, 115, 224, 225, 226, 146, 227, 228, 229, 89, 171, 144, 170, 230,
    231, 168, 93, 143, 151, 232, 233, 152, 234, 169, 176, 148, 147, 235, 236, 133, 172, 237, 153,
    159, 149, 154, 173, 150, 238, 239, 178, 240, 155, 157, 174, 179, 132, 184, 131, 156, 158, 175,
    160, 161, 241, 137, 180, 242, 243, 162, 182, 244, 185, 183, 245, 177, 181, 246, 247, 248, 249,
    187, 250, 251, 186, 252, 253, 254, 255,
)
backward_table = (
    0, 1, 2, 3, 4, 5, 6, 7, 8, 9, 10, 11, 12, 13, 14, 15, 16, 17, 87, 18, 19, 20, 21, 85, 96, 22,
    23, 88, 24, 25, 26, 27, 28, 29, 86, 90, 108, 30, 89, 109, 31, 32, 99, 110, 107, 33, 34, 35,
    111, 98, 92, 91, 36, 97, 37, 113, 38, 100, 114, 101, 122, 93, 121, 112, 103, 102, 125, 39,
    123, 40, 126, 94, 41, 124, 127, 42, 104, 105, 95, 43, 115, 44, 45, 46, 47, 116, 106, 48, 49,
    50, 51, 52, 128, 53, 54, 55, 136, 56, 117, 129, 57, 118, 58, 130, 59, 60, 61, 62, 131, 63,
    120, 132, 119, 137, 64, 65, 66, 67, 68, 69, 138, 70, 71, 135, 146, 72, 133, 73, 74, 134, 140,
    149, 139, 157, 75, 76, 77, 148, 147, 151, 141, 171, 150, 142, 78, 79, 159, 172, 80, 175, 158,
    81, 82, 153, 83, 173, 160, 84, 161, 152, 185, 177, 174, 163, 144, 162, 164, 186, 178, 165,
    154, 187, 143, 176, 166, 167, 180, 189, 179, 168, 155, 188, 181, 182, 170, 190, 145, 191, 169,
    156, 183, 192, 184, 193,
)


def program(dp_size, mp_size, args):
    (
        inputs, documents, cotangent,
        qkv_weight, qkv_moment, qkv_square,
        proj_weight, proj_moment, proj_square,
        upper_weight, upper_moment, upper_square,
        lower_weight, lower_moment, lower_square,
        hidden_bias, bias_moment, bias_square,
        norm_gains, gains_moment, gains_square,
        shift_params, shifts_moment, shifts_square,
    ) = args
    layers = qkv_weight.shape[0]
    tokens, features = inputs.shape
    length = documents.shape[1]
    pieces = length // tokens
    slots = mp_size // pieces
    wide = features // dp_size
    z_cols = qkv_weight.shape[3]
    heads_slot = z_cols // HD
    me_dp = lax.axis_index(DP)
    me_mp = lax.axis_index(MP)
    core = me_dp % 2

    def swap(values):
        return lax.ppermute(values, DP, [(at, at ^ 1) for at in range(dp_size)])

    def by_core(own, other, axis):
        first = jnp.where(core == 0, own, other)
        second = jnp.where(core == 0, other, own)
        return jnp.concatenate([first, second], axis=axis)

    paired = pieces == 2 and dp_size % 2 == 0 and mp_size % 2 == 0
    if paired:
        moved = core != me_mp % 2
        doc_rows = jnp.where(moved, swap(documents), documents)
        docs = lax.dynamic_index_in_dim(doc_rows, me_mp // 2, 0, False)

        def share_heads(values):
            half = values.shape[1] // 2
            own = lax.dynamic_slice_in_dim(values, core * half, half, 1)
            sent = lax.dynamic_slice_in_dim(values, (1 - core) * half, half, 1)
            return by_core(own, swap(sent), 0)

        def return_heads(values):
            own = lax.dynamic_slice_in_dim(values, core * tokens, tokens, 0)
            sent = lax.dynamic_slice_in_dim(values, (1 - core) * tokens, tokens, 0)
            return by_core(own, swap(sent), 1)

        first_slot = core * slots
    else:
        groups = [list(range(g * pieces, (g + 1) * pieces)) for g in range(mp_size // pieces)]

        docs = lax.dynamic_index_in_dim(documents, me_mp // pieces, 0, False)

        def share_heads(values):
            return lax.all_to_all(values, MP, 1, 0, axis_index_groups=groups, tiled=True)

        def return_heads(values):
            return lax.all_to_all(values, MP, 0, 1, axis_index_groups=groups, tiled=True)

        moved = False
        first_slot = (me_mp % pieces) * slots
    slope_table = jnp.asarray(0.5 ** (np.arange(H) + 1.0), dtype=f32)
    slopes = lax.dynamic_slice_in_dim(
        slope_table, first_slot * heads_slot, slots * heads_slot
    )

    bits = bits_of(dp_size)[1:]
    line_first = [(MP, *bits), (MP, *bits[::-1])]
    line_second = [(bits[0], MP, *bits[1:]), (bits[-1], MP, *bits[:-1][::-1])]

    gain_rows = norm_gains.shape[1]
    shift_rows = shift_params.shape[1]
    vector_count = layers * (gain_rows + shift_rows)
    bias_wide = hidden_bias.shape[1]
    lanes = max(wide, HD)
    small_rows = -(-(vector_count + layers) // 16) * 16

    def padded(values):
        return jnp.pad(values, [(0, 0)] * (values.ndim - 1) + [(0, lanes - values.shape[-1])])

    spreads = []
    for layer in range(layers):
        spreads += line_first[:: 1 if layer % 2 == 0 else -1] + line_second
    spreads.append(line_first[0])
    qkv_by_part = qkv_weight.transpose(0, 2, 1, 3)
    if paired and wide == lanes and bias_wide == lanes:
        shards = prepare_all(
            [
                qkv_by_part, proj_weight, upper_weight, lower_weight, norm_gains,
                shift_params.transpose(1, 0, 2), hidden_bias,
            ],
            small_rows,
        )
    else:
        small = jnp.concatenate(
            [
                padded(norm_gains.reshape(-1, wide)),
                padded(shift_params.reshape(-1, wide)),
                padded(hidden_bias),
                jnp.zeros((small_rows - vector_count - layers, lanes), f32),
            ],
            axis=0,
        ).astype(bf16)
        shards = []
        for layer in range(layers):
            shards += [
                qkv_weight[layer].astype(bf16).reshape(wide, 3 * z_cols),
                proj_weight[layer].astype(bf16).T,
                upper_weight[layer].astype(bf16),
                lower_weight[layer].astype(bf16).T,
            ]
        shards.append(small)
    spreads = [Spread(dims, mp_size) for dims in spreads]
    tabled = dp_size == 8 and mp_size == 4 and layers == 2
    if paired:
        spread_order = forward_order(spreads, layers, forward_table if tabled else ())
        full, stored, stream, stream_low, cotangent, vectors = forward_all(
            shards, inputs, cotangent, docs, spreads, spread_order, dp_size, mp_size, layers,
            vector_count, gain_rows, shift_rows,
        )
    else:
        spread_order = step_order(spreads, (), lambda t, stage: t // 2 + stage)
        full = spread_all(shards, spreads, spread_order, dp_size, mp_size)
    if not paired:
        small_all = full[-1].reshape(dp_size, small_rows, mp_size, lanes).astype(f32)
        vectors = small_all[:, :vector_count, 0, :wide].transpose(1, 0, 2)
        vectors = vectors.reshape(vector_count, features)
        gains = vectors[: layers * gain_rows].reshape(layers, gain_rows, features)
        shifts = vectors[layers * gain_rows :].reshape(layers, shift_rows, features)
        biases = small_all[:, vector_count : vector_count + layers, :, :bias_wide]
        biases = biases.transpose(1, 2, 0, 3).reshape(layers, -1)
        stream = inputs.astype(f32)
        stored = []
        for layer in range(layers):
            qkv_w, proj_w, upper_w, lower_w = full[4 * layer : 4 * layer + 4]
            normed = layer_norm(stream, gains[layer, 0], shifts[layer, 0]).astype(bf16)
            qkv = share_heads(dot(normed, qkv_w).astype(bf16))
            mixed = attend(slopes, docs, qkv, slots)
            attended = return_heads(mixed)
            middle = stream + dot_cols(attended, proj_w)
            normed_two = layer_norm(middle, gains[layer, 1], shifts[layer, 1]).astype(bf16)
            hidden = dot(normed_two, upper_w) + biases[layer]
            active = gelu_tanh(hidden).astype(bf16)
            stored.append(
                (stream, middle, normed, qkv, mixed, attended, normed_two, hidden, active)
            )
            stream = middle + dot_cols(active, lower_w) + shifts[layer, 2]
    output_stream = stream

    ways = []
    for layer in reversed(range(layers)):
        ways += fold_dims(line_first, line_second, layer)
    ways.append(line_first[0][::-1])
    if paired:
        ways[-1] = (1,) + ways[-1]
        folds = [Rows(dims, mp_size, at == 8) for at, dims in enumerate(ways)]
        fold_order = backward_order(folds, layers, backward_table if tabled else ())
        owned, norm_tile, input_grad, stream_other, grad_other = backward_all(
            full, cotangent, stream_low, vectors, docs, stored, folds, fold_order, dp_size, mp_size, layers,
            vector_count, gain_rows, shift_rows,
        )
    else:
        grad_stream = cotangent.astype(f32)
        weight_grads = [None] * layers
        vector_grads = [None] * layers
        bias_grads = [None] * layers
        no_shift = jnp.zeros((features,), f32)
        for layer in reversed(range(layers)):
            qkv_w, proj_w, upper_w, lower_w = full[4 * layer : 4 * layer + 4]
            stream_in, middle, normed, qkv, mixed, attended, normed_two, hidden, active = stored[layer]
            out_shift_grad = jnp.sum(grad_stream, axis=0)
            grad_low = grad_stream.astype(bf16)
            active_grad = dot(grad_low, lower_w)
            _, pull_gelu = jax.vjp(gelu_tanh, hidden.astype(f32))
            hidden_grad = pull_gelu(active_grad)[0].astype(bf16)
            lower_grad = dot_rows(grad_low, active).astype(bf16)
            upper_grad = dot_rows(normed_two, hidden_grad).astype(bf16)
            bias_grads[layer] = jnp.sum(hidden_grad, axis=0, dtype=f32)
            normed_two_grad = dot_cols(hidden_grad, upper_w)
            _, pull_two = jax.vjp(layer_norm, middle, gains[layer, 1], no_shift)
            middle_part, gain_two, shift_two = pull_two(normed_two_grad)
            middle_grad = grad_stream + middle_part
            middle_low = middle_grad.astype(bf16)
            mixed_grad = share_heads(dot(middle_low, proj_w).astype(bf16))
            proj_grad = dot_rows(middle_low, attended).astype(bf16)
            qkv_grad = return_heads(attend_back(slopes, docs, qkv, mixed, mixed_grad, slots))
            normed_grad = dot_cols(qkv_grad, qkv_w)
            qkv_weight_grad = dot_rows(normed, qkv_grad).astype(bf16)
            _, pull_one = jax.vjp(layer_norm, stream_in, gains[layer, 0], no_shift)
            stream_part, gain_one, shift_one = pull_one(normed_grad)
            grad_stream = middle_grad + stream_part
            weight_grads[layer] = (lower_grad, upper_grad, proj_grad, qkv_weight_grad)
            vector_grads[layer] = (
                jnp.stack([gain_one, gain_two]),
                jnp.stack([shift_one, shift_two, out_shift_grad]),
            )
        input_grad = grad_stream

        vector_sums = jnp.concatenate(
            [jnp.concatenate([vector_grads[at][kind] for at in range(layers)]) for kind in (0, 1)]
        )
        vector_sums = padded(vector_sums.reshape(vector_count, dp_size, wide)).transpose(1, 0, 2)
        vector_sums = jnp.broadcast_to(
            vector_sums[:, :, None], (dp_size, vector_count, mp_size, lanes)
        )
        bias_sums = padded(jnp.stack(bias_grads).reshape(layers, mp_size, dp_size, bias_wide))
        bias_sums = bias_sums.transpose(2, 0, 1, 3)
        rest = jnp.zeros((dp_size, small_rows - vector_count - layers, mp_size, lanes), f32)
        small_grad = jnp.concatenate([vector_sums, bias_sums, rest], axis=1)
        small_grad = small_grad.reshape(dp_size * small_rows, mp_size * lanes).astype(bf16)

        local = []
        for layer in reversed(range(layers)):
            local += weight_grads[layer]
        local.append(small_grad)
        folds = [Fold(dims, mp_size) for dims in ways]
        fold_order = step_order(folds, (), lambda t, stage: t // 2 + stage)
        owned, norm_tile = fold_all(local, folds, fold_order, dp_size, mp_size, vector_count)
    small_owned = owned.pop()

    def by_row(values):
        return values.transpose(1, 0, 2)

    states = [qkv_by_part, qkv_moment.transpose(0, 2, 1, 3), qkv_square.transpose(0, 2, 1, 3)]
    states += [
        proj_weight, proj_moment, proj_square, upper_weight, upper_moment, upper_square,
        lower_weight, lower_moment, lower_square,
    ]
    ordered = [owned[4 * layer + kind] for kind in (3, 2, 1, 0) for layer in range(layers)]
    small_states = [
        hidden_bias, bias_moment, bias_square, norm_gains, gains_moment, gains_square,
        by_row(shift_params), by_row(shifts_moment), by_row(shifts_square),
    ]
    if wide < lanes or bias_wide < lanes:
        small_states = [padded(each) for each in small_states]
    streams = [output_stream, stream_other, input_grad, grad_other] if paired else []
    results = list(
        adam_all(
            ordered, states, small_owned, norm_tile, small_states, streams, vector_count, gain_rows
        )
    )
    if paired:
        output_stream, input_grad = results[22:]
    grad_norm = results[21][0, 0]
    results[:3] = [each.transpose(0, 2, 1, 3) for each in results[:3]]
    results[18:21] = [by_row(each) for each in results[18:21]]
    results[12:15] = [each[:, :bias_wide] for each in results[12:15]]
    results[15:21] = [each[:, :, :wide] for each in results[15:21]]
    return (output_stream, input_grad, *results[:21], grad_norm)


def fold_dims(line_first, line_second, layer):
    first = [dims[::-1] for dims in line_first]
    second = [dims[::-1] for dims in line_second]
    return second + (first if layer % 2 else first[::-1])


def solution(mesh):
    dp_size = mesh.shape[DP]
    mp_size = mesh.shape[MP]
    rows = P((DP, MP), None)
    split_rows = P(None, DP, None, MP)
    split_upper = P(None, DP, MP)
    split_lower = P(None, MP, DP)
    split_bias = P(None, (MP, DP))
    split_vector = P(None, None, DP)
    groups = (
        split_rows, split_lower, split_upper, split_lower, split_bias, split_vector, split_vector
    )
    placed = tuple(spec for spec in groups for _ in range(3))

    def shards(*args):
        return program(dp_size, mp_size, args)

    return jax.shard_map(
        shards,
        mesh=mesh,
        in_specs=(rows, P(DP, None), rows) + placed,
        out_specs=(rows, rows) + placed + (P(),),
        check_vma=False,
    )
```
